32 devices in a mesh: dp: 4 (over y, core), expert: 8 (over z, x).
Axes of the slice: x: 2, y: 2, z: 4, core: 2. Of those that a mesh axis runs over, the one named last changes fastest.
Arguments:
- tokens: bfloat16 [4096, 2560], P(('dp', 'expert')), may hold values from -6 to 6
- cotangent: bfloat16 [4096, 2560], P(('dp', 'expert')), may hold values from -6 to 6
- routes: int32 [4096, 1], P(('dp', 'expert')), may hold values from 0 to 7; in each aligned block of 128 rows (0 to 127, 128 to 255, ...) at most 24 rows name the same one
- gates: float32 [4096, 1], P(('dp', 'expert')), may hold values from 0.25 to 1
- hot_index: int32 [512], P(('dp', 'expert')), may hold values from 0 to 127, as said below
- hot_gate: float32 [512], P(('dp', 'expert')), may hold values from 0.25 to 1
- w_gate_up: bfloat16 [8, 2560, 1536], P('expert', 'dp'), may hold values from -0.125 to 0.125
- w_down: bfloat16 [8, 768, 2560], P('expert', 'dp'), may hold values from -0.21875 to 0.21875
- w_hot_gu: bfloat16 [2, 768, 2560], P(None, 'dp', 'expert'), may hold values from -0.125 to 0.125
- w_hot_dn: bfloat16 [768, 2560], P('dp', 'expert'), may hold values from -0.21875 to 0.21875
Outputs:
- layer_out: bfloat16 [4096, 2560], P(('dp', 'expert'))
- input_grad: bfloat16 [4096, 2560], P(('dp', 'expert'))
- grad_gate_up: bfloat16 [8, 2560, 1536], P('expert', 'dp')
- grad_down: bfloat16 [8, 768, 2560], P('expert', 'dp')
- grad_hot_gu: bfloat16 [2, 768, 2560], P(None, 'dp', 'expert')
- grad_hot_dn: bfloat16 [768, 2560], P('dp', 'expert')
The draws below stay inside these ranges and needn't reach their ends.
Inputs may be any that keep to these rules, and one draw needn't show every extreme that they name: `routes`: each token names 1 different routed experts; the tokens of one device name any one routed expert at most 24 times, some expert exactly 24 times. `hot_index`: the 16 entries of one device name different tokens of that device, by their index within the device.
All inputs are finite; a program needn't handle non-finite values.
Results may differ from the reference program's by a relative error of at most 0.018.
Values may be sent and summed in bfloat16 or wider, within the bound.
No kernel may reach another device: no remote copies, remote signals or barrier semaphores. Data moves between devices by JAX's collectives and lax.ppermute only.
A program may use at most 128 MiB of HBM per device.

```python
import math
import jax
import jax.numpy as jnp
import numpy as np
from jax import lax

D = 2560
H = 768
TOPK = 1
TOK_DEV = 128
HOT_DEV = 16
EXPERTS = 8
CAP = 24
GRAD_DIV = 16
TOKENS = 4096
TOKENS_HOT = 512
N_DP = 4
N_EXPERT = 8


def draw_hot_index(key, part):
    blocks = TOKENS // TOK_DEV
    keys = jax.random.split(key, blocks)
    picks = jax.vmap(lambda one: jax.random.permutation(one, TOK_DEV)[:HOT_DEV])(keys)
    return picks.reshape(-1).astype(jnp.int32)


def block_scale(stream_key, extent, cuts, low, top_value):
    def one(dim, blocks):
        heights = jax.random.uniform(jax.random.fold_in(jax.random.fold_in(stream_key, 6), dim), (blocks,), jnp.float32, low / len(cuts), top_value / len(cuts))
        return jnp.repeat(jnp.exp(heights), extent[dim] // blocks).reshape((-1,) + (1,) * (len(extent) - dim - 1))

    gain = one(*cuts[0])
    for cut in cuts[1:]:
        gain = gain * one(*cut)
    return gain


def assign_block(stream_key, own, number, rows, amount, top, reach, slope):
    sequence = jax.random.permutation(stream_key, amount)
    packed, common = portions_of(amount, rows * top, reach, slope, True), portions_of(amount, rows * top, reach, slope, False)
    places = jnp.arange(amount)

    def named(lengths, rotation):
        used = int((lengths > 0).sum())
        fixed = max(1, used // 4)
        passed = fixed + (places - fixed + rotation * (used - fixed)) % max(1, amount - fixed)
        return jnp.zeros((amount,), jnp.int32).at[sequence[jnp.where(places < fixed, places, passed)]].set(jnp.asarray(lengths, jnp.int32))

    lengths = jnp.where(number % 4 == 0, named(packed, number // 4), named(common, number - number // 4 - 1))
    mixed = jax.random.permutation(jax.random.fold_in(own, 3), amount)
    giver, sink = mixed[0:amount // 2 * 2:2], mixed[1:amount // 2 * 2:2]
    room = jnp.minimum(lengths[giver] - 1, reach - lengths[sink]) // 2
    room = jnp.where((giver == sequence[0]) | (sink == sequence[0]) | (lengths[sink] == 0), 0, jnp.maximum(room, 0))
    passed = jax.random.randint(jax.random.fold_in(own, 4), (amount // 2,), 0, 1 << 20) % (room + 1)
    lengths = lengths.at[giver].add(-passed).at[sink].add(passed)
    items = jnp.searchsorted(jnp.cumsum(lengths), jnp.arange(rows * top), side="right").astype(jnp.int32)
    table = items.reshape(top, rows).T
    table = table[jax.random.permutation(jax.random.fold_in(own, 1), rows)]
    rotation = jax.random.randint(jax.random.fold_in(own, 2), (rows, 1), 0, top)
    return jnp.take_along_axis(table, (jnp.arange(top)[None, :] + rotation) % top, axis=1)


def portions_of(count, total, limit, slope, full):
    portions = [(1 << 20) // math.isqrt(standing ** slope) + 1 for standing in range(1, count + 1)]
    largest = limit if full else min(limit, max(-(-total // count), total * portions[0] // sum(portions)))
    least = 1 if total - largest >= count - 1 else 0
    counts, surplus = [largest] + [least] * (count - 1), total - largest - least * (count - 1)
    while surplus > 0:
        movable = [i for i in range(1, count) if counts[i] < largest] or [i for i in range(1, count) if counts[i] < limit]
        pool, budget = sum([portions[i] for i in movable]), surplus
        for i in movable:
            more = min(limit - counts[i], max(1, budget * portions[i] // pool), surplus)
            counts[i] = counts[i] + more
            surplus = surplus - more
    return np.array(counts)


def centred(key, extent, scale, reach, cuts=(), kind=jnp.bfloat16):
    values = scale * jax.random.normal(key, extent, jnp.float32)
    if cuts:
        values = values * block_scale(key, extent, cuts, -0.22, 0.18)
    return jnp.clip(values, -reach, reach).astype(kind)


def setup_inputs(seed: int = 0) -> dict:
    key_of = jax.random.split(jax.random.key(seed), 11)
    tokens = centred(key_of[0], (TOKENS, D), 1.0, 6.0, ((0, 32),))
    cotangent = centred(key_of[1], (TOKENS, D), 1.0, 6.0, ((0, 32),))
    routes_keys = jax.random.split(jax.random.fold_in(key_of[2], 1), TOKENS // TOK_DEV)
    routes_turns = jax.random.permutation(jax.random.fold_in(key_of[2], 3), TOKENS // TOK_DEV)
    routes = jax.vmap(lambda own, number: assign_block(jax.random.fold_in(key_of[2], 2), own, number, TOK_DEV, EXPERTS, TOPK, CAP, 2))(routes_keys, routes_turns).reshape((TOKENS, TOPK))
    gates = jnp.clip(0.25 + 0.75 * jax.random.uniform(key_of[3], (TOKENS, TOPK), jnp.float32) ** block_scale(key_of[3], (TOKENS, TOPK), ((0, 32),), -0.2, 0.2), 0.25, 1.0)
    hot_index = draw_hot_index(jax.random.fold_in(key_of[10], 71), 0)
    hot_gate = jnp.clip(0.25 + 0.75 * jax.random.uniform(key_of[5], (TOKENS_HOT,), jnp.float32) ** block_scale(key_of[5], (TOKENS_HOT,), ((0, 32),), -0.2, 0.2), 0.25, 1.0)
    w_gate_up = centred(key_of[6], (EXPERTS, D, 2 * H), D ** -0.5, 0.125, ((0, 8), (1, 4)))
    w_down = centred(key_of[7], (EXPERTS, H, D), H ** -0.5, 0.21875, ((0, 8), (1, 4)))
    w_hot_gu = centred(key_of[8], (2, H, D), D ** -0.5, 0.125, ((1, 4), (2, 8)))
    w_hot_dn = centred(key_of[9], (H, D), H ** -0.5, 0.21875, ((0, 4), (1, 8)))
    return {"tokens": tokens, "cotangent": cotangent, "routes": routes, "gates": gates, "hot_index": hot_index, "hot_gate": hot_gate, "w_gate_up": w_gate_up, "w_down": w_down, "w_hot_gu": w_hot_gu, "w_hot_dn": w_hot_dn}


def slot_positions(route_block, count):
    flat = route_block.reshape(-1).astype(jnp.int32)
    onehot = (flat[:, None] == jnp.arange(count, dtype=jnp.int32)[None, :]).astype(jnp.int32)
    before = jnp.cumsum(onehot, axis=0) - onehot
    return flat, jnp.sum(before * onehot, axis=1).astype(jnp.int32)


def expert_forward(rows_x, w_gu):
    width = w_gu.shape[1] // 2
    act = jnp.dot(rows_x, w_gu, preferred_element_type=jnp.float32)
    gate_part = act[:, :width]
    up_part = act[:, width:]
    hidden = (gate_part * jax.nn.sigmoid(gate_part) * up_part).astype(jnp.bfloat16)
    return act, hidden


def expert_output(hidden, w_dn):
    return jnp.dot(hidden, w_dn, preferred_element_type=jnp.float32).astype(jnp.bfloat16)


def expert_delta(scaled_rows, act, w_gu, w_dn):
    width = w_gu.shape[1] // 2
    gate_part = act[:, :width]
    up_part = act[:, width:]
    sigma = jax.nn.sigmoid(gate_part)
    d_hidden = lax.dot_general(scaled_rows, w_dn, (((1,), (1,)), ((), ())), preferred_element_type=jnp.float32)
    d_gate = d_hidden * up_part * sigma * (1.0 + gate_part * (1.0 - sigma))
    d_up = d_hidden * gate_part * sigma
    d_act = jnp.concatenate([d_gate, d_up], axis=1).astype(jnp.bfloat16)
    d_rows = lax.dot_general(d_act, w_gu, (((1,), (1,)), ((), ())), preferred_element_type=jnp.float32).astype(jnp.bfloat16)
    return d_act, d_rows


def popular_expert(tokens, cotangent, hot_index, hot_gate, w_hot_gu, w_hot_dn):
    blocks = N_DP * N_EXPERT
    local = hot_index.reshape(blocks, HOT_DEV).astype(jnp.int32)
    global_rows = (local + jnp.arange(blocks, dtype=jnp.int32)[:, None] * TOK_DEV).reshape(-1).astype(jnp.int32)
    hot_x = tokens[global_rows]
    hot_s = (hot_gate[:, None] * cotangent[global_rows].astype(jnp.float32)).astype(jnp.bfloat16)
    feature_dims = (((1,), (1,)), ((), ()))
    gate_part = lax.dot_general(hot_x, w_hot_gu[0], feature_dims, preferred_element_type=jnp.float32)
    up_part = lax.dot_general(hot_x, w_hot_gu[1], feature_dims, preferred_element_type=jnp.float32)
    sigma = jax.nn.sigmoid(gate_part)
    hidden = (gate_part * sigma * up_part).astype(jnp.bfloat16)
    hot_out = jnp.dot(hidden, w_hot_dn, preferred_element_type=jnp.float32)
    d_hidden = lax.dot_general(hot_s, w_hot_dn, feature_dims, preferred_element_type=jnp.float32)
    d_gate = (d_hidden * up_part * sigma * (1.0 + gate_part * (1.0 - sigma))).astype(jnp.bfloat16)
    d_up = (d_hidden * gate_part * sigma).astype(jnp.bfloat16)
    hot_back = jnp.dot(d_gate, w_hot_gu[0], preferred_element_type=jnp.float32) + jnp.dot(d_up, w_hot_gu[1], preferred_element_type=jnp.float32)
    inverse = 1.0 / GRAD_DIV

    def by_column(array):
        width = array.shape[-1]
        return array.reshape(N_DP, N_EXPERT, HOT_DEV, width).transpose(1, 0, 2, 3).reshape(N_EXPERT, N_DP * HOT_DEV, width)

    def column(carry, piece):
        acc_gu, acc_dn = carry
        col_x, col_g, col_u, col_h, col_s = piece
        row_dims = (((0,), (0,)), ((), ()))
        part_gu = jnp.stack([lax.dot_general(col_g, col_x, row_dims, preferred_element_type=jnp.float32), lax.dot_general(col_u, col_x, row_dims, preferred_element_type=jnp.float32)]) * inverse
        part_dn = lax.dot_general(col_h, col_s, row_dims, preferred_element_type=jnp.float32) * inverse
        acc_gu = acc_gu + lax.optimization_barrier(part_gu.astype(jnp.bfloat16)).astype(jnp.float32)
        acc_dn = acc_dn + lax.optimization_barrier(part_dn.astype(jnp.bfloat16)).astype(jnp.float32)
        return (acc_gu, acc_dn), None

    init = (jnp.zeros(w_hot_gu.shape, jnp.float32), jnp.zeros(w_hot_dn.shape, jnp.float32))
    (acc_gu, acc_dn), unused = lax.scan(column, init, (by_column(hot_x), by_column(d_gate), by_column(d_up), by_column(hidden), by_column(hot_s)))
    return global_rows, hot_out, hot_back, acc_gu.astype(jnp.bfloat16), acc_dn.astype(jnp.bfloat16)


def reference(tokens, cotangent, routes, gates, hot_index, hot_gate, w_gate_up, w_down, w_hot_gu, w_hot_dn):
    width_d = tokens.shape[1]
    inverse = 1.0 / GRAD_DIV
    entries = TOK_DEV * TOPK
    total = EXPERTS * N_EXPERT * CAP
    x_groups = tokens.reshape(N_DP, N_EXPERT, TOK_DEV, width_d)
    dy_groups = cotangent.reshape(N_DP, N_EXPERT, TOK_DEV, width_d)
    r_groups = routes.reshape(N_DP, N_EXPERT, TOK_DEV, TOPK)
    g_groups = gates.reshape(N_DP, N_EXPERT, TOK_DEV, TOPK)

    def one_group(carry, item):
        acc_gu, acc_dn = carry
        x_g, dy_g, r_g, g_g = item
        flat, pos = jax.vmap(lambda block: slot_positions(block, EXPERTS))(r_g)
        source = jnp.arange(N_EXPERT, dtype=jnp.int32)[:, None]
        entry = jnp.arange(entries, dtype=jnp.int32)[None, :]
        dest = (flat * (N_EXPERT * CAP) + source * CAP + pos).reshape(-1).astype(jnp.int32)
        entry_ids = (source * entries + entry).reshape(-1).astype(jnp.int32)
        table = jnp.full((total,), N_EXPERT * entries, jnp.int32).at[dest].set(entry_ids)
        gate_flat = g_g.reshape(N_EXPERT * entries)
        scaled = (g_g[:, :, :, None] * dy_g[:, :, None, :].astype(jnp.float32)).astype(jnp.bfloat16)
        scaled_pad = jnp.concatenate([scaled.reshape(-1, width_d), jnp.zeros((1, width_d), jnp.bfloat16)], axis=0)
        x_pad = jnp.concatenate([x_g.reshape(-1, width_d), jnp.zeros((1, width_d), jnp.bfloat16)], axis=0)
        rows_x = x_pad[table // TOPK].reshape(EXPERTS, N_EXPERT * CAP, width_d)
        rows_s = scaled_pad[table].reshape(EXPERTS, N_EXPERT * CAP, width_d)

        def per_expert(piece):
            rx, rs, wgu, wdn = piece
            act, hidden = expert_forward(rx, wgu)
            out = expert_output(hidden, wdn)
            d_act, d_rows = expert_delta(rs, act, wgu, wdn)
            grad_gu = lax.dot_general(rx, d_act, (((0,), (0,)), ((), ())), preferred_element_type=jnp.float32) * inverse
            grad_dn = lax.dot_general(hidden, rs, (((0,), (0,)), ((), ())), preferred_element_type=jnp.float32) * inverse
            return out, d_rows, grad_gu, grad_dn

        out, d_rows, grad_gu, grad_dn = lax.map(per_expert, (rows_x, rows_s, w_gate_up, w_down))
        acc_gu = acc_gu + lax.optimization_barrier(grad_gu.astype(jnp.bfloat16)).astype(jnp.float32)
        acc_dn = acc_dn + lax.optimization_barrier(grad_dn.astype(jnp.bfloat16)).astype(jnp.float32)
        picked = out.reshape(total, width_d)[dest].astype(jnp.float32)
        layer_out = (gate_flat[:, None] * picked).reshape(N_EXPERT, TOK_DEV, TOPK, width_d).sum(axis=2)
        back = d_rows.reshape(total, width_d)[dest].astype(jnp.float32)
        input_grad = back.reshape(N_EXPERT, TOK_DEV, TOPK, width_d).sum(axis=2)
        return (acc_gu, acc_dn), (layer_out, input_grad)

    init = (jnp.zeros(w_gate_up.shape, jnp.float32), jnp.zeros(w_down.shape, jnp.float32))
    (acc_gu, acc_dn), (outs, grads) = lax.scan(one_group, init, (x_groups, dy_groups, r_groups, g_groups))
    global_rows, hot_out, hot_back, hot_gu, hot_dn = popular_expert(tokens, cotangent, hot_index, hot_gate, w_hot_gu, w_hot_dn)
    layer_all = outs.reshape(TOKENS, width_d).at[global_rows].add(hot_gate[:, None] * hot_out)
    grad_all = grads.reshape(TOKENS, width_d).at[global_rows].add(hot_back)
    return (layer_all.astype(jnp.bfloat16), grad_all.astype(jnp.bfloat16), acc_gu.astype(jnp.bfloat16), acc_dn.astype(jnp.bfloat16), hot_gu, hot_dn)
```

```python
import jax
import jax.numpy as jnp
from jax import lax
from jax.sharding import PartitionSpec as P

BF = jnp.bfloat16
F32 = jnp.float32
NT = (((1,), (1,)), ((), ()))
TN = (((0,), (0,)), ((), ()))


def mm(a, b, dims=(((1,), (0,)), ((), ()))):
    return lax.dot_general(a, b, dims, preferred_element_type=F32)


def slot_positions(route_block, count):
    flat = route_block.reshape(-1)
    onehot = (flat[:, None] == jnp.arange(count, dtype=jnp.int32)[None, :]).astype(jnp.int32)
    before = jnp.cumsum(onehot, axis=0) - onehot
    return (flat, jnp.sum(before * onehot, axis=1))


def exchange(blocks):
    return lax.all_to_all(blocks, "expert", split_axis=0, concat_axis=0, tiled=True)


def local(
    tokens, cotangent, routes, gates, hot_index, hot_gate, w_gate_up, w_down, w_hot_gu, w_hot_dn
):
    owners = lax.axis_size("expert")
    groups = lax.axis_size("dp")
    cores = 2 if groups % 2 == 0 else 1
    chips = groups // cores
    tok_dev, width_d = tokens.shape
    topk = routes.shape[1]
    slots = max(2, 3 * tok_dev * topk // (2 * owners))
    entries = tok_dev * topk
    rows = owners * slots
    inverse = 1.0 / (4 * groups)
    me = lax.axis_index("dp")
    chip, core = me // cores, me % cores

    order = [
        ((chip - r) % chips) * cores + (core + k) % cores
        for r in range(chips)
        for k in range(cores)
    ]

    def shift(value, r):
        pairs = [
            (i, ((i // cores + r) % chips) * cores + i % cores) for i in range(groups)
        ]
        return lax.ppermute(value, "dp", pairs)

    def swap(value):
        pairs = [(i, (i // cores) * cores + (i + 1) % cores) for i in range(groups)]
        return lax.ppermute(value, "dp", pairs)

    def gather(block):
        found = []
        for r in range(chips):
            near = block if r == 0 else shift(block, r)
            found.append(near)
            if cores == 2:
                found.append(swap(near))
        return found

    def reduce(parts):
        total = None
        for r in list(range(1, chips)) + [0]:
            mine = parts(r, 0)
            if cores == 2:
                mine = mine + swap(parts(r, 1).astype(BF)).astype(F32)
            if r > 0:
                mine = shift(mine.astype(BF), -r).astype(F32)
            total = mine if total is None else total + mine
        return total.astype(BF)

    gu_blocks = gather(w_gate_up[0])
    dn_blocks = gather(w_down[0])
    hot_blocks = gather(jnp.concatenate([w_hot_gu, w_hot_dn[None]], axis=0))

    flat, pos = slot_positions(routes, owners)
    dest = flat * slots + pos
    pick = (jnp.arange(rows, dtype=jnp.int32)[:, None] == dest[None, :]).astype(BF)
    wide = width_d // groups
    tok_rel = jnp.concatenate(
        [lax.dynamic_slice_in_dim(tokens, i * wide, wide, 1) for i in order], axis=1
    )
    tok_rows = jnp.repeat(tok_rel, topk, axis=0)
    send_x = mm(pick, tok_rows).astype(BF).reshape(owners, slots, width_d)
    recv_x = exchange(send_x)
    scaled = (gates[:, :, None] * cotangent[:, None, :].astype(F32)).astype(BF)
    send_s = mm(pick, scaled.reshape(entries, width_d)).astype(BF).reshape(owners, slots, width_d)
    recv_s = exchange(send_s)

    hot_dev = hot_index.shape[0]
    narrow = width_d // owners
    hot_pick = (
        hot_index[:, None] == jnp.arange(tok_dev, dtype=jnp.int32)[None, :]
    ).astype(BF)
    hot_x = mm(hot_pick, tokens).astype(BF)
    hot_s = (hot_gate[:, None] * mm(hot_pick, cotangent)).astype(BF)
    hot_send = (
        jnp.stack([hot_x, hot_s])
        .reshape(2, hot_dev, owners, narrow)
        .transpose(2, 0, 1, 3)
    )
    hot_recv = exchange(hot_send)
    all_x = hot_recv[:, 0].reshape(owners * hot_dev, narrow)
    all_s = hot_recv[:, 1].reshape(owners * hot_dev, narrow)
    hid = w_hot_dn.shape[0]
    hidden_all = hid * groups
    hot_gate_w = jnp.concatenate([b[0] for b in hot_blocks], axis=0)
    hot_up_w = jnp.concatenate([b[1] for b in hot_blocks], axis=0)
    hot_down_w = jnp.concatenate([b[2] for b in hot_blocks], axis=0)
    partial = jnp.concatenate(
        [mm(all_x, hot_gate_w, NT), mm(all_x, hot_up_w, NT), mm(all_s, hot_down_w, NT)], axis=1
    ).astype(BF)
    hot_act = exchange(partial.reshape(owners, hot_dev, 3 * hidden_all)).astype(F32).sum(axis=0)
    hot_g = hot_act[:, :hidden_all]
    hot_u = hot_act[:, hidden_all : 2 * hidden_all]
    hot_dh = hot_act[:, 2 * hidden_all :]
    hot_sigma = jax.nn.sigmoid(hot_g)
    hot_own = jnp.concatenate(
        [
            hot_dh * hot_u * hot_sigma * (1.0 + hot_g * (1.0 - hot_sigma)),
            hot_dh * hot_g * hot_sigma,
            hot_g * hot_sigma * hot_u,
        ],
        axis=1,
    ).astype(BF)
    hot_full = exchange(
        jnp.broadcast_to(hot_own[None], (owners, hot_dev, 3 * hidden_all))
    ).reshape(owners * hot_dev, 3 * hidden_all)
    hot_dg = hot_full[:, :hidden_all]
    hot_du = hot_full[:, hidden_all : 2 * hidden_all]
    hot_hidden = hot_full[:, 2 * hidden_all :]
    hot_out = mm(hot_hidden, hot_down_w)
    hot_grad = mm(hot_dg, hot_gate_w) + mm(hot_du, hot_up_w)
    hot_back = exchange(
        jnp.stack([hot_out, hot_grad], axis=0)
        .astype(BF)
        .reshape(2, owners, hot_dev, narrow)
        .transpose(1, 0, 2, 3)
    )
    hot_back = hot_back.transpose(1, 2, 0, 3).reshape(2, hot_dev, width_d)

    rows_x = recv_x.reshape(rows, width_d)
    rows_s = recv_s.reshape(rows, width_d)
    act = None
    for j, block in enumerate(gu_blocks):
        term = mm(rows_x[:, j * wide : (j + 1) * wide], block)
        act = term if act is None else act + term
    half = w_gate_up.shape[2] // 2
    gate_part = act[:, :half]
    up_part = act[:, half:]
    sigma = jax.nn.sigmoid(gate_part)
    hidden = (gate_part * sigma * up_part).astype(BF)
    deep = w_down.shape[1]
    w_dn = jnp.zeros((groups * deep, width_d), BF)
    for i, block in zip(order, dn_blocks):
        w_dn = lax.dynamic_update_slice_in_dim(w_dn, block, i * deep, 0)
    out = mm(hidden, w_dn).astype(BF)
    back_out = exchange(out.reshape(owners, slots, width_d))
    d_hidden = mm(rows_s, w_dn, NT)
    d_gate = d_hidden * up_part * sigma * (1.0 + gate_part * (1.0 - sigma))
    d_up = d_hidden * gate_part * sigma
    d_act = jnp.concatenate([d_gate, d_up], axis=1).astype(BF)
    d_rows = jnp.concatenate([mm(d_act, block, NT).astype(BF) for block in gu_blocks], axis=1)
    back_rows = exchange(d_rows.reshape(owners, slots, width_d))

    def part_dn(r, k):
        i = order[r * cores + k]
        return mm(lax.dynamic_slice_in_dim(hidden, i * deep, deep, 1), rows_s, TN) * inverse

    def part_gu(r, k):
        j = r * cores + k
        return mm(rows_x[:, j * wide : (j + 1) * wide], d_act, TN) * inverse

    def part_hot(r, k):
        j = r * cores + k
        span = slice(j * hid, (j + 1) * hid)
        return jnp.stack(
            [mm(hot_dg[:, span], all_x, TN), mm(hot_du[:, span], all_x, TN), mm(hot_hidden[:, span], all_s, TN)]
        ) * inverse

    grad_dn = reduce(part_dn)
    grad_gu = reduce(part_gu)
    grad_hot = reduce(part_hot)

    picked = mm(pick, back_out.reshape(rows, width_d), TN)
    layer_out = (
        (gates.reshape(entries)[:, None] * picked).reshape(tok_dev, topk, width_d).sum(axis=1)
    )
    token_gate = jnp.sum(jnp.where(hot_pick > 0, hot_gate[:, None], 0.0), axis=0)
    layer_out = layer_out + token_gate[:, None] * mm(hot_pick, hot_back[0], TN)
    returned = mm(pick, back_rows.reshape(rows, width_d), TN)
    input_grad = returned.reshape(tok_dev, topk, width_d).sum(axis=1).astype(F32)
    hot_part = mm(hot_pick, hot_back[1], TN)
    result = jnp.zeros((tok_dev, width_d), F32)
    for j, i in enumerate(order):
        result = lax.dynamic_update_slice_in_dim(
            result, input_grad[:, j * wide : (j + 1) * wide], i * wide, 1
        )
    input_grad = result + hot_part
    return (
        layer_out.astype(BF),
        input_grad.astype(BF),
        grad_gu[None],
        grad_dn[None],
        grad_hot[:2],
        grad_hot[2],
    )


def solution(mesh):
    tok = P(("dp", "expert"), None)
    flat = P(("dp", "expert"))
    rows = P("expert", "dp", None)
    hot = (P(None, "dp", "expert"), P("dp", "expert"))
    return jax.shard_map(
        local,
        mesh=mesh,
        in_specs=(tok, tok, tok, tok, flat, flat, rows, rows) + hot,
        out_specs=(tok, tok, rows, rows) + hot,
        check_vma=False,
    )
```

```python
import jax
import jax.numpy as jnp
from jax import lax
from jax.sharding import PartitionSpec as P

BF = jnp.bfloat16
F32 = jnp.float32
NT = (((1,), (1,)), ((), ()))
TN = (((0,), (0,)), ((), ()))


def mm(a, b, dims=(((1,), (0,)), ((), ()))):
    return lax.dot_general(a, b, dims, preferred_element_type=F32)


def slot_positions(route_block, count):
    flat = route_block.reshape(-1)
    onehot = (flat[:, None] == jnp.arange(count, dtype=jnp.int32)[None, :]).astype(jnp.int32)
    before = jnp.cumsum(onehot, axis=0) - onehot
    return (flat, jnp.sum(before * onehot, axis=1))


def exchange(blocks):
    return lax.all_to_all(blocks, "expert", split_axis=0, concat_axis=0, tiled=True)


def local(
    tokens, cotangent, routes, gates, hot_index, hot_gate, w_gate_up, w_down, w_hot_gu, w_hot_dn
):
    owners = lax.axis_size("expert")
    groups = lax.axis_size("dp")
    cores = 2 if groups % 2 == 0 else 1
    chips = groups // cores
    tok_dev, width_d = tokens.shape
    topk = routes.shape[1]
    slots = max(2, 3 * tok_dev * topk // (2 * owners))
    entries = tok_dev * topk
    rows = owners * slots
    inverse = 1.0 / (4 * groups)
    me = lax.axis_index("dp")
    chip, core = me // cores, me % cores

    order = [
        ((chip - r) % chips) * cores + (core + k) % cores
        for r in range(chips)
        for k in range(cores)
    ]

    def shift(value, r):
        pairs = [
            (i, ((i // cores + r) % chips) * cores + i % cores) for i in range(groups)
        ]
        return lax.ppermute(value, "dp", pairs)

    def swap(value):
        pairs = [(i, (i // cores) * cores + (i + 1) % cores) for i in range(groups)]
        return lax.ppermute(value, "dp", pairs)

    def gather(block):
        found = []
        for r in range(chips):
            near = block if r == 0 else shift(block, r)
            found.append(near)
            if cores == 2:
                found.append(swap(near))
        return found

    def reduce(parts):
        total = None
        for r in list(range(1, chips)) + [0]:
            mine = parts(r, 0)
            if cores == 2:
                mine = mine + swap(parts(r, 1).astype(BF)).astype(F32)
            if r > 0:
                mine = shift(mine.astype(BF), -r).astype(F32)
            total = mine if total is None else total + mine
        return total.astype(BF)

    wide = width_d // groups
    span = wide * cores

    def features_of(value, r):
        base = ((chip + r) % chips) * cores
        return jnp.concatenate(
            [
                lax.dynamic_slice_in_dim(value, (base + (core + k) % cores) * wide, wide, 1)
                for k in range(cores)
            ],
            axis=1,
        )

    flat, pos = slot_positions(routes, owners)
    dest = flat * slots + pos
    dests = [dest] + [shift(dest, r) for r in range(1, chips)]
    halves = [features_of(tokens, 0)] + [
        shift(features_of(tokens, r), r) for r in range(1, chips)
    ]
    gu_chip = [w_gate_up[0]] + ([swap(w_gate_up[0])] if cores == 2 else [])
    hot_blocks = gather(jnp.concatenate([w_hot_gu, w_hot_dn[None]], axis=0))
    dn_blocks = gather(w_down[0])

    slot_ids = jnp.arange(rows, dtype=jnp.int32)[:, None]
    picks = [(slot_ids == one[None, :]).astype(BF) for one in dests]

    hot_dev = hot_index.shape[0]
    narrow = width_d // owners
    hot_pick = (
        hot_index[:, None] == jnp.arange(tok_dev, dtype=jnp.int32)[None, :]
    ).astype(BF)
    hot_x = mm(hot_pick, tokens).astype(BF)
    hot_s = (hot_gate[:, None] * mm(hot_pick, cotangent)).astype(BF)
    hot_send = (
        jnp.stack([hot_x, hot_s])
        .reshape(2, hot_dev, owners, narrow)
        .transpose(2, 0, 1, 3)
    )

    def as_rows(value, width):
        value = value.reshape(owners, -1)
        spare = -value.shape[1] % width
        return jnp.pad(value, ((0, 0), (0, spare))).reshape(owners, -1, width)

    def as_columns(value, width):
        spare = -value.shape[2] % width
        value = jnp.pad(value, ((0, 0), (0, 0), (0, spare)))
        chunks = value.shape[2] // width
        return jnp.concatenate(
            [value[:, :, i * width : (i + 1) * width] for i in range(chunks)], axis=1
        )

    def from_columns(value, count, total):
        chunks = value.shape[1] // count
        whole = jnp.concatenate(
            [value[:, i * count : (i + 1) * count] for i in range(chunks)], axis=2
        )
        return whole[:, :, :total]

    packed = [
        mm(one, jnp.repeat(part, topk, axis=0) if topk > 1 else part)
        .astype(BF)
        .reshape(owners, slots, span)
        for one, part in zip(picks, halves)
    ]
    first = exchange(jnp.concatenate(packed + [as_rows(hot_send, span)], axis=1))
    rows_x = first[:, : chips * slots].reshape(owners * chips * slots, span)
    hot_recv = first[:, chips * slots :].reshape(owners, -1)[:, : 2 * hot_dev * narrow]
    hot_recv = hot_recv.reshape(owners, 2, hot_dev, narrow)

    scaled = (gates[:, :, None] * cotangent[:, None, :].astype(F32)).astype(BF)
    send_s = mm(picks[0], scaled.reshape(entries, width_d)).astype(BF)
    rows_s = exchange(send_s.reshape(owners, slots, width_d)).reshape(rows, width_d)

    act_part = None
    for k, block in enumerate(gu_chip):
        term = mm(rows_x[:, k * wide : (k + 1) * wide], block)
        act_part = term if act_part is None else act_part + term
    act_part = act_part.reshape(owners, chips, slots, -1)
    act = act_part[:, 0]
    for r in range(1, chips):
        act = act + shift(act_part[:, r].astype(BF), -r).astype(F32)
    act = act.reshape(rows, -1)
    half = w_gate_up.shape[2] // 2
    gate_part = act[:, :half]
    up_part = act[:, half:]
    sigma = jax.nn.sigmoid(gate_part)
    hidden = (gate_part * sigma * up_part).astype(BF)

    all_x = hot_recv[:, 0].reshape(owners * hot_dev, narrow)
    all_s = hot_recv[:, 1].reshape(owners * hot_dev, narrow)
    hid = w_hot_dn.shape[0]
    hidden_all = hid * groups
    hot_gate_w = jnp.concatenate([b[0] for b in hot_blocks], axis=0)
    hot_up_w = jnp.concatenate([b[1] for b in hot_blocks], axis=0)
    hot_down_w = jnp.concatenate([b[2] for b in hot_blocks], axis=0)
    partial = jnp.concatenate(
        [mm(all_x, hot_gate_w, NT), mm(all_x, hot_up_w, NT), mm(all_s, hot_down_w, NT)], axis=1
    ).astype(BF)
    partial = partial.reshape(owners, hot_dev, 3 * hidden_all)

    deep = w_down.shape[1]
    w_dn = jnp.zeros((groups * deep, width_d), BF)
    for i, block in zip(order, dn_blocks):
        w_dn = lax.dynamic_update_slice_in_dim(w_dn, block, i * deep, 0)
    out = mm(hidden, w_dn).astype(BF).reshape(owners, slots, width_d)
    third = exchange(jnp.concatenate([out, as_columns(partial, width_d)], axis=1))
    back_out = third[:, :slots].reshape(rows, width_d)
    hot_act = from_columns(third[:, slots:], hot_dev, 3 * hidden_all).astype(F32).sum(axis=0)

    d_hidden = mm(rows_s, w_dn, NT)
    d_gate = d_hidden * up_part * sigma * (1.0 + gate_part * (1.0 - sigma))
    d_up = d_hidden * gate_part * sigma
    d_act = jnp.concatenate([d_gate, d_up], axis=1).astype(BF).reshape(owners, slots, -1)
    d_all = jnp.stack([d_act] + [shift(d_act, r) for r in range(1, chips)], axis=1)
    d_all = d_all.reshape(owners * chips * slots, -1)
    d_rows = jnp.concatenate([mm(d_all, block, NT).astype(BF) for block in gu_chip], axis=1)

    hot_g = hot_act[:, :hidden_all]
    hot_u = hot_act[:, hidden_all : 2 * hidden_all]
    hot_dh = hot_act[:, 2 * hidden_all :]
    hot_sigma = jax.nn.sigmoid(hot_g)
    hot_own = jnp.concatenate(
        [
            hot_dh * hot_u * hot_sigma * (1.0 + hot_g * (1.0 - hot_sigma)),
            hot_dh * hot_g * hot_sigma,
            hot_g * hot_sigma * hot_u,
        ],
        axis=1,
    ).astype(BF)
    hot_own = jnp.broadcast_to(hot_own[None], (owners, hot_dev, 3 * hidden_all))
    fourth = exchange(
        jnp.concatenate(
            [d_rows.reshape(owners, chips * slots, span), as_columns(hot_own, span)], axis=1
        )
    )
    back_rows = fourth[:, : chips * slots].reshape(owners, chips, slots, span)
    hot_full = from_columns(fourth[:, chips * slots :], hot_dev, 3 * hidden_all)
    hot_full = hot_full.reshape(owners * hot_dev, 3 * hidden_all)
    hot_dg = hot_full[:, :hidden_all]
    hot_du = hot_full[:, hidden_all : 2 * hidden_all]
    hot_hidden = hot_full[:, 2 * hidden_all :]
    hot_out = mm(hot_hidden, hot_down_w)
    hot_grad = mm(hot_dg, hot_gate_w) + mm(hot_du, hot_up_w)
    hot_back = exchange(
        jnp.stack([hot_out, hot_grad], axis=0)
        .astype(BF)
        .reshape(2, owners, hot_dev, narrow)
        .transpose(1, 0, 2, 3)
    )
    hot_back = hot_back.transpose(1, 2, 0, 3).reshape(2, hot_dev, width_d)

    def part_dn(r, k):
        i = order[r * cores + k]
        return mm(lax.dynamic_slice_in_dim(hidden, i * deep, deep, 1), rows_s, TN) * inverse

    def part_hot(r, k):
        j = r * cores + k
        cut = slice(j * hid, (j + 1) * hid)
        return jnp.stack(
            [
                mm(hot_dg[:, cut], all_x, TN),
                mm(hot_du[:, cut], all_x, TN),
                mm(hot_hidden[:, cut], all_s, TN),
            ]
        ) * inverse

    def part_gu(k):
        return mm(rows_x[:, k * wide : (k + 1) * wide], d_all, TN) * inverse

    grad_dn = reduce(part_dn)
    grad_gu = part_gu(0)
    if cores == 2:
        grad_gu = grad_gu + swap(part_gu(1).astype(BF)).astype(F32)
    grad_gu = grad_gu.astype(BF)
    grad_hot = reduce(part_hot)

    picked = mm(picks[0], back_out, TN)
    layer_out = (
        (gates.reshape(entries)[:, None] * picked).reshape(tok_dev, topk, width_d).sum(axis=1)
    )
    token_gate = jnp.sum(jnp.where(hot_pick > 0, hot_gate[:, None], 0.0), axis=0)
    layer_out = layer_out + token_gate[:, None] * mm(hot_pick, hot_back[0], TN)
    pieces = []
    for r in range(chips):
        piece = mm(picks[r], back_rows[:, r].reshape(rows, span), TN)
        piece = piece.reshape(tok_dev, topk, span).sum(axis=1).astype(BF)
        if r > 0:
            piece = shift(piece, -r)
        pieces += [piece[:, k * wide : (k + 1) * wide] for k in range(cores)]
    pieces = jnp.stack(pieces)
    input_grad = jnp.concatenate(
        [
            lax.dynamic_index_in_dim(
                pieces,
                ((p - chip) % chips) * cores + (q - core) % cores,
                0,
                keepdims=False,
            )
            for p in range(chips)
            for q in range(cores)
        ],
        axis=1,
    ).astype(F32)
    input_grad = input_grad + mm(hot_pick, hot_back[1], TN)
    return (
        layer_out.astype(BF),
        input_grad.astype(BF),
        grad_gu[None],
        grad_dn[None],
        grad_hot[:2],
        grad_hot[2],
    )


def solution(mesh):
    tok = P(("dp", "expert"), None)
    flat = P(("dp", "expert"))
    rows = P("expert", "dp", None)
    hot = (P(None, "dp", "expert"), P("dp", "expert"))
    return jax.shard_map(
        local,
        mesh=mesh,
        in_specs=(tok, tok, tok, tok, flat, flat, rows, rows) + hot,
        out_specs=(tok, tok, rows, rows) + hot,
        check_vma=False,
    )
```

```python
import jax
import jax.numpy as jnp
from jax import lax
from jax.sharding import PartitionSpec as P

BF = jnp.bfloat16
F32 = jnp.float32
NT = (((1,), (1,)), ((), ()))
TN = (((0,), (0,)), ((), ()))


def mm(a, b, dims=(((1,), (0,)), ((), ()))):
    return lax.dot_general(a, b, dims, preferred_element_type=F32)


def slot_positions(route_block, count):
    flat = route_block.reshape(-1)
    onehot = (flat[:, None] == jnp.arange(count, dtype=jnp.int32)[None, :]).astype(jnp.int32)
    before = jnp.cumsum(onehot, axis=0) - onehot
    return (flat, jnp.sum(before * onehot, axis=1))


def exchange(blocks):
    return lax.all_to_all(blocks, "expert", split_axis=0, concat_axis=0, tiled=True)


def local(
    tokens, cotangent, routes, gates, hot_index, hot_gate, w_gate_up, w_down, w_hot_gu, w_hot_dn
):
    owners = lax.axis_size("expert")
    groups = lax.axis_size("dp")
    cores = 2 if groups % 2 == 0 else 1
    chips = groups // cores
    tok_dev, width_d = tokens.shape
    topk = routes.shape[1]
    slots = max(2, 3 * tok_dev * topk // (2 * owners))
    entries = tok_dev * topk
    rows = owners * slots
    inverse = 1.0 / (4 * groups)
    me = lax.axis_index("dp")
    chip, core = me // cores, me % cores

    order = [
        ((chip - r) % chips) * cores + (core + k) % cores
        for r in range(chips)
        for k in range(cores)
    ]

    def shift(value, r):
        pairs = [
            (i, ((i // cores + r) % chips) * cores + i % cores) for i in range(groups)
        ]
        return lax.ppermute(value, "dp", pairs)

    def swap(value):
        pairs = [(i, (i // cores) * cores + (i + 1) % cores) for i in range(groups)]
        return lax.ppermute(value, "dp", pairs)

    def gather(block):
        found = []
        for r in range(chips):
            near = block if r == 0 else shift(block, r)
            found.append(near)
            if cores == 2:
                found.append(swap(near))
        return found

    def reduce(parts):
        total = None
        for r in list(range(1, chips)) + [0]:
            mine = parts(r, 0)
            if cores == 2:
                mine = mine + swap(parts(r, 1).astype(BF)).astype(F32)
            if r > 0:
                mine = shift(mine.astype(BF), -r).astype(F32)
            total = mine if total is None else total + mine
        return total.astype(BF)

    across = 1
    while 2 * (2 * across) ** 2 <= owners:
        across *= 2
    depths = owners // across
    spot = lax.axis_index("expert")

    def hop(value, j):
        return lax.ppermute(value, "expert", [(i, i ^ j) for i in range(owners)])

    def relative(value):
        return jnp.concatenate(
            [lax.dynamic_slice_in_dim(value, spot ^ j, 1, 0) for j in range(owners)], axis=0
        )

    wide = width_d // groups
    span = wide * cores

    def features_of(value, r):
        base = ((chip + r) % chips) * cores
        return jnp.concatenate(
            [
                lax.dynamic_slice_in_dim(value, (base + (core + k) % cores) * wide, wide, 1)
                for k in range(cores)
            ],
            axis=1,
        )

    flat, pos = slot_positions(routes, owners)
    dest = flat * slots + pos
    dests = [dest] + [shift(dest, r) for r in range(1, chips)]
    halves = [features_of(tokens, 0)] + [
        shift(features_of(tokens, r), r) for r in range(1, chips)
    ]
    gu_chip = [w_gate_up[0]] + ([swap(w_gate_up[0])] if cores == 2 else [])
    dn_own, hot_own_w, halves[-1] = lax.optimization_barrier(
        (w_down[0], jnp.concatenate([w_hot_gu, w_hot_dn[None]], axis=0), halves[-1])
    )
    hot_blocks = gather(hot_own_w)
    dn_blocks = gather(dn_own)

    slot_ids = jnp.arange(rows, dtype=jnp.int32)[:, None]
    picks = [(slot_ids == one[None, :]).astype(BF) for one in dests]

    hot_dev = hot_index.shape[0]
    narrow = width_d // owners
    hot_pick = (
        hot_index[:, None] == jnp.arange(tok_dev, dtype=jnp.int32)[None, :]
    ).astype(BF)
    hot_x = mm(hot_pick, tokens).astype(BF)
    hot_s = (hot_gate[:, None] * mm(hot_pick, cotangent)).astype(BF)
    hot_send = (
        jnp.stack([hot_x, hot_s])
        .reshape(2, hot_dev, owners, narrow)
        .transpose(2, 0, 1, 3)
    )

    def as_rows(value, width):
        value = value.reshape(owners, -1)
        spare = -value.shape[1] % width
        return jnp.pad(value, ((0, 0), (0, spare))).reshape(owners, -1, width)

    packed = [
        mm(one, jnp.repeat(part, topk, axis=0) if topk > 1 else part)
        .astype(BF)
        .reshape(owners, slots, span)
        for one, part in zip(picks, halves)
    ]
    first = exchange(jnp.concatenate(packed + [as_rows(hot_send, span)], axis=1))
    rows_x = first[:, : chips * slots].reshape(owners * chips * slots, span)
    hot_recv = first[:, chips * slots :].reshape(owners, -1)[:, : 2 * hot_dev * narrow]
    hot_recv = hot_recv.reshape(owners, 2, hot_dev, narrow)

    scaled = (gates[:, :, None] * cotangent[:, None, :].astype(F32)).astype(BF)
    send_s = mm(picks[0], scaled.reshape(entries, width_d)).astype(BF)
    rows_s = exchange(send_s.reshape(owners, slots, width_d)).reshape(rows, width_d)

    act_part = None
    for k, block in enumerate(gu_chip):
        term = mm(rows_x[:, k * wide : (k + 1) * wide], block)
        act_part = term if act_part is None else act_part + term
    act_part = act_part.reshape(owners, chips, slots, -1)
    act = act_part[:, 0]
    for r in range(1, chips):
        act = act + shift(act_part[:, r].astype(BF), -r).astype(F32)
    act = act.reshape(rows, -1)
    half = w_gate_up.shape[2] // 2
    gate_part = act[:, :half]
    up_part = act[:, half:]
    sigma = jax.nn.sigmoid(gate_part)
    hidden = (gate_part * sigma * up_part).astype(BF)

    hot_recv = relative(hot_recv)
    all_x = hot_recv[:, 0].reshape(owners * hot_dev, narrow)
    all_s = hot_recv[:, 1].reshape(owners * hot_dev, narrow)
    hid = w_hot_dn.shape[0]
    hidden_all = hid * groups
    hot_gate_w = jnp.concatenate([b[0] for b in hot_blocks], axis=0)
    hot_up_w = jnp.concatenate([b[1] for b in hot_blocks], axis=0)
    hot_down_w = jnp.concatenate([b[2] for b in hot_blocks], axis=0)
    partial = jnp.concatenate(
        [mm(all_x, hot_gate_w, NT), mm(all_x, hot_up_w, NT), mm(all_s, hot_down_w, NT)], axis=1
    ).astype(BF)
    partial = partial.reshape(depths, across, hot_dev, 3 * hidden_all)
    level = partial[:, 0].astype(F32)
    for j in range(1, across):
        level = level + hop(partial[:, j], j).astype(F32)
    level = level.astype(BF)
    hot_act = level[0].astype(F32)
    for j in range(1, depths):
        hot_act = hot_act + hop(level[j], j * across).astype(F32)
    hot_g = hot_act[:, :hidden_all]
    hot_u = hot_act[:, hidden_all : 2 * hidden_all]
    hot_dh = hot_act[:, 2 * hidden_all :]
    hot_sigma = jax.nn.sigmoid(hot_g)
    hot_own = jnp.concatenate(
        [
            hot_dh * hot_u * hot_sigma * (1.0 + hot_g * (1.0 - hot_sigma)),
            hot_dh * hot_g * hot_sigma,
            hot_g * hot_sigma * hot_u,
        ],
        axis=1,
    ).astype(BF)
    line = jnp.stack([hot_own] + [hop(hot_own, j * across) for j in range(1, depths)])
    hot_full = jnp.stack([line] + [hop(line, j) for j in range(1, across)], axis=1)
    hot_full = hot_full.reshape(owners * hot_dev, 3 * hidden_all)
    hot_dg = hot_full[:, :hidden_all]
    hot_du = hot_full[:, hidden_all : 2 * hidden_all]
    hot_hidden = hot_full[:, 2 * hidden_all :]
    hot_out = mm(hot_hidden, hot_down_w)
    hot_grad = mm(hot_dg, hot_gate_w) + mm(hot_du, hot_up_w)
    hot_send = jnp.stack(
        [hot_out.reshape(owners, hot_dev, narrow), hot_grad.reshape(owners, hot_dev, narrow)],
        axis=1,
    )
    hot_send = relative(hot_send.astype(BF))

    deep = w_down.shape[1]
    w_dn = jnp.zeros((groups * deep, width_d), BF)
    for i, block in zip(order, dn_blocks):
        w_dn = lax.dynamic_update_slice_in_dim(w_dn, block, i * deep, 0)
    out = mm(hidden, w_dn).astype(BF).reshape(owners, slots, width_d)
    back_out = exchange(out).reshape(rows, width_d)

    d_hidden = mm(rows_s, w_dn, NT)
    d_gate = d_hidden * up_part * sigma * (1.0 + gate_part * (1.0 - sigma))
    d_up = d_hidden * gate_part * sigma
    d_act = jnp.concatenate([d_gate, d_up], axis=1).astype(BF).reshape(owners, slots, -1)
    d_all = jnp.stack([d_act] + [shift(d_act, r) for r in range(1, chips)], axis=1)
    d_all = d_all.reshape(owners * chips * slots, -1)
    d_rows = jnp.concatenate([mm(d_all, block, NT).astype(BF) for block in gu_chip], axis=1)

    fourth = exchange(
        jnp.concatenate(
            [d_rows.reshape(owners, chips * slots, span), as_rows(hot_send, span)], axis=1
        )
    )
    back_rows = fourth[:, : chips * slots].reshape(owners, chips, slots, span)
    hot_back = fourth[:, chips * slots :].reshape(owners, -1)[:, : 2 * hot_dev * narrow]
    hot_back = hot_back.reshape(owners, 2, hot_dev, narrow)
    hot_back = hot_back.transpose(1, 2, 0, 3).reshape(2, hot_dev, width_d)

    def part_dn(r, k):
        i = order[r * cores + k]
        return mm(lax.dynamic_slice_in_dim(hidden, i * deep, deep, 1), rows_s, TN) * inverse

    def part_hot(r, k):
        j = r * cores + k
        cut = slice(j * hid, (j + 1) * hid)
        return jnp.stack(
            [
                mm(hot_dg[:, cut], all_x, TN),
                mm(hot_du[:, cut], all_x, TN),
                mm(hot_hidden[:, cut], all_s, TN),
            ]
        ) * inverse

    def part_gu(k):
        return mm(rows_x[:, k * wide : (k + 1) * wide], d_all, TN) * inverse

    grad_dn = reduce(part_dn)
    grad_gu = part_gu(0)
    if cores == 2:
        grad_gu = grad_gu + swap(part_gu(1).astype(BF)).astype(F32)
    grad_gu = grad_gu.astype(BF)
    grad_hot = reduce(part_hot)

    picked = mm(picks[0], back_out, TN)
    layer_out = (
        (gates.reshape(entries)[:, None] * picked).reshape(tok_dev, topk, width_d).sum(axis=1)
    )
    token_gate = jnp.sum(jnp.where(hot_pick > 0, hot_gate[:, None], 0.0), axis=0)
    layer_out = layer_out + token_gate[:, None] * mm(hot_pick, hot_back[0], TN)
    pieces = []
    for r in range(chips):
        piece = mm(picks[r], back_rows[:, r].reshape(rows, span), TN)
        piece = piece.reshape(tok_dev, topk, span).sum(axis=1).astype(BF)
        if r > 0:
            piece = shift(piece, -r)
        pieces += [piece[:, k * wide : (k + 1) * wide] for k in range(cores)]
    pieces = jnp.stack(pieces)
    input_grad = jnp.concatenate(
        [
            lax.dynamic_index_in_dim(
                pieces,
                ((p - chip) % chips) * cores + (q - core) % cores,
                0,
                keepdims=False,
            )
            for p in range(chips)
            for q in range(cores)
        ],
        axis=1,
    ).astype(F32)
    input_grad = input_grad + mm(hot_pick, hot_back[1], TN)
    return (
        layer_out.astype(BF),
        input_grad.astype(BF),
        grad_gu[None],
        grad_dn[None],
        grad_hot[:2],
        grad_hot[2],
    )


def solution(mesh):
    tok = P(("dp", "expert"), None)
    flat = P(("dp", "expert"))
    rows = P("expert", "dp", None)
    hot = (P(None, "dp", "expert"), P("dp", "expert"))
    return jax.shard_map(
        local,
        mesh=mesh,
        in_specs=(tok, tok, tok, tok, flat, flat, rows, rows) + hot,
        out_specs=(tok, tok, rows, rows) + hot,
        check_vma=False,
    )
```

```python
import jax
import jax.numpy as jnp
from jax import lax
from jax.experimental import pallas as pl
from jax.experimental.pallas import tpu as pltpu
from jax.sharding import PartitionSpec as P

BF = jnp.bfloat16
F32 = jnp.float32
NN = (((1,), (0,)), ((), ()))
NT = (((1,), (1,)), ((), ()))
TN = (((0,), (0,)), ((), ()))
ROOM = 40 * 1024 * 1024


def mm(a, b, dims=NN):
    return lax.dot_general(a, b, dims, preferred_element_type=F32)


def after(value, *earlier):
    return lax.optimization_barrier((value,) + earlier)[0]


def params():
    return pltpu.CompilerParams(vmem_limit_bytes=ROOM)


def cost(flops, *arrays):
    size = sum(a.size * a.dtype.itemsize for a in arrays)
    return pl.CostEstimate(flops=flops, bytes_accessed=size, transcendentals=0)


def struct(*shape, dtype=BF):
    return jax.ShapeDtypeStruct(shape, dtype)


def whole(array):
    return pl.BlockSpec(array.shape, lambda *_: (0,) * len(array.shape))


def stack_rows(refs, scratch):
    rows = refs[0].shape[0]
    for i, ref in enumerate(refs):
        scratch[i * rows : (i + 1) * rows, :] = ref[...]


def activations(xs, w):
    n, rows, depth, width = len(xs), xs[0].shape[0], w.shape[0], w.shape[1]
    step = 512 if width % 512 == 0 else width

    def body(*refs):
        ins, w_ref, outs, scratch = refs[:n], refs[n], refs[n + 1 : 2 * n + 1], refs[-1]

        @pl.when(pl.program_id(0) == 0)
        def _():
            stack_rows(ins, scratch)

        found = mm(scratch[...], w_ref[...])
        outs[0][...] = found[:rows]
        for i in range(1, n):
            outs[i][...] = found[i * rows : (i + 1) * rows].astype(BF)

    shapes = [struct(rows, width, dtype=F32)] + [struct(rows, width)] * (n - 1)
    return pl.pallas_call(
        body,
        grid=(width // step,),
        in_specs=[whole(x) for x in xs] + [pl.BlockSpec((depth, step), lambda i: (0, i))],
        out_specs=[pl.BlockSpec((rows, step), lambda i: (0, i))] * n,
        out_shape=shapes,
        scratch_shapes=[pltpu.VMEM((n * rows, depth), BF)],
        compiler_params=params(),
        cost_estimate=cost(2 * n * rows * depth * width, w, *xs, *shapes),
        name="activations",
    )(*xs, w)


def fetch(order_ref, blocks, w_ref, sems):
    deep = blocks[0].shape[0]
    copies = []
    for j, block in enumerate(blocks):
        place = pl.multiple_of(order_ref[j] * deep, deep)
        copies.append(pltpu.make_async_copy(block, w_ref.at[pl.ds(place, deep)], sems.at[j]))
        copies[-1].start()
    return copies


def down_scratch(blocks):
    deep, width = blocks[0].shape
    return [pltpu.VMEM((len(blocks) * deep, width), BF), pltpu.SemaphoreType.DMA((len(blocks),))]


SMEM = pl.BlockSpec(memory_space=pltpu.SMEM)
ANYWHERE = pl.BlockSpec(memory_space=pl.ANY)
INSIDE = pl.BlockSpec(memory_space=pltpu.VMEM)


def outputs(order, own, others, blocks):
    rows, width = own.shape
    half = width // 2
    wide = blocks[0].shape[1]
    n, m = len(others), len(blocks)
    step = 512 if wide % 512 == 0 else wide

    def body(order_ref, own_ref, *refs):
        parts, down, (out_ref, hid_ref, fac_ref, w_ref, sems) = refs[:n], refs[n : n + m], refs[n + m :]
        copies = fetch(order_ref, down, w_ref, sems)
        act = own_ref[...]
        for part in parts:
            act = act + part[...].astype(F32)
        g = act[:, :half]
        u = act[:, half:]
        s = jax.nn.sigmoid(g)
        fac_ref[:, :half] = u * s * (1.0 + g * (1.0 - s))
        fac_ref[:, half:] = g * s
        hid_ref[...] = (g * s * u).astype(BF)
        for copy in copies:
            copy.wait()
        for c in range(0, wide, step):
            out_ref[:, c : c + step] = mm(hid_ref[...], w_ref[:, c : c + step]).astype(BF)

    shapes = [struct(rows, wide), struct(rows, half), struct(rows, width, dtype=F32)]
    return pl.pallas_call(
        body,
        in_specs=[SMEM] + [INSIDE] * (1 + n) + [ANYWHERE] * m,
        out_specs=[INSIDE] * 3,
        out_shape=shapes,
        scratch_shapes=down_scratch(blocks),
        compiler_params=params(),
        cost_estimate=cost(2 * rows * half * wide, own, *others, *blocks, *shapes),
        name="outputs",
    )(order, own, *others, *blocks)


def deltas(order, rows_s, factors, blocks):
    rows, width = factors.shape
    half = width // 2
    m = len(blocks)

    def body(order_ref, s_ref, fac_ref, *refs):
        down, (d_ref, w_ref, sems) = refs[:m], refs[m:]
        for copy in fetch(order_ref, down, w_ref, sems):
            copy.wait()
        d_hidden = mm(s_ref[...], w_ref[...], NT)
        d_ref[:, :half] = (d_hidden * fac_ref[:, :half]).astype(BF)
        d_ref[:, half:] = (d_hidden * fac_ref[:, half:]).astype(BF)

    shape = struct(rows, width)
    return pl.pallas_call(
        body,
        in_specs=[SMEM, INSIDE, INSIDE] + [ANYWHERE] * m,
        out_specs=INSIDE,
        out_shape=shape,
        scratch_shapes=down_scratch(blocks),
        compiler_params=params(),
        cost_estimate=cost(2 * rows * half * rows_s.shape[1], rows_s, factors, shape, *blocks),
        name="deltas",
    )(order, rows_s, factors, *blocks)


def row_grads(ds, w):
    n, rows, width, depth = len(ds), ds[0].shape[0], ds[0].shape[1], w.shape[0]
    step = 256 if depth % 256 == 0 else depth

    def body(*refs):
        ins, w_ref, outs, scratch = refs[:n], refs[n], refs[n + 1 : 2 * n + 1], refs[-1]

        @pl.when(pl.program_id(0) == 0)
        def _():
            stack_rows(ins, scratch)

        found = mm(scratch[...], w_ref[...], NT).astype(BF)
        for i in range(n):
            outs[i][...] = found[i * rows : (i + 1) * rows]

    shapes = [struct(rows, depth)] * n
    return pl.pallas_call(
        body,
        grid=(depth // step,),
        in_specs=[whole(d) for d in ds] + [pl.BlockSpec((step, width), lambda i: (i, 0))],
        out_specs=[pl.BlockSpec((rows, step), lambda i: (0, i))] * n,
        out_shape=shapes,
        scratch_shapes=[pltpu.VMEM((n * rows, width), BF)],
        compiler_params=params(),
        cost_estimate=cost(2 * n * rows * depth * width, w, *ds, *shapes),
        name="row_grads",
    )(*ds, w)


def gate_up_grads(xs, ds, k, wide, scale, received):
    n, rows, width = len(xs), xs[0].shape[0], ds[0].shape[1]
    step = 512 if width % 512 == 0 else width
    extra = [] if received is None else [received]
    if wide % 128 != 0:
        xs, k = [x[:, k * wide : (k + 1) * wide] for x in xs], 0

    def body(*refs):
        x_refs, d_refs, rest = refs[:n], refs[n : 2 * n], refs[2 * n :]
        out_ref, x_scr, d_scr = rest[-3:]

        @pl.when(pl.program_id(0) == 0)
        def _():
            stack_rows(x_refs, x_scr)

        stack_rows(d_refs, d_scr)
        found = mm(x_scr[...], d_scr[...], TN) * scale
        if extra:
            found = found + rest[0][...].astype(F32)
        out_ref[...] = found.astype(BF)

    shape = struct(wide, width)
    column = lambda i: (0, i)
    return pl.pallas_call(
        body,
        grid=(width // step,),
        in_specs=[pl.BlockSpec((rows, wide), lambda i: (0, k))] * n
        + [pl.BlockSpec((rows, step), column)] * n
        + [pl.BlockSpec((wide, step), column)] * len(extra),
        out_specs=pl.BlockSpec((wide, step), column),
        out_shape=shape,
        scratch_shapes=[pltpu.VMEM((n * rows, wide), BF), pltpu.VMEM((n * rows, step), BF)],
        compiler_params=params(),
        cost_estimate=cost(2 * n * rows * wide * width, *xs, *ds, *extra, shape),
        name="gate_up_grads",
    )(*xs, *ds, *extra)


def down_grads(order, hidden, rows_s, count, scale):
    rows, half = hidden.shape
    wide = rows_s.shape[1]
    deep = half // count
    step = 512 if wide % 512 == 0 else wide

    def body(order_ref, h_ref, s_ref, *refs):
        outs, scratch = refs[:count], refs[count]
        scratch[...] = mm(h_ref[...], s_ref[...], TN) * scale
        for j in range(count):
            place = pl.multiple_of(order_ref[j] * deep, deep)
            outs[j][...] = scratch[pl.ds(place, deep), :].astype(BF)

    shapes = [struct(deep, wide)] * count
    return pl.pallas_call(
        body,
        grid=(wide // step,),
        in_specs=[SMEM, whole(hidden), pl.BlockSpec((rows, step), lambda i: (0, i))],
        out_specs=[pl.BlockSpec((deep, step), lambda i: (0, i))] * count,
        out_shape=shapes,
        scratch_shapes=[pltpu.VMEM((half, step), F32)],
        compiler_params=params(),
        cost_estimate=cost(2 * rows * half * wide, hidden, rows_s, *shapes),
        name="down_grads",
    )(order, hidden, rows_s)


def slot_positions(route_block, count):
    flat = route_block.reshape(-1)
    onehot = (flat[:, None] == jnp.arange(count, dtype=jnp.int32)[None, :]).astype(jnp.int32)
    before = jnp.cumsum(onehot, axis=0) - onehot
    return (flat, jnp.sum(before * onehot, axis=1))


def exchange(blocks):
    return lax.all_to_all(blocks, "expert", split_axis=0, concat_axis=0, tiled=True)


def local(
    tokens, cotangent, routes, gates, hot_index, hot_gate, w_gate_up, w_down, w_hot_gu, w_hot_dn
):
    owners = lax.axis_size("expert")
    groups = lax.axis_size("dp")
    cores = 2 if groups % 2 == 0 else 1
    chips = groups // cores
    tok_dev, width_d = tokens.shape
    topk = routes.shape[1]
    slots = max(2, 3 * tok_dev * topk // (2 * owners))
    entries = tok_dev * topk
    rows = owners * slots
    inverse = 1.0 / (4 * groups)
    me = lax.axis_index("dp")
    chip, core = me // cores, me % cores

    def shift(value, r):
        pairs = [
            (i, ((i // cores + r) % chips) * cores + i % cores) for i in range(groups)
        ]
        return lax.ppermute(value, "dp", pairs)

    def swap(value):
        pairs = [(i, (i // cores) * cores + (i + 1) % cores) for i in range(groups)]
        return lax.ppermute(value, "dp", pairs)

    order = jnp.stack(
        [
            ((chip - r) % chips) * cores + (core + k) % cores
            for k in range(cores)
            for r in range(chips)
        ]
    ).astype(jnp.int32)

    across = 1
    while 2 * (2 * across) ** 2 <= owners:
        across *= 2
    depths = owners // across
    spot = lax.axis_index("expert")

    def hop(value, j):
        return lax.ppermute(value, "expert", [(i, i ^ j) for i in range(owners)])

    def relative(value):
        return jnp.concatenate(
            [lax.dynamic_slice_in_dim(value, spot ^ j, 1, 0) for j in range(owners)], axis=0
        )

    wide = width_d // groups
    span = wide * cores

    def features_of(value, r):
        base = ((chip + r) % chips) * cores
        return jnp.concatenate(
            [
                lax.dynamic_slice_in_dim(value, (base + (core + k) % cores) * wide, wide, 1)
                for k in range(cores)
            ],
            axis=1,
        )

    flat, pos = slot_positions(routes, owners)
    dest = flat * slots + pos
    dests = [dest] + [shift(dest, r) for r in range(1, chips)]
    halves = [features_of(tokens, 0)] + [
        shift(features_of(tokens, r), r) for r in range(1, chips)
    ]
    gu_chip = w_gate_up[0]
    if cores == 2:
        gu_chip = jnp.concatenate([gu_chip, swap(gu_chip)], axis=0)

    slot_ids = jnp.arange(rows, dtype=jnp.int32)[:, None]
    picks = [(slot_ids == one[None, :]).astype(BF) for one in dests]

    hot_dev = hot_index.shape[0]
    narrow = width_d // owners
    hot_pick = (
        hot_index[:, None] == jnp.arange(tok_dev, dtype=jnp.int32)[None, :]
    ).astype(BF)
    hot_x = mm(hot_pick, tokens).astype(BF)
    hot_s = (hot_gate[:, None] * mm(hot_pick, cotangent)).astype(BF)
    hot_send = (
        jnp.stack([hot_x, hot_s])
        .reshape(2, hot_dev, owners, narrow)
        .transpose(2, 0, 1, 3)
    )

    def as_rows(value, width):
        value = value.reshape(owners, -1)
        spare = -value.shape[1] % width
        return jnp.pad(value, ((0, 0), (0, spare))).reshape(owners, -1, width)

    scaled = (gates[:, :, None] * cotangent[:, None, :].astype(F32)).astype(BF)
    send_s = mm(picks[0], scaled.reshape(entries, width_d)).astype(BF)
    hot_rows = as_rows(hot_send, span)

    hid = w_hot_dn.shape[0]
    hot_w = jnp.concatenate([w_hot_gu, w_hot_dn[None]], axis=0).reshape(3 * hid, narrow)
    hot_w, down, halves[-1] = lax.optimization_barrier((hot_w, w_down[0], halves[-1]))
    hot_near = [hot_w] + [shift(hot_w, r) for r in range(1, chips)]
    down_near = [down] + [shift(down, r) for r in range(1, chips)]

    packed = [
        mm(one, jnp.repeat(part, topk, axis=0) if topk > 1 else part)
        .astype(BF)
        .reshape(owners, slots, span)
        for one, part in zip(picks, halves)
    ]
    first = exchange(jnp.concatenate(packed + [hot_rows], axis=1))
    xs = [
        first[:, r * slots : (r + 1) * slots].reshape(rows, span) for r in range(chips)
    ]
    hot_recv = first[:, chips * slots :].reshape(owners, -1)[:, : 2 * hot_dev * narrow]
    hot_recv = hot_recv.reshape(owners, 2, hot_dev, narrow)
    send_s = after(send_s, first)
    rows_s = exchange(send_s.reshape(owners, slots, width_d)).reshape(rows, width_d)

    parts = activations(xs, gu_chip)
    act_in = [shift(parts[r], -r) for r in range(1, chips)]

    hot_near = list(after(tuple(hot_near), parts[-1]))
    hot_all = jnp.concatenate(hot_near, axis=0)
    down_near = list(after(tuple(down_near), parts[-1]))
    down_blocks = list(down_near)
    if cores == 2:
        hot_all = jnp.concatenate([hot_all, swap(hot_all)], axis=0)
        down_blocks = down_blocks + [swap(block) for block in down_near]
    columns = groups * 3 * hid
    kind = (jnp.arange(columns, dtype=jnp.int32) // hid) % 3
    from_x = kind < 2
    hot_recv = after(relative(hot_recv), parts[-1])
    xs_hot = hot_recv.transpose(1, 0, 2, 3).reshape(2 * owners * hot_dev, narrow)
    both = mm(xs_hot, hot_all, NT).reshape(2, owners * hot_dev, columns)
    partial = jnp.where(from_x[None, :], both[0], both[1]).astype(BF)
    partial = partial.reshape(depths, across, hot_dev, columns)
    level_in = [hop(partial[:, j], j) for j in range(1, across)]
    act_in, level_in = lax.optimization_barrier((act_in, level_in))
    level = partial[:, 0].astype(F32)
    for value in level_in:
        level = level + value.astype(F32)
    level = level.astype(BF)
    depth_in = [hop(level[j], j * across) for j in range(1, depths)]

    out, hidden, factors = outputs(order, parts[0], act_in, down_blocks)
    out = after(out, rows_s)
    back_out = exchange(out.reshape(owners, slots, width_d)).reshape(rows, width_d)
    d_act = deltas(order, rows_s, factors, down_blocks)
    ds = [d_act] + [shift(d_act, r) for r in range(1, chips)]

    depth_in = list(after(tuple(depth_in), d_act))
    hot_act = level[0].astype(F32)
    for value in depth_in:
        hot_act = hot_act + value.astype(F32)
    hot_act = hot_act.reshape(hot_dev, groups, 3, hid)
    hot_g, hot_u, hot_dh = hot_act[:, :, 0], hot_act[:, :, 1], hot_act[:, :, 2]
    hot_sigma = jax.nn.sigmoid(hot_g)
    hot_own = jnp.stack(
        [
            hot_dh * hot_u * hot_sigma * (1.0 + hot_g * (1.0 - hot_sigma)),
            hot_dh * hot_g * hot_sigma,
            hot_g * hot_sigma * hot_u,
        ],
        axis=2,
    )
    hot_own = hot_own.astype(BF).reshape(hot_dev, columns)
    line = jnp.stack([hot_own] + [hop(hot_own, j * across) for j in range(1, depths)])

    hidden_dn = after(hidden, d_act)
    dn_parts = down_grads(order, hidden_dn, rows_s, groups, inverse)
    if cores == 2:
        dn_in = [swap(part) for part in dn_parts[chips:]]
    ds, line = lax.optimization_barrier((ds, line))
    full = jnp.stack([line] + [hop(line, j) for j in range(1, across)], axis=1)

    backs = row_grads(ds, gu_chip)
    full = after(full, backs[0])
    full = full.reshape(owners * hot_dev, columns)
    zero = jnp.zeros((), BF)
    masked = jnp.concatenate(
        [jnp.where(from_x[None, :], full, zero), jnp.where(from_x[None, :], zero, full)], axis=0
    )
    hot_back = mm(masked, hot_all).astype(BF).reshape(2, owners, hot_dev, narrow)
    hot_back = relative(hot_back.transpose(1, 0, 2, 3))
    fourth_in = jnp.concatenate(
        [back.reshape(owners, slots, span) for back in backs] + [as_rows(hot_back, span)], axis=1
    )
    fourth = exchange(fourth_in)

    xs_late = list(after(tuple(xs), fourth_in))
    if cores == 2:
        gu_in = swap(gate_up_grads(xs_late, ds, 1, wide, inverse, None))
        dn_sum = [
            (part.astype(F32) + value.astype(F32)).astype(BF)
            for part, value in zip(dn_parts, dn_in)
        ]
    else:
        gu_in = None
        dn_sum = list(dn_parts)
    dn_total = dn_sum[0].astype(F32)
    for r in range(1, chips):
        dn_total = dn_total + shift(dn_sum[r], -r).astype(F32)
    grad_dn = dn_total.astype(BF)
    masked_late = after(masked, fourth_in)
    share = chips * 3 * hid
    hot_sum = mm(masked_late[:, :share], xs_hot, TN) * inverse
    if cores == 2:
        hot_sum = hot_sum + swap(
            (mm(masked_late[:, share:], xs_hot, TN) * inverse).astype(BF)
        ).astype(F32)
    hot_sum = hot_sum.astype(BF).reshape(chips, 3 * hid, narrow)
    hot_total = hot_sum[0].astype(F32)
    for r in range(1, chips):
        hot_total = hot_total + shift(hot_sum[r], -r).astype(F32)
    grad_hot = hot_total.astype(BF).reshape(3, hid, narrow)
    grad_gu = gate_up_grads(xs_late, ds, 0, wide, inverse, gu_in)

    hot_back = fourth[:, chips * slots :].reshape(owners, -1)[:, : 2 * hot_dev * narrow]
    hot_back = hot_back.reshape(owners, 2, hot_dev, narrow)
    hot_back = hot_back.transpose(1, 2, 0, 3).reshape(2, hot_dev, width_d)
    picked = mm(picks[0], back_out, TN)
    layer_out = (
        (gates.reshape(entries)[:, None] * picked).reshape(tok_dev, topk, width_d).sum(axis=1)
    )
    token_gate = jnp.sum(jnp.where(hot_pick > 0, hot_gate[:, None], 0.0), axis=0)
    layer_out = layer_out + token_gate[:, None] * mm(hot_pick, hot_back[1], TN)
    pieces = []
    for r in range(chips):
        back = fourth[:, r * slots : (r + 1) * slots].reshape(rows, span)
        piece = mm(picks[r], back, TN)
        piece = piece.reshape(tok_dev, topk, span).sum(axis=1).astype(BF)
        if r > 0:
            piece = shift(piece, -r)
        pieces += [piece[:, k * wide : (k + 1) * wide] for k in range(cores)]
    pieces = jnp.stack(pieces)
    input_grad = jnp.concatenate(
        [
            lax.dynamic_index_in_dim(
                pieces,
                ((p - chip) % chips) * cores + (q - core) % cores,
                0,
                keepdims=False,
            )
            for p in range(chips)
            for q in range(cores)
        ],
        axis=1,
    ).astype(F32)
    input_grad = input_grad + mm(hot_pick, hot_back[0], TN)
    return (
        layer_out.astype(BF),
        input_grad.astype(BF),
        grad_gu[None],
        grad_dn[None],
        grad_hot[:2],
        grad_hot[2],
    )


def solution(mesh):
    tok = P(("dp", "expert"), None)
    flat = P(("dp", "expert"))
    rows = P("expert", "dp", None)
    hot = (P(None, "dp", "expert"), P("dp", "expert"))
    return jax.shard_map(
        local,
        mesh=mesh,
        in_specs=(tok, tok, tok, tok, flat, flat, rows, rows) + hot,
        out_specs=(tok, tok, rows, rows) + hot,
        check_vma=False,
    )
```

```python
import jax
import jax.numpy as jnp
from jax import lax
from jax.experimental import pallas as pl
from jax.experimental.pallas import tpu as pltpu
from jax.sharding import PartitionSpec as P

BF = jnp.bfloat16
F32 = jnp.float32
NN = (((1,), (0,)), ((), ()))
NT = (((1,), (1,)), ((), ()))
TN = (((0,), (0,)), ((), ()))
ROOM = 56 * 1024 * 1024


def mm(a, b, dims=NN):
    return lax.dot_general(a, b, dims, preferred_element_type=F32)


def after(value, *earlier):
    return lax.optimization_barrier((value,) + earlier)[0]


def params():
    return pltpu.CompilerParams(vmem_limit_bytes=ROOM)


LIGHT = pl.CostEstimate(flops=1, bytes_accessed=1, transcendentals=0)


def struct(*shape, dtype=BF):
    return jax.ShapeDtypeStruct(shape, dtype)


def whole(array):
    return pl.BlockSpec(array.shape, lambda *_: (0,) * len(array.shape))


def stack_rows(refs, scratch):
    rows = refs[0].shape[0]
    for i, ref in enumerate(refs):
        scratch[i * rows : (i + 1) * rows, :] = ref[...]


def activations(xs, w):
    n, rows, depth, width = len(xs), xs[0].shape[0], w.shape[0], w.shape[1]
    step = 512 if width % 512 == 0 else width

    def body(*refs):
        ins, w_ref, outs, scratch = refs[:n], refs[n], refs[n + 1 : 2 * n + 1], refs[-1]

        @pl.when(pl.program_id(0) == 0)
        def _():
            stack_rows(ins, scratch)

        found = mm(scratch[...], w_ref[...])
        outs[0][...] = found[:rows]
        for i in range(1, n):
            outs[i][...] = found[i * rows : (i + 1) * rows].astype(BF)

    shapes = [struct(rows, width, dtype=F32)] + [struct(rows, width)] * (n - 1)
    return pl.pallas_call(
        body,
        grid=(width // step,),
        in_specs=[whole(x) for x in xs] + [pl.BlockSpec((depth, step), lambda i: (0, i))],
        out_specs=[pl.BlockSpec((rows, step), lambda i: (0, i))] * n,
        out_shape=shapes,
        scratch_shapes=[pltpu.VMEM((n * rows, depth), BF)],
        compiler_params=params(),
        cost_estimate=LIGHT,
        name="activations",
    )(*xs, w)


def fetch(order_ref, blocks, w_ref, sems):
    deep = blocks[0].shape[0]
    copies = []
    for j, block in enumerate(blocks):
        place = pl.multiple_of(order_ref[j] * deep, deep)
        copies.append(pltpu.make_async_copy(block, w_ref.at[pl.ds(place, deep)], sems.at[j]))
        copies[-1].start()
    return copies


def down_scratch(blocks):
    deep, width = blocks[0].shape
    return [pltpu.VMEM((len(blocks) * deep, width), BF), pltpu.SemaphoreType.DMA((len(blocks),))]


SMEM = pl.BlockSpec(memory_space=pltpu.SMEM)
ANYWHERE = pl.BlockSpec(memory_space=pl.ANY)
INSIDE = pl.BlockSpec(memory_space=pltpu.VMEM)


def outputs(order, own, others, blocks):
    rows, width = own.shape
    half = width // 2
    wide = blocks[0].shape[1]
    n, m = len(others), len(blocks)
    step = 512 if wide % 512 == 0 else wide

    def body(order_ref, own_ref, *refs):
        parts, down, (out_ref, hid_ref, fac_ref, w_ref, sems) = refs[:n], refs[n : n + m], refs[n + m :]
        copies = fetch(order_ref, down, w_ref, sems)
        act = own_ref[...]
        for part in parts:
            act = act + part[...].astype(F32)
        g = act[:, :half]
        u = act[:, half:]
        s = jax.nn.sigmoid(g)
        fac_ref[:, :half] = u * s * (1.0 + g * (1.0 - s))
        fac_ref[:, half:] = g * s
        hid_ref[...] = (g * s * u).astype(BF)
        for copy in copies:
            copy.wait()
        for c in range(0, wide, step):
            out_ref[:, c : c + step] = mm(hid_ref[...], w_ref[:, c : c + step]).astype(BF)

    shapes = [struct(rows, wide), struct(rows, half), struct(rows, width, dtype=F32)]
    return pl.pallas_call(
        body,
        in_specs=[SMEM] + [INSIDE] * (1 + n) + [ANYWHERE] * m,
        out_specs=[INSIDE] * 3,
        out_shape=shapes,
        scratch_shapes=down_scratch(blocks),
        compiler_params=params(),
        cost_estimate=LIGHT,
        name="outputs",
    )(order, own, *others, *blocks)


def deltas(order, rows_s, factors, blocks):
    rows, width = factors.shape
    half = width // 2
    m = len(blocks)

    def body(order_ref, s_ref, fac_ref, *refs):
        down, (d_ref, w_ref, sems) = refs[:m], refs[m:]
        for copy in fetch(order_ref, down, w_ref, sems):
            copy.wait()
        d_hidden = mm(s_ref[...], w_ref[...], NT)
        d_ref[:, :half] = (d_hidden * fac_ref[:, :half]).astype(BF)
        d_ref[:, half:] = (d_hidden * fac_ref[:, half:]).astype(BF)

    shape = struct(rows, width)
    return pl.pallas_call(
        body,
        in_specs=[SMEM, INSIDE, INSIDE] + [ANYWHERE] * m,
        out_specs=INSIDE,
        out_shape=shape,
        scratch_shapes=down_scratch(blocks),
        compiler_params=params(),
        cost_estimate=LIGHT,
        name="deltas",
    )(order, rows_s, factors, *blocks)


def row_grads(ds, w):
    n, rows, width, depth = len(ds), ds[0].shape[0], ds[0].shape[1], w.shape[0]
    step = 256 if depth % 256 == 0 else depth

    def body(*refs):
        ins, w_ref, outs, scratch = refs[:n], refs[n], refs[n + 1 : 2 * n + 1], refs[-1]

        @pl.when(pl.program_id(0) == 0)
        def _():
            stack_rows(ins, scratch)

        found = mm(scratch[...], w_ref[...], NT).astype(BF)
        for i in range(n):
            outs[i][...] = found[i * rows : (i + 1) * rows]

    shapes = [struct(rows, depth)] * n
    return pl.pallas_call(
        body,
        grid=(depth // step,),
        in_specs=[whole(d) for d in ds] + [pl.BlockSpec((step, width), lambda i: (i, 0))],
        out_specs=[pl.BlockSpec((rows, step), lambda i: (0, i))] * n,
        out_shape=shapes,
        scratch_shapes=[pltpu.VMEM((n * rows, width), BF)],
        compiler_params=params(),
        cost_estimate=LIGHT,
        name="row_grads",
    )(*ds, w)


def gate_up_grads(xs, ds, k, wide, scale, received):
    n, rows, width = len(xs), xs[0].shape[0], ds[0].shape[1]
    step = 512 if width % 512 == 0 else width
    extra = [] if received is None else [received]
    if wide % 128 != 0:
        xs, k = [x[:, k * wide : (k + 1) * wide] for x in xs], 0

    def body(*refs):
        x_refs, d_refs, rest = refs[:n], refs[n : 2 * n], refs[2 * n :]
        out_ref, x_scr, d_scr = rest[-3:]

        @pl.when(pl.program_id(0) == 0)
        def _():
            stack_rows(x_refs, x_scr)

        stack_rows(d_refs, d_scr)
        found = mm(x_scr[...], d_scr[...], TN) * scale
        if extra:
            found = found + rest[0][...].astype(F32)
        out_ref[...] = found.astype(BF)

    shape = struct(wide, width)
    column = lambda i: (0, i)
    return pl.pallas_call(
        body,
        grid=(width // step,),
        in_specs=[pl.BlockSpec((rows, wide), lambda i: (0, k))] * n
        + [pl.BlockSpec((rows, step), column)] * n
        + [pl.BlockSpec((wide, step), column)] * len(extra),
        out_specs=pl.BlockSpec((wide, step), column),
        out_shape=shape,
        scratch_shapes=[pltpu.VMEM((n * rows, wide), BF), pltpu.VMEM((n * rows, step), BF)],
        compiler_params=params(),
        cost_estimate=LIGHT,
        name="gate_up_grads",
    )(*xs, *ds, *extra)


def down_grads(order, hidden, rows_s, count, scale):
    rows, half = hidden.shape
    wide = rows_s.shape[1]
    deep = half // count
    step = 512 if wide % 512 == 0 else wide

    def body(order_ref, h_ref, s_ref, *refs):
        outs, scratch = refs[:count], refs[count]
        scratch[...] = mm(h_ref[...], s_ref[...], TN) * scale
        for j in range(count):
            place = pl.multiple_of(order_ref[j] * deep, deep)
            outs[j][...] = scratch[pl.ds(place, deep), :].astype(BF)

    shapes = [struct(deep, wide)] * count
    return pl.pallas_call(
        body,
        grid=(wide // step,),
        in_specs=[SMEM, whole(hidden), pl.BlockSpec((rows, step), lambda i: (0, i))],
        out_specs=[pl.BlockSpec((deep, step), lambda i: (0, i))] * count,
        out_shape=shapes,
        scratch_shapes=[pltpu.VMEM((half, step), F32)],
        compiler_params=params(),
        cost_estimate=LIGHT,
        name="down_grads",
    )(order, hidden, rows_s)


def popular_partials(select, packed, near, far, hid):
    count = select.shape[1]
    narrow = packed.shape[1] // 4
    blocks = (near.shape[0] + (0 if far is None else far.shape[0])) // (3 * hid)
    columns = blocks * 3 * hid
    weights = [near] if far is None else [near, far]

    def body(sel_ref, in_ref, *refs):
        w_refs, (x_ref, s_ref, p_ref) = refs[: len(weights)], refs[len(weights) :]
        t0 = mm(sel_ref[0], in_ref[...])
        t1 = mm(sel_ref[1], in_ref[...])
        x = (t0[:, :narrow] + t1[:, narrow : 2 * narrow]).astype(BF)
        s = (t0[:, 2 * narrow : 3 * narrow] + t1[:, 3 * narrow :]).astype(BF)
        x_ref[...] = x
        s_ref[...] = s
        at = 0
        for w_ref in w_refs:
            for top in range(0, w_ref.shape[0], 3 * hid):
                p_ref[:, at : at + 2 * hid] = mm(x, w_ref[top : top + 2 * hid, :], NT).astype(BF)
                p_ref[:, at + 2 * hid : at + 3 * hid] = mm(
                    s, w_ref[top + 2 * hid : top + 3 * hid, :], NT
                ).astype(BF)
                at += 3 * hid

    return pl.pallas_call(
        body,
        in_specs=[INSIDE] * (2 + len(weights)),
        out_specs=[INSIDE] * 3,
        out_shape=[struct(count, narrow), struct(count, narrow), struct(count, columns)],
        compiler_params=params(),
        cost_estimate=LIGHT,
        name="popular_partials",
    )(select, packed, *weights)


def popular_middle(own, others, hid):
    rows, columns = own.shape

    def body(own_ref, *refs):
        parts, out_ref = refs[:-1], refs[-1]
        act = own_ref[...].astype(F32)
        for part in parts:
            act = act + part[...].astype(F32)
        for at in range(0, columns, 3 * hid):
            g = act[:, at : at + hid]
            u = act[:, at + hid : at + 2 * hid]
            dh = act[:, at + 2 * hid : at + 3 * hid]
            s = jax.nn.sigmoid(g)
            out_ref[:, at : at + hid] = (dh * u * s * (1.0 + g * (1.0 - s))).astype(BF)
            out_ref[:, at + hid : at + 2 * hid] = (dh * g * s).astype(BF)
            out_ref[:, at + 2 * hid : at + 3 * hid] = (g * s * u).astype(BF)

    return pl.pallas_call(
        body,
        in_specs=[INSIDE] * (1 + len(others)),
        out_specs=INSIDE,
        out_shape=struct(rows, columns),
        compiler_params=params(),
        cost_estimate=LIGHT,
        name="popular_middle",
    )(own, *others)


def popular_back(select, pieces, x, s, near, far, hid, scale):
    count, narrow = x.shape
    columns = pieces[0].shape[1]
    blocks = columns // (3 * hid)
    spots = select.shape[2]
    weights = [near] if far is None else [near, far]
    n, m = len(pieces), len(weights)
    share = columns // m

    def body(sel_ref, x_ref, s_ref, *refs):
        ins, w_refs, back_ref = refs[:n], refs[n : n + m], refs[n + m]
        grads, scratch = refs[n + m + 1 : -1], refs[-1]
        stack_rows(ins, scratch)
        grad = None
        out = None
        at = 0
        for w_ref, g_ref in zip(w_refs, grads):
            for top in range(0, share, 3 * hid):
                d = scratch[:, at : at + 2 * hid]
                h = scratch[:, at + 2 * hid : at + 3 * hid]
                first = mm(d, w_ref[top : top + 2 * hid, :])
                second = mm(h, w_ref[top + 2 * hid : top + 3 * hid, :])
                grad = first if grad is None else grad + first
                out = second if out is None else out + second
                g_ref[top : top + 2 * hid, :] = (mm(d, x_ref[...], TN) * scale).astype(BF)
                g_ref[top + 2 * hid : top + 3 * hid, :] = (mm(h, s_ref[...], TN) * scale).astype(BF)
                at += 3 * hid
        grad = grad.astype(BF)
        out = out.astype(BF)
        for i in range(2):
            back_ref[:, i * narrow : (i + 1) * narrow] = mm(sel_ref[i], grad, TN).astype(BF)
            back_ref[:, (2 + i) * narrow : (3 + i) * narrow] = mm(sel_ref[i], out, TN).astype(BF)

    return pl.pallas_call(
        body,
        in_specs=[INSIDE] * (3 + n + m),
        out_specs=[INSIDE] * (1 + m),
        out_shape=[struct(spots, 4 * narrow)] + [struct(share, narrow)] * m,
        scratch_shapes=[pltpu.VMEM((count, columns), BF)],
        compiler_params=params(),
        cost_estimate=LIGHT,
        name="popular_back",
    )(select, x, s, *pieces, *weights)


def slot_positions(route_block, count):
    flat = route_block.reshape(-1)
    onehot = (flat[:, None] == jnp.arange(count, dtype=jnp.int32)[None, :]).astype(jnp.int32)
    before = jnp.cumsum(onehot, axis=0) - onehot
    return (flat, jnp.sum(before * onehot, axis=1))


def exchange(blocks):
    return lax.all_to_all(blocks, "expert", split_axis=0, concat_axis=0, tiled=True)


def local(
    tokens, cotangent, routes, gates, hot_index, hot_gate, w_gate_up, w_down, w_hot_gu, w_hot_dn
):
    owners = lax.axis_size("expert")
    groups = lax.axis_size("dp")
    cores = 2 if groups % 2 == 0 else 1
    chips = groups // cores
    tok_dev, width_d = tokens.shape
    topk = routes.shape[1]
    slots = max(2, 3 * tok_dev * topk // (2 * owners))
    entries = tok_dev * topk
    rows = owners * slots
    inverse = 1.0 / (4 * groups)
    me = lax.axis_index("dp")
    chip, core = me // cores, me % cores

    def shift(value, r):
        pairs = [
            (i, ((i // cores + r) % chips) * cores + i % cores) for i in range(groups)
        ]
        return lax.ppermute(value, "dp", pairs)

    def swap(value):
        pairs = [(i, (i // cores) * cores + (i + 1) % cores) for i in range(groups)]
        return lax.ppermute(value, "dp", pairs)

    order = jnp.stack(
        [
            ((chip - r) % chips) * cores + (core + k) % cores
            for k in range(cores)
            for r in range(chips)
        ]
    ).astype(jnp.int32)

    across = 1
    while 2 * (2 * across) ** 2 <= owners:
        across *= 2
    depths = owners // across
    spot = lax.axis_index("expert")

    def hop(value, j):
        return lax.ppermute(value, "expert", [(i, i ^ j) for i in range(owners)])

    wide = width_d // groups
    span = wide * cores

    def features_of(value, r):
        base = ((chip + r) % chips) * cores
        return jnp.concatenate(
            [
                lax.dynamic_slice_in_dim(value, (base + (core + k) % cores) * wide, wide, 1)
                for k in range(cores)
            ],
            axis=1,
        )

    sent = [features_of(tokens, r) for r in range(1, chips)]
    routes, sent = lax.optimization_barrier((routes, sent))
    halves = [features_of(tokens, 0)] + [shift(sent[r - 1], r) for r in range(1, chips)]
    flat, pos = slot_positions(routes, owners)
    dest = flat * slots + pos
    dests = [dest] + [shift(dest, r) for r in range(1, chips)]
    gu_chip = w_gate_up[0]
    if cores == 2:
        gu_chip = jnp.concatenate([gu_chip, swap(gu_chip)], axis=0)

    slot_ids = jnp.arange(rows, dtype=jnp.int32)[:, None]
    picks = [(slot_ids == one[None, :]).astype(BF) for one in dests]

    hot_dev = hot_index.shape[0]
    narrow = width_d // owners
    hot_pick = (
        hot_index[:, None] == jnp.arange(tok_dev, dtype=jnp.int32)[None, :]
    ).astype(BF)
    hot_x = mm(hot_pick, tokens).astype(BF)
    hot_s = (hot_gate[:, None] * mm(hot_pick, cotangent)).astype(BF)
    hot_half = hot_dev // 2
    hot_send = jnp.concatenate([hot_x, hot_s], axis=0).reshape(4, hot_half, owners, narrow)
    hot_send = hot_send.transpose(2, 1, 0, 3)
    count = owners * hot_dev
    row = jnp.arange(count, dtype=jnp.int32)
    step = row // hot_dev
    source = spot ^ ((step % depths) * across + step // depths)
    packed_row = source * hot_half + row % hot_half
    hit = packed_row[:, None] == jnp.arange(owners * hot_half, dtype=jnp.int32)[None, :]
    low = (row % hot_dev < hot_half)[:, None]
    select = jnp.stack([hit & low, hit & ~low]).astype(BF)

    def as_rows(value, width):
        value = value.reshape(owners, -1)
        spare = -value.shape[1] % width
        return jnp.pad(value, ((0, 0), (0, spare))).reshape(owners, -1, width)

    scaled = (gates[:, :, None] * cotangent[:, None, :].astype(F32)).astype(BF)
    send_s = mm(picks[0], scaled.reshape(entries, width_d)).astype(BF)
    hot_rows = as_rows(hot_send, span)

    hid = w_hot_dn.shape[0]
    hot_w = jnp.concatenate([w_hot_gu, w_hot_dn[None]], axis=0).reshape(3 * hid, narrow)
    hot_w, down, halves[-1] = lax.optimization_barrier((hot_w, w_down[0], halves[-1]))
    hot_near = [hot_w] + [shift(hot_w, r) for r in range(1, chips)]
    down_near = [down] + [shift(down, r) for r in range(1, chips)]

    packed = [
        mm(one, jnp.repeat(part, topk, axis=0) if topk > 1 else part)
        .astype(BF)
        .reshape(owners, slots, span)
        for one, part in zip(picks, halves)
    ]
    first = exchange(jnp.concatenate(packed + [hot_rows], axis=1))
    xs = [
        first[:, r * slots : (r + 1) * slots].reshape(rows, span) for r in range(chips)
    ]
    hot_recv = first[:, chips * slots :].reshape(owners, -1)[:, : 2 * hot_dev * narrow]
    hot_recv = hot_recv.reshape(owners * hot_half, 4 * narrow)
    send_s = after(send_s, first)
    rows_s = exchange(send_s.reshape(owners, slots, width_d)).reshape(rows, width_d)

    parts = activations(xs, gu_chip)
    act_in = [shift(parts[r], -r) for r in range(1, chips)]

    hot_near = list(after(tuple(hot_near), parts[-1]))
    hot_near = jnp.concatenate(hot_near, axis=0)
    hot_far = swap(hot_near) if cores == 2 else None
    down_near = list(after(tuple(down_near), parts[-1]))
    down_blocks = list(down_near)
    if cores == 2:
        down_blocks = down_blocks + [swap(block) for block in down_near]
    columns = groups * 3 * hid
    hot_recv = after(hot_recv, parts[-1])
    hot_x, hot_s, partial = popular_partials(select, hot_recv, hot_near, hot_far, hid)
    share = depths * hot_dev
    level_in = [hop(partial[j * share : (j + 1) * share], j) for j in range(1, across)]

    out, hidden, factors = outputs(order, parts[0], act_in, down_blocks)
    level_in = list(after(tuple(level_in), out))
    level = partial[:share].astype(F32)
    for value in level_in:
        level = level + value.astype(F32)
    level = level.astype(BF)
    level = [level[j * hot_dev : (j + 1) * hot_dev] for j in range(depths)]
    depth_in = [hop(level[j], j * across) for j in range(1, depths)]
    out = after(out, rows_s)
    back_out = exchange(out.reshape(owners, slots, width_d)).reshape(rows, width_d)
    d_act = deltas(order, rows_s, factors, down_blocks)
    ds = [d_act] + [shift(d_act, r) for r in range(1, chips)]

    depth_in = list(after(tuple(depth_in), d_act))
    hot_own = popular_middle(level[0], depth_in, hid)
    line = jnp.concatenate([hot_own] + [hop(hot_own, j * across) for j in range(1, depths)])

    hidden_dn = after(hidden, d_act)
    dn_parts = down_grads(order, hidden_dn, rows_s, groups, inverse)
    if cores == 2:
        dn_in = [swap(part) for part in dn_parts[chips:]]
    lines = [line] + [hop(line, j) for j in range(1, across)]

    backs = row_grads(ds, gu_chip)
    lines = list(after(tuple(lines), backs[0]))
    hot_back, *hot_grads = popular_back(
        select, lines, hot_x, hot_s, hot_near, hot_far, hid, inverse
    )
    hot_back = hot_back.reshape(owners, hot_half, 4 * narrow)
    fourth_in = jnp.concatenate(
        [back.reshape(owners, slots, span) for back in backs] + [as_rows(hot_back, span)], axis=1
    )
    fourth = exchange(fourth_in)

    xs_late = list(after(tuple(xs), fourth_in))
    if cores == 2:
        gu_in = swap(gate_up_grads(xs_late, ds, 1, wide, inverse, None))
        dn_sum = [
            (part.astype(F32) + value.astype(F32)).astype(BF)
            for part, value in zip(dn_parts, dn_in)
        ]
    else:
        gu_in = None
        dn_sum = list(dn_parts)
    dn_total = dn_sum[0].astype(F32)
    for r in range(1, chips):
        dn_total = dn_total + shift(dn_sum[r], -r).astype(F32)
    grad_dn = dn_total.astype(BF)
    hot_sum = hot_grads[0]
    if cores == 2:
        hot_sum = (hot_sum.astype(F32) + swap(hot_grads[1]).astype(F32)).astype(BF)
    hot_sum = hot_sum.reshape(chips, 3 * hid, narrow)
    hot_total = hot_sum[0].astype(F32)
    for r in range(1, chips):
        hot_total = hot_total + shift(hot_sum[r], -r).astype(F32)
    grad_hot = hot_total.astype(BF).reshape(3, hid, narrow)
    grad_gu = gate_up_grads(xs_late, ds, 0, wide, inverse, gu_in)

    hot_back = fourth[:, chips * slots :].reshape(owners, -1)[:, : 2 * hot_dev * narrow]
    hot_back = hot_back.reshape(owners, hot_half, 4, narrow)
    hot_back = hot_back.transpose(2, 1, 0, 3).reshape(2, hot_dev, width_d)
    picked = mm(picks[0], back_out, TN)
    layer_out = (
        (gates.reshape(entries)[:, None] * picked).reshape(tok_dev, topk, width_d).sum(axis=1)
    )
    token_gate = jnp.sum(jnp.where(hot_pick > 0, hot_gate[:, None], 0.0), axis=0)
    layer_out = layer_out + token_gate[:, None] * mm(hot_pick, hot_back[1], TN)
    pieces = []
    for r in range(chips):
        back = fourth[:, r * slots : (r + 1) * slots].reshape(rows, span)
        piece = mm(picks[r], back, TN)
        piece = piece.reshape(tok_dev, topk, span).sum(axis=1).astype(BF)
        if r > 0:
            piece = shift(piece, -r)
        pieces += [piece[:, k * wide : (k + 1) * wide] for k in range(cores)]
    pieces = jnp.stack(pieces)
    input_grad = jnp.concatenate(
        [
            lax.dynamic_index_in_dim(
                pieces,
                ((p - chip) % chips) * cores + (q - core) % cores,
                0,
                keepdims=False,
            )
            for p in range(chips)
            for q in range(cores)
        ],
        axis=1,
    ).astype(F32)
    input_grad = input_grad + mm(hot_pick, hot_back[0], TN)
    return (
        layer_out.astype(BF),
        input_grad.astype(BF),
        grad_gu[None],
        grad_dn[None],
        grad_hot[:2],
        grad_hot[2],
    )


def solution(mesh):
    tok = P(("dp", "expert"), None)
    flat = P(("dp", "expert"))
    rows = P("expert", "dp", None)
    hot = (P(None, "dp", "expert"), P("dp", "expert"))
    return jax.shard_map(
        local,
        mesh=mesh,
        in_specs=(tok, tok, tok, tok, flat, flat, rows, rows) + hot,
        out_specs=(tok, tok, rows, rows) + hot,
        check_vma=False,
    )
```

```python
import jax
import jax.numpy as jnp
from jax import lax
from jax.experimental import pallas as pl
from jax.experimental.pallas import tpu as pltpu
from jax.sharding import PartitionSpec as P

BF = jnp.bfloat16
F32 = jnp.float32
NN = (((1,), (0,)), ((), ()))
NT = (((1,), (1,)), ((), ()))
TN = (((0,), (0,)), ((), ()))
ROOM = 56 * 1024 * 1024


def mm(a, b, dims=NN):
    return lax.dot_general(a, b, dims, preferred_element_type=F32)


def after(value, *earlier):
    return lax.optimization_barrier((value,) + earlier)[0]


def params():
    return pltpu.CompilerParams(vmem_limit_bytes=ROOM)


LIGHT = pl.CostEstimate(flops=1, bytes_accessed=1, transcendentals=0)


def struct(*shape, dtype=BF):
    return jax.ShapeDtypeStruct(shape, dtype)


def whole(array):
    return pl.BlockSpec(array.shape, lambda *_: (0,) * len(array.shape))


def stack_rows(refs, scratch):
    rows = refs[0].shape[0]
    for i, ref in enumerate(refs):
        scratch[i * rows : (i + 1) * rows, :] = ref[...]


def activations(xs, w):
    n, rows, depth, width = len(xs), xs[0].shape[0], w.shape[0], w.shape[1]
    step = 512 if width % 512 == 0 else width

    def body(*refs):
        ins, w_ref, outs, scratch = refs[:n], refs[n], refs[n + 1 : 2 * n + 1], refs[-1]

        @pl.when(pl.program_id(0) == 0)
        def _():
            stack_rows(ins, scratch)

        found = mm(scratch[...], w_ref[...])
        outs[0][...] = found[:rows]
        for i in range(1, n):
            outs[i][...] = found[i * rows : (i + 1) * rows].astype(BF)

    shapes = [struct(rows, width, dtype=F32)] + [struct(rows, width)] * (n - 1)
    return pl.pallas_call(
        body,
        grid=(width // step,),
        in_specs=[whole(x) for x in xs] + [pl.BlockSpec((depth, step), lambda i: (0, i))],
        out_specs=[pl.BlockSpec((rows, step), lambda i: (0, i))] * n,
        out_shape=shapes,
        scratch_shapes=[pltpu.VMEM((n * rows, depth), BF)],
        compiler_params=params(),
        cost_estimate=LIGHT,
        name="activations",
    )(*xs, w)


def fetch(order_ref, blocks, w_ref, sems):
    deep = blocks[0].shape[0]
    copies = []
    for j, block in enumerate(blocks):
        place = pl.multiple_of(order_ref[j] * deep, deep)
        copies.append(pltpu.make_async_copy(block, w_ref.at[pl.ds(place, deep)], sems.at[j]))
        copies[-1].start()
    return copies


def down_scratch(blocks):
    deep, width = blocks[0].shape
    return [pltpu.VMEM((len(blocks) * deep, width), BF), pltpu.SemaphoreType.DMA((len(blocks),))]


SMEM = pl.BlockSpec(memory_space=pltpu.SMEM)
ANYWHERE = pl.BlockSpec(memory_space=pl.ANY)
INSIDE = pl.BlockSpec(memory_space=pltpu.VMEM)


def middle(order, own, others, rows_s, blocks):
    rows, width = own.shape
    half = width // 2
    wide = blocks[0].shape[1]
    n, m = len(others), len(blocks)
    step = 512 if wide % 512 == 0 else wide

    def body(order_ref, own_ref, s_ref, *refs):
        parts, down = refs[:n], refs[n : n + m]
        out_ref, hid_ref, d_ref, w_ref, sems = refs[n + m :]
        copies = fetch(order_ref, down, w_ref, sems)
        act = own_ref[...]
        for part in parts:
            act = act + part[...].astype(F32)
        g = act[:, :half]
        u = act[:, half:]
        s = jax.nn.sigmoid(g)
        hid_ref[...] = (g * s * u).astype(BF)
        for copy in copies:
            copy.wait()
        d_hidden = mm(s_ref[...], w_ref[...], NT)
        d_ref[:, :half] = (d_hidden * u * s * (1.0 + g * (1.0 - s))).astype(BF)
        d_ref[:, half:] = (d_hidden * g * s).astype(BF)
        for c in range(0, wide, step):
            out_ref[:, c : c + step] = mm(hid_ref[...], w_ref[:, c : c + step]).astype(BF)

    return pl.pallas_call(
        body,
        in_specs=[SMEM] + [INSIDE] * (2 + n) + [ANYWHERE] * m,
        out_specs=[INSIDE] * 3,
        out_shape=[struct(rows, wide), struct(rows, half), struct(rows, width)],
        scratch_shapes=down_scratch(blocks),
        compiler_params=params(),
        cost_estimate=LIGHT,
        name="middle",
    )(order, own, rows_s, *others, *blocks)


def row_grads(ds, w):
    n, rows, width, depth = len(ds), ds[0].shape[0], ds[0].shape[1], w.shape[0]
    step = 256 if depth % 256 == 0 else depth

    def body(*refs):
        ins, w_ref, outs, scratch = refs[:n], refs[n], refs[n + 1 : 2 * n + 1], refs[-1]

        @pl.when(pl.program_id(0) == 0)
        def _():
            stack_rows(ins, scratch)

        found = mm(scratch[...], w_ref[...], NT).astype(BF)
        for i in range(n):
            outs[i][...] = found[i * rows : (i + 1) * rows]

    shapes = [struct(rows, depth)] * n
    return pl.pallas_call(
        body,
        grid=(depth // step,),
        in_specs=[whole(d) for d in ds] + [pl.BlockSpec((step, width), lambda i: (i, 0))],
        out_specs=[pl.BlockSpec((rows, step), lambda i: (0, i))] * n,
        out_shape=shapes,
        scratch_shapes=[pltpu.VMEM((n * rows, width), BF)],
        compiler_params=params(),
        cost_estimate=LIGHT,
        name="row_grads",
    )(*ds, w)


def gate_up_grads(xs, ds, k, wide, scale, received):
    n, rows, width = len(xs), xs[0].shape[0], ds[0].shape[1]
    step = 512 if width % 512 == 0 else width
    extra = [] if received is None else [received]
    if wide % 128 != 0:
        xs, k = [x[:, k * wide : (k + 1) * wide] for x in xs], 0

    def body(*refs):
        x_refs, d_refs, rest = refs[:n], refs[n : 2 * n], refs[2 * n :]
        out_ref, x_scr, d_scr = rest[-3:]

        @pl.when(pl.program_id(0) == 0)
        def _():
            stack_rows(x_refs, x_scr)

        stack_rows(d_refs, d_scr)
        found = mm(x_scr[...], d_scr[...], TN) * scale
        if extra:
            found = found + rest[0][...].astype(F32)
        out_ref[...] = found.astype(BF)

    shape = struct(wide, width)
    column = lambda i: (0, i)
    return pl.pallas_call(
        body,
        grid=(width // step,),
        in_specs=[pl.BlockSpec((rows, wide), lambda i: (0, k))] * n
        + [pl.BlockSpec((rows, step), column)] * n
        + [pl.BlockSpec((wide, step), column)] * len(extra),
        out_specs=pl.BlockSpec((wide, step), column),
        out_shape=shape,
        scratch_shapes=[pltpu.VMEM((n * rows, wide), BF), pltpu.VMEM((n * rows, step), BF)],
        compiler_params=params(),
        cost_estimate=LIGHT,
        name="gate_up_grads",
    )(*xs, *ds, *extra)


def down_grads(order, hidden, rows_s, count, scale):
    rows, half = hidden.shape
    wide = rows_s.shape[1]
    deep = half // count
    step = 512 if wide % 512 == 0 else wide

    def body(order_ref, h_ref, s_ref, *refs):
        outs, scratch = refs[:count], refs[count]
        scratch[...] = mm(h_ref[...], s_ref[...], TN) * scale
        for j in range(count):
            place = pl.multiple_of(order_ref[j] * deep, deep)
            outs[j][...] = scratch[pl.ds(place, deep), :].astype(BF)

    shapes = [struct(deep, wide)] * count
    return pl.pallas_call(
        body,
        grid=(wide // step,),
        in_specs=[SMEM, whole(hidden), pl.BlockSpec((rows, step), lambda i: (0, i))],
        out_specs=[pl.BlockSpec((deep, step), lambda i: (0, i))] * count,
        out_shape=shapes,
        scratch_shapes=[pltpu.VMEM((half, step), F32)],
        compiler_params=params(),
        cost_estimate=LIGHT,
        name="down_grads",
    )(order, hidden, rows_s)


def popular_partials(select, packed, near, far, hid):
    count = select.shape[1]
    narrow = packed.shape[1] // 4
    blocks = (near.shape[0] + (0 if far is None else far.shape[0])) // (3 * hid)
    columns = blocks * 3 * hid
    weights = [near] if far is None else [near, far]

    def body(sel_ref, in_ref, *refs):
        w_refs, (x_ref, s_ref, p_ref) = refs[: len(weights)], refs[len(weights) :]
        t0 = mm(sel_ref[0], in_ref[...])
        t1 = mm(sel_ref[1], in_ref[...])
        x = (t0[:, :narrow] + t1[:, narrow : 2 * narrow]).astype(BF)
        s = (t0[:, 2 * narrow : 3 * narrow] + t1[:, 3 * narrow :]).astype(BF)
        x_ref[...] = x
        s_ref[...] = s
        at = 0
        for w_ref in w_refs:
            for top in range(0, w_ref.shape[0], 3 * hid):
                p_ref[:, at : at + 2 * hid] = mm(x, w_ref[top : top + 2 * hid, :], NT).astype(BF)
                p_ref[:, at + 2 * hid : at + 3 * hid] = mm(
                    s, w_ref[top + 2 * hid : top + 3 * hid, :], NT
                ).astype(BF)
                at += 3 * hid

    return pl.pallas_call(
        body,
        in_specs=[INSIDE] * (2 + len(weights)),
        out_specs=[INSIDE] * 3,
        out_shape=[struct(count, narrow), struct(count, narrow), struct(count, columns)],
        compiler_params=params(),
        cost_estimate=LIGHT,
        name="popular_partials",
    )(select, packed, *weights)


def popular_middle(own, others, hid):
    rows, columns = own.shape

    def body(own_ref, *refs):
        parts, out_ref = refs[:-1], refs[-1]
        act = own_ref[...].astype(F32)
        for part in parts:
            act = act + part[...].astype(F32)
        for at in range(0, columns, 3 * hid):
            g = act[:, at : at + hid]
            u = act[:, at + hid : at + 2 * hid]
            dh = act[:, at + 2 * hid : at + 3 * hid]
            s = jax.nn.sigmoid(g)
            out_ref[:, at : at + hid] = (dh * u * s * (1.0 + g * (1.0 - s))).astype(BF)
            out_ref[:, at + hid : at + 2 * hid] = (dh * g * s).astype(BF)
            out_ref[:, at + 2 * hid : at + 3 * hid] = (g * s * u).astype(BF)

    return pl.pallas_call(
        body,
        in_specs=[INSIDE] * (1 + len(others)),
        out_specs=INSIDE,
        out_shape=struct(rows, columns),
        compiler_params=params(),
        cost_estimate=LIGHT,
        name="popular_middle",
    )(own, *others)


def popular_back(select, pieces, x, s, near, far, hid, scale):
    count, narrow = x.shape
    columns = pieces[0].shape[1]
    blocks = columns // (3 * hid)
    spots = select.shape[2]
    weights = [near] if far is None else [near, far]
    n, m = len(pieces), len(weights)
    share = columns // m

    def body(sel_ref, x_ref, s_ref, *refs):
        ins, w_refs, back_ref = refs[:n], refs[n : n + m], refs[n + m]
        grads, scratch = refs[n + m + 1 : -1], refs[-1]
        stack_rows(ins, scratch)
        grad = None
        out = None
        at = 0
        for w_ref, g_ref in zip(w_refs, grads):
            for top in range(0, share, 3 * hid):
                d = scratch[:, at : at + 2 * hid]
                h = scratch[:, at + 2 * hid : at + 3 * hid]
                first = mm(d, w_ref[top : top + 2 * hid, :])
                second = mm(h, w_ref[top + 2 * hid : top + 3 * hid, :])
                grad = first if grad is None else grad + first
                out = second if out is None else out + second
                g_ref[top : top + 2 * hid, :] = (mm(d, x_ref[...], TN) * scale).astype(BF)
                g_ref[top + 2 * hid : top + 3 * hid, :] = (mm(h, s_ref[...], TN) * scale).astype(BF)
                at += 3 * hid
        grad = grad.astype(BF)
        out = out.astype(BF)
        for i in range(2):
            back_ref[:, i * narrow : (i + 1) * narrow] = mm(sel_ref[i], grad, TN).astype(BF)
            back_ref[:, (2 + i) * narrow : (3 + i) * narrow] = mm(sel_ref[i], out, TN).astype(BF)

    return pl.pallas_call(
        body,
        in_specs=[INSIDE] * (3 + n + m),
        out_specs=[INSIDE] * (1 + m),
        out_shape=[struct(spots, 4 * narrow)] + [struct(share, narrow)] * m,
        scratch_shapes=[pltpu.VMEM((count, columns), BF)],
        compiler_params=params(),
        cost_estimate=LIGHT,
        name="popular_back",
    )(select, x, s, *pieces, *weights)


def slot_positions(route_block, count):
    flat = route_block.reshape(-1)
    onehot = (flat[:, None] == jnp.arange(count, dtype=jnp.int32)[None, :]).astype(jnp.int32)
    before = jnp.cumsum(onehot, axis=0) - onehot
    return (flat, jnp.sum(before * onehot, axis=1))


def exchange(blocks):
    return lax.all_to_all(blocks, "expert", split_axis=0, concat_axis=0, tiled=True)


def local(
    tokens, cotangent, routes, gates, hot_index, hot_gate, w_gate_up, w_down, w_hot_gu, w_hot_dn
):
    owners = lax.axis_size("expert")
    groups = lax.axis_size("dp")
    cores = 2 if groups % 2 == 0 else 1
    chips = groups // cores
    tok_dev, width_d = tokens.shape
    topk = routes.shape[1]
    slots = max(2, 3 * tok_dev * topk // (2 * owners))
    entries = tok_dev * topk
    rows = owners * slots
    inverse = 1.0 / (4 * groups)
    me = lax.axis_index("dp")
    chip, core = me // cores, me % cores

    def shift(value, r):
        pairs = [
            (i, ((i // cores + r) % chips) * cores + i % cores) for i in range(groups)
        ]
        return lax.ppermute(value, "dp", pairs)

    def swap(value):
        pairs = [(i, (i // cores) * cores + (i + 1) % cores) for i in range(groups)]
        return lax.ppermute(value, "dp", pairs)

    order = jnp.stack(
        [
            ((chip - r) % chips) * cores + (core + k) % cores
            for k in range(cores)
            for r in range(chips)
        ]
    ).astype(jnp.int32)

    across = 1
    while 2 * (2 * across) ** 2 <= owners:
        across *= 2
    depths = owners // across
    spot = lax.axis_index("expert")

    def hop(value, j):
        return lax.ppermute(value, "expert", [(i, i ^ j) for i in range(owners)])

    wide = width_d // groups
    span = wide * cores

    def features_of(value, r):
        base = ((chip + r) % chips) * cores
        return jnp.concatenate(
            [
                lax.dynamic_slice_in_dim(value, (base + (core + k) % cores) * wide, wide, 1)
                for k in range(cores)
            ],
            axis=1,
        )

    sent = [features_of(tokens, r) for r in range(1, chips)]
    routes, sent = lax.optimization_barrier((routes, sent))
    halves = [features_of(tokens, 0)] + [shift(sent[r - 1], r) for r in range(1, chips)]
    flat, pos = slot_positions(routes, owners)
    dest = flat * slots + pos
    dests = [dest] + [shift(dest, r) for r in range(1, chips)]
    gu_chip = w_gate_up[0]
    if cores == 2:
        gu_chip = jnp.concatenate([gu_chip, swap(gu_chip)], axis=0)

    slot_ids = jnp.arange(rows, dtype=jnp.int32)[:, None]
    picks = [(slot_ids == one[None, :]).astype(BF) for one in dests]

    hot_dev = hot_index.shape[0]
    narrow = width_d // owners
    hot_pick = (
        hot_index[:, None] == jnp.arange(tok_dev, dtype=jnp.int32)[None, :]
    ).astype(BF)
    hot_x = mm(hot_pick, tokens).astype(BF)
    hot_s = (hot_gate[:, None] * mm(hot_pick, cotangent)).astype(BF)
    hot_half = hot_dev // 2
    hot_send = jnp.concatenate([hot_x, hot_s], axis=0).reshape(4, hot_half, owners, narrow)
    hot_send = hot_send.transpose(2, 1, 0, 3).reshape(owners * hot_half, 4 * narrow)
    packed_id = jnp.arange(owners * hot_half, dtype=jnp.int32)
    turn = packed_id ^ (spot * hot_half)
    turn = (turn[:, None] == packed_id[None, :]).astype(BF)
    row = jnp.arange(owners * hot_dev, dtype=jnp.int32)
    hit = (row // hot_dev * hot_half + row % hot_half)[:, None] == packed_id[None, :]
    low = (row % hot_dev < hot_half)[:, None]
    select = jnp.stack([hit & low, hit & ~low]).astype(BF)

    scaled = (gates[:, :, None] * cotangent[:, None, :].astype(F32)).astype(BF)
    send_s = mm(picks[0], scaled.reshape(entries, width_d)).astype(BF)
    rows_s = exchange(send_s.reshape(owners, slots, width_d)).reshape(rows, width_d)

    hot_send = mm(turn, hot_send).astype(BF).reshape(depths, across, hot_half, 4 * narrow)
    near = [hot_send[0]] + [hop(hot_send[j], j * across) for j in range(1, depths)]
    near = jnp.stack(near, axis=1)
    hot_recv = jnp.concatenate([near[0]] + [hop(near[j], j) for j in range(1, across)])
    hot_recv = hot_recv.reshape(owners * hot_half, 4 * narrow)

    hid = w_hot_dn.shape[0]
    hot_w = jnp.concatenate([w_hot_gu, w_hot_dn[None]], axis=0).reshape(3 * hid, narrow)
    hot_w, halves[-1] = lax.optimization_barrier((hot_w, halves[-1]))
    hot_near = [hot_w] + [shift(hot_w, r) for r in range(1, chips)]
    down, hot_near[-1] = lax.optimization_barrier((w_down[0], hot_near[-1]))
    down_near = [down] + [shift(down, r) for r in range(1, chips)]

    packed = [
        mm(one, jnp.repeat(part, topk, axis=0) if topk > 1 else part)
        .astype(BF)
        .reshape(owners, slots, span)
        for one, part in zip(picks, halves)
    ]
    first = exchange(jnp.concatenate(packed, axis=1))
    xs = [
        first[:, r * slots : (r + 1) * slots].reshape(rows, span) for r in range(chips)
    ]

    hot_near = jnp.concatenate(hot_near, axis=0)
    hot_far = swap(hot_near) if cores == 2 else None
    columns = groups * 3 * hid
    hot_x, hot_s, partial = popular_partials(select, hot_recv, hot_near, hot_far, hid)
    share = depths * hot_dev
    level_in = [hop(partial[j * share : (j + 1) * share], j) for j in range(1, across)]
    level_in = list(after(tuple(level_in), rows_s))
    level = partial[:share].astype(F32)
    for value in level_in:
        level = level + value.astype(F32)
    level = level.astype(BF)
    xs = list(after(tuple(xs), level))
    level = [level[j * hot_dev : (j + 1) * hot_dev] for j in range(depths)]
    depth_in = [hop(level[j], j * across) for j in range(1, depths)]

    parts = activations(xs, gu_chip)
    act_in = [shift(parts[r], -r) for r in range(1, chips)]

    down_near = list(after(tuple(down_near), rows_s))
    down_blocks = list(down_near)
    if cores == 2:
        down_blocks = down_blocks + [swap(block) for block in down_near]

    hot_own = popular_middle(level[0], depth_in, hid)
    act_in = list(after(tuple(act_in), hot_own))
    out, hidden, d_act = middle(order, parts[0], act_in, rows_s, down_blocks)
    back_out = exchange(out.reshape(owners, slots, width_d)).reshape(rows, width_d)
    ds = [d_act] + [shift(d_act, r) for r in range(1, chips)]
    backs = row_grads(ds, gu_chip)

    line = [hot_own] + [hop(hot_own, j * across) for j in range(1, depths)]
    line = after(jnp.concatenate(line), backs[0])

    hidden_dn = after(hidden, backs[0])
    dn_parts = down_grads(order, hidden_dn, rows_s, groups, inverse)
    if cores == 2:
        dn_in = [swap(part) for part in dn_parts[chips:]]
    lines = [line] + [hop(line, j) for j in range(1, across)]

    fourth_in = jnp.concatenate(
        [back.reshape(owners, slots, span) for back in backs], axis=1
    )
    fourth = exchange(fourth_in)
    lines = list(after(tuple(lines), fourth_in))
    hot_back, *hot_grads = popular_back(
        select, lines, hot_x, hot_s, hot_near, hot_far, hid, inverse
    )
    hot_back = hot_back.reshape(across, depths, hot_half, 4 * narrow)
    hot_back = [hot_back[0]] + [hop(hot_back[j], j) for j in range(1, across)]
    hot_back = jnp.stack(hot_back, axis=1)
    hot_back = [hot_back[0]] + [hop(hot_back[j], j * across) for j in range(1, depths)]
    hot_back = jnp.concatenate(hot_back).reshape(owners * hot_half, 4 * narrow)
    hot_back = mm(turn, hot_back).astype(BF)

    xs_late = list(after(tuple(xs), fourth_in))
    if cores == 2:
        gu_in = swap(gate_up_grads(xs_late, ds, 1, wide, inverse, None))
        dn_sum = [
            (part.astype(F32) + value.astype(F32)).astype(BF)
            for part, value in zip(dn_parts, dn_in)
        ]
    else:
        gu_in = None
        dn_sum = list(dn_parts)
    dn_total = dn_sum[0].astype(F32)
    for r in range(1, chips):
        dn_total = dn_total + shift(dn_sum[r], -r).astype(F32)
    grad_dn = dn_total.astype(BF)
    hot_sum = hot_grads[0]
    if cores == 2:
        hot_sum = (hot_sum.astype(F32) + swap(hot_grads[1]).astype(F32)).astype(BF)
    hot_sum = hot_sum.reshape(chips, 3 * hid, narrow)
    hot_total = hot_sum[0].astype(F32)
    for r in range(1, chips):
        hot_total = hot_total + shift(hot_sum[r], -r).astype(F32)
    grad_hot = hot_total.astype(BF).reshape(3, hid, narrow)
    grad_gu = gate_up_grads(xs_late, ds, 0, wide, inverse, gu_in)

    hot_back = hot_back.reshape(owners, hot_half, 4, narrow)
    hot_back = hot_back.transpose(2, 1, 0, 3).reshape(2, hot_dev, width_d)
    picked = mm(picks[0], back_out, TN)
    layer_out = (
        (gates.reshape(entries)[:, None] * picked).reshape(tok_dev, topk, width_d).sum(axis=1)
    )
    token_gate = jnp.sum(jnp.where(hot_pick > 0, hot_gate[:, None], 0.0), axis=0)
    layer_out = layer_out + token_gate[:, None] * mm(hot_pick, hot_back[1], TN)
    pieces = []
    for r in range(chips):
        back = fourth[:, r * slots : (r + 1) * slots].reshape(rows, span)
        piece = mm(picks[r], back, TN)
        piece = piece.reshape(tok_dev, topk, span).sum(axis=1).astype(BF)
        if r > 0:
            piece = shift(piece, -r)
        pieces += [piece[:, k * wide : (k + 1) * wide] for k in range(cores)]
    pieces = jnp.stack(pieces)
    input_grad = jnp.concatenate(
        [
            lax.dynamic_index_in_dim(
                pieces,
                ((p - chip) % chips) * cores + (q - core) % cores,
                0,
                keepdims=False,
            )
            for p in range(chips)
            for q in range(cores)
        ],
        axis=1,
    ).astype(F32)
    input_grad = input_grad + mm(hot_pick, hot_back[0], TN)
    return (
        layer_out.astype(BF),
        input_grad.astype(BF),
        grad_gu[None],
        grad_dn[None],
        grad_hot[:2],
        grad_hot[2],
    )


def solution(mesh):
    tok = P(("dp", "expert"), None)
    flat = P(("dp", "expert"))
    rows = P("expert", "dp", None)
    hot = (P(None, "dp", "expert"), P("dp", "expert"))
    return jax.shard_map(
        local,
        mesh=mesh,
        in_specs=(tok, tok, tok, tok, flat, flat, rows, rows) + hot,
        out_specs=(tok, tok, rows, rows) + hot,
        check_vma=False,
    )
```

```python
import jax
import jax.numpy as jnp
from jax import lax
from jax.experimental import pallas as pl
from jax.experimental.pallas import tpu as pltpu
from jax.sharding import PartitionSpec as P

BF = jnp.bfloat16
F32 = jnp.float32
NN = (((1,), (0,)), ((), ()))
NT = (((1,), (1,)), ((), ()))
TN = (((0,), (0,)), ((), ()))
ROOM = 56 * 1024 * 1024


def mm(a, b, dims=NN):
    return lax.dot_general(a, b, dims, preferred_element_type=F32)


def after(value, *earlier):
    return lax.optimization_barrier((value,) + earlier)[0]


def params():
    return pltpu.CompilerParams(vmem_limit_bytes=ROOM)


LIGHT = pl.CostEstimate(flops=1, bytes_accessed=1, transcendentals=0)


def struct(*shape, dtype=BF):
    return jax.ShapeDtypeStruct(shape, dtype)


def whole(array):
    return pl.BlockSpec(array.shape, lambda *_: (0,) * len(array.shape))


def stack_rows(refs, scratch):
    rows = refs[0].shape[0]
    for i, ref in enumerate(refs):
        scratch[i * rows : (i + 1) * rows, :] = ref[...]


def activations(xs, w):
    n, rows, depth, width = len(xs), xs[0].shape[0], w.shape[0], w.shape[1]
    step = 512 if width % 512 == 0 else width

    def body(*refs):
        ins, w_ref, outs, scratch = refs[:n], refs[n], refs[n + 1 : 2 * n + 1], refs[-1]

        @pl.when(pl.program_id(0) == 0)
        def _():
            stack_rows(ins, scratch)

        found = mm(scratch[...], w_ref[...])
        outs[0][...] = found[:rows]
        for i in range(1, n):
            outs[i][...] = found[i * rows : (i + 1) * rows].astype(BF)

    shapes = [struct(rows, width, dtype=F32)] + [struct(rows, width)] * (n - 1)
    return pl.pallas_call(
        body,
        grid=(width // step,),
        in_specs=[whole(x) for x in xs] + [pl.BlockSpec((depth, step), lambda i: (0, i))],
        out_specs=[pl.BlockSpec((rows, step), lambda i: (0, i))] * n,
        out_shape=shapes,
        scratch_shapes=[pltpu.VMEM((n * rows, depth), BF)],
        compiler_params=params(),
        cost_estimate=LIGHT,
        name="activations",
    )(*xs, w)


def fetch(order_ref, blocks, w_ref, sems):
    deep = blocks[0].shape[0]
    copies = []
    for j, block in enumerate(blocks):
        place = pl.multiple_of(order_ref[j] * deep, deep)
        copies.append(pltpu.make_async_copy(block, w_ref.at[pl.ds(place, deep)], sems.at[j]))
        copies[-1].start()
    return copies


def down_scratch(blocks):
    deep, width = blocks[0].shape
    return [pltpu.VMEM((len(blocks) * deep, width), BF), pltpu.SemaphoreType.DMA((len(blocks),))]


SMEM = pl.BlockSpec(memory_space=pltpu.SMEM)
ANYWHERE = pl.BlockSpec(memory_space=pl.ANY)
INSIDE = pl.BlockSpec(memory_space=pltpu.VMEM)


def middle(order, to_own, to_away, own, others, rows_s, blocks):
    rows, width = own.shape
    half = width // 2
    wide = blocks[0].shape[1]
    n, m = len(others), len(blocks)
    step = 512 if wide % 512 == 0 else wide

    def body(order_ref, in_ref, away_ref, own_ref, s_ref, *refs):
        parts, down = refs[:n], refs[n : n + m]
        out_ref, hid_ref, d_ref, turned_ref, w_ref, sems = refs[n + m :]
        copies = fetch(order_ref, down, w_ref, sems)
        act = own_ref[...]
        for part in parts:
            act = act + part[...].astype(F32)
        g = act[:, :half]
        u = act[:, half:]
        s = jax.nn.sigmoid(g)
        hid_ref[...] = (g * s * u).astype(BF)
        turned_ref[...] = mm(in_ref[...], s_ref[...]).astype(BF)
        sent = mm(away_ref[...], hid_ref[...]).astype(BF)
        for copy in copies:
            copy.wait()
        d_hidden = mm(turned_ref[...], w_ref[...], NT)
        d_ref[:, :half] = (d_hidden * u * s * (1.0 + g * (1.0 - s))).astype(BF)
        d_ref[:, half:] = (d_hidden * g * s).astype(BF)
        for c in range(0, wide, step):
            out_ref[:, c : c + step] = mm(sent, w_ref[:, c : c + step]).astype(BF)

    return pl.pallas_call(
        body,
        in_specs=[SMEM] + [INSIDE] * (4 + n) + [ANYWHERE] * m,
        out_specs=[INSIDE] * 4,
        out_shape=[struct(rows, wide), struct(rows, half), struct(rows, width), struct(rows, wide)],
        scratch_shapes=down_scratch(blocks),
        compiler_params=params(),
        cost_estimate=LIGHT,
        name="middle",
    )(order, to_own, to_away, own, rows_s, *others, *blocks)


def row_grads(ds, w):
    n, rows, width, depth = len(ds), ds[0].shape[0], ds[0].shape[1], w.shape[0]
    step = 256 if depth % 256 == 0 else depth

    def body(*refs):
        ins, w_ref, outs, scratch = refs[:n], refs[n], refs[n + 1 : 2 * n + 1], refs[-1]

        @pl.when(pl.program_id(0) == 0)
        def _():
            stack_rows(ins, scratch)

        found = mm(scratch[...], w_ref[...], NT).astype(BF)
        for i in range(n):
            outs[i][...] = found[i * rows : (i + 1) * rows]

    shapes = [struct(rows, depth)] * n
    return pl.pallas_call(
        body,
        grid=(depth // step,),
        in_specs=[whole(d) for d in ds] + [pl.BlockSpec((step, width), lambda i: (i, 0))],
        out_specs=[pl.BlockSpec((rows, step), lambda i: (0, i))] * n,
        out_shape=shapes,
        scratch_shapes=[pltpu.VMEM((n * rows, width), BF)],
        compiler_params=params(),
        cost_estimate=LIGHT,
        name="row_grads",
    )(*ds, w)


def gate_up_grads(xs, ds, k, wide, scale, received):
    n, rows, width = len(xs), xs[0].shape[0], ds[0].shape[1]
    step = 512 if width % 512 == 0 else width
    extra = [] if received is None else [received]
    if wide % 128 != 0:
        xs, k = [x[:, k * wide : (k + 1) * wide] for x in xs], 0

    def body(*refs):
        x_refs, d_refs, rest = refs[:n], refs[n : 2 * n], refs[2 * n :]
        out_ref, x_scr, d_scr = rest[-3:]

        @pl.when(pl.program_id(0) == 0)
        def _():
            stack_rows(x_refs, x_scr)

        stack_rows(d_refs, d_scr)
        found = mm(x_scr[...], d_scr[...], TN) * scale
        if extra:
            found = found + rest[0][...].astype(F32)
        out_ref[...] = found.astype(BF)

    shape = struct(wide, width)
    column = lambda i: (0, i)
    return pl.pallas_call(
        body,
        grid=(width // step,),
        in_specs=[pl.BlockSpec((rows, wide), lambda i: (0, k))] * n
        + [pl.BlockSpec((rows, step), column)] * n
        + [pl.BlockSpec((wide, step), column)] * len(extra),
        out_specs=pl.BlockSpec((wide, step), column),
        out_shape=shape,
        scratch_shapes=[pltpu.VMEM((n * rows, wide), BF), pltpu.VMEM((n * rows, step), BF)],
        compiler_params=params(),
        cost_estimate=LIGHT,
        name="gate_up_grads",
    )(*xs, *ds, *extra)


def down_grads(order, hidden, rows_s, count, scale):
    rows, half = hidden.shape
    wide = rows_s.shape[1]
    deep = half // count
    step = 512 if wide % 512 == 0 else wide

    def body(order_ref, h_ref, s_ref, *refs):
        outs, scratch = refs[:count], refs[count]
        scratch[...] = mm(h_ref[...], s_ref[...], TN) * scale
        for j in range(count):
            place = pl.multiple_of(order_ref[j] * deep, deep)
            outs[j][...] = scratch[pl.ds(place, deep), :].astype(BF)

    shapes = [struct(deep, wide)] * count
    return pl.pallas_call(
        body,
        grid=(wide // step,),
        in_specs=[SMEM, whole(hidden), pl.BlockSpec((rows, step), lambda i: (0, i))],
        out_specs=[pl.BlockSpec((deep, step), lambda i: (0, i))] * count,
        out_shape=shapes,
        scratch_shapes=[pltpu.VMEM((half, step), F32)],
        compiler_params=params(),
        cost_estimate=LIGHT,
        name="down_grads",
    )(order, hidden, rows_s)


def popular_partials(select, packed, near, far, hid):
    count = select.shape[1]
    narrow = packed.shape[1] // 4
    blocks = (near.shape[0] + (0 if far is None else far.shape[0])) // (3 * hid)
    columns = blocks * 3 * hid
    weights = [near] if far is None else [near, far]

    def body(sel_ref, in_ref, *refs):
        w_refs, (x_ref, s_ref, p_ref) = refs[: len(weights)], refs[len(weights) :]
        t0 = mm(sel_ref[0], in_ref[...])
        t1 = mm(sel_ref[1], in_ref[...])
        x = (t0[:, :narrow] + t1[:, narrow : 2 * narrow]).astype(BF)
        s = (t0[:, 2 * narrow : 3 * narrow] + t1[:, 3 * narrow :]).astype(BF)
        x_ref[...] = x
        s_ref[...] = s
        at = 0
        for w_ref in w_refs:
            for top in range(0, w_ref.shape[0], 3 * hid):
                p_ref[:, at : at + 2 * hid] = mm(x, w_ref[top : top + 2 * hid, :], NT).astype(BF)
                p_ref[:, at + 2 * hid : at + 3 * hid] = mm(
                    s, w_ref[top + 2 * hid : top + 3 * hid, :], NT
                ).astype(BF)
                at += 3 * hid

    return pl.pallas_call(
        body,
        in_specs=[INSIDE] * (2 + len(weights)),
        out_specs=[INSIDE] * 3,
        out_shape=[struct(count, narrow), struct(count, narrow), struct(count, columns)],
        compiler_params=params(),
        cost_estimate=LIGHT,
        name="popular_partials",
    )(select, packed, *weights)


def popular_middle(own, others, hid):
    rows, columns = own.shape

    def body(own_ref, *refs):
        parts, out_ref = refs[:-1], refs[-1]
        act = own_ref[...].astype(F32)
        for part in parts:
            act = act + part[...].astype(F32)
        for at in range(0, columns, 3 * hid):
            g = act[:, at : at + hid]
            u = act[:, at + hid : at + 2 * hid]
            dh = act[:, at + 2 * hid : at + 3 * hid]
            s = jax.nn.sigmoid(g)
            out_ref[:, at : at + hid] = (dh * u * s * (1.0 + g * (1.0 - s))).astype(BF)
            out_ref[:, at + hid : at + 2 * hid] = (dh * g * s).astype(BF)
            out_ref[:, at + 2 * hid : at + 3 * hid] = (g * s * u).astype(BF)

    return pl.pallas_call(
        body,
        in_specs=[INSIDE] * (1 + len(others)),
        out_specs=INSIDE,
        out_shape=struct(rows, columns),
        compiler_params=params(),
        cost_estimate=LIGHT,
        name="popular_middle",
    )(own, *others)


def popular_back(select, pieces, x, s, near, far, hid, scale):
    count, narrow = x.shape
    columns = pieces[0].shape[1]
    blocks = columns // (3 * hid)
    spots = select.shape[2]
    weights = [near] if far is None else [near, far]
    n, m = len(pieces), len(weights)
    share = columns // m

    def body(sel_ref, x_ref, s_ref, *refs):
        ins, w_refs, back_ref = refs[:n], refs[n : n + m], refs[n + m]
        grads, scratch = refs[n + m + 1 : -1], refs[-1]
        stack_rows(ins, scratch)
        grad = None
        out = None
        at = 0
        for w_ref, g_ref in zip(w_refs, grads):
            for top in range(0, share, 3 * hid):
                d = scratch[:, at : at + 2 * hid]
                h = scratch[:, at + 2 * hid : at + 3 * hid]
                first = mm(d, w_ref[top : top + 2 * hid, :])
                second = mm(h, w_ref[top + 2 * hid : top + 3 * hid, :])
                grad = first if grad is None else grad + first
                out = second if out is None else out + second
                g_ref[top : top + 2 * hid, :] = (mm(d, x_ref[...], TN) * scale).astype(BF)
                g_ref[top + 2 * hid : top + 3 * hid, :] = (mm(h, s_ref[...], TN) * scale).astype(BF)
                at += 3 * hid
        grad = grad.astype(BF)
        out = out.astype(BF)
        for i in range(2):
            back_ref[:, i * narrow : (i + 1) * narrow] = mm(sel_ref[i], grad, TN).astype(BF)
            back_ref[:, (2 + i) * narrow : (3 + i) * narrow] = mm(sel_ref[i], out, TN).astype(BF)

    return pl.pallas_call(
        body,
        in_specs=[INSIDE] * (3 + n + m),
        out_specs=[INSIDE] * (1 + m),
        out_shape=[struct(spots, 4 * narrow)] + [struct(share, narrow)] * m,
        scratch_shapes=[pltpu.VMEM((count, columns), BF)],
        compiler_params=params(),
        cost_estimate=LIGHT,
        name="popular_back",
    )(select, x, s, *pieces, *weights)


def slot_positions(route_block, count):
    flat = route_block.reshape(-1)
    onehot = (flat[:, None] == jnp.arange(count, dtype=jnp.int32)[None, :]).astype(jnp.int32)
    before = jnp.cumsum(onehot, axis=0) - onehot
    return (flat, jnp.sum(before * onehot, axis=1))


def exchange(blocks):
    return lax.all_to_all(blocks, "expert", split_axis=0, concat_axis=0, tiled=True)


def local(
    tokens, cotangent, routes, gates, hot_index, hot_gate, w_gate_up, w_down, w_hot_gu, w_hot_dn
):
    owners = lax.axis_size("expert")
    groups = lax.axis_size("dp")
    cores = 2 if groups % 2 == 0 else 1
    chips = groups // cores
    tok_dev, width_d = tokens.shape
    topk = routes.shape[1]
    slots = max(2, 3 * tok_dev * topk // (2 * owners))
    entries = tok_dev * topk
    rows = owners * slots
    inverse = 1.0 / (4 * groups)
    me = lax.axis_index("dp")
    chip, core = me // cores, me % cores

    def shift(value, r):
        pairs = [
            (i, ((i // cores + r) % chips) * cores + i % cores) for i in range(groups)
        ]
        return lax.ppermute(value, "dp", pairs)

    def swap(value):
        pairs = [(i, (i // cores) * cores + (i + 1) % cores) for i in range(groups)]
        return lax.ppermute(value, "dp", pairs)

    order = jnp.stack(
        [
            ((chip - r) % chips) * cores + (core + k) % cores
            for k in range(cores)
            for r in range(chips)
        ]
    ).astype(jnp.int32)

    across = 1
    while 2 * (2 * across) ** 2 <= owners:
        across *= 2
    depths = owners // across
    spot = lax.axis_index("expert")

    def hop(value, j):
        return lax.ppermute(value, "expert", [(i, i ^ j) for i in range(owners)])

    paths = [(d, j) for j in range(across) for d in range(depths)]
    rank = [paths.index((j // across, j % across)) for j in range(owners)]

    def ranked(index):
        return sum(jnp.where(index == j, rank[j], 0) for j in range(owners))

    def travel_depth(value):
        value = value.reshape(depths, across, -1, value.shape[1])
        return [value[0]] + [hop(value[d], d * across) for d in range(1, depths)]

    def travel_side(near):
        found = [
            jnp.concatenate([near[d][j] for d in range(depths)]) for j in range(across)
        ]
        return jnp.concatenate([found[0]] + [hop(found[j], j) for j in range(1, across)])

    wide = width_d // groups
    span = wide * cores

    def features_of(value, r):
        base = ((chip + r) % chips) * cores
        return jnp.concatenate(
            [
                lax.dynamic_slice_in_dim(value, (base + (core + k) % cores) * wide, wide, 1)
                for k in range(cores)
            ],
            axis=1,
        )

    sent = [features_of(tokens, r) for r in range(1, chips)]
    routes, sent = lax.optimization_barrier((routes, sent))
    halves = [features_of(tokens, 0)] + [shift(sent[r - 1], r) for r in range(1, chips)]
    flat, pos = slot_positions(routes, owners)
    dest = flat * slots + pos
    dests = [dest] + [shift(dest, r) for r in range(1, chips)]
    gu_chip = gu_far = w_gate_up[0]
    if cores == 2:
        gu_far = swap(gu_chip)
        gu_chip = jnp.concatenate([gu_chip, gu_far], axis=0)

    slot_ids = jnp.arange(rows, dtype=jnp.int32)[:, None]
    picks = [(slot_ids == one[None, :]).astype(BF) for one in dests]

    hot_dev = hot_index.shape[0]
    narrow = width_d // owners
    hot_pick = (
        hot_index[:, None] == jnp.arange(tok_dev, dtype=jnp.int32)[None, :]
    ).astype(BF)
    hot_x = mm(hot_pick, tokens).astype(BF)
    hot_s = (hot_gate[:, None] * mm(hot_pick, cotangent)).astype(BF)
    hot_half = hot_dev // 2
    hot_send = jnp.concatenate([hot_x, hot_s], axis=0).reshape(4, hot_half, owners, narrow)
    hot_send = hot_send.transpose(2, 1, 0, 3).reshape(owners * hot_half, 4 * narrow)
    packed_id = jnp.arange(owners * hot_half, dtype=jnp.int32)
    turn = packed_id ^ (spot * hot_half)
    turn = (turn[:, None] == packed_id[None, :]).astype(BF)
    row = jnp.arange(owners * hot_dev, dtype=jnp.int32)
    hit = (row // hot_dev * hot_half + row % hot_half)[:, None] == packed_id[None, :]
    low = (row % hot_dev < hot_half)[:, None]
    select = jnp.stack([hit & low, hit & ~low]).astype(BF)

    scaled = (gates[:, :, None] * cotangent[:, None, :].astype(F32)).astype(BF)
    away = flat ^ spot
    pick_away = (slot_ids == (away * slots + pos)[None, :]).astype(BF)
    pick_back = (slot_ids == (ranked(away) * slots + pos)[None, :]).astype(BF)
    send_s = mm(pick_away, scaled.reshape(entries, width_d)).astype(BF)
    row_id = jnp.arange(rows, dtype=jnp.int32)
    owner = (row_id // slots) ^ spot
    to_own = ranked(owner) * slots + row_id % slots
    to_own = (to_own[:, None] == row_id[None, :]).astype(BF)
    to_away = owner * slots + row_id % slots
    to_away = (to_away[:, None] == row_id[None, :]).astype(BF)

    hid = w_hot_dn.shape[0]
    hot_w = jnp.concatenate([w_hot_gu, w_hot_dn[None]], axis=0).reshape(3 * hid, narrow)
    hot_w, halves[-1] = lax.optimization_barrier((hot_w, halves[-1]))
    hot_near = [hot_w] + [shift(hot_w, r) for r in range(1, chips)]
    down, hot_near[-1] = lax.optimization_barrier((w_down[0], hot_near[-1]))
    down_near = [down] + [shift(down, r) for r in range(1, chips)]

    packed = [
        mm(one, jnp.repeat(part, topk, axis=0) if topk > 1 else part)
        .astype(BF)
        .reshape(owners, slots, span)
        for one, part in zip(picks, halves)
    ]
    first_in = jnp.concatenate(packed, axis=1)
    first = exchange(first_in)
    xs = [
        first[:, r * slots : (r + 1) * slots].reshape(rows, span) for r in range(chips)
    ]

    hot_send = after(hot_send, first_in, gu_far)
    hot_send = mm(turn, hot_send).astype(BF).reshape(depths, across, hot_half, 4 * narrow)
    near = [hot_send[0]] + [hop(hot_send[j], j * across) for j in range(1, depths)]
    send_s, near = lax.optimization_barrier((send_s, near))
    near_s = travel_depth(send_s)
    near = jnp.stack(near, axis=1)
    hot_recv = jnp.concatenate([near[0]] + [hop(near[j], j) for j in range(1, across)])
    hot_recv = hot_recv.reshape(owners * hot_half, 4 * narrow)

    hot_near = jnp.concatenate(hot_near, axis=0)
    hot_far = swap(hot_near) if cores == 2 else None
    columns = groups * 3 * hid
    hot_x, hot_s, partial = popular_partials(select, hot_recv, hot_near, hot_far, hid)
    share = depths * hot_dev
    level_in = [hop(partial[j * share : (j + 1) * share], j) for j in range(1, across)]
    level = partial[:share].astype(F32)
    for value in level_in:
        level = level + value.astype(F32)
    level = level.astype(BF)
    xs = list(after(tuple(xs), level))
    down_near = list(after(tuple(down_near), level))
    level = [level[j * hot_dev : (j + 1) * hot_dev] for j in range(depths)]
    depth_in = [hop(level[j], j * across) for j in range(1, depths)]

    parts = activations(xs, gu_chip)
    act_in = [shift(parts[r], -r) for r in range(1, chips)]
    rows_s = travel_side(list(after(tuple(near_s), parts[-1])))

    down_blocks = list(down_near)
    if cores == 2:
        down_blocks = down_blocks + [swap(block) for block in down_near]

    hot_own = popular_middle(level[0], depth_in, hid)
    act_in = list(after(tuple(act_in), hot_own))
    out, hidden, d_act, rows_s = middle(
        order, to_own, to_away, parts[0], act_in, rows_s, down_blocks
    )
    near_out = travel_depth(out)
    ds = [d_act] + [shift(d_act, r) for r in range(1, chips)]
    backs = row_grads(ds, gu_chip)
    fourth_in = jnp.concatenate(
        [back.reshape(owners, slots, span) for back in backs], axis=1
    )
    fourth = exchange(fourth_in)
    back_out = travel_side(list(after(tuple(near_out), fourth_in)))

    hot_own = after(hot_own, fourth_in)
    line = [hot_own] + [hop(hot_own, j * across) for j in range(1, depths)]
    line = jnp.concatenate(line)

    hidden_dn = after(hidden, fourth_in)
    dn_parts = down_grads(order, hidden_dn, rows_s, groups, inverse)
    if cores == 2:
        dn_in = [swap(part) for part in dn_parts[chips:]]
    lines = [line] + [hop(line, j) for j in range(1, across)]

    hot_back, *hot_grads = popular_back(
        select, lines, hot_x, hot_s, hot_near, hot_far, hid, inverse
    )
    hot_back = hot_back.reshape(across, depths, hot_half, 4 * narrow)
    hot_back = [hot_back[0]] + [hop(hot_back[j], j) for j in range(1, across)]
    hot_back = jnp.stack(hot_back, axis=1)
    hot_back = [hot_back[0]] + [hop(hot_back[j], j * across) for j in range(1, depths)]
    hot_back = jnp.concatenate(hot_back).reshape(owners * hot_half, 4 * narrow)
    hot_back = mm(turn, hot_back).astype(BF)

    xs_late = list(after(tuple(xs), dn_parts[0]))
    if cores == 2:
        gu_in = swap(gate_up_grads(xs_late, ds, 1, wide, inverse, None))
        dn_sum = [
            (part.astype(F32) + value.astype(F32)).astype(BF)
            for part, value in zip(dn_parts, dn_in)
        ]
    else:
        gu_in = None
        dn_sum = list(dn_parts)
    dn_total = dn_sum[0].astype(F32)
    for r in range(1, chips):
        dn_total = dn_total + shift(dn_sum[r], -r).astype(F32)
    grad_dn = dn_total.astype(BF)
    hot_sum = hot_grads[0]
    if cores == 2:
        hot_sum = (hot_sum.astype(F32) + swap(hot_grads[1]).astype(F32)).astype(BF)
    hot_sum = hot_sum.reshape(chips, 3 * hid, narrow)
    hot_total = hot_sum[0].astype(F32)
    for r in range(1, chips):
        hot_total = hot_total + shift(hot_sum[r], -r).astype(F32)
    grad_hot = hot_total.astype(BF).reshape(3, hid, narrow)
    grad_gu = gate_up_grads(xs_late, ds, 0, wide, inverse, gu_in)

    hot_back = hot_back.reshape(owners, hot_half, 4, narrow)
    hot_back = hot_back.transpose(2, 1, 0, 3).reshape(2, hot_dev, width_d)
    picked = mm(pick_back, back_out, TN)
    layer_out = (
        (gates.reshape(entries)[:, None] * picked).reshape(tok_dev, topk, width_d).sum(axis=1)
    )
    token_gate = jnp.sum(jnp.where(hot_pick > 0, hot_gate[:, None], 0.0), axis=0)
    layer_out = layer_out + token_gate[:, None] * mm(hot_pick, hot_back[1], TN)
    pieces = []
    for r in range(chips):
        back = fourth[:, r * slots : (r + 1) * slots].reshape(rows, span)
        piece = mm(picks[r], back, TN)
        piece = piece.reshape(tok_dev, topk, span).sum(axis=1).astype(BF)
        if r > 0:
            piece = shift(piece, -r)
        pieces += [piece[:, k * wide : (k + 1) * wide] for k in range(cores)]
    pieces = jnp.stack(pieces)
    input_grad = jnp.concatenate(
        [
            lax.dynamic_index_in_dim(
                pieces,
                ((p - chip) % chips) * cores + (q - core) % cores,
                0,
                keepdims=False,
            )
            for p in range(chips)
            for q in range(cores)
        ],
        axis=1,
    ).astype(F32)
    input_grad = input_grad + mm(hot_pick, hot_back[0], TN)
    return (
        layer_out.astype(BF),
        input_grad.astype(BF),
        grad_gu[None],
        grad_dn[None],
        grad_hot[:2],
        grad_hot[2],
    )


def solution(mesh):
    tok = P(("dp", "expert"), None)
    flat = P(("dp", "expert"))
    rows = P("expert", "dp", None)
    hot = (P(None, "dp", "expert"), P("dp", "expert"))
    return jax.shard_map(
        local,
        mesh=mesh,
        in_specs=(tok, tok, tok, tok, flat, flat, rows, rows) + hot,
        out_specs=(tok, tok, rows, rows) + hot,
        check_vma=False,
    )
```

```python
import jax
import jax.numpy as jnp
from jax import lax
from jax.experimental import pallas as pl
from jax.experimental.pallas import tpu as pltpu
from jax.sharding import PartitionSpec as P

BF = jnp.bfloat16
F32 = jnp.float32
NN = (((1,), (0,)), ((), ()))
NT = (((1,), (1,)), ((), ()))
TN = (((0,), (0,)), ((), ()))
ROOM = 56 * 1024 * 1024


def mm(a, b, dims=NN):
    return lax.dot_general(a, b, dims, preferred_element_type=F32)


def after(value, *earlier):
    return lax.optimization_barrier((value,) + earlier)[0]


def params():
    return pltpu.CompilerParams(vmem_limit_bytes=ROOM)


LIGHT = pl.CostEstimate(flops=1, bytes_accessed=1, transcendentals=0)


def struct(*shape, dtype=BF):
    return jax.ShapeDtypeStruct(shape, dtype)


def whole(array):
    return pl.BlockSpec(array.shape, lambda *_: (0,) * len(array.shape))


def stack_rows(refs, scratch):
    rows = refs[0].shape[0]
    for i, ref in enumerate(refs):
        scratch[i * rows : (i + 1) * rows, :] = ref[...]


def activations(xs, w):
    n, rows, depth, width = len(xs), xs[0].shape[0], w.shape[0], w.shape[1]
    step = 512 if width % 512 == 0 else width

    def body(*refs):
        ins, w_ref, outs, scratch = refs[:n], refs[n], refs[n + 1 : 2 * n + 1], refs[-1]

        @pl.when(pl.program_id(0) == 0)
        def _():
            stack_rows(ins, scratch)

        found = mm(scratch[...], w_ref[...])
        outs[0][...] = found[:rows]
        for i in range(1, n):
            outs[i][...] = found[i * rows : (i + 1) * rows].astype(BF)

    shapes = [struct(rows, width, dtype=F32)] + [struct(rows, width)] * (n - 1)
    return pl.pallas_call(
        body,
        grid=(width // step,),
        in_specs=[whole(x) for x in xs] + [pl.BlockSpec((depth, step), lambda i: (0, i))],
        out_specs=[pl.BlockSpec((rows, step), lambda i: (0, i))] * n,
        out_shape=shapes,
        scratch_shapes=[pltpu.VMEM((n * rows, depth), BF)],
        compiler_params=params(),
        cost_estimate=LIGHT,
        name="activations",
    )(*xs, w)


def fetch(order_ref, blocks, w_ref, sems):
    deep = blocks[0].shape[0]
    copies = []
    for j, block in enumerate(blocks):
        place = pl.multiple_of(order_ref[j] * deep, deep)
        copies.append(pltpu.make_async_copy(block, w_ref.at[pl.ds(place, deep)], sems.at[j]))
        copies[-1].start()
    return copies


def down_scratch(blocks):
    deep, width = blocks[0].shape
    return [pltpu.VMEM((len(blocks) * deep, width), BF), pltpu.SemaphoreType.DMA((len(blocks),))]


SMEM = pl.BlockSpec(memory_space=pltpu.SMEM)
ANYWHERE = pl.BlockSpec(memory_space=pl.ANY)
INSIDE = pl.BlockSpec(memory_space=pltpu.VMEM)


def middle(order, to_away, own, others, rows_s, blocks):
    rows, width = own.shape
    half = width // 2
    wide = blocks[0].shape[1]
    n, m = len(others), len(blocks)
    step = 512 if wide % 512 == 0 else wide

    def body(order_ref, away_ref, own_ref, s_ref, *refs):
        parts, down = refs[:n], refs[n : n + m]
        out_ref, hid_ref, d_ref, w_ref, sems = refs[n + m :]
        copies = fetch(order_ref, down, w_ref, sems)
        act = own_ref[...]
        for part in parts:
            act = act + part[...].astype(F32)
        g = act[:, :half]
        u = act[:, half:]
        s = jax.nn.sigmoid(g)
        hid_ref[...] = (g * s * u).astype(BF)
        sent = mm(away_ref[...], hid_ref[...]).astype(BF)
        for copy in copies:
            copy.wait()
        d_hidden = mm(s_ref[...], w_ref[...], NT)
        d_ref[:, :half] = (d_hidden * u * s * (1.0 + g * (1.0 - s))).astype(BF)
        d_ref[:, half:] = (d_hidden * g * s).astype(BF)
        for c in range(0, wide, step):
            out_ref[:, c : c + step] = mm(sent, w_ref[:, c : c + step]).astype(BF)

    return pl.pallas_call(
        body,
        in_specs=[SMEM] + [INSIDE] * (3 + n) + [ANYWHERE] * m,
        out_specs=[INSIDE] * 3,
        out_shape=[struct(rows, wide), struct(rows, half), struct(rows, width)],
        scratch_shapes=down_scratch(blocks),
        compiler_params=params(),
        cost_estimate=LIGHT,
        name="middle",
    )(order, to_away, own, rows_s, *others, *blocks)


def row_grads(ds, w):
    n, rows, width, depth = len(ds), ds[0].shape[0], ds[0].shape[1], w.shape[0]
    step = 256 if depth % 256 == 0 else depth

    def body(*refs):
        ins, w_ref, outs, scratch = refs[:n], refs[n], refs[n + 1 : 2 * n + 1], refs[-1]

        @pl.when(pl.program_id(0) == 0)
        def _():
            stack_rows(ins, scratch)

        found = mm(scratch[...], w_ref[...], NT).astype(BF)
        for i in range(n):
            outs[i][...] = found[i * rows : (i + 1) * rows]

    shapes = [struct(rows, depth)] * n
    return pl.pallas_call(
        body,
        grid=(depth // step,),
        in_specs=[whole(d) for d in ds] + [pl.BlockSpec((step, width), lambda i: (i, 0))],
        out_specs=[pl.BlockSpec((rows, step), lambda i: (0, i))] * n,
        out_shape=shapes,
        scratch_shapes=[pltpu.VMEM((n * rows, width), BF)],
        compiler_params=params(),
        cost_estimate=LIGHT,
        name="row_grads",
    )(*ds, w)


def gate_up_grads(xs, ds, k, wide, scale, received):
    n, rows, width = len(xs), xs[0].shape[0], ds[0].shape[1]
    step = 512 if width % 512 == 0 else width
    extra = [] if received is None else [received]
    if wide % 128 != 0:
        xs, k = [x[:, k * wide : (k + 1) * wide] for x in xs], 0

    def body(*refs):
        x_refs, d_refs, rest = refs[:n], refs[n : 2 * n], refs[2 * n :]
        out_ref, x_scr, d_scr = rest[-3:]

        @pl.when(pl.program_id(0) == 0)
        def _():
            stack_rows(x_refs, x_scr)

        stack_rows(d_refs, d_scr)
        found = mm(x_scr[...], d_scr[...], TN) * scale
        if extra:
            found = found + rest[0][...].astype(F32)
        out_ref[...] = found.astype(BF)

    shape = struct(wide, width)
    column = lambda i: (0, i)
    return pl.pallas_call(
        body,
        grid=(width // step,),
        in_specs=[pl.BlockSpec((rows, wide), lambda i: (0, k))] * n
        + [pl.BlockSpec((rows, step), column)] * n
        + [pl.BlockSpec((wide, step), column)] * len(extra),
        out_specs=pl.BlockSpec((wide, step), column),
        out_shape=shape,
        scratch_shapes=[pltpu.VMEM((n * rows, wide), BF), pltpu.VMEM((n * rows, step), BF)],
        compiler_params=params(),
        cost_estimate=LIGHT,
        name="gate_up_grads",
    )(*xs, *ds, *extra)


def down_grads(order, hidden, rows_s, count, scale):
    rows, half = hidden.shape
    wide = rows_s.shape[1]
    deep = half // count
    step = 512 if wide % 512 == 0 else wide

    def body(order_ref, h_ref, s_ref, *refs):
        outs, scratch = refs[:count], refs[count]
        scratch[...] = mm(h_ref[...], s_ref[...], TN) * scale
        for j in range(count):
            place = pl.multiple_of(order_ref[j] * deep, deep)
            outs[j][...] = scratch[pl.ds(place, deep), :].astype(BF)

    shapes = [struct(deep, wide)] * count
    return pl.pallas_call(
        body,
        grid=(wide // step,),
        in_specs=[SMEM, whole(hidden), pl.BlockSpec((rows, step), lambda i: (0, i))],
        out_specs=[pl.BlockSpec((deep, step), lambda i: (0, i))] * count,
        out_shape=shapes,
        scratch_shapes=[pltpu.VMEM((half, step), F32)],
        compiler_params=params(),
        cost_estimate=LIGHT,
        name="down_grads",
    )(order, hidden, rows_s)


def popular_partials(select, packed, near, far, hid):
    count = select.shape[1]
    narrow = packed.shape[1] // 4
    blocks = (near.shape[0] + (0 if far is None else far.shape[0])) // (3 * hid)
    columns = blocks * 3 * hid
    weights = [near] if far is None else [near, far]

    def body(sel_ref, in_ref, *refs):
        w_refs, (x_ref, s_ref, p_ref) = refs[: len(weights)], refs[len(weights) :]
        t0 = mm(sel_ref[0], in_ref[...])
        t1 = mm(sel_ref[1], in_ref[...])
        x = (t0[:, :narrow] + t1[:, narrow : 2 * narrow]).astype(BF)
        s = (t0[:, 2 * narrow : 3 * narrow] + t1[:, 3 * narrow :]).astype(BF)
        x_ref[...] = x
        s_ref[...] = s
        at = 0
        for w_ref in w_refs:
            for top in range(0, w_ref.shape[0], 3 * hid):
                p_ref[:, at : at + 2 * hid] = mm(x, w_ref[top : top + 2 * hid, :], NT).astype(BF)
                p_ref[:, at + 2 * hid : at + 3 * hid] = mm(
                    s, w_ref[top + 2 * hid : top + 3 * hid, :], NT
                ).astype(BF)
                at += 3 * hid

    return pl.pallas_call(
        body,
        in_specs=[INSIDE] * (2 + len(weights)),
        out_specs=[INSIDE] * 3,
        out_shape=[struct(count, narrow), struct(count, narrow), struct(count, columns)],
        compiler_params=params(),
        cost_estimate=LIGHT,
        name="popular_partials",
    )(select, packed, *weights)


def popular_middle(own, others, hid):
    rows, columns = own.shape

    def body(own_ref, *refs):
        parts, out_ref = refs[:-1], refs[-1]
        act = own_ref[...].astype(F32)
        for part in parts:
            act = act + part[...].astype(F32)
        for at in range(0, columns, 3 * hid):
            g = act[:, at : at + hid]
            u = act[:, at + hid : at + 2 * hid]
            dh = act[:, at + 2 * hid : at + 3 * hid]
            s = jax.nn.sigmoid(g)
            out_ref[:, at : at + hid] = (dh * u * s * (1.0 + g * (1.0 - s))).astype(BF)
            out_ref[:, at + hid : at + 2 * hid] = (dh * g * s).astype(BF)
            out_ref[:, at + 2 * hid : at + 3 * hid] = (g * s * u).astype(BF)

    return pl.pallas_call(
        body,
        in_specs=[INSIDE] * (1 + len(others)),
        out_specs=INSIDE,
        out_shape=struct(rows, columns),
        compiler_params=params(),
        cost_estimate=LIGHT,
        name="popular_middle",
    )(own, *others)


def popular_back(select, pieces, x, s, near, far, hid, scale):
    count, narrow = x.shape
    columns = pieces[0].shape[1]
    blocks = columns // (3 * hid)
    spots = select.shape[2]
    weights = [near] if far is None else [near, far]
    n, m = len(pieces), len(weights)
    share = columns // m

    def body(sel_ref, x_ref, s_ref, *refs):
        ins, w_refs, back_ref = refs[:n], refs[n : n + m], refs[n + m]
        grads, scratch = refs[n + m + 1 : -1], refs[-1]
        stack_rows(ins, scratch)
        grad = None
        out = None
        at = 0
        for w_ref, g_ref in zip(w_refs, grads):
            for top in range(0, share, 3 * hid):
                d = scratch[:, at : at + 2 * hid]
                h = scratch[:, at + 2 * hid : at + 3 * hid]
                first = mm(d, w_ref[top : top + 2 * hid, :])
                second = mm(h, w_ref[top + 2 * hid : top + 3 * hid, :])
                grad = first if grad is None else grad + first
                out = second if out is None else out + second
                g_ref[top : top + 2 * hid, :] = (mm(d, x_ref[...], TN) * scale).astype(BF)
                g_ref[top + 2 * hid : top + 3 * hid, :] = (mm(h, s_ref[...], TN) * scale).astype(BF)
                at += 3 * hid
        grad = grad.astype(BF)
        out = out.astype(BF)
        for i in range(2):
            back_ref[:, i * narrow : (i + 1) * narrow] = mm(sel_ref[i], grad, TN).astype(BF)
            back_ref[:, (2 + i) * narrow : (3 + i) * narrow] = mm(sel_ref[i], out, TN).astype(BF)

    return pl.pallas_call(
        body,
        in_specs=[INSIDE] * (3 + n + m),
        out_specs=[INSIDE] * (1 + m),
        out_shape=[struct(spots, 4 * narrow)] + [struct(share, narrow)] * m,
        scratch_shapes=[pltpu.VMEM((count, columns), BF)],
        compiler_params=params(),
        cost_estimate=LIGHT,
        name="popular_back",
    )(select, x, s, *pieces, *weights)


def slot_positions(route_block, count):
    flat = route_block.reshape(-1)
    onehot = (flat[:, None] == jnp.arange(count, dtype=jnp.int32)[None, :]).astype(jnp.int32)
    before = jnp.cumsum(onehot, axis=0) - onehot
    return (flat, jnp.sum(before * onehot, axis=1))


def exchange(blocks):
    return lax.all_to_all(blocks, "expert", split_axis=0, concat_axis=0, tiled=True)


def local(
    tokens, cotangent, routes, gates, hot_index, hot_gate, w_gate_up, w_down, w_hot_gu, w_hot_dn
):
    owners = lax.axis_size("expert")
    groups = lax.axis_size("dp")
    cores = 2 if groups % 2 == 0 else 1
    chips = groups // cores
    tok_dev, width_d = tokens.shape
    topk = routes.shape[1]
    slots = max(2, 3 * tok_dev * topk // (2 * owners))
    entries = tok_dev * topk
    rows = owners * slots
    inverse = 1.0 / (4 * groups)
    me = lax.axis_index("dp")
    chip, core = me // cores, me % cores

    def shift(value, r):
        pairs = [
            (i, ((i // cores + r) % chips) * cores + i % cores) for i in range(groups)
        ]
        return lax.ppermute(value, "dp", pairs)

    def swap(value):
        pairs = [(i, (i // cores) * cores + (i + 1) % cores) for i in range(groups)]
        return lax.ppermute(value, "dp", pairs)

    order = jnp.stack(
        [
            ((chip - r) % chips) * cores + (core + k) % cores
            for k in range(cores)
            for r in range(chips)
        ]
    ).astype(jnp.int32)

    across = 1
    while 2 * (2 * across) ** 2 <= owners:
        across *= 2
    depths = owners // across
    spot = lax.axis_index("expert")

    def hop(value, j):
        return lax.ppermute(value, "expert", [(i, i ^ j) for i in range(owners)])

    paths = [(d, j) for j in range(across) for d in range(depths)]
    rank = [paths.index((j // across, j % across)) for j in range(owners)]

    def ranked(index):
        return sum(jnp.where(index == j, rank[j], 0) for j in range(owners))

    def travel_depth(value):
        value = value.reshape(depths, across, -1, value.shape[1])
        return [value[0]] + [hop(value[d], d * across) for d in range(1, depths)]

    def travel_side(near):
        found = [
            jnp.concatenate([near[d][j] for d in range(depths)]) for j in range(across)
        ]
        return jnp.concatenate([found[0]] + [hop(found[j], j) for j in range(1, across)])

    wide = width_d // groups
    span = wide * cores

    def features_of(value, r):
        base = ((chip + r) % chips) * cores
        return jnp.concatenate(
            [
                lax.dynamic_slice_in_dim(value, (base + (core + k) % cores) * wide, wide, 1)
                for k in range(cores)
            ],
            axis=1,
        )

    sent = [features_of(tokens, r) for r in range(1, chips)]
    routes, sent = lax.optimization_barrier((routes, sent))
    halves = [features_of(tokens, 0)] + [shift(sent[r - 1], r) for r in range(1, chips)]
    flat, pos = slot_positions(routes, owners)
    dest = flat * slots + pos
    dests = [dest] + [shift(dest, r) for r in range(1, chips)]
    gu_chip = gu_far = w_gate_up[0]
    if cores == 2:
        gu_far = swap(gu_chip)
        gu_chip = jnp.concatenate([gu_chip, gu_far], axis=0)

    slot_ids = jnp.arange(rows, dtype=jnp.int32)[:, None]
    picks = [(slot_ids == one[None, :]).astype(BF) for one in dests]

    hot_dev = hot_index.shape[0]
    narrow = width_d // owners
    hot_pick = (
        hot_index[:, None] == jnp.arange(tok_dev, dtype=jnp.int32)[None, :]
    ).astype(BF)
    hot_x = mm(hot_pick, tokens).astype(BF)
    hot_s = (hot_gate[:, None] * mm(hot_pick, cotangent)).astype(BF)
    hot_half = hot_dev // 2
    hot_send = jnp.concatenate([hot_x, hot_s], axis=0).reshape(4, hot_half, owners, narrow)
    hot_send = hot_send.transpose(2, 1, 0, 3).reshape(owners * hot_half, 4 * narrow)
    packed_id = jnp.arange(owners * hot_half, dtype=jnp.int32)
    turn = packed_id ^ (spot * hot_half)
    turn = (turn[:, None] == packed_id[None, :]).astype(BF)
    row = jnp.arange(owners * hot_dev, dtype=jnp.int32)
    hit = (row // hot_dev * hot_half + row % hot_half)[:, None] == packed_id[None, :]
    low = (row % hot_dev < hot_half)[:, None]
    select = jnp.stack([hit & low, hit & ~low]).astype(BF)

    scaled = (gates[:, :, None] * cotangent[:, None, :].astype(F32)).astype(BF)
    away = flat ^ spot
    pick_back = (slot_ids == (ranked(away) * slots + pos)[None, :]).astype(BF)
    send_s = mm(picks[0], scaled.reshape(entries, width_d)).astype(BF)
    row_id = jnp.arange(rows, dtype=jnp.int32)
    owner = (row_id // slots) ^ spot
    rows_s = exchange(send_s.reshape(owners, slots, width_d)).reshape(rows, width_d)
    to_away = owner * slots + row_id % slots
    to_away = (to_away[:, None] == row_id[None, :]).astype(BF)

    hid = w_hot_dn.shape[0]
    hot_w = jnp.concatenate([w_hot_gu, w_hot_dn[None]], axis=0).reshape(3 * hid, narrow)
    hot_w, halves[-1] = lax.optimization_barrier((hot_w, halves[-1]))
    hot_near = [hot_w] + [shift(hot_w, r) for r in range(1, chips)]
    down, hot_near[-1] = lax.optimization_barrier((w_down[0], hot_near[-1]))
    down_near = [down] + [shift(down, r) for r in range(1, chips)]

    packed = [
        mm(one, jnp.repeat(part, topk, axis=0) if topk > 1 else part)
        .astype(BF)
        .reshape(owners, slots, span)
        for one, part in zip(picks, halves)
    ]
    first_in = jnp.concatenate(packed, axis=1)
    first = exchange(first_in)
    xs = [
        first[:, r * slots : (r + 1) * slots].reshape(rows, span) for r in range(chips)
    ]

    hot_send = after(hot_send, send_s, gu_far)
    hot_send = mm(turn, hot_send).astype(BF).reshape(depths, across, hot_half, 4 * narrow)
    near = [hot_send[0]] + [hop(hot_send[j], j * across) for j in range(1, depths)]
    near = jnp.stack(near, axis=1)
    hot_recv = jnp.concatenate([near[0]] + [hop(near[j], j) for j in range(1, across)])
    hot_recv = hot_recv.reshape(owners * hot_half, 4 * narrow)

    hot_near = jnp.concatenate(list(after(tuple(hot_near), first_in, gu_chip)), axis=0)
    hot_far = swap(hot_near) if cores == 2 else None
    columns = groups * 3 * hid
    hot_x, hot_s, partial = popular_partials(select, hot_recv, hot_near, hot_far, hid)
    share = depths * hot_dev
    level_in = [hop(partial[j * share : (j + 1) * share], j) for j in range(1, across)]
    level_in = list(after(tuple(level_in), rows_s))
    level = partial[:share].astype(F32)
    for value in level_in:
        level = level + value.astype(F32)
    level = level.astype(BF)
    xs = list(after(tuple(xs), level))
    down_near = list(after(tuple(down_near), rows_s))
    level = [level[j * hot_dev : (j + 1) * hot_dev] for j in range(depths)]
    depth_in = [hop(level[j], j * across) for j in range(1, depths)]

    parts = activations(xs, gu_chip)
    act_in = [shift(parts[r], -r) for r in range(1, chips)]

    down_blocks = list(down_near)
    if cores == 2:
        down_blocks = down_blocks + [swap(block) for block in down_near]

    hot_own = popular_middle(level[0], depth_in, hid)
    act_in = list(after(tuple(act_in), hot_own))
    out, hidden, d_act = middle(
        order, to_away, parts[0], act_in, rows_s, down_blocks
    )
    near_out = travel_depth(out)
    ds = [d_act] + [shift(d_act, r) for r in range(1, chips)]

    dn_parts = down_grads(order, hidden, rows_s, groups, inverse)
    dn_sum = list(dn_parts[:chips])
    if cores == 2:
        dn_in = [swap(part) for part in dn_parts[chips:]]
        for r in range(1, chips):
            dn_sum[r] = (dn_sum[r].astype(F32) + dn_in[r].astype(F32)).astype(BF)
    ds[-1] = after(ds[-1], dn_sum[-1])

    backs = row_grads(ds, gu_chip)
    fourth_in = jnp.concatenate(
        [back.reshape(owners, slots, span) for back in backs], axis=1
    )
    fourth = exchange(fourth_in)
    back_out = travel_side(list(after(tuple(near_out), fourth_in)))

    line = [hot_own] + [hop(hot_own, j * across) for j in range(1, depths)]
    line = jnp.concatenate(list(after(tuple(line), fourth_in)))

    lines = [line] + [hop(line, j) for j in range(1, across)]

    dn_recv = [shift(dn_sum[r], -r) for r in range(1, chips)]
    xs_late = list(after(tuple(xs), fourth_in))
    gu_sent = gate_up_grads(xs_late, ds, min(1, cores - 1), wide, inverse, None)
    lines = list(after(tuple(lines), gu_sent, *dn_recv))
    hot_back, *hot_grads = popular_back(
        select, lines, hot_x, hot_s, hot_near, hot_far, hid, inverse
    )
    hot_back = hot_back.reshape(across, depths, hot_half, 4 * narrow)
    hot_back = [hot_back[0]] + [hop(hot_back[j], j) for j in range(1, across)]
    hot_back = jnp.stack(hot_back, axis=1)
    hot_back = [hot_back[0]] + [hop(hot_back[j], j * across) for j in range(1, depths)]
    hot_back = jnp.concatenate(hot_back).reshape(owners * hot_half, 4 * narrow)
    hot_back = mm(turn, hot_back).astype(BF)

    if cores == 2:
        gu_in = swap(gu_sent)
    else:
        gu_in = None
    dn_total = dn_sum[0].astype(F32)
    if cores == 2:
        dn_total = dn_total + dn_in[0].astype(F32)
    for value in dn_recv:
        dn_total = dn_total + value.astype(F32)
    grad_dn = dn_total.astype(BF)
    hot_sum = hot_grads[0]
    if cores == 2:
        hot_sum = (hot_sum.astype(F32) + swap(hot_grads[1]).astype(F32)).astype(BF)
    hot_sum = hot_sum.reshape(chips, 3 * hid, narrow)
    hot_total = hot_sum[0].astype(F32)
    for r in range(1, chips):
        hot_total = hot_total + shift(hot_sum[r], -r).astype(F32)
    grad_hot = hot_total.astype(BF).reshape(3, hid, narrow)
    grad_gu = gate_up_grads(xs_late, ds, 0, wide, inverse, gu_in)

    hot_back = hot_back.reshape(owners, hot_half, 4, narrow)
    hot_back = hot_back.transpose(2, 1, 0, 3).reshape(2, hot_dev, width_d)
    picked = mm(pick_back, back_out, TN)
    layer_out = (
        (gates.reshape(entries)[:, None] * picked).reshape(tok_dev, topk, width_d).sum(axis=1)
    )
    token_gate = jnp.sum(jnp.where(hot_pick > 0, hot_gate[:, None], 0.0), axis=0)
    layer_out = layer_out + token_gate[:, None] * mm(hot_pick, hot_back[1], TN)
    pieces = []
    for r in range(chips):
        back = fourth[:, r * slots : (r + 1) * slots].reshape(rows, span)
        piece = mm(picks[r], back, TN)
        piece = piece.reshape(tok_dev, topk, span).sum(axis=1).astype(BF)
        if r > 0:
            piece = shift(piece, -r)
        pieces += [piece[:, k * wide : (k + 1) * wide] for k in range(cores)]
    pieces = jnp.stack(pieces)
    input_grad = jnp.concatenate(
        [
            lax.dynamic_index_in_dim(
                pieces,
                ((p - chip) % chips) * cores + (q - core) % cores,
                0,
                keepdims=False,
            )
            for p in range(chips)
            for q in range(cores)
        ],
        axis=1,
    ).astype(F32)
    input_grad = input_grad + mm(hot_pick, hot_back[0], TN)
    return (
        layer_out.astype(BF),
        input_grad.astype(BF),
        grad_gu[None],
        grad_dn[None],
        grad_hot[:2],
        grad_hot[2],
    )


def solution(mesh):
    tok = P(("dp", "expert"), None)
    flat = P(("dp", "expert"))
    rows = P("expert", "dp", None)
    hot = (P(None, "dp", "expert"), P("dp", "expert"))
    return jax.shard_map(
        local,
        mesh=mesh,
        in_specs=(tok, tok, tok, tok, flat, flat, rows, rows) + hot,
        out_specs=(tok, tok, rows, rows) + hot,
        check_vma=False,
    )
```

```python
import jax
import jax.numpy as jnp
from jax import lax
from jax.experimental import pallas as pl
from jax.experimental.pallas import tpu as pltpu
from jax.sharding import PartitionSpec as P

BF = jnp.bfloat16
F32 = jnp.float32
NN = (((1,), (0,)), ((), ()))
NT = (((1,), (1,)), ((), ()))
TN = (((0,), (0,)), ((), ()))
ROOM = 56 * 1024 * 1024
LIGHT = pl.CostEstimate(flops=1, bytes_accessed=1, transcendentals=0)
INSIDE = pl.BlockSpec(memory_space=pltpu.VMEM)
PIECES = 8


def mm(a, b, dims=NN):
    return lax.dot_general(a, b, dims, preferred_element_type=F32)


def after(value, *earlier):
    return lax.optimization_barrier((value,) + earlier)[0]


def params():
    return pltpu.CompilerParams(vmem_limit_bytes=ROOM)


LIGHT = pl.CostEstimate(flops=1, bytes_accessed=1, transcendentals=0)


def struct(*shape, dtype=BF):
    return jax.ShapeDtypeStruct(shape, dtype)


def whole(array):
    return pl.BlockSpec(array.shape, lambda *_: (0,) * len(array.shape))


def stack_rows(refs, scratch):
    rows = refs[0].shape[0]
    for i, ref in enumerate(refs):
        scratch[i * rows : (i + 1) * rows, :] = ref[...]


def activations(xs, w):
    n, rows, depth, width = len(xs), xs[0].shape[0], w.shape[0], w.shape[1]
    step = 512 if width % 512 == 0 else width

    def body(*refs):
        ins, w_ref, outs, scratch = refs[:n], refs[n], refs[n + 1 : 2 * n + 1], refs[-1]

        @pl.when(pl.program_id(0) == 0)
        def _():
            stack_rows(ins, scratch)

        found = mm(scratch[...], w_ref[...])
        outs[0][...] = found[:rows]
        for i in range(1, n):
            outs[i][...] = found[i * rows : (i + 1) * rows].astype(BF)

    shapes = [struct(rows, width, dtype=F32)] + [struct(rows, width)] * (n - 1)
    return pl.pallas_call(
        body,
        grid=(width // step,),
        in_specs=[whole(x) for x in xs] + [pl.BlockSpec((depth, step), lambda i: (0, i))],
        out_specs=[pl.BlockSpec((rows, step), lambda i: (0, i))] * n,
        out_shape=shapes,
        scratch_shapes=[pltpu.VMEM((n * rows, depth), BF)],
        compiler_params=params(),
        cost_estimate=LIGHT,
        name="activations",
    )(*xs, w)


def middle(own, others, rows_s, w):
    rows, width = own.shape
    half = width // 2
    wide = w.shape[1]
    n = len(others)
    step = 512 if wide % 512 == 0 else wide

    def body(own_ref, s_ref, w_ref, *refs):
        parts, (out_ref, hid_ref, d_ref) = refs[:n], refs[n:]
        act = own_ref[...]
        for part in parts:
            act = act + part[...].astype(F32)
        g = act[:, :half]
        u = act[:, half:]
        s = jax.nn.sigmoid(g)
        hid_ref[...] = (g * s * u).astype(BF)
        d_hidden = mm(s_ref[...], w_ref[...], NT)
        d_ref[:, :half] = (d_hidden * u * s * (1.0 + g * (1.0 - s))).astype(BF)
        d_ref[:, half:] = (d_hidden * g * s).astype(BF)
        for c in range(0, wide, step):
            out_ref[:, c : c + step] = mm(hid_ref[...], w_ref[:, c : c + step]).astype(BF)

    return pl.pallas_call(
        body,
        in_specs=[INSIDE] * (3 + n),
        out_specs=[INSIDE] * 3,
        out_shape=[struct(rows, wide), struct(rows, half), struct(rows, width)],
        compiler_params=params(),
        cost_estimate=LIGHT,
        name="middle",
    )(own, rows_s, w, *others)


def row_grads(ds, w):
    n, rows, width, depth = len(ds), ds[0].shape[0], ds[0].shape[1], w.shape[0]
    step = 256 if depth % 256 == 0 else depth

    def body(*refs):
        ins, w_ref, outs, scratch = refs[:n], refs[n], refs[n + 1 : 2 * n + 1], refs[-1]

        @pl.when(pl.program_id(0) == 0)
        def _():
            stack_rows(ins, scratch)

        found = mm(scratch[...], w_ref[...], NT).astype(BF)
        for i in range(n):
            outs[i][...] = found[i * rows : (i + 1) * rows]

    shapes = [struct(rows, depth)] * n
    return pl.pallas_call(
        body,
        grid=(depth // step,),
        in_specs=[whole(d) for d in ds] + [pl.BlockSpec((step, width), lambda i: (i, 0))],
        out_specs=[pl.BlockSpec((rows, step), lambda i: (0, i))] * n,
        out_shape=shapes,
        scratch_shapes=[pltpu.VMEM((n * rows, width), BF)],
        compiler_params=params(),
        cost_estimate=LIGHT,
        name="row_grads",
    )(*ds, w)


def gate_up_grads(xs, ds, k, wide, scale, received):
    n, rows, width = len(xs), xs[0].shape[0], ds[0].shape[1]
    step = 512 if width % 512 == 0 else width
    extra = [] if received is None else [received]
    if wide % 128 != 0:
        xs, k = [x[:, k * wide : (k + 1) * wide] for x in xs], 0

    def body(*refs):
        x_refs, d_refs, rest = refs[:n], refs[n : 2 * n], refs[2 * n :]
        out_ref, x_scr, d_scr = rest[-3:]

        @pl.when(pl.program_id(0) == 0)
        def _():
            stack_rows(x_refs, x_scr)

        stack_rows(d_refs, d_scr)
        found = mm(x_scr[...], d_scr[...], TN) * scale
        if extra:
            found = found + rest[0][...].astype(F32)
        out_ref[...] = found.astype(BF)

    shape = struct(wide, width)
    column = lambda i: (0, i)
    return pl.pallas_call(
        body,
        grid=(width // step,),
        in_specs=[pl.BlockSpec((rows, wide), lambda i: (0, k))] * n
        + [pl.BlockSpec((rows, step), column)] * n
        + [pl.BlockSpec((wide, step), column)] * len(extra),
        out_specs=pl.BlockSpec((wide, step), column),
        out_shape=shape,
        scratch_shapes=[pltpu.VMEM((n * rows, wide), BF), pltpu.VMEM((n * rows, step), BF)],
        compiler_params=params(),
        cost_estimate=LIGHT,
        name="gate_up_grads",
    )(*xs, *ds, *extra)


def down_grads(hidden, rows_s, scale):
    rows, half = hidden.shape
    wide = rows_s.shape[1]
    step = 512 if wide % 512 == 0 else wide

    def body(h_ref, s_ref, out_ref):
        out_ref[...] = (mm(h_ref[...], s_ref[...], TN) * scale).astype(BF)

    return pl.pallas_call(
        body,
        grid=(wide // step,),
        in_specs=[whole(hidden), pl.BlockSpec((rows, step), lambda i: (0, i))],
        out_specs=pl.BlockSpec((half, step), lambda i: (0, i)),
        out_shape=struct(half, wide),
        compiler_params=params(),
        cost_estimate=LIGHT,
        name="down_grads",
    )(hidden, rows_s)


def popular_partials(select, packed, weights, hid):
    parts, count = select.shape[:2]
    narrow = packed.shape[1] // (2 * parts)
    columns = sum(w.shape[0] for w in weights)

    def body(sel_ref, in_ref, *refs):
        w_refs, (x_ref, s_ref, p_ref) = refs[: len(weights)], refs[len(weights) :]
        x = None
        s = None
        for q in range(parts):
            rows = mm(sel_ref[q], in_ref[...])
            one = rows[:, q * narrow : (q + 1) * narrow]
            two = rows[:, (parts + q) * narrow : (parts + q + 1) * narrow]
            x = one if x is None else x + one
            s = two if s is None else s + two
        x = x.astype(BF)
        s = s.astype(BF)
        x_ref[...] = x
        s_ref[...] = s
        at = 0
        for w_ref in w_refs:
            for top in range(0, w_ref.shape[0], 3 * hid):
                p_ref[:, at : at + 2 * hid] = mm(x, w_ref[top : top + 2 * hid, :], NT)
                p_ref[:, at + 2 * hid : at + 3 * hid] = mm(
                    s, w_ref[top + 2 * hid : top + 3 * hid, :], NT
                )
                at += 3 * hid

    return pl.pallas_call(
        body,
        in_specs=[INSIDE] * (2 + len(weights)),
        out_specs=[INSIDE] * 3,
        out_shape=[
            struct(count, narrow),
            struct(count, narrow),
            struct(count, columns, dtype=F32),
        ],
        compiler_params=params(),
        cost_estimate=LIGHT,
        name="popular_partials",
    )(select, packed, *weights)


def popular_back(select, act, x, s, weights, hid, scale):
    parts, count, spots = select.shape
    narrow = x.shape[1]
    m = len(weights)

    def body(sel_ref, act_ref, x_ref, s_ref, *refs):
        w_refs, back_ref, grads = refs[:m], refs[m], refs[m + 1 :]
        grad = None
        out = None
        at = 0
        for w_ref, g_ref in zip(w_refs, grads):
            for top in range(0, w_ref.shape[0], 3 * hid):
                g = act_ref[:, at : at + hid]
                u = act_ref[:, at + hid : at + 2 * hid]
                dh = act_ref[:, at + 2 * hid : at + 3 * hid]
                sigma = jax.nn.sigmoid(g)
                dg = (dh * u * sigma * (1.0 + g * (1.0 - sigma))).astype(BF)
                du = (dh * g * sigma).astype(BF)
                h = (g * sigma * u).astype(BF)
                for i, (left, right) in enumerate(((dg, x_ref), (du, x_ref), (h, s_ref))):
                    here = slice(top + i * hid, top + (i + 1) * hid)
                    product = mm(left, w_ref[here, :])
                    if i == 2:
                        out = product if out is None else out + product
                    else:
                        grad = product if grad is None else grad + product
                    g_ref[here, :] = (mm(left, right[...], TN) * scale).astype(BF)
                at += 3 * hid
        grad = grad.astype(BF)
        out = out.astype(BF)
        for q in range(parts):
            back_ref[:, q * narrow : (q + 1) * narrow] = mm(sel_ref[q], grad, TN).astype(BF)
            back_ref[:, (parts + q) * narrow : (parts + q + 1) * narrow] = mm(
                sel_ref[q], out, TN
            ).astype(BF)

    return pl.pallas_call(
        body,
        in_specs=[INSIDE] * (4 + m),
        out_specs=[INSIDE] * (1 + m),
        out_shape=[struct(spots, 2 * parts * narrow)]
        + [struct(w.shape[0], narrow) for w in weights],
        compiler_params=params(),
        cost_estimate=LIGHT,
        name="popular_back",
    )(select, act, x, s, *weights)


def slot_positions(route_block, count):
    flat = route_block.reshape(-1)
    onehot = (flat[:, None] == jnp.arange(count, dtype=jnp.int32)[None, :]).astype(jnp.int32)
    before = jnp.cumsum(onehot, axis=0) - onehot
    return (flat, jnp.sum(before * onehot, axis=1))


def exchange(blocks):
    return lax.all_to_all(blocks, "expert", split_axis=0, concat_axis=0, tiled=True)


def local(
    tokens, cotangent, routes, gates, hot_index, hot_gate, w_gate_up, w_down, w_hot_gu, w_hot_dn
):
    owners = lax.axis_size("expert")
    groups = lax.axis_size("dp")
    cores = 2 if groups % 2 == 0 else 1
    chips = groups // cores
    tok_dev, width_d = tokens.shape
    topk = routes.shape[1]
    slots = max(2, 3 * tok_dev * topk // (2 * owners))
    entries = tok_dev * topk
    rows = owners * slots
    inverse = 1.0 / (4 * groups)
    me = lax.axis_index("dp")
    chip, core = me // cores, me % cores

    def shift(value, r):
        pairs = [
            (i, ((i // cores + r) % chips) * cores + i % cores) for i in range(groups)
        ]
        return lax.ppermute(value, "dp", pairs)

    def swap(value):
        pairs = [(i, (i // cores) * cores + (i + 1) % cores) for i in range(groups)]
        return lax.ppermute(value, "dp", pairs)

    wide = width_d // groups
    span = wide * cores

    def features_of(value, r):
        base = ((chip + r) % chips) * cores
        return jnp.concatenate(
            [
                lax.dynamic_slice_in_dim(value, (base + (core + k) % cores) * wide, wide, 1)
                for k in range(cores)
            ],
            axis=1,
        )

    sent = [features_of(tokens, r) for r in range(1, chips)]
    routes, sent = lax.optimization_barrier((routes, sent))
    halves = [features_of(tokens, 0)] + [shift(sent[r - 1], r) for r in range(1, chips)]
    flat, pos = slot_positions(routes, owners)
    dest = flat * slots + pos
    dests = [dest] + [shift(dest, r) for r in range(1, chips)]
    gu_chip = gu_far = w_gate_up[0]
    if cores == 2:
        gu_far = swap(gu_chip)
        gu_chip = jnp.concatenate([gu_chip, gu_far], axis=0)

    slot_ids = jnp.arange(rows, dtype=jnp.int32)[:, None]
    picks = [(slot_ids == one[None, :]).astype(BF) for one in dests]

    def as_rows(value, width):
        value = value.reshape(owners, -1)
        spare = -value.shape[1] % width
        return jnp.pad(value, ((0, 0), (0, spare))).reshape(owners, -1, width)

    hot_dev = hot_index.shape[0]
    narrow = width_d // owners
    few = 2 * hot_dev // PIECES
    hot_pick = (
        hot_index[:, None] == jnp.arange(tok_dev, dtype=jnp.int32)[None, :]
    ).astype(BF)
    hot_x = mm(hot_pick, tokens).astype(BF)
    hot_s = (hot_gate[:, None] * mm(hot_pick, cotangent)).astype(BF)
    hot_send = jnp.concatenate([hot_x, hot_s], axis=0).reshape(PIECES, few, owners, narrow)
    hot_send = hot_send.transpose(2, 1, 0, 3)
    row = jnp.arange(owners * hot_dev, dtype=jnp.int32)
    packed_id = jnp.arange(owners * few, dtype=jnp.int32)
    hit = (row // hot_dev * few + row % few)[:, None] == packed_id[None, :]
    piece = (row % hot_dev) // few
    select = jnp.stack([hit & (piece == q)[:, None] for q in range(PIECES // 2)]).astype(BF)

    scaled = (gates[:, :, None] * cotangent[:, None, :].astype(F32)).astype(BF)
    send_s = mm(picks[0], scaled.reshape(entries, width_d)).astype(BF)
    early = exchange(
        jnp.concatenate([send_s.reshape(owners, slots, width_d), as_rows(hot_send, width_d)], axis=1)
    )
    rows_s = early[:, :slots].reshape(rows, width_d)
    hot_recv = early[:, slots:].reshape(owners, -1)[:, : 2 * hot_dev * narrow]
    hot_recv = hot_recv.reshape(owners * few, PIECES * narrow)

    packed = [
        mm(one, jnp.repeat(part, topk, axis=0) if topk > 1 else part)
        .astype(BF)
        .reshape(owners, slots, span)
        for one, part in zip(picks, halves)
    ]
    first_in = jnp.concatenate(packed, axis=1)
    first = exchange(first_in)
    xs = [
        first[:, r * slots : (r + 1) * slots].reshape(rows, span) for r in range(chips)
    ]

    hid = w_hot_dn.shape[0]
    hot_w = jnp.concatenate([w_hot_gu, w_hot_dn[None]], axis=0).reshape(3 * hid, narrow)
    hot_w, halves[-1] = lax.optimization_barrier((hot_w, halves[-1]))
    hot_near = [hot_w] + [shift(hot_w, r) for r in range(1, chips)]
    hot_near = jnp.concatenate(list(after(tuple(hot_near), first_in, gu_chip)), axis=0)
    hot_ws = [hot_near] + ([swap(hot_near)] if cores == 2 else [])
    w_dn = lax.all_gather(w_down[0], "dp", axis=0, tiled=True)

    hot_x, hot_s, partial = popular_partials(select, hot_recv, hot_ws, hid)
    xs = list(after(tuple(xs), partial))
    hot_act = lax.psum(partial, "expert")

    parts = activations(xs, gu_chip)
    act_in = [shift(parts[r], -r) for r in range(1, chips)]

    out, hidden, d_act = middle(parts[0], act_in, rows_s, w_dn)
    back_out = exchange(out.reshape(owners, slots, width_d)).reshape(rows, width_d)
    ds = [d_act] + [shift(d_act, r) for r in range(1, chips)]
    backs = row_grads(ds, gu_chip)

    hidden_dn = after(hidden, backs[0])
    part_dn = down_grads(hidden_dn, rows_s, inverse)
    grad_dn = lax.psum_scatter(part_dn, "dp", scatter_dimension=0, tiled=True)

    hot_act = after(hot_act, backs[0])
    hot_back, *hot_grads = popular_back(select, hot_act, hot_x, hot_s, hot_ws, hid, inverse)
    fourth_in = jnp.concatenate(
        [back.reshape(owners, slots, span) for back in backs] + [as_rows(hot_back, span)], axis=1
    )
    fourth = exchange(fourth_in)

    xs_late = list(after(tuple(xs), back_out))
    if cores == 2:
        gu_in = swap(gate_up_grads(xs_late, ds, 1, wide, inverse, None))
    else:
        gu_in = None
    hot_sum = hot_grads[0]
    if cores == 2:
        hot_sum = (hot_sum.astype(F32) + swap(hot_grads[1]).astype(F32)).astype(BF)
    hot_sum = hot_sum.reshape(chips, 3 * hid, narrow)
    hot_total = hot_sum[0].astype(F32)
    for r in range(1, chips):
        hot_total = hot_total + shift(hot_sum[r], -r).astype(F32)
    grad_hot = hot_total.astype(BF).reshape(3, hid, narrow)
    grad_gu = gate_up_grads(xs_late, ds, 0, wide, inverse, gu_in)

    hot_back = fourth[:, chips * slots :].reshape(owners, -1)[:, : 2 * hot_dev * narrow]
    hot_back = hot_back.reshape(owners, few, PIECES, narrow)
    hot_back = hot_back.transpose(2, 1, 0, 3).reshape(2, hot_dev, width_d)
    picked = mm(picks[0], back_out, TN)
    layer_out = (
        (gates.reshape(entries)[:, None] * picked).reshape(tok_dev, topk, width_d).sum(axis=1)
    )
    token_gate = jnp.sum(jnp.where(hot_pick > 0, hot_gate[:, None], 0.0), axis=0)
    layer_out = layer_out + token_gate[:, None] * mm(hot_pick, hot_back[1], TN)
    pieces = []
    for r in range(chips):
        back = fourth[:, r * slots : (r + 1) * slots].reshape(rows, span)
        piece = mm(picks[r], back, TN)
        piece = piece.reshape(tok_dev, topk, span).sum(axis=1).astype(BF)
        if r > 0:
            piece = shift(piece, -r)
        pieces += [piece[:, k * wide : (k + 1) * wide] for k in range(cores)]
    pieces = jnp.stack(pieces)
    input_grad = jnp.concatenate(
        [
            lax.dynamic_index_in_dim(
                pieces,
                ((p - chip) % chips) * cores + (q - core) % cores,
                0,
                keepdims=False,
            )
            for p in range(chips)
            for q in range(cores)
        ],
        axis=1,
    ).astype(F32)
    input_grad = input_grad + mm(hot_pick, hot_back[0], TN)
    return (
        layer_out.astype(BF),
        input_grad.astype(BF),
        grad_gu[None],
        grad_dn[None],
        grad_hot[:2],
        grad_hot[2],
    )


def solution(mesh):
    tok = P(("dp", "expert"), None)
    flat = P(("dp", "expert"))
    rows = P("expert", "dp", None)
    hot = (P(None, "dp", "expert"), P("dp", "expert"))
    return jax.shard_map(
        local,
        mesh=mesh,
        in_specs=(tok, tok, tok, tok, flat, flat, rows, rows) + hot,
        out_specs=(tok, tok, rows, rows) + hot,
        check_vma=False,
    )
```

```python
import jax
import jax.numpy as jnp
from jax import lax
from jax.experimental import pallas as pl
from jax.experimental.pallas import tpu as pltpu
from jax.sharding import PartitionSpec as P

BF = jnp.bfloat16
F32 = jnp.float32
NN = (((1,), (0,)), ((), ()))
NT = (((1,), (1,)), ((), ()))
TN = (((0,), (0,)), ((), ()))
ROOM = 56 * 1024 * 1024
LIGHT = pl.CostEstimate(flops=1, bytes_accessed=1, transcendentals=0)
SMEM = pl.BlockSpec(memory_space=pltpu.SMEM)
ANYWHERE = pl.BlockSpec(memory_space=pl.ANY)
INSIDE = pl.BlockSpec(memory_space=pltpu.VMEM)
PIECES = 8


def mm(a, b, dims=NN):
    return lax.dot_general(a, b, dims, preferred_element_type=F32)


def after(value, *earlier):
    return lax.optimization_barrier((value,) + earlier)[0]


def params():
    return pltpu.CompilerParams(vmem_limit_bytes=ROOM)


LIGHT = pl.CostEstimate(flops=1, bytes_accessed=1, transcendentals=0)


def struct(*shape, dtype=BF):
    return jax.ShapeDtypeStruct(shape, dtype)


def whole(array):
    return pl.BlockSpec(array.shape, lambda *_: (0,) * len(array.shape))


def stack_rows(refs, scratch):
    rows = refs[0].shape[0]
    for i, ref in enumerate(refs):
        scratch[i * rows : (i + 1) * rows, :] = ref[...]


def fetch(order_ref, blocks, w_ref, sems):
    deep = blocks[0].shape[0]
    copies = []
    for j, block in enumerate(blocks):
        place = pl.multiple_of(order_ref[j] * deep, deep)
        copies.append(pltpu.make_async_copy(block, w_ref.at[pl.ds(place, deep)], sems.at[j]))
        copies[-1].start()
    return copies


def down_scratch(blocks):
    deep, width = blocks[0].shape
    return [pltpu.VMEM((len(blocks) * deep, width), BF), pltpu.SemaphoreType.DMA((len(blocks),))]


def fetch_each(blocks, w_ref, sems):
    copies = []
    for j, block in enumerate(blocks):
        copies.append(pltpu.make_async_copy(block, w_ref.at[j], sems.at[j]))
        copies[-1].start()
    return copies


def each_scratch(blocks):
    return [
        pltpu.VMEM((len(blocks),) + blocks[0].shape, BF),
        pltpu.SemaphoreType.DMA((len(blocks),)),
    ]


def activations(x, blocks):
    rows = x.shape[0]
    depth, width = blocks[0].shape
    half = width // 2
    m = len(blocks)

    def body(x_ref, *refs):
        ins, (hid_ref, fg_ref, fu_ref, acc, w_ref, sems) = refs[:m], refs[m:]
        copies = fetch_each(ins, w_ref, sems)
        for j, copy in enumerate(copies):
            copy.wait()
            found = mm(x_ref[:, j * depth : (j + 1) * depth], w_ref[j])
            if j == 0:
                acc[...] = found
            else:
                acc[...] += found
        g = acc[:, :half]
        u = acc[:, half:]
        s = jax.nn.sigmoid(g)
        hid_ref[...] = (g * s * u).astype(BF)
        fg_ref[...] = u * s * (1.0 + g * (1.0 - s))
        fu_ref[...] = g * s

    factor = struct(rows, half, dtype=F32)
    return pl.pallas_call(
        body,
        in_specs=[INSIDE] + [ANYWHERE] * m,
        out_specs=[INSIDE] * 3,
        out_shape=[struct(rows, half), factor, factor],
        scratch_shapes=[pltpu.VMEM((rows, width), F32)] + each_scratch(blocks),
        compiler_params=params(),
        cost_estimate=LIGHT,
        name="activations",
    )(x, *blocks)


def middle(order, hidden, f_gate, f_up, rows_s, blocks):
    rows, half = hidden.shape
    wide = rows_s.shape[1]
    m = len(blocks)
    step = 512 if wide % 512 == 0 else wide

    def body(order_ref, hid_ref, fg_ref, fu_ref, s_ref, *refs):
        down, (out_ref, d_ref, w_ref, sems) = refs[:m], refs[m:]
        for copy in fetch(order_ref, down, w_ref, sems):
            copy.wait()
        d_hidden = mm(s_ref[...], w_ref[...], NT)
        d_ref[:, :half] = (d_hidden * fg_ref[...]).astype(BF)
        d_ref[:, half:] = (d_hidden * fu_ref[...]).astype(BF)
        for c in range(0, wide, step):
            out_ref[:, c : c + step] = mm(hid_ref[...], w_ref[:, c : c + step]).astype(BF)

    return pl.pallas_call(
        body,
        in_specs=[SMEM] + [INSIDE] * 4 + [ANYWHERE] * m,
        out_specs=[INSIDE] * 2,
        out_shape=[struct(rows, wide), struct(rows, 2 * half)],
        scratch_shapes=down_scratch(blocks),
        compiler_params=params(),
        cost_estimate=LIGHT,
        name="middle",
    )(order, hidden, f_gate, f_up, rows_s, *blocks)


def row_grads(d_act, blocks):
    rows, width = d_act.shape
    depth = blocks[0].shape[0]
    m = len(blocks)

    def body(d_ref, *refs):
        ins, (out_ref, w_ref, sems) = refs[:m], refs[m:]
        copies = fetch_each(ins, w_ref, sems)
        for j, copy in enumerate(copies):
            copy.wait()
            out_ref[:, j * depth : (j + 1) * depth] = mm(d_ref[...], w_ref[j], NT).astype(BF)

    return pl.pallas_call(
        body,
        in_specs=[INSIDE] + [ANYWHERE] * m,
        out_specs=INSIDE,
        out_shape=struct(rows, m * depth),
        scratch_shapes=each_scratch(blocks),
        compiler_params=params(),
        cost_estimate=LIGHT,
        name="row_grads",
    )(d_act, *blocks)


def gate_up_grads(xs, ds, k, wide, scale, received):
    n, rows, width = len(xs), xs[0].shape[0], ds[0].shape[1]
    step = 512 if width % 512 == 0 else width
    extra = [] if received is None else [received]
    if wide % 128 != 0:
        xs, k = [x[:, k * wide : (k + 1) * wide] for x in xs], 0

    def body(*refs):
        x_refs, d_refs, rest = refs[:n], refs[n : 2 * n], refs[2 * n :]
        out_ref, x_scr, d_scr = rest[-3:]

        @pl.when(pl.program_id(0) == 0)
        def _():
            stack_rows(x_refs, x_scr)

        stack_rows(d_refs, d_scr)
        found = mm(x_scr[...], d_scr[...], TN) * scale
        if extra:
            found = found + rest[0][...].astype(F32)
        out_ref[...] = found.astype(BF)

    shape = struct(wide, width)
    column = lambda i: (0, i)
    return pl.pallas_call(
        body,
        grid=(width // step,),
        in_specs=[pl.BlockSpec((rows, wide), lambda i: (0, k))] * n
        + [pl.BlockSpec((rows, step), column)] * n
        + [pl.BlockSpec((wide, step), column)] * len(extra),
        out_specs=pl.BlockSpec((wide, step), column),
        out_shape=shape,
        scratch_shapes=[pltpu.VMEM((n * rows, wide), BF), pltpu.VMEM((n * rows, step), BF)],
        compiler_params=params(),
        cost_estimate=LIGHT,
        name="gate_up_grads",
    )(*xs, *ds, *extra)


def down_grads(order, hidden, rows_s, count, scale):
    rows, half = hidden.shape
    wide = rows_s.shape[1]
    deep = half // count
    step = 512 if wide % 512 == 0 else wide

    def body(order_ref, h_ref, s_ref, *refs):
        outs, scratch = refs[:count], refs[count]
        scratch[...] = mm(h_ref[...], s_ref[...], TN) * scale
        for j in range(count):
            place = pl.multiple_of(order_ref[j] * deep, deep)
            outs[j][...] = scratch[pl.ds(place, deep), :].astype(BF)

    shapes = [struct(deep, wide)] * count
    return pl.pallas_call(
        body,
        grid=(wide // step,),
        in_specs=[SMEM, whole(hidden), pl.BlockSpec((rows, step), lambda i: (0, i))],
        out_specs=[pl.BlockSpec((deep, step), lambda i: (0, i))] * count,
        out_shape=shapes,
        scratch_shapes=[pltpu.VMEM((half, step), F32)],
        compiler_params=params(),
        cost_estimate=LIGHT,
        name="down_grads",
    )(order, hidden, rows_s)


def popular_partials(select, packed, weights, hid):
    parts, count = select.shape[:2]
    narrow = packed.shape[1] // (2 * parts)
    columns = sum(w.shape[0] for w in weights)

    def body(sel_ref, in_ref, *refs):
        w_refs, (x_ref, s_ref, p_ref) = refs[: len(weights)], refs[len(weights) :]
        x = None
        s = None
        for q in range(parts):
            rows = mm(sel_ref[q], in_ref[...])
            one = rows[:, q * narrow : (q + 1) * narrow]
            two = rows[:, (parts + q) * narrow : (parts + q + 1) * narrow]
            x = one if x is None else x + one
            s = two if s is None else s + two
        x = x.astype(BF)
        s = s.astype(BF)
        x_ref[...] = x
        s_ref[...] = s
        at = 0
        for w_ref in w_refs:
            for top in range(0, w_ref.shape[0], 3 * hid):
                p_ref[:, at : at + 2 * hid] = mm(x, w_ref[top : top + 2 * hid, :], NT).astype(BF)
                p_ref[:, at + 2 * hid : at + 3 * hid] = mm(
                    s, w_ref[top + 2 * hid : top + 3 * hid, :], NT
                ).astype(BF)
                at += 3 * hid

    return pl.pallas_call(
        body,
        in_specs=[INSIDE] * (2 + len(weights)),
        out_specs=[INSIDE] * 3,
        out_shape=[
            struct(count, narrow),
            struct(count, narrow),
            struct(count, columns),
        ],
        compiler_params=params(),
        cost_estimate=LIGHT,
        name="popular_partials",
    )(select, packed, *weights)


def popular_middle(own, others, hid):
    rows, columns = own.shape

    def body(own_ref, *refs):
        parts, out_ref = refs[:-1], refs[-1]
        act = own_ref[...].astype(F32)
        for part in parts:
            act = act + part[...].astype(F32)
        for at in range(0, columns, 3 * hid):
            g = act[:, at : at + hid]
            u = act[:, at + hid : at + 2 * hid]
            dh = act[:, at + 2 * hid : at + 3 * hid]
            s = jax.nn.sigmoid(g)
            out_ref[:, at : at + hid] = (dh * u * s * (1.0 + g * (1.0 - s))).astype(BF)
            out_ref[:, at + hid : at + 2 * hid] = (dh * g * s).astype(BF)
            out_ref[:, at + 2 * hid : at + 3 * hid] = (g * s * u).astype(BF)

    return pl.pallas_call(
        body,
        in_specs=[INSIDE] * (1 + len(others)),
        out_specs=INSIDE,
        out_shape=struct(rows, columns),
        compiler_params=params(),
        cost_estimate=LIGHT,
        name="popular_middle",
    )(own, *others)


def popular_back(select, lines, x, s, weights, hid, scale):
    parts, count, spots = select.shape
    narrow = x.shape[1]
    m = len(weights)
    n = len(lines)
    columns = lines[0].shape[1]

    def body(sel_ref, x_ref, s_ref, *refs):
        ins, w_refs, back_ref = refs[:n], refs[n : n + m], refs[n + m]
        grads, mid_ref = refs[n + m + 1 : -1], refs[-1]
        stack_rows(ins, mid_ref)
        grad = None
        out = None
        at = 0
        for w_ref, g_ref in zip(w_refs, grads):
            for top in range(0, w_ref.shape[0], 3 * hid):
                d_gate = mid_ref[:, at : at + hid]
                d_up = mid_ref[:, at + hid : at + 2 * hid]
                hidden = mid_ref[:, at + 2 * hid : at + 3 * hid]
                sides = ((d_gate, x_ref), (d_up, x_ref), (hidden, s_ref))
                for i, (left, right) in enumerate(sides):
                    here = slice(top + i * hid, top + (i + 1) * hid)
                    product = mm(left, w_ref[here, :])
                    if i == 2:
                        out = product if out is None else out + product
                    else:
                        grad = product if grad is None else grad + product
                    g_ref[here, :] = (mm(left, right[...], TN) * scale).astype(BF)
                at += 3 * hid
        grad = grad.astype(BF)
        out = out.astype(BF)
        for q in range(parts):
            back_ref[:, q * narrow : (q + 1) * narrow] = mm(sel_ref[q], grad, TN).astype(BF)
            back_ref[:, (parts + q) * narrow : (parts + q + 1) * narrow] = mm(
                sel_ref[q], out, TN
            ).astype(BF)

    return pl.pallas_call(
        body,
        in_specs=[INSIDE] * (3 + n + m),
        out_specs=[INSIDE] * (1 + m),
        out_shape=[struct(spots, 2 * parts * narrow)]
        + [struct(w.shape[0], narrow) for w in weights],
        scratch_shapes=[pltpu.VMEM((count, columns), BF)],
        compiler_params=params(),
        cost_estimate=LIGHT,
        name="popular_back",
    )(select, x, s, *lines, *weights)


def slot_positions(route_block, count):
    flat = route_block.reshape(-1)
    onehot = (flat[:, None] == jnp.arange(count, dtype=jnp.int32)[None, :]).astype(jnp.int32)
    before = jnp.cumsum(onehot, axis=0) - onehot
    return (flat, jnp.sum(before * onehot, axis=1))


def exchange(blocks):
    return lax.all_to_all(blocks, "expert", split_axis=0, concat_axis=0, tiled=True)


def local(
    tokens, cotangent, routes, gates, hot_index, hot_gate, w_gate_up, w_down, w_hot_gu, w_hot_dn
):
    owners = lax.axis_size("expert")
    groups = lax.axis_size("dp")
    cores = 2 if groups % 2 == 0 else 1
    chips = groups // cores
    tok_dev, width_d = tokens.shape
    topk = routes.shape[1]
    slots = max(2, 3 * tok_dev * topk // (2 * owners))
    entries = tok_dev * topk
    rows = owners * slots
    inverse = 1.0 / (4 * groups)
    me = lax.axis_index("dp")
    chip, core = me // cores, me % cores

    def shift(value, r):
        pairs = [
            (i, ((i // cores + r) % chips) * cores + i % cores) for i in range(groups)
        ]
        return lax.ppermute(value, "dp", pairs)

    def swap(value):
        pairs = [(i, (i // cores) * cores + (i + 1) % cores) for i in range(groups)]
        return lax.ppermute(value, "dp", pairs)

    def gather(block):
        near = [block] + [shift(block, r) for r in range(1, chips)]
        return near + ([swap(one) for one in near] if cores == 2 else [])

    order = jnp.stack(
        [
            ((chip - r) % chips) * cores + (core + k) % cores
            for k in range(cores)
            for r in range(chips)
        ]
    ).astype(jnp.int32)

    across = 1
    while 2 * (2 * across) ** 2 <= owners:
        across *= 2
    depths = owners // across
    spot = lax.axis_index("expert")

    def hop(value, j):
        return lax.ppermute(value, "expert", [(i, i ^ j) for i in range(owners)])

    wide = width_d // groups
    hid = w_hot_dn.shape[0]
    narrow = width_d // owners
    hot_w = jnp.concatenate([w_hot_gu, w_hot_dn[None]], axis=0).reshape(3 * hid, narrow)
    hot_near = [hot_w] + [shift(hot_w, r) for r in range(1, chips)]
    gu_blocks = gather(w_gate_up[0])
    down = after(w_down[0], hot_near[-1])
    down_blocks = gather(down)

    flat, pos = slot_positions(routes, owners)
    dest = flat * slots + pos
    slot_ids = jnp.arange(rows, dtype=jnp.int32)[:, None]
    pick = (slot_ids == dest[None, :]).astype(BF)

    def as_rows(value, width):
        value = value.reshape(owners, -1)
        spare = -value.shape[1] % width
        return jnp.pad(value, ((0, 0), (0, spare))).reshape(owners, -1, width)

    hot_dev = hot_index.shape[0]
    few = 2 * hot_dev // PIECES
    hot_pick = (
        hot_index[:, None] == jnp.arange(tok_dev, dtype=jnp.int32)[None, :]
    ).astype(BF)
    hot_x = mm(hot_pick, tokens).astype(BF)
    hot_s = (hot_gate[:, None] * mm(hot_pick, cotangent)).astype(BF)
    hot_send = jnp.concatenate([hot_x, hot_s], axis=0).reshape(PIECES, few, owners, narrow)
    hot_send = hot_send.transpose(2, 1, 0, 3)
    row = jnp.arange(owners * hot_dev, dtype=jnp.int32)
    packed_id = jnp.arange(owners * few, dtype=jnp.int32)
    step = row // hot_dev
    owner = spot ^ ((step % depths) * across + step // depths)
    hit = (owner * few + row % few)[:, None] == packed_id[None, :]
    piece = (row % hot_dev) // few
    select = jnp.stack([hit & (piece == q)[:, None] for q in range(PIECES // 2)]).astype(BF)

    scaled = (gates[:, :, None] * cotangent[:, None, :].astype(F32)).astype(BF)
    send_s = mm(pick, scaled.reshape(entries, width_d)).astype(BF)
    early = exchange(
        jnp.concatenate([send_s.reshape(owners, slots, width_d), as_rows(hot_send, width_d)], axis=1)
    )
    rows_s = early[:, :slots].reshape(rows, width_d)
    hot_recv = early[:, slots:].reshape(owners, -1)[:, : 2 * hot_dev * narrow]
    hot_recv = hot_recv.reshape(owners * few, PIECES * narrow)

    tok_rel = jnp.concatenate(
        [
            lax.dynamic_slice_in_dim(tokens, order[j] * wide, wide, 1)
            for j in range(groups)
        ],
        axis=1,
    )
    tok_rel = jnp.repeat(tok_rel, topk, axis=0) if topk > 1 else tok_rel
    send_x = mm(pick, tok_rel).astype(BF).reshape(owners, slots, width_d)
    rows_x = exchange(send_x).reshape(rows, width_d)

    hot_near = jnp.concatenate(list(after(tuple(hot_near), send_x)), axis=0)
    hot_ws = [hot_near] + ([swap(hot_near)] if cores == 2 else [])
    hot_x, hot_s, partial = popular_partials(select, hot_recv, hot_ws, hid)
    share = depths * hot_dev
    level_in = [hop(partial[j * share : (j + 1) * share], j) for j in range(1, across)]
    level = partial[:share].astype(F32)
    for value in level_in:
        level = level + value.astype(F32)
    level = level.astype(BF)
    rows_x = after(rows_x, level)
    level = [level[j * hot_dev : (j + 1) * hot_dev] for j in range(depths)]
    depth_in = [hop(level[j], j * across) for j in range(1, depths)]

    hidden, f_gate, f_up = activations(rows_x, gu_blocks)
    depth_in = list(after(tuple(depth_in), hidden))
    hot_own = popular_middle(level[0], depth_in, hid)
    hidden = after(hidden, hot_own)
    out, d_act = middle(order, hidden, f_gate, f_up, rows_s, down_blocks)
    back_out = exchange(out.reshape(owners, slots, width_d)).reshape(rows, width_d)
    d_rows = row_grads(d_act, gu_blocks)

    line = [hot_own] + [hop(hot_own, j * across) for j in range(1, depths)]
    line = jnp.concatenate(list(after(tuple(line), d_act)))
    lines = [line] + [hop(line, j) for j in range(1, across)]
    lines = list(after(tuple(lines), d_rows))
    hot_back, *hot_grads = popular_back(select, lines, hot_x, hot_s, hot_ws, hid, inverse)

    fourth_in = jnp.concatenate(
        [d_rows.reshape(owners, slots, width_d), as_rows(hot_back, width_d)], axis=1
    )
    fourth = exchange(fourth_in)

    dn_parts = down_grads(order, after(hidden, d_rows), rows_s, groups, inverse)
    dn_sum = list(dn_parts[:chips])
    if cores == 2:
        dn_in = [swap(part) for part in dn_parts[chips:]]
        dn_sum = [
            (one.astype(F32) + two.astype(F32)).astype(BF) for one, two in zip(dn_sum, dn_in)
        ]
    dn_total = dn_sum[0].astype(F32)
    for r in range(1, chips):
        dn_total = dn_total + shift(dn_sum[r], -r).astype(F32)
    grad_dn = dn_total.astype(BF)

    def columns_of(r):
        return jnp.concatenate(
            [
                rows_x[:, (k * chips + r) * wide : (k * chips + r + 1) * wide]
                for k in range(cores)
            ],
            axis=1,
        )

    xs = [columns_of(0)] + [shift(columns_of(r), -r) for r in range(1, chips)]
    ds = [d_act] + [shift(d_act, -r) for r in range(1, chips)]
    xs = list(after(tuple(xs), back_out))
    gu_in = None
    if cores == 2:
        gu_in = swap(gate_up_grads(xs, ds, 1, wide, inverse, None))
    grad_gu = gate_up_grads(xs, ds, 0, wide, inverse, gu_in)

    hot_sum = hot_grads[0]
    if cores == 2:
        hot_sum = (hot_sum.astype(F32) + swap(hot_grads[1]).astype(F32)).astype(BF)
    hot_sum = hot_sum.reshape(chips, 3 * hid, narrow)
    hot_total = hot_sum[0].astype(F32)
    for r in range(1, chips):
        hot_total = hot_total + shift(hot_sum[r], -r).astype(F32)
    grad_hot = hot_total.astype(BF).reshape(3, hid, narrow)

    hot_back = fourth[:, slots:].reshape(owners, -1)[:, : 2 * hot_dev * narrow]
    hot_back = hot_back.reshape(owners, few, PIECES, narrow)
    hot_back = hot_back.transpose(2, 1, 0, 3).reshape(2, hot_dev, width_d)
    picked = mm(pick, back_out, TN)
    layer_out = (
        (gates.reshape(entries)[:, None] * picked).reshape(tok_dev, topk, width_d).sum(axis=1)
    )
    token_gate = jnp.sum(jnp.where(hot_pick > 0, hot_gate[:, None], 0.0), axis=0)
    layer_out = layer_out + token_gate[:, None] * mm(hot_pick, hot_back[1], TN)
    returned = mm(pick, fourth[:, :slots].reshape(rows, width_d), TN)
    returned = returned.reshape(tok_dev, topk, width_d).sum(axis=1)
    blocks = jnp.stack([returned[:, j * wide : (j + 1) * wide] for j in range(groups)])
    input_grad = jnp.concatenate(
        [
            lax.dynamic_index_in_dim(
                blocks,
                ((q - core) % cores) * chips + (chip - p) % chips,
                0,
                keepdims=False,
            )
            for p in range(chips)
            for q in range(cores)
        ],
        axis=1,
    )
    input_grad = input_grad + mm(hot_pick, hot_back[0], TN)
    return (
        layer_out.astype(BF),
        input_grad.astype(BF),
        grad_gu[None],
        grad_dn[None],
        grad_hot[:2],
        grad_hot[2],
    )


def solution(mesh):
    tok = P(("dp", "expert"), None)
    flat = P(("dp", "expert"))
    rows = P("expert", "dp", None)
    hot = (P(None, "dp", "expert"), P("dp", "expert"))
    return jax.shard_map(
        local,
        mesh=mesh,
        in_specs=(tok, tok, tok, tok, flat, flat, rows, rows) + hot,
        out_specs=(tok, tok, rows, rows) + hot,
        check_vma=False,
    )
```

```python
import jax
import jax.numpy as jnp
from jax import lax
from jax.experimental import pallas as pl
from jax.experimental.pallas import tpu as pltpu
from jax.sharding import PartitionSpec as P

BF = jnp.bfloat16
F32 = jnp.float32
NN = (((1,), (0,)), ((), ()))
NT = (((1,), (1,)), ((), ()))
TN = (((0,), (0,)), ((), ()))
ROOM = 56 * 1024 * 1024
LIGHT = pl.CostEstimate(flops=1, bytes_accessed=1, transcendentals=0)
SMEM = pl.BlockSpec(memory_space=pltpu.SMEM)
ANYWHERE = pl.BlockSpec(memory_space=pl.ANY)
INSIDE = pl.BlockSpec(memory_space=pltpu.VMEM)
PIECES = 8


def mm(a, b, dims=NN):
    return lax.dot_general(a, b, dims, preferred_element_type=F32)


def after(value, *earlier):
    return lax.optimization_barrier((value,) + earlier)[0]


def params():
    return pltpu.CompilerParams(vmem_limit_bytes=ROOM)


LIGHT = pl.CostEstimate(flops=1, bytes_accessed=1, transcendentals=0)


def struct(*shape, dtype=BF):
    return jax.ShapeDtypeStruct(shape, dtype)


def whole(array):
    return pl.BlockSpec(array.shape, lambda *_: (0,) * len(array.shape))


def stack_rows(refs, scratch):
    rows = refs[0].shape[0]
    for i, ref in enumerate(refs):
        scratch[i * rows : (i + 1) * rows, :] = ref[...]


def fetch(order_ref, blocks, w_ref, sems):
    deep = blocks[0].shape[0]
    copies = []
    for j, block in enumerate(blocks):
        place = pl.multiple_of(order_ref[j] * deep, deep)
        copies.append(pltpu.make_async_copy(block, w_ref.at[pl.ds(place, deep)], sems.at[j]))
        copies[-1].start()
    return copies


def down_scratch(blocks):
    deep, width = blocks[0].shape
    return [pltpu.VMEM((len(blocks) * deep, width), BF), pltpu.SemaphoreType.DMA((len(blocks),))]


def fetch_each(blocks, w_ref, sems):
    copies = []
    for j, block in enumerate(blocks):
        copies.append(pltpu.make_async_copy(block, w_ref.at[j], sems.at[j]))
        copies[-1].start()
    return copies


def each_scratch(blocks):
    return [
        pltpu.VMEM((len(blocks),) + blocks[0].shape, BF),
        pltpu.SemaphoreType.DMA((len(blocks),)),
    ]


def activations(x, blocks):
    rows = x.shape[0]
    depth, width = blocks[0].shape
    half = width // 2
    m = len(blocks)

    def body(x_ref, *refs):
        ins, (hid_ref, fg_ref, fu_ref, acc, w_ref, sems) = refs[:m], refs[m:]
        copies = fetch_each(ins, w_ref, sems)
        for j, copy in enumerate(copies):
            copy.wait()
            found = mm(x_ref[:, j * depth : (j + 1) * depth], w_ref[j])
            if j == 0:
                acc[...] = found
            else:
                acc[...] += found
        g = acc[:, :half]
        u = acc[:, half:]
        s = jax.nn.sigmoid(g)
        hid_ref[...] = (g * s * u).astype(BF)
        fg_ref[...] = u * s * (1.0 + g * (1.0 - s))
        fu_ref[...] = g * s

    factor = struct(rows, half, dtype=F32)
    return pl.pallas_call(
        body,
        in_specs=[INSIDE] + [ANYWHERE] * m,
        out_specs=[INSIDE] * 3,
        out_shape=[struct(rows, half), factor, factor],
        scratch_shapes=[pltpu.VMEM((rows, width), F32)] + each_scratch(blocks),
        compiler_params=params(),
        cost_estimate=LIGHT,
        name="activations",
    )(x, *blocks)


def middle(order, hidden, f_gate, f_up, rows_s, blocks):
    rows, half = hidden.shape
    wide = rows_s.shape[1]
    m = len(blocks)
    step = 512 if wide % 512 == 0 else wide

    def body(order_ref, hid_ref, fg_ref, fu_ref, s_ref, *refs):
        down, (out_ref, d_ref, w_ref, sems) = refs[:m], refs[m:]
        for copy in fetch(order_ref, down, w_ref, sems):
            copy.wait()
        d_hidden = mm(s_ref[...], w_ref[...], NT)
        d_ref[:, :half] = (d_hidden * fg_ref[...]).astype(BF)
        d_ref[:, half:] = (d_hidden * fu_ref[...]).astype(BF)
        for c in range(0, wide, step):
            out_ref[:, c : c + step] = mm(hid_ref[...], w_ref[:, c : c + step]).astype(BF)

    return pl.pallas_call(
        body,
        in_specs=[SMEM] + [INSIDE] * 4 + [ANYWHERE] * m,
        out_specs=[INSIDE] * 2,
        out_shape=[struct(rows, wide), struct(rows, 2 * half)],
        scratch_shapes=down_scratch(blocks),
        compiler_params=params(),
        cost_estimate=LIGHT,
        name="middle",
    )(order, hidden, f_gate, f_up, rows_s, *blocks)


def row_grads(d_act, blocks):
    rows, width = d_act.shape
    depth = blocks[0].shape[0]
    m = len(blocks)

    def body(d_ref, *refs):
        ins, (out_ref, w_ref, sems) = refs[:m], refs[m:]
        copies = fetch_each(ins, w_ref, sems)
        for j, copy in enumerate(copies):
            copy.wait()
            out_ref[:, j * depth : (j + 1) * depth] = mm(d_ref[...], w_ref[j], NT).astype(BF)

    return pl.pallas_call(
        body,
        in_specs=[INSIDE] + [ANYWHERE] * m,
        out_specs=INSIDE,
        out_shape=struct(rows, m * depth),
        scratch_shapes=each_scratch(blocks),
        compiler_params=params(),
        cost_estimate=LIGHT,
        name="row_grads",
    )(d_act, *blocks)


def gate_up_grads(xs, ds, k, wide, scale, received):
    n, rows, width = len(xs), xs[0].shape[0], ds[0].shape[1]
    step = 512 if width % 512 == 0 else width
    extra = [] if received is None else [received]
    if wide % 128 != 0:
        xs, k = [x[:, k * wide : (k + 1) * wide] for x in xs], 0

    def body(*refs):
        x_refs, d_refs, rest = refs[:n], refs[n : 2 * n], refs[2 * n :]
        out_ref, x_scr, d_scr = rest[-3:]

        @pl.when(pl.program_id(0) == 0)
        def _():
            stack_rows(x_refs, x_scr)

        stack_rows(d_refs, d_scr)
        found = mm(x_scr[...], d_scr[...], TN) * scale
        if extra:
            found = found + rest[0][...].astype(F32)
        out_ref[...] = found.astype(BF)

    shape = struct(wide, width)
    column = lambda i: (0, i)
    return pl.pallas_call(
        body,
        grid=(width // step,),
        in_specs=[pl.BlockSpec((rows, wide), lambda i: (0, k))] * n
        + [pl.BlockSpec((rows, step), column)] * n
        + [pl.BlockSpec((wide, step), column)] * len(extra),
        out_specs=pl.BlockSpec((wide, step), column),
        out_shape=shape,
        scratch_shapes=[pltpu.VMEM((n * rows, wide), BF), pltpu.VMEM((n * rows, step), BF)],
        compiler_params=params(),
        cost_estimate=LIGHT,
        name="gate_up_grads",
    )(*xs, *ds, *extra)


def down_grads(order, hidden, rows_s, count, scale):
    rows, half = hidden.shape
    wide = rows_s.shape[1]
    deep = half // count
    step = 512 if wide % 512 == 0 else wide

    def body(order_ref, h_ref, s_ref, *refs):
        outs, scratch = refs[:count], refs[count]
        scratch[...] = mm(h_ref[...], s_ref[...], TN) * scale
        for j in range(count):
            place = pl.multiple_of(order_ref[j] * deep, deep)
            outs[j][...] = scratch[pl.ds(place, deep), :].astype(BF)

    shapes = [struct(deep, wide)] * count
    return pl.pallas_call(
        body,
        grid=(wide // step,),
        in_specs=[SMEM, whole(hidden), pl.BlockSpec((rows, step), lambda i: (0, i))],
        out_specs=[pl.BlockSpec((deep, step), lambda i: (0, i))] * count,
        out_shape=shapes,
        scratch_shapes=[pltpu.VMEM((half, step), F32)],
        compiler_params=params(),
        cost_estimate=LIGHT,
        name="down_grads",
    )(order, hidden, rows_s)


def popular_partials(select, packed, weights, hid):
    parts, count = select.shape[:2]
    narrow = packed.shape[1] // (2 * parts)
    columns = sum(w.shape[0] for w in weights)

    def body(sel_ref, in_ref, *refs):
        w_refs, (x_ref, s_ref, p_ref) = refs[: len(weights)], refs[len(weights) :]
        x = None
        s = None
        for q in range(parts):
            rows = mm(sel_ref[q], in_ref[...])
            one = rows[:, q * narrow : (q + 1) * narrow]
            two = rows[:, (parts + q) * narrow : (parts + q + 1) * narrow]
            x = one if x is None else x + one
            s = two if s is None else s + two
        x = x.astype(BF)
        s = s.astype(BF)
        x_ref[...] = x
        s_ref[...] = s
        at = 0
        for w_ref in w_refs:
            for top in range(0, w_ref.shape[0], 3 * hid):
                p_ref[:, at : at + 2 * hid] = mm(x, w_ref[top : top + 2 * hid, :], NT).astype(BF)
                p_ref[:, at + 2 * hid : at + 3 * hid] = mm(
                    s, w_ref[top + 2 * hid : top + 3 * hid, :], NT
                ).astype(BF)
                at += 3 * hid

    return pl.pallas_call(
        body,
        in_specs=[INSIDE] * (2 + len(weights)),
        out_specs=[INSIDE] * 3,
        out_shape=[
            struct(count, narrow),
            struct(count, narrow),
            struct(count, columns),
        ],
        compiler_params=params(),
        cost_estimate=LIGHT,
        name="popular_partials",
    )(select, packed, *weights)


def popular_middle(own, others, hid):
    rows, columns = own.shape

    def body(own_ref, *refs):
        parts, out_ref = refs[:-1], refs[-1]
        act = own_ref[...].astype(F32)
        for part in parts:
            act = act + part[...].astype(F32)
        for at in range(0, columns, 3 * hid):
            g = act[:, at : at + hid]
            u = act[:, at + hid : at + 2 * hid]
            dh = act[:, at + 2 * hid : at + 3 * hid]
            s = jax.nn.sigmoid(g)
            out_ref[:, at : at + hid] = (dh * u * s * (1.0 + g * (1.0 - s))).astype(BF)
            out_ref[:, at + hid : at + 2 * hid] = (dh * g * s).astype(BF)
            out_ref[:, at + 2 * hid : at + 3 * hid] = (g * s * u).astype(BF)

    return pl.pallas_call(
        body,
        in_specs=[INSIDE] * (1 + len(others)),
        out_specs=INSIDE,
        out_shape=struct(rows, columns),
        compiler_params=params(),
        cost_estimate=LIGHT,
        name="popular_middle",
    )(own, *others)


def popular_back(select, lines, x, s, weights, hid, scale):
    parts, count, spots = select.shape
    narrow = x.shape[1]
    m = len(weights)
    n = len(lines)
    columns = lines[0].shape[1]

    def body(sel_ref, x_ref, s_ref, *refs):
        ins, w_refs, back_ref = refs[:n], refs[n : n + m], refs[n + m]
        grads, mid_ref = refs[n + m + 1 : -1], refs[-1]
        stack_rows(ins, mid_ref)
        grad = None
        out = None
        at = 0
        for w_ref, g_ref in zip(w_refs, grads):
            for top in range(0, w_ref.shape[0], 3 * hid):
                d_gate = mid_ref[:, at : at + hid]
                d_up = mid_ref[:, at + hid : at + 2 * hid]
                hidden = mid_ref[:, at + 2 * hid : at + 3 * hid]
                sides = ((d_gate, x_ref), (d_up, x_ref), (hidden, s_ref))
                for i, (left, right) in enumerate(sides):
                    here = slice(top + i * hid, top + (i + 1) * hid)
                    product = mm(left, w_ref[here, :])
                    if i == 2:
                        out = product if out is None else out + product
                    else:
                        grad = product if grad is None else grad + product
                    g_ref[here, :] = (mm(left, right[...], TN) * scale).astype(BF)
                at += 3 * hid
        grad = grad.astype(BF)
        out = out.astype(BF)
        for q in range(parts):
            back_ref[:, q * narrow : (q + 1) * narrow] = mm(sel_ref[q], grad, TN).astype(BF)
            back_ref[:, (parts + q) * narrow : (parts + q + 1) * narrow] = mm(
                sel_ref[q], out, TN
            ).astype(BF)

    return pl.pallas_call(
        body,
        in_specs=[INSIDE] * (3 + n + m),
        out_specs=[INSIDE] * (1 + m),
        out_shape=[struct(spots, 2 * parts * narrow)]
        + [struct(w.shape[0], narrow) for w in weights],
        scratch_shapes=[pltpu.VMEM((count, columns), BF)],
        compiler_params=params(),
        cost_estimate=LIGHT,
        name="popular_back",
    )(select, x, s, *lines, *weights)


def slot_positions(route_block, count):
    flat = route_block.reshape(-1)
    onehot = (flat[:, None] == jnp.arange(count, dtype=jnp.int32)[None, :]).astype(jnp.int32)
    before = jnp.cumsum(onehot, axis=0) - onehot
    return (flat, jnp.sum(before * onehot, axis=1))


def exchange(blocks):
    return lax.all_to_all(blocks, "expert", split_axis=0, concat_axis=0, tiled=True)


def local(
    tokens, cotangent, routes, gates, hot_index, hot_gate, w_gate_up, w_down, w_hot_gu, w_hot_dn
):
    owners = lax.axis_size("expert")
    groups = lax.axis_size("dp")
    cores = 2 if groups % 2 == 0 else 1
    chips = groups // cores
    tok_dev, width_d = tokens.shape
    topk = routes.shape[1]
    slots = max(2, 3 * tok_dev * topk // (2 * owners))
    entries = tok_dev * topk
    rows = owners * slots
    inverse = 1.0 / (4 * groups)
    me = lax.axis_index("dp")
    chip, core = me // cores, me % cores

    def shift(value, r):
        pairs = [
            (i, ((i // cores + r) % chips) * cores + i % cores) for i in range(groups)
        ]
        return lax.ppermute(value, "dp", pairs)

    def swap(value):
        pairs = [(i, (i // cores) * cores + (i + 1) % cores) for i in range(groups)]
        return lax.ppermute(value, "dp", pairs)

    def gather(block):
        near = [block] + [shift(block, r) for r in range(1, chips)]
        return near + ([swap(one) for one in near] if cores == 2 else [])

    order = jnp.stack(
        [
            ((chip - r) % chips) * cores + (core + k) % cores
            for k in range(cores)
            for r in range(chips)
        ]
    ).astype(jnp.int32)

    across = 1
    while 2 * (2 * across) ** 2 <= owners:
        across *= 2
    depths = owners // across
    spot = lax.axis_index("expert")

    def hop(value, j):
        return lax.ppermute(value, "expert", [(i, i ^ j) for i in range(owners)])

    wide = width_d // groups
    hid = w_hot_dn.shape[0]
    narrow = width_d // owners
    hot_w = jnp.concatenate([w_hot_gu, w_hot_dn[None]], axis=0).reshape(3 * hid, narrow)
    hot_near = [hot_w] + [shift(hot_w, r) for r in range(1, chips)]
    gu_blocks = gather(after(w_gate_up[0], hot_near[-1]))
    down_blocks = gather(after(w_down[0], hot_near[-1]))

    flat, pos = slot_positions(routes, owners)
    dest = flat * slots + pos
    slot_ids = jnp.arange(rows, dtype=jnp.int32)[:, None]
    pick = (slot_ids == dest[None, :]).astype(BF)

    def as_rows(value, width):
        value = value.reshape(owners, -1)
        spare = -value.shape[1] % width
        return jnp.pad(value, ((0, 0), (0, spare))).reshape(owners, -1, width)

    hot_dev = hot_index.shape[0]
    few = 2 * hot_dev // PIECES
    hot_pick = (
        hot_index[:, None] == jnp.arange(tok_dev, dtype=jnp.int32)[None, :]
    ).astype(BF)
    hot_x = mm(hot_pick, tokens).astype(BF)
    hot_s = (hot_gate[:, None] * mm(hot_pick, cotangent)).astype(BF)
    hot_send = jnp.concatenate([hot_x, hot_s], axis=0).reshape(PIECES, few, owners, narrow)
    hot_send = hot_send.transpose(2, 1, 0, 3).reshape(owners * few, PIECES * narrow)
    packed_id = jnp.arange(owners * few, dtype=jnp.int32)
    turn = ((packed_id ^ (spot * few))[:, None] == packed_id[None, :]).astype(BF)
    row = jnp.arange(owners * hot_dev, dtype=jnp.int32)
    step = row // hot_dev
    owner = spot ^ ((step % depths) * across + step // depths)
    piece = (row % hot_dev) // few

    def selection(index):
        hit = (index * few + row % few)[:, None] == packed_id[None, :]
        return jnp.stack([hit & (piece == q)[:, None] for q in range(PIECES // 2)]).astype(BF)

    hot_send = mm(turn, hot_send).astype(BF).reshape(depths, across, few, PIECES * narrow)
    near = [hot_send[0]] + [hop(hot_send[j], j * across) for j in range(1, depths)]
    near = jnp.stack(near, axis=1)
    hot_recv = jnp.concatenate([near[0]] + [hop(near[j], j) for j in range(1, across)])
    hot_recv = hot_recv.reshape(owners * few, PIECES * narrow)

    scaled = (gates[:, :, None] * cotangent[:, None, :].astype(F32)).astype(BF)
    send_s = mm(pick, scaled.reshape(entries, width_d)).astype(BF)
    rows_s = exchange(send_s.reshape(owners, slots, width_d)).reshape(rows, width_d)

    tok_rel = jnp.concatenate(
        [
            lax.dynamic_slice_in_dim(tokens, order[j] * wide, wide, 1)
            for j in range(groups)
        ],
        axis=1,
    )
    tok_rel = jnp.repeat(tok_rel, topk, axis=0) if topk > 1 else tok_rel
    send_x = mm(pick, tok_rel).astype(BF).reshape(owners, slots, width_d)
    rows_x = exchange(send_x).reshape(rows, width_d)

    hot_near = jnp.concatenate(list(after(tuple(hot_near), send_x)), axis=0)
    hot_ws = [hot_near] + ([swap(hot_near)] if cores == 2 else [])
    hot_x, hot_s, partial = popular_partials(selection(step), hot_recv, hot_ws, hid)
    share = depths * hot_dev
    level_in = [hop(partial[j * share : (j + 1) * share], j) for j in range(1, across)]
    level_in = list(after(tuple(level_in), rows_s))
    level = partial[:share].astype(F32)
    for value in level_in:
        level = level + value.astype(F32)
    level = level.astype(BF)
    level = [level[j * hot_dev : (j + 1) * hot_dev] for j in range(depths)]
    depth_in = [hop(level[j], j * across) for j in range(1, depths)]

    rows_x = after(rows_x, *depth_in)

    hidden, f_gate, f_up = activations(rows_x, gu_blocks)
    depth_in = list(after(tuple(depth_in), hidden))
    hot_own = popular_middle(level[0], depth_in, hid)
    hidden = after(hidden, hot_own)
    out, d_act = middle(order, hidden, f_gate, f_up, rows_s, down_blocks)

    def columns_of(r):
        return jnp.concatenate(
            [
                rows_x[:, (k * chips + r) * wide : (k * chips + r + 1) * wide]
                for k in range(cores)
            ],
            axis=1,
        )

    xs = [columns_of(0)] + [shift(columns_of(r), -r) for r in range(1, chips)]
    ds = [d_act] + [shift(d_act, -r) for r in range(1, chips)]
    d_rows = row_grads(d_act, gu_blocks)
    back_rows = exchange(d_rows.reshape(owners, slots, width_d)).reshape(rows, width_d)

    line = [hot_own] + [hop(hot_own, j * across) for j in range(1, depths)]
    line = jnp.concatenate(list(after(tuple(line), d_act)))
    lines = [line] + [hop(line, j) for j in range(1, across)]
    lines = list(after(tuple(lines), d_rows, xs[-1], ds[-1]))
    hot_back, *hot_grads = popular_back(
        selection(owner), lines, hot_x, hot_s, hot_ws, hid, inverse
    )

    dn_parts = down_grads(order, after(hidden, d_rows), rows_s, groups, inverse)
    dn_sum = list(dn_parts[:chips])
    if cores == 2:
        dn_in = [swap(part) for part in dn_parts[chips:]]
        dn_sum = [
            (one.astype(F32) + two.astype(F32)).astype(BF) for one, two in zip(dn_sum, dn_in)
        ]
    dn_total = dn_sum[0].astype(F32)
    dn_recv = [shift(dn_sum[r], -r) for r in range(1, chips)]
    for value in dn_recv:
        dn_total = dn_total + value.astype(F32)
    grad_dn = dn_total.astype(BF)

    last_in = jnp.concatenate(
        [out.reshape(owners, slots, width_d), as_rows(hot_back, width_d)], axis=1
    )
    last_in = after(last_in, dn_sum[-1])
    last = exchange(last_in)
    back_out = last[:, :slots].reshape(rows, width_d)

    xs_late = list(after(tuple(xs), back_rows, *dn_recv))
    gu_in = None
    if cores == 2:
        gu_in = swap(gate_up_grads(xs_late, ds, 1, wide, inverse, None))

    hot_sum = hot_grads[0]
    if cores == 2:
        hot_sum = (hot_sum.astype(F32) + swap(hot_grads[1]).astype(F32)).astype(BF)
    hot_sum = hot_sum.reshape(chips, 3 * hid, narrow)
    hot_total = hot_sum[0].astype(F32)
    hot_far = [shift(hot_sum[r], -r) for r in range(1, chips)]
    for value in hot_far:
        hot_total = hot_total + value.astype(F32)
    grad_hot = hot_total.astype(BF).reshape(3, hid, narrow)
    xs_last = list(after(tuple(xs_late), *hot_far))
    grad_gu = gate_up_grads(xs_last, ds, 0, wide, inverse, gu_in)

    hot_back = last[:, slots:].reshape(owners, -1)[:, : 2 * hot_dev * narrow]
    hot_back = hot_back.reshape(owners, few, PIECES, narrow)
    hot_back = hot_back.transpose(2, 1, 0, 3).reshape(2, hot_dev, width_d)
    picked = mm(pick, back_out, TN)
    layer_out = (
        (gates.reshape(entries)[:, None] * picked).reshape(tok_dev, topk, width_d).sum(axis=1)
    )
    token_gate = jnp.sum(jnp.where(hot_pick > 0, hot_gate[:, None], 0.0), axis=0)
    layer_out = layer_out + token_gate[:, None] * mm(hot_pick, hot_back[1], TN)
    returned = mm(pick, back_rows, TN)
    returned = returned.reshape(tok_dev, topk, width_d).sum(axis=1)
    blocks = jnp.stack([returned[:, j * wide : (j + 1) * wide] for j in range(groups)])
    input_grad = jnp.concatenate(
        [
            lax.dynamic_index_in_dim(
                blocks,
                ((q - core) % cores) * chips + (chip - p) % chips,
                0,
                keepdims=False,
            )
            for p in range(chips)
            for q in range(cores)
        ],
        axis=1,
    )
    input_grad = input_grad + mm(hot_pick, hot_back[0], TN)
    return (
        layer_out.astype(BF),
        input_grad.astype(BF),
        grad_gu[None],
        grad_dn[None],
        grad_hot[:2],
        grad_hot[2],
    )


def solution(mesh):
    tok = P(("dp", "expert"), None)
    flat = P(("dp", "expert"))
    rows = P("expert", "dp", None)
    hot = (P(None, "dp", "expert"), P("dp", "expert"))
    return jax.shard_map(
        local,
        mesh=mesh,
        in_specs=(tok, tok, tok, tok, flat, flat, rows, rows) + hot,
        out_specs=(tok, tok, rows, rows) + hot,
        check_vma=False,
    )
```

```python
import jax
import jax.numpy as jnp
from jax import lax
from jax.experimental import pallas as pl
from jax.experimental.pallas import tpu as pltpu
from jax.sharding import PartitionSpec as P

BF = jnp.bfloat16
F32 = jnp.float32
NN = (((1,), (0,)), ((), ()))
NT = (((1,), (1,)), ((), ()))
TN = (((0,), (0,)), ((), ()))
ROOM = 56 * 1024 * 1024
LIGHT = pl.CostEstimate(flops=1, bytes_accessed=1, transcendentals=0)
SMEM = pl.BlockSpec(memory_space=pltpu.SMEM)
ANYWHERE = pl.BlockSpec(memory_space=pl.ANY)
INSIDE = pl.BlockSpec(memory_space=pltpu.VMEM)
PIECES = 8


def mm(a, b, dims=NN):
    return lax.dot_general(a, b, dims, preferred_element_type=F32)


def after(value, *earlier):
    return lax.optimization_barrier((value,) + earlier)[0]


def params():
    return pltpu.CompilerParams(vmem_limit_bytes=ROOM)


LIGHT = pl.CostEstimate(flops=1, bytes_accessed=1, transcendentals=0)


def struct(*shape, dtype=BF):
    return jax.ShapeDtypeStruct(shape, dtype)


def whole(array):
    return pl.BlockSpec(array.shape, lambda *_: (0,) * len(array.shape))


def stack_rows(refs, scratch):
    rows = refs[0].shape[0]
    for i, ref in enumerate(refs):
        scratch[i * rows : (i + 1) * rows, :] = ref[...]


def fetch(order_ref, blocks, w_ref, sems):
    deep = blocks[0].shape[0]
    copies = []
    for j, block in enumerate(blocks):
        place = pl.multiple_of(order_ref[j] * deep, deep)
        copies.append(pltpu.make_async_copy(block, w_ref.at[pl.ds(place, deep)], sems.at[j]))
        copies[-1].start()
    return copies


def down_scratch(blocks):
    deep, width = blocks[0].shape
    return [pltpu.VMEM((len(blocks) * deep, width), BF), pltpu.SemaphoreType.DMA((len(blocks),))]


def fetch_each(blocks, w_ref, sems):
    copies = []
    for j, block in enumerate(blocks):
        copies.append(pltpu.make_async_copy(block, w_ref.at[j], sems.at[j]))
        copies[-1].start()
    return copies


def each_scratch(blocks):
    return [
        pltpu.VMEM((len(blocks),) + blocks[0].shape, BF),
        pltpu.SemaphoreType.DMA((len(blocks),)),
    ]


def activations(x, blocks):
    rows = x.shape[0]
    depth, width = blocks[0].shape
    half = width // 2
    m = len(blocks)

    def body(x_ref, *refs):
        ins, (hid_ref, fg_ref, fu_ref, acc, w_ref, sems) = refs[:m], refs[m:]
        copies = fetch_each(ins, w_ref, sems)
        for j, copy in enumerate(copies):
            copy.wait()
            found = mm(x_ref[:, j * depth : (j + 1) * depth], w_ref[j])
            if j == 0:
                acc[...] = found
            else:
                acc[...] += found
        g = acc[:, :half]
        u = acc[:, half:]
        s = jax.nn.sigmoid(g)
        hid_ref[...] = (g * s * u).astype(BF)
        fg_ref[...] = u * s * (1.0 + g * (1.0 - s))
        fu_ref[...] = g * s

    factor = struct(rows, half, dtype=F32)
    return pl.pallas_call(
        body,
        in_specs=[INSIDE] + [ANYWHERE] * m,
        out_specs=[INSIDE] * 3,
        out_shape=[struct(rows, half), factor, factor],
        scratch_shapes=[pltpu.VMEM((rows, width), F32)] + each_scratch(blocks),
        compiler_params=params(),
        cost_estimate=LIGHT,
        name="activations",
    )(x, *blocks)


def middle(order, hidden, f_gate, f_up, rows_s, blocks):
    rows, half = hidden.shape
    wide = rows_s.shape[1]
    m = len(blocks)
    step = 512 if wide % 512 == 0 else wide

    def body(order_ref, hid_ref, fg_ref, fu_ref, s_ref, *refs):
        down, (out_ref, d_ref, w_ref, sems) = refs[:m], refs[m:]
        for copy in fetch(order_ref, down, w_ref, sems):
            copy.wait()
        d_hidden = mm(s_ref[...], w_ref[...], NT)
        d_ref[:, :half] = (d_hidden * fg_ref[...]).astype(BF)
        d_ref[:, half:] = (d_hidden * fu_ref[...]).astype(BF)
        for c in range(0, wide, step):
            out_ref[:, c : c + step] = mm(hid_ref[...], w_ref[:, c : c + step]).astype(BF)

    return pl.pallas_call(
        body,
        in_specs=[SMEM] + [INSIDE] * 4 + [ANYWHERE] * m,
        out_specs=[INSIDE] * 2,
        out_shape=[struct(rows, wide), struct(rows, 2 * half)],
        scratch_shapes=down_scratch(blocks),
        compiler_params=params(),
        cost_estimate=LIGHT,
        name="middle",
    )(order, hidden, f_gate, f_up, rows_s, *blocks)


def row_grads(d_act, blocks):
    rows, width = d_act.shape
    depth = blocks[0].shape[0]
    m = len(blocks)

    def body(d_ref, *refs):
        ins, (out_ref, w_ref, sems) = refs[:m], refs[m:]
        copies = fetch_each(ins, w_ref, sems)
        for j, copy in enumerate(copies):
            copy.wait()
            out_ref[:, j * depth : (j + 1) * depth] = mm(d_ref[...], w_ref[j], NT).astype(BF)

    return pl.pallas_call(
        body,
        in_specs=[INSIDE] + [ANYWHERE] * m,
        out_specs=INSIDE,
        out_shape=struct(rows, m * depth),
        scratch_shapes=each_scratch(blocks),
        compiler_params=params(),
        cost_estimate=LIGHT,
        name="row_grads",
    )(d_act, *blocks)


def gate_up_grads(xs, ds, k, wide, scale, received):
    n, rows, width = len(xs), xs[0].shape[0], ds[0].shape[1]
    step = 512 if width % 512 == 0 else width
    extra = [] if received is None else [received]
    if wide % 128 != 0:
        xs, k = [x[:, k * wide : (k + 1) * wide] for x in xs], 0

    def body(*refs):
        x_refs, d_refs, rest = refs[:n], refs[n : 2 * n], refs[2 * n :]
        out_ref, x_scr, d_scr = rest[-3:]

        @pl.when(pl.program_id(0) == 0)
        def _():
            stack_rows(x_refs, x_scr)

        stack_rows(d_refs, d_scr)
        found = mm(x_scr[...], d_scr[...], TN) * scale
        if extra:
            found = found + rest[0][...].astype(F32)
        out_ref[...] = found.astype(BF)

    shape = struct(wide, width)
    column = lambda i: (0, i)
    return pl.pallas_call(
        body,
        grid=(width // step,),
        in_specs=[pl.BlockSpec((rows, wide), lambda i: (0, k))] * n
        + [pl.BlockSpec((rows, step), column)] * n
        + [pl.BlockSpec((wide, step), column)] * len(extra),
        out_specs=pl.BlockSpec((wide, step), column),
        out_shape=shape,
        scratch_shapes=[pltpu.VMEM((n * rows, wide), BF), pltpu.VMEM((n * rows, step), BF)],
        compiler_params=params(),
        cost_estimate=LIGHT,
        name="gate_up_grads",
    )(*xs, *ds, *extra)


def down_grads(order, hidden, rows_s, count, scale):
    rows, half = hidden.shape
    wide = rows_s.shape[1]
    deep = half // count
    step = 512 if wide % 512 == 0 else wide

    def body(order_ref, h_ref, s_ref, *refs):
        outs, scratch = refs[:count], refs[count]
        scratch[...] = mm(h_ref[...], s_ref[...], TN) * scale
        for j in range(count):
            place = pl.multiple_of(order_ref[j] * deep, deep)
            outs[j][...] = scratch[pl.ds(place, deep), :].astype(BF)

    shapes = [struct(deep, wide)] * count
    return pl.pallas_call(
        body,
        grid=(wide // step,),
        in_specs=[SMEM, whole(hidden), pl.BlockSpec((rows, step), lambda i: (0, i))],
        out_specs=[pl.BlockSpec((deep, step), lambda i: (0, i))] * count,
        out_shape=shapes,
        scratch_shapes=[pltpu.VMEM((half, step), F32)],
        compiler_params=params(),
        cost_estimate=LIGHT,
        name="down_grads",
    )(order, hidden, rows_s)


def popular_partials(select, packed, weights, hid):
    parts, count = select.shape[:2]
    narrow = packed.shape[1] // (2 * parts)
    columns = sum(w.shape[0] for w in weights)

    def body(sel_ref, in_ref, *refs):
        w_refs, (x_ref, s_ref, p_ref) = refs[: len(weights)], refs[len(weights) :]
        x = None
        s = None
        for q in range(parts):
            rows = mm(sel_ref[q], in_ref[...])
            one = rows[:, q * narrow : (q + 1) * narrow]
            two = rows[:, (parts + q) * narrow : (parts + q + 1) * narrow]
            x = one if x is None else x + one
            s = two if s is None else s + two
        x = x.astype(BF)
        s = s.astype(BF)
        x_ref[...] = x
        s_ref[...] = s
        at = 0
        for w_ref in w_refs:
            for top in range(0, w_ref.shape[0], 3 * hid):
                p_ref[:, at : at + 2 * hid] = mm(x, w_ref[top : top + 2 * hid, :], NT).astype(BF)
                p_ref[:, at + 2 * hid : at + 3 * hid] = mm(
                    s, w_ref[top + 2 * hid : top + 3 * hid, :], NT
                ).astype(BF)
                at += 3 * hid

    return pl.pallas_call(
        body,
        in_specs=[INSIDE] * (2 + len(weights)),
        out_specs=[INSIDE] * 3,
        out_shape=[
            struct(count, narrow),
            struct(count, narrow),
            struct(count, columns),
        ],
        compiler_params=params(),
        cost_estimate=LIGHT,
        name="popular_partials",
    )(select, packed, *weights)


def popular_middle(own, others, hid):
    rows, columns = own.shape

    def body(own_ref, *refs):
        parts, out_ref = refs[:-1], refs[-1]
        act = own_ref[...].astype(F32)
        for part in parts:
            act = act + part[...].astype(F32)
        for at in range(0, columns, 3 * hid):
            g = act[:, at : at + hid]
            u = act[:, at + hid : at + 2 * hid]
            dh = act[:, at + 2 * hid : at + 3 * hid]
            s = jax.nn.sigmoid(g)
            out_ref[:, at : at + hid] = (dh * u * s * (1.0 + g * (1.0 - s))).astype(BF)
            out_ref[:, at + hid : at + 2 * hid] = (dh * g * s).astype(BF)
            out_ref[:, at + 2 * hid : at + 3 * hid] = (g * s * u).astype(BF)

    return pl.pallas_call(
        body,
        in_specs=[INSIDE] * (1 + len(others)),
        out_specs=INSIDE,
        out_shape=struct(rows, columns),
        compiler_params=params(),
        cost_estimate=LIGHT,
        name="popular_middle",
    )(own, *others)


def popular_back(select, lines, x, s, weights, hid, scale):
    parts, count, spots = select.shape
    narrow = x.shape[1]
    m = len(weights)
    n = len(lines)
    columns = lines[0].shape[1]

    def body(sel_ref, x_ref, s_ref, *refs):
        ins, w_refs, back_ref = refs[:n], refs[n : n + m], refs[n + m]
        grads, mid_ref = refs[n + m + 1 : -1], refs[-1]
        stack_rows(ins, mid_ref)
        grad = None
        out = None
        at = 0
        for w_ref, g_ref in zip(w_refs, grads):
            for top in range(0, w_ref.shape[0], 3 * hid):
                d_gate = mid_ref[:, at : at + hid]
                d_up = mid_ref[:, at + hid : at + 2 * hid]
                hidden = mid_ref[:, at + 2 * hid : at + 3 * hid]
                sides = ((d_gate, x_ref), (d_up, x_ref), (hidden, s_ref))
                for i, (left, right) in enumerate(sides):
                    here = slice(top + i * hid, top + (i + 1) * hid)
                    product = mm(left, w_ref[here, :])
                    if i == 2:
                        out = product if out is None else out + product
                    else:
                        grad = product if grad is None else grad + product
                    g_ref[here, :] = (mm(left, right[...], TN) * scale).astype(BF)
                at += 3 * hid
        grad = grad.astype(BF)
        out = out.astype(BF)
        for q in range(parts):
            back_ref[:, q * narrow : (q + 1) * narrow] = mm(sel_ref[q], grad, TN).astype(BF)
            back_ref[:, (parts + q) * narrow : (parts + q + 1) * narrow] = mm(
                sel_ref[q], out, TN
            ).astype(BF)

    return pl.pallas_call(
        body,
        in_specs=[INSIDE] * (3 + n + m),
        out_specs=[INSIDE] * (1 + m),
        out_shape=[struct(spots, 2 * parts * narrow)]
        + [struct(w.shape[0], narrow) for w in weights],
        scratch_shapes=[pltpu.VMEM((count, columns), BF)],
        compiler_params=params(),
        cost_estimate=LIGHT,
        name="popular_back",
    )(select, x, s, *lines, *weights)


def slot_positions(route_block, count):
    flat = route_block.reshape(-1)
    onehot = (flat[:, None] == jnp.arange(count, dtype=jnp.int32)[None, :]).astype(jnp.int32)
    before = jnp.cumsum(onehot, axis=0) - onehot
    return (flat, jnp.sum(before * onehot, axis=1))


def exchange(blocks):
    return lax.all_to_all(blocks, "expert", split_axis=0, concat_axis=0, tiled=True)


def local(
    tokens, cotangent, routes, gates, hot_index, hot_gate, w_gate_up, w_down, w_hot_gu, w_hot_dn
):
    owners = lax.axis_size("expert")
    groups = lax.axis_size("dp")
    cores = 2 if groups % 2 == 0 else 1
    chips = groups // cores
    tok_dev, width_d = tokens.shape
    topk = routes.shape[1]
    slots = max(2, 3 * tok_dev * topk // (2 * owners))
    entries = tok_dev * topk
    rows = owners * slots
    inverse = 1.0 / (4 * groups)
    me = lax.axis_index("dp")
    chip, core = me // cores, me % cores

    def shift(value, r):
        pairs = [
            (i, ((i // cores + r) % chips) * cores + i % cores) for i in range(groups)
        ]
        return lax.ppermute(value, "dp", pairs)

    def swap(value):
        pairs = [(i, (i // cores) * cores + (i + 1) % cores) for i in range(groups)]
        return lax.ppermute(value, "dp", pairs)

    order = jnp.stack(
        [
            ((chip - r) % chips) * cores + (core + k) % cores
            for k in range(cores)
            for r in range(chips)
        ]
    ).astype(jnp.int32)

    across = 1
    while 2 * (2 * across) ** 2 <= owners:
        across *= 2
    depths = owners // across
    spot = lax.axis_index("expert")

    def hop(value, j):
        return lax.ppermute(value, "expert", [(i, i ^ j) for i in range(owners)])

    wide = width_d // groups
    hid = w_hot_dn.shape[0]
    narrow = width_d // owners
    hot_w = jnp.concatenate([w_hot_gu, w_hot_dn[None]], axis=0).reshape(3 * hid, narrow)
    hot_near = [hot_w] + [shift(hot_w, r) for r in range(1, chips)]
    down_own = after(w_down[0], hot_near[-1])
    gu_near = [w_gate_up[0]] + [shift(w_gate_up[0], r) for r in range(1, chips)]
    down_near = [w_down[0]] + [shift(down_own, r) for r in range(1, chips)]
    gu_far = [swap(w_gate_up[0])] if cores == 2 else []
    down_far = [swap(w_down[0])] if cores == 2 else []

    flat, pos = slot_positions(routes, owners)
    dest = flat * slots + pos
    slot_ids = jnp.arange(rows, dtype=jnp.int32)[:, None]
    pick = (slot_ids == dest[None, :]).astype(BF)

    def as_rows(value, width):
        value = value.reshape(owners, -1)
        spare = -value.shape[1] % width
        return jnp.pad(value, ((0, 0), (0, spare))).reshape(owners, -1, width)

    hot_dev = hot_index.shape[0]
    few = 2 * hot_dev // PIECES
    hot_pick = (
        hot_index[:, None] == jnp.arange(tok_dev, dtype=jnp.int32)[None, :]
    ).astype(BF)
    hot_x = mm(hot_pick, tokens).astype(BF)
    hot_s = (hot_gate[:, None] * mm(hot_pick, cotangent)).astype(BF)
    hot_send = jnp.concatenate([hot_x, hot_s], axis=0).reshape(PIECES, few, owners, narrow)
    hot_send = hot_send.transpose(2, 1, 0, 3).reshape(owners * few, PIECES * narrow)
    packed_id = jnp.arange(owners * few, dtype=jnp.int32)
    turn = ((packed_id ^ (spot * few))[:, None] == packed_id[None, :]).astype(BF)
    row = jnp.arange(owners * hot_dev, dtype=jnp.int32)
    step = row // hot_dev
    piece = (row % hot_dev) // few

    def selection(index):
        hit = (index * few + row % few)[:, None] == packed_id[None, :]
        return jnp.stack([hit & (piece == q)[:, None] for q in range(PIECES // 2)]).astype(BF)

    hot_send = mm(turn, hot_send).astype(BF).reshape(depths, across, few, PIECES * narrow)
    near = [hot_send[0]] + [hop(hot_send[j], j * across) for j in range(1, depths)]
    near = jnp.stack(near, axis=1)
    hot_recv = jnp.concatenate([near[0]] + [hop(near[j], j) for j in range(1, across)])
    hot_recv = hot_recv.reshape(owners * few, PIECES * narrow)

    scaled = (gates[:, :, None] * cotangent[:, None, :].astype(F32)).astype(BF)
    send_s = mm(pick, scaled.reshape(entries, width_d)).astype(BF)
    rows_s = exchange(send_s.reshape(owners, slots, width_d)).reshape(rows, width_d)

    tok_rel = jnp.concatenate(
        [
            lax.dynamic_slice_in_dim(tokens, order[j] * wide, wide, 1)
            for j in range(groups)
        ],
        axis=1,
    )
    tok_rel = jnp.repeat(tok_rel, topk, axis=0) if topk > 1 else tok_rel
    send_x = mm(pick, tok_rel).astype(BF).reshape(owners, slots, width_d)
    rows_x = exchange(send_x).reshape(rows, width_d)

    hot_near = jnp.concatenate(list(after(tuple(hot_near), send_x, *gu_far, *down_far)), axis=0)
    hot_ws = [hot_near] + ([swap(hot_near)] if cores == 2 else [])
    hot_x, hot_s, partial = popular_partials(selection(step), hot_recv, hot_ws, hid)
    share = depths * hot_dev
    level_in = [hop(partial[j * share : (j + 1) * share], j) for j in range(1, across)]
    if cores == 2:
        gu_far = gu_far + [swap(block) for block in gu_near[1:]]
    gu_blocks = gu_near + gu_far
    hidden, f_gate, f_up = activations(rows_x, gu_blocks)
    level_in = list(after(tuple(level_in), hidden))
    level = partial[:share].astype(F32)
    for value in level_in:
        level = level + value.astype(F32)
    level = level.astype(BF)
    level = [level[j * hot_dev : (j + 1) * hot_dev] for j in range(depths)]
    depth_in = [hop(level[j], j * across) for j in range(1, depths)]
    down_near = list(after(tuple(down_near), hidden))
    if cores == 2:
        down_far = down_far + [swap(block) for block in down_near[1:]]
    down_blocks = down_near + down_far
    out, d_act = middle(order, hidden, f_gate, f_up, rows_s, down_blocks)

    def columns_of(r):
        return jnp.concatenate(
            [
                rows_x[:, (k * chips + r) * wide : (k * chips + r + 1) * wide]
                for k in range(cores)
            ],
            axis=1,
        )

    xs = [columns_of(0)] + [shift(columns_of(r), -r) for r in range(1, chips)]
    ds = [d_act] + [shift(d_act, -r) for r in range(1, chips)]
    d_rows = row_grads(d_act, gu_blocks)
    back_out = exchange(out.reshape(owners, slots, width_d)).reshape(rows, width_d)
    d_rows = after(d_rows, xs[-1], ds[-1])
    back_rows = exchange(d_rows.reshape(owners, slots, width_d)).reshape(rows, width_d)

    depth_in = list(after(tuple(depth_in), d_act))
    hot_own = popular_middle(level[0], depth_in, hid)
    line = [hot_own] + [hop(hot_own, j * across) for j in range(1, depths)]
    line = jnp.concatenate(list(after(tuple(line), d_act)))
    lines = [line] + [hop(line, j) for j in range(1, across)]
    lines = list(after(tuple(lines), d_rows))
    hot_back, *hot_grads = popular_back(
        selection(step), lines, hot_x, hot_s, hot_ws, hid, inverse
    )

    dn_parts = down_grads(order, after(hidden, d_rows), rows_s, groups, inverse)
    dn_sum = list(dn_parts[:chips])
    if cores == 2:
        dn_in = [swap(part) for part in dn_parts[chips:]]
        dn_sum = [
            (one.astype(F32) + two.astype(F32)).astype(BF) for one, two in zip(dn_sum, dn_in)
        ]
    dn_total = dn_sum[0].astype(F32)
    dn_recv = [shift(dn_sum[r], -r) for r in range(1, chips)]
    for value in dn_recv:
        dn_total = dn_total + value.astype(F32)
    grad_dn = dn_total.astype(BF)

    hot_back = hot_back.reshape(across, depths, few, PIECES * narrow)
    hot_back = [hot_back[0]] + [hop(hot_back[j], j) for j in range(1, across)]
    hot_back = jnp.stack(hot_back, axis=1)
    hot_back = [hot_back[0]] + [hop(hot_back[j], j * across) for j in range(1, depths)]
    hot_back = jnp.concatenate(hot_back).reshape(owners * few, PIECES * narrow)
    hot_back = mm(turn, hot_back).astype(BF)

    xs_late = list(after(tuple(xs), d_rows))
    gu_in = None
    if cores == 2:
        gu_in = swap(gate_up_grads(xs_late, ds, 1, wide, inverse, None))

    hot_sum = hot_grads[0]
    if cores == 2:
        hot_sum = (hot_sum.astype(F32) + swap(hot_grads[1]).astype(F32)).astype(BF)
    hot_sum = hot_sum.reshape(chips, 3 * hid, narrow)
    hot_total = hot_sum[0].astype(F32)
    hot_far = [shift(hot_sum[r], -r) for r in range(1, chips)]
    for value in hot_far:
        hot_total = hot_total + value.astype(F32)
    grad_hot = hot_total.astype(BF).reshape(3, hid, narrow)
    xs_last = list(after(tuple(xs_late), *hot_far, *dn_recv))
    grad_gu = gate_up_grads(xs_last, ds, 0, wide, inverse, gu_in)

    hot_back = hot_back.reshape(owners, few, PIECES, narrow)
    hot_back = hot_back.transpose(2, 1, 0, 3).reshape(2, hot_dev, width_d)
    picked = mm(pick, back_out, TN)
    layer_out = (
        (gates.reshape(entries)[:, None] * picked).reshape(tok_dev, topk, width_d).sum(axis=1)
    )
    token_gate = jnp.sum(jnp.where(hot_pick > 0, hot_gate[:, None], 0.0), axis=0)
    layer_out = layer_out + token_gate[:, None] * mm(hot_pick, hot_back[1], TN)
    returned = mm(pick, back_rows, TN)
    returned = returned.reshape(tok_dev, topk, width_d).sum(axis=1)
    blocks = jnp.stack([returned[:, j * wide : (j + 1) * wide] for j in range(groups)])
    input_grad = jnp.concatenate(
        [
            lax.dynamic_index_in_dim(
                blocks,
                ((q - core) % cores) * chips + (chip - p) % chips,
                0,
                keepdims=False,
            )
            for p in range(chips)
            for q in range(cores)
        ],
        axis=1,
    )
    input_grad = input_grad + mm(hot_pick, hot_back[0], TN)
    return (
        layer_out.astype(BF),
        input_grad.astype(BF),
        grad_gu[None],
        grad_dn[None],
        grad_hot[:2],
        grad_hot[2],
    )


def solution(mesh):
    tok = P(("dp", "expert"), None)
    flat = P(("dp", "expert"))
    rows = P("expert", "dp", None)
    hot = (P(None, "dp", "expert"), P("dp", "expert"))
    return jax.shard_map(
        local,
        mesh=mesh,
        in_specs=(tok, tok, tok, tok, flat, flat, rows, rows) + hot,
        out_specs=(tok, tok, rows, rows) + hot,
        check_vma=False,
    )
```

```python
import jax
import jax.numpy as jnp
from jax import lax
from jax.experimental import pallas as pl
from jax.experimental.pallas import tpu as pltpu
from jax.sharding import PartitionSpec as P

BF = jnp.bfloat16
F32 = jnp.float32
NN = (((1,), (0,)), ((), ()))
NT = (((1,), (1,)), ((), ()))
TN = (((0,), (0,)), ((), ()))
ROOM = 56 * 1024 * 1024
LIGHT = pl.CostEstimate(flops=1, bytes_accessed=1, transcendentals=0)
SMEM = pl.BlockSpec(memory_space=pltpu.SMEM)
ANYWHERE = pl.BlockSpec(memory_space=pl.ANY)
INSIDE = pl.BlockSpec(memory_space=pltpu.VMEM)
PIECES = 8


def mm(a, b, dims=NN):
    return lax.dot_general(a, b, dims, preferred_element_type=F32)


def after(value, *earlier):
    return lax.optimization_barrier((value,) + earlier)[0]


def params():
    return pltpu.CompilerParams(vmem_limit_bytes=ROOM)


LIGHT = pl.CostEstimate(flops=1, bytes_accessed=1, transcendentals=0)


def struct(*shape, dtype=BF):
    return jax.ShapeDtypeStruct(shape, dtype)


def whole(array):
    return pl.BlockSpec(array.shape, lambda *_: (0,) * len(array.shape))


def stack_rows(refs, scratch):
    rows = refs[0].shape[0]
    for i, ref in enumerate(refs):
        scratch[i * rows : (i + 1) * rows, :] = ref[...]


def fetch(order_ref, blocks, w_ref, sems):
    deep = blocks[0].shape[0]
    copies = []
    for j, block in enumerate(blocks):
        place = pl.multiple_of(order_ref[j] * deep, deep)
        copies.append(pltpu.make_async_copy(block, w_ref.at[pl.ds(place, deep)], sems.at[j]))
        copies[-1].start()
    return copies


def down_scratch(blocks):
    deep, width = blocks[0].shape
    return [pltpu.VMEM((len(blocks) * deep, width), BF), pltpu.SemaphoreType.DMA((len(blocks),))]


def fetch_each(blocks, w_ref, sems):
    copies = []
    for j, block in enumerate(blocks):
        copies.append(pltpu.make_async_copy(block, w_ref.at[j], sems.at[j]))
        copies[-1].start()
    return copies


def each_scratch(blocks):
    return [
        pltpu.VMEM((len(blocks),) + blocks[0].shape, BF),
        pltpu.SemaphoreType.DMA((len(blocks),)),
    ]


def expert(order, received, w_gu, w_down):
    rows = received.shape[0]
    depth, width = w_gu[0].shape
    deep, wide = w_down[0].shape
    half = width // 2
    m = len(w_gu)
    step = 512 if wide % 512 == 0 else wide

    def body(order_ref, in_ref, *refs):
        gu_in, dn_in, rest = refs[:m], refs[m : 2 * m], refs[2 * m :]
        back_ref, hid_ref, d_ref, acc, gu_ref, gu_sems, dn_ref, dn_sems = rest
        gu_copies = fetch_each(gu_in, gu_ref, gu_sems)
        dn_copies = fetch(order_ref, dn_in, dn_ref, dn_sems)
        for j, copy in enumerate(gu_copies):
            copy.wait()
            found = mm(in_ref[:, wide + j * depth : wide + (j + 1) * depth], gu_ref[j])
            if j == 0:
                acc[...] = found
            else:
                acc[...] += found
        g = acc[:, :half]
        u = acc[:, half:]
        s = jax.nn.sigmoid(g)
        hid_ref[...] = (g * s * u).astype(BF)
        for copy in dn_copies:
            copy.wait()
        d_hidden = mm(in_ref[:, :wide], dn_ref[...], NT)
        d_ref[:, :half] = (d_hidden * u * s * (1.0 + g * (1.0 - s))).astype(BF)
        d_ref[:, half:] = (d_hidden * g * s).astype(BF)
        for j in range(m):
            at = wide + j * depth
            back_ref[:, at : at + depth] = mm(d_ref[...], gu_ref[j], NT).astype(BF)
        for c in range(0, wide, step):
            back_ref[:, c : c + step] = mm(hid_ref[...], dn_ref[:, c : c + step]).astype(BF)

    return pl.pallas_call(
        body,
        in_specs=[SMEM, INSIDE] + [ANYWHERE] * (2 * m),
        out_specs=[INSIDE] * 3,
        out_shape=[struct(rows, 2 * wide), struct(rows, half), struct(rows, width)],
        scratch_shapes=[pltpu.VMEM((rows, width), F32)]
        + each_scratch(w_gu)
        + down_scratch(w_down),
        compiler_params=params(),
        cost_estimate=LIGHT,
        name="expert",
    )(order, received, *w_gu, *w_down)


def gate_up_grads(xs, ds, k, wide, scale, received):
    n, rows, width = len(xs), xs[0].shape[0], ds[0].shape[1]
    step = 512 if width % 512 == 0 else width
    extra = [] if received is None else [received]
    if wide % 128 != 0:
        xs, k = [x[:, k * wide : (k + 1) * wide] for x in xs], 0

    def body(*refs):
        x_refs, d_refs, rest = refs[:n], refs[n : 2 * n], refs[2 * n :]
        out_ref, x_scr, d_scr = rest[-3:]

        @pl.when(pl.program_id(0) == 0)
        def _():
            stack_rows(x_refs, x_scr)

        stack_rows(d_refs, d_scr)
        found = mm(x_scr[...], d_scr[...], TN) * scale
        if extra:
            found = found + rest[0][...].astype(F32)
        out_ref[...] = found.astype(BF)

    shape = struct(wide, width)
    column = lambda i: (0, i)
    return pl.pallas_call(
        body,
        grid=(width // step,),
        in_specs=[pl.BlockSpec((rows, wide), lambda i: (0, k))] * n
        + [pl.BlockSpec((rows, step), column)] * n
        + [pl.BlockSpec((wide, step), column)] * len(extra),
        out_specs=pl.BlockSpec((wide, step), column),
        out_shape=shape,
        scratch_shapes=[pltpu.VMEM((n * rows, wide), BF), pltpu.VMEM((n * rows, step), BF)],
        compiler_params=params(),
        cost_estimate=LIGHT,
        name="gate_up_grads",
    )(*xs, *ds, *extra)


def down_grads(order, hidden, rows_s, wide, count, scale):
    rows, half = hidden.shape
    deep = half // count
    step = 512 if wide % 512 == 0 else wide

    def body(order_ref, h_ref, s_ref, *refs):
        outs, scratch = refs[:count], refs[count]
        scratch[...] = mm(h_ref[...], s_ref[...], TN) * scale
        for j in range(count):
            place = pl.multiple_of(order_ref[j] * deep, deep)
            outs[j][...] = scratch[pl.ds(place, deep), :].astype(BF)

    shapes = [struct(deep, wide)] * count
    return pl.pallas_call(
        body,
        grid=(wide // step,),
        in_specs=[SMEM, whole(hidden), pl.BlockSpec((rows, step), lambda i: (0, i))],
        out_specs=[pl.BlockSpec((deep, step), lambda i: (0, i))] * count,
        out_shape=shapes,
        scratch_shapes=[pltpu.VMEM((half, step), F32)],
        compiler_params=params(),
        cost_estimate=LIGHT,
        name="down_grads",
    )(order, hidden, rows_s)


def popular_partials(select, packed, weights, hid):
    parts, count = select.shape[:2]
    narrow = packed.shape[1] // (2 * parts)
    columns = sum(w.shape[0] for w in weights)

    def body(sel_ref, in_ref, *refs):
        w_refs, (x_ref, s_ref, p_ref) = refs[: len(weights)], refs[len(weights) :]
        x = None
        s = None
        for q in range(parts):
            rows = mm(sel_ref[q], in_ref[...])
            one = rows[:, q * narrow : (q + 1) * narrow]
            two = rows[:, (parts + q) * narrow : (parts + q + 1) * narrow]
            x = one if x is None else x + one
            s = two if s is None else s + two
        x = x.astype(BF)
        s = s.astype(BF)
        x_ref[...] = x
        s_ref[...] = s
        at = 0
        for w_ref in w_refs:
            for top in range(0, w_ref.shape[0], 3 * hid):
                p_ref[:, at : at + 2 * hid] = mm(x, w_ref[top : top + 2 * hid, :], NT).astype(BF)
                p_ref[:, at + 2 * hid : at + 3 * hid] = mm(
                    s, w_ref[top + 2 * hid : top + 3 * hid, :], NT
                ).astype(BF)
                at += 3 * hid

    return pl.pallas_call(
        body,
        in_specs=[INSIDE] * (2 + len(weights)),
        out_specs=[INSIDE] * 3,
        out_shape=[
            struct(count, narrow),
            struct(count, narrow),
            struct(count, columns),
        ],
        compiler_params=params(),
        cost_estimate=LIGHT,
        name="popular_partials",
    )(select, packed, *weights)


def popular_middle(own, others, hid):
    rows, columns = own.shape

    def body(own_ref, *refs):
        parts, out_ref = refs[:-1], refs[-1]
        act = own_ref[...].astype(F32)
        for part in parts:
            act = act + part[...].astype(F32)
        for at in range(0, columns, 3 * hid):
            g = act[:, at : at + hid]
            u = act[:, at + hid : at + 2 * hid]
            dh = act[:, at + 2 * hid : at + 3 * hid]
            s = jax.nn.sigmoid(g)
            out_ref[:, at : at + hid] = (dh * u * s * (1.0 + g * (1.0 - s))).astype(BF)
            out_ref[:, at + hid : at + 2 * hid] = (dh * g * s).astype(BF)
            out_ref[:, at + 2 * hid : at + 3 * hid] = (g * s * u).astype(BF)

    return pl.pallas_call(
        body,
        in_specs=[INSIDE] * (1 + len(others)),
        out_specs=INSIDE,
        out_shape=struct(rows, columns),
        compiler_params=params(),
        cost_estimate=LIGHT,
        name="popular_middle",
    )(own, *others)


def popular_back(select, lines, x, s, weights, hid, scale):
    parts, count, spots = select.shape
    narrow = x.shape[1]
    m = len(weights)
    n = len(lines)
    columns = lines[0].shape[1]

    def body(sel_ref, x_ref, s_ref, *refs):
        ins, w_refs, back_ref = refs[:n], refs[n : n + m], refs[n + m]
        grads, mid_ref = refs[n + m + 1 : -1], refs[-1]
        stack_rows(ins, mid_ref)
        grad = None
        out = None
        at = 0
        for w_ref, g_ref in zip(w_refs, grads):
            for top in range(0, w_ref.shape[0], 3 * hid):
                d_gate = mid_ref[:, at : at + hid]
                d_up = mid_ref[:, at + hid : at + 2 * hid]
                hidden = mid_ref[:, at + 2 * hid : at + 3 * hid]
                sides = ((d_gate, x_ref), (d_up, x_ref), (hidden, s_ref))
                for i, (left, right) in enumerate(sides):
                    here = slice(top + i * hid, top + (i + 1) * hid)
                    product = mm(left, w_ref[here, :])
                    if i == 2:
                        out = product if out is None else out + product
                    else:
                        grad = product if grad is None else grad + product
                    g_ref[here, :] = (mm(left, right[...], TN) * scale).astype(BF)
                at += 3 * hid
        grad = grad.astype(BF)
        out = out.astype(BF)
        for q in range(parts):
            back_ref[:, q * narrow : (q + 1) * narrow] = mm(sel_ref[q], grad, TN).astype(BF)
            back_ref[:, (parts + q) * narrow : (parts + q + 1) * narrow] = mm(
                sel_ref[q], out, TN
            ).astype(BF)

    return pl.pallas_call(
        body,
        in_specs=[INSIDE] * (3 + n + m),
        out_specs=[INSIDE] * (1 + m),
        out_shape=[struct(spots, 2 * parts * narrow)]
        + [struct(w.shape[0], narrow) for w in weights],
        scratch_shapes=[pltpu.VMEM((count, columns), BF)],
        compiler_params=params(),
        cost_estimate=LIGHT,
        name="popular_back",
    )(select, x, s, *lines, *weights)


def slot_positions(route_block, count):
    flat = route_block.reshape(-1)
    onehot = (flat[:, None] == jnp.arange(count, dtype=jnp.int32)[None, :]).astype(jnp.int32)
    before = jnp.cumsum(onehot, axis=0) - onehot
    return (flat, jnp.sum(before * onehot, axis=1))


def exchange(blocks):
    return lax.all_to_all(blocks, "expert", split_axis=0, concat_axis=0, tiled=True)


def local(
    tokens, cotangent, routes, gates, hot_index, hot_gate, w_gate_up, w_down, w_hot_gu, w_hot_dn
):
    owners = lax.axis_size("expert")
    groups = lax.axis_size("dp")
    cores = 2 if groups % 2 == 0 else 1
    chips = groups // cores
    tok_dev, width_d = tokens.shape
    topk = routes.shape[1]
    slots = max(2, 3 * tok_dev * topk // (2 * owners))
    entries = tok_dev * topk
    rows = owners * slots
    inverse = 1.0 / (4 * groups)
    me = lax.axis_index("dp")
    chip, core = me // cores, me % cores

    def shift(value, r):
        pairs = [
            (i, ((i // cores + r) % chips) * cores + i % cores) for i in range(groups)
        ]
        return lax.ppermute(value, "dp", pairs)

    def swap(value):
        pairs = [(i, (i // cores) * cores + (i + 1) % cores) for i in range(groups)]
        return lax.ppermute(value, "dp", pairs)

    order = jnp.stack(
        [
            ((chip - r) % chips) * cores + (core + k) % cores
            for k in range(cores)
            for r in range(chips)
        ]
    ).astype(jnp.int32)

    across = 1
    while 2 * (2 * across) ** 2 <= owners:
        across *= 2
    depths = owners // across
    spot = lax.axis_index("expert")

    def hop(value, j):
        return lax.ppermute(value, "expert", [(i, i ^ j) for i in range(owners)])

    wide = width_d // groups
    hid = w_hot_dn.shape[0]
    narrow = width_d // owners
    hot_w = jnp.concatenate([w_hot_gu, w_hot_dn[None]], axis=0).reshape(3 * hid, narrow)
    hot_near = [hot_w] + [shift(hot_w, r) for r in range(1, chips)]
    down_own = after(w_down[0], hot_near[-1])
    gu_near = [w_gate_up[0]] + [shift(w_gate_up[0], r) for r in range(1, chips)]
    down_near = [w_down[0]] + [shift(down_own, r) for r in range(1, chips)]
    gu_far = [swap(w_gate_up[0])] if cores == 2 else []
    down_far = [swap(w_down[0])] if cores == 2 else []

    flat, pos = slot_positions(routes, owners)
    dest = flat * slots + pos
    slot_ids = jnp.arange(rows, dtype=jnp.int32)[:, None]
    pick = (slot_ids == dest[None, :]).astype(BF)

    def as_rows(value, width):
        value = value.reshape(owners, -1)
        spare = -value.shape[1] % width
        return jnp.pad(value, ((0, 0), (0, spare))).reshape(owners, -1, width)

    hot_dev = hot_index.shape[0]
    few = 2 * hot_dev // PIECES
    hot_pick = (
        hot_index[:, None] == jnp.arange(tok_dev, dtype=jnp.int32)[None, :]
    ).astype(BF)
    hot_x = mm(hot_pick, tokens).astype(BF)
    hot_s = (hot_gate[:, None] * mm(hot_pick, cotangent)).astype(BF)
    hot_send = jnp.concatenate([hot_x, hot_s], axis=0).reshape(PIECES, few, owners, narrow)
    hot_send = hot_send.transpose(2, 1, 0, 3).reshape(owners * few, PIECES * narrow)
    packed_id = jnp.arange(owners * few, dtype=jnp.int32)
    turn = ((packed_id ^ (spot * few))[:, None] == packed_id[None, :]).astype(BF)
    row = jnp.arange(owners * hot_dev, dtype=jnp.int32)
    step = row // hot_dev
    source = spot ^ ((step % depths) * across + step // depths)
    piece = (row % hot_dev) // few

    def selection(index):
        hit = (index * few + row % few)[:, None] == packed_id[None, :]
        return jnp.stack([hit & (piece == q)[:, None] for q in range(PIECES // 2)]).astype(BF)

    scaled = (gates[:, :, None] * cotangent[:, None, :].astype(F32)).astype(BF)
    tok_rel = jnp.concatenate(
        [
            lax.dynamic_slice_in_dim(tokens, order[j] * wide, wide, 1)
            for j in range(groups)
        ],
        axis=1,
    )
    tok_rel = jnp.repeat(tok_rel, topk, axis=0) if topk > 1 else tok_rel
    both = jnp.concatenate([scaled.reshape(entries, width_d), tok_rel], axis=1)
    both = mm(pick, both).astype(BF).reshape(owners, slots, 2 * width_d)
    load = 2 * hot_dev * narrow
    extra = -(-load // (slots * 512)) * 512
    hot_send = jnp.pad(hot_send.reshape(owners, load), ((0, 0), (0, slots * extra - load)))
    send = jnp.concatenate([both, hot_send.reshape(owners, slots, extra)], axis=2)
    received = exchange(send)
    hot_recv = received[:, :, 2 * width_d :].reshape(owners, slots * extra)[:, :load]
    hot_recv = hot_recv.reshape(owners * few, PIECES * narrow)
    received = received.reshape(rows, 2 * width_d + extra)

    hot_near = jnp.concatenate(list(after(tuple(hot_near), send, *gu_far, *down_far)), axis=0)
    hot_ws = [hot_near] + ([swap(hot_near)] if cores == 2 else [])
    hot_x, hot_s, partial = popular_partials(selection(source), hot_recv, hot_ws, hid)
    share = depths * hot_dev
    level_in = [hop(partial[j * share : (j + 1) * share], j) for j in range(1, across)]
    if cores == 2:
        gu_far = gu_far + [swap(block) for block in gu_near[1:]]
        down_far = down_far + [swap(block) for block in down_near[1:]]
    level = partial[:share].astype(F32)
    for value in level_in:
        level = level + value.astype(F32)
    level = level.astype(BF)
    level = [level[j * hot_dev : (j + 1) * hot_dev] for j in range(depths)]
    depth_in = [hop(level[j], j * across) for j in range(1, depths)]
    hot_own = popular_middle(level[0], depth_in, hid)
    line = [hot_own] + [hop(hot_own, j * across) for j in range(1, depths)]
    work = after(received, hot_own)
    back, hidden, d_act = expert(order, work, gu_near + gu_far, down_near + down_far)

    def columns_of(r):
        return jnp.concatenate(
            [
                received[:, width_d + (k * chips + r) * wide : width_d + (k * chips + r + 1) * wide]
                for k in range(cores)
            ],
            axis=1,
        )

    xs = [columns_of(0)] + [shift(columns_of(r), -r) for r in range(1, chips)]
    ds = [d_act] + [shift(d_act, -r) for r in range(1, chips)]
    back = after(back, xs[-1], *line[1:])
    back = exchange(back.reshape(owners, slots, 2 * width_d)).reshape(rows, 2 * width_d)

    line = jnp.concatenate(list(after(tuple(line), d_act)))
    lines = [line] + [hop(line, j) for j in range(1, across)]
    lines = list(after(tuple(lines), ds[-1]))
    hot_back, *hot_grads = popular_back(
        selection(step), lines, hot_x, hot_s, hot_ws, hid, inverse
    )

    dn_parts = down_grads(order, hidden, received, width_d, groups, inverse)
    dn_sum = list(dn_parts[:chips])
    if cores == 2:
        dn_in = [swap(part) for part in dn_parts[chips:]]
        dn_sum = [
            (one.astype(F32) + two.astype(F32)).astype(BF) for one, two in zip(dn_sum, dn_in)
        ]
    dn_total = dn_sum[0].astype(F32)
    dn_recv = [shift(dn_sum[r], -r) for r in range(1, chips)]
    for value in dn_recv:
        dn_total = dn_total + value.astype(F32)
    grad_dn = dn_total.astype(BF)

    hot_back = hot_back.reshape(across, depths, few, PIECES * narrow)
    hot_back = [hot_back[0]] + [hop(hot_back[j], j) for j in range(1, across)]
    hot_back = jnp.stack(hot_back, axis=1)
    hot_back = [hot_back[0]] + [hop(hot_back[j], j * across) for j in range(1, depths)]
    hot_back = jnp.concatenate(hot_back).reshape(owners * few, PIECES * narrow)
    hot_back = mm(turn, hot_back).astype(BF)

    xs_late = list(after(tuple(xs), d_act))
    gu_in = None
    if cores == 2:
        gu_in = swap(gate_up_grads(xs_late, ds, 1, wide, inverse, None))

    hot_sum = hot_grads[0]
    if cores == 2:
        hot_sum = (hot_sum.astype(F32) + swap(hot_grads[1]).astype(F32)).astype(BF)
    hot_sum = hot_sum.reshape(chips, 3 * hid, narrow)
    hot_total = hot_sum[0].astype(F32)
    hot_far = [shift(hot_sum[r], -r) for r in range(1, chips)]
    for value in hot_far:
        hot_total = hot_total + value.astype(F32)
    grad_hot = hot_total.astype(BF).reshape(3, hid, narrow)
    xs_last = list(after(tuple(xs_late), *hot_far, *dn_recv))
    grad_gu = gate_up_grads(xs_last, ds, 0, wide, inverse, gu_in)

    hot_back = hot_back.reshape(owners, few, PIECES, narrow)
    hot_back = hot_back.transpose(2, 1, 0, 3).reshape(2, hot_dev, width_d)
    landed = mm(pick, back, TN)
    picked = landed[:, :width_d]
    layer_out = (
        (gates.reshape(entries)[:, None] * picked).reshape(tok_dev, topk, width_d).sum(axis=1)
    )
    token_gate = jnp.sum(jnp.where(hot_pick > 0, hot_gate[:, None], 0.0), axis=0)
    layer_out = layer_out + token_gate[:, None] * mm(hot_pick, hot_back[1], TN)
    returned = landed[:, width_d:]
    returned = returned.reshape(tok_dev, topk, width_d).sum(axis=1)
    blocks = jnp.stack([returned[:, j * wide : (j + 1) * wide] for j in range(groups)])
    input_grad = jnp.concatenate(
        [
            lax.dynamic_index_in_dim(
                blocks,
                ((q - core) % cores) * chips + (chip - p) % chips,
                0,
                keepdims=False,
            )
            for p in range(chips)
            for q in range(cores)
        ],
        axis=1,
    )
    input_grad = input_grad + mm(hot_pick, hot_back[0], TN)
    return (
        layer_out.astype(BF),
        input_grad.astype(BF),
        grad_gu[None],
        grad_dn[None],
        grad_hot[:2],
        grad_hot[2],
    )


def solution(mesh):
    tok = P(("dp", "expert"), None)
    flat = P(("dp", "expert"))
    rows = P("expert", "dp", None)
    hot = (P(None, "dp", "expert"), P("dp", "expert"))
    return jax.shard_map(
        local,
        mesh=mesh,
        in_specs=(tok, tok, tok, tok, flat, flat, rows, rows) + hot,
        out_specs=(tok, tok, rows, rows) + hot,
        check_vma=False,
    )
```

```python
import jax
import jax.numpy as jnp
from jax import lax
from jax.experimental import pallas as pl
from jax.experimental.pallas import tpu as pltpu
from jax.sharding import PartitionSpec as P

BF = jnp.bfloat16
F32 = jnp.float32
NN = (((1,), (0,)), ((), ()))
NT = (((1,), (1,)), ((), ()))
TN = (((0,), (0,)), ((), ()))
ROOM = 56 * 1024 * 1024
LIGHT = pl.CostEstimate(flops=1, bytes_accessed=1, transcendentals=0)
SMEM = pl.BlockSpec(memory_space=pltpu.SMEM)
ANYWHERE = pl.BlockSpec(memory_space=pl.ANY)
INSIDE = pl.BlockSpec(memory_space=pltpu.VMEM)
PIECES = 8


def mm(a, b, dims=NN):
    return lax.dot_general(a, b, dims, preferred_element_type=F32)


def after(value, *earlier):
    return lax.optimization_barrier((value,) + earlier)[0]


def params():
    return pltpu.CompilerParams(vmem_limit_bytes=ROOM)


LIGHT = pl.CostEstimate(flops=1, bytes_accessed=1, transcendentals=0)


def struct(*shape, dtype=BF):
    return jax.ShapeDtypeStruct(shape, dtype)


def whole(array):
    return pl.BlockSpec(array.shape, lambda *_: (0,) * len(array.shape))


def stack_rows(refs, scratch):
    rows = refs[0].shape[0]
    for i, ref in enumerate(refs):
        scratch[i * rows : (i + 1) * rows, :] = ref[...]


def fetch(order_ref, blocks, w_ref, sems):
    deep = blocks[0].shape[0]
    copies = []
    for j, block in enumerate(blocks):
        place = pl.multiple_of(order_ref[j] * deep, deep)
        copies.append(pltpu.make_async_copy(block, w_ref.at[pl.ds(place, deep)], sems.at[j]))
        copies[-1].start()
    return copies


def down_scratch(blocks):
    deep, width = blocks[0].shape
    return [pltpu.VMEM((len(blocks) * deep, width), BF), pltpu.SemaphoreType.DMA((len(blocks),))]


def fetch_each(blocks, w_ref, sems):
    copies = []
    for j, block in enumerate(blocks):
        copies.append(pltpu.make_async_copy(block, w_ref.at[j], sems.at[j]))
        copies[-1].start()
    return copies


def each_scratch(blocks):
    return [
        pltpu.VMEM((len(blocks),) + blocks[0].shape, BF),
        pltpu.SemaphoreType.DMA((len(blocks),)),
    ]


def expert(order, rows_s, rows_x, w_gu, w_down):
    rows = rows_s.shape[0]
    depth, width = w_gu[0].shape
    deep, wide = w_down[0].shape
    half = width // 2
    m = len(w_gu)
    step = 512 if wide % 512 == 0 else wide

    def body(order_ref, s_ref, x_ref, *refs):
        gu_in, dn_in, rest = refs[:m], refs[m : 2 * m], refs[2 * m :]
        back_ref, hid_ref, d_ref, acc, gu_ref, gu_sems, dn_ref, dn_sems = rest
        gu_copies = fetch_each(gu_in, gu_ref, gu_sems)
        dn_copies = fetch(order_ref, dn_in, dn_ref, dn_sems)
        for j, copy in enumerate(gu_copies):
            copy.wait()
            found = mm(x_ref[:, j * depth : (j + 1) * depth], gu_ref[j])
            if j == 0:
                acc[...] = found
            else:
                acc[...] += found
        g = acc[:, :half]
        u = acc[:, half:]
        s = jax.nn.sigmoid(g)
        hid_ref[...] = (g * s * u).astype(BF)
        for copy in dn_copies:
            copy.wait()
        d_hidden = mm(s_ref[...], dn_ref[...], NT)
        d_ref[:, :half] = (d_hidden * u * s * (1.0 + g * (1.0 - s))).astype(BF)
        d_ref[:, half:] = (d_hidden * g * s).astype(BF)
        for j in range(m):
            at = wide + j * depth
            back_ref[:, at : at + depth] = mm(d_ref[...], gu_ref[j], NT).astype(BF)
        for c in range(0, wide, step):
            back_ref[:, c : c + step] = mm(hid_ref[...], dn_ref[:, c : c + step]).astype(BF)

    return pl.pallas_call(
        body,
        in_specs=[SMEM, INSIDE, INSIDE] + [ANYWHERE] * (2 * m),
        out_specs=[INSIDE] * 3,
        out_shape=[struct(rows, 2 * wide), struct(rows, half), struct(rows, width)],
        scratch_shapes=[pltpu.VMEM((rows, width), F32)]
        + each_scratch(w_gu)
        + down_scratch(w_down),
        compiler_params=params(),
        cost_estimate=LIGHT,
        name="expert",
    )(order, rows_s, rows_x, *w_gu, *w_down)


def gate_up_grads(xs, ds, k, wide, scale, received):
    n, rows, width = len(xs), xs[0].shape[0], ds[0].shape[1]
    step = 512 if width % 512 == 0 else width
    extra = [] if received is None else [received]
    if wide % 128 != 0:
        xs, k = [x[:, k * wide : (k + 1) * wide] for x in xs], 0

    def body(*refs):
        x_refs, d_refs, rest = refs[:n], refs[n : 2 * n], refs[2 * n :]
        out_ref, x_scr, d_scr = rest[-3:]

        @pl.when(pl.program_id(0) == 0)
        def _():
            stack_rows(x_refs, x_scr)

        stack_rows(d_refs, d_scr)
        found = mm(x_scr[...], d_scr[...], TN) * scale
        if extra:
            found = found + rest[0][...].astype(F32)
        out_ref[...] = found.astype(BF)

    shape = struct(wide, width)
    column = lambda i: (0, i)
    return pl.pallas_call(
        body,
        grid=(width // step,),
        in_specs=[pl.BlockSpec((rows, wide), lambda i: (0, k))] * n
        + [pl.BlockSpec((rows, step), column)] * n
        + [pl.BlockSpec((wide, step), column)] * len(extra),
        out_specs=pl.BlockSpec((wide, step), column),
        out_shape=shape,
        scratch_shapes=[pltpu.VMEM((n * rows, wide), BF), pltpu.VMEM((n * rows, step), BF)],
        compiler_params=params(),
        cost_estimate=LIGHT,
        name="gate_up_grads",
    )(*xs, *ds, *extra)


def down_grads(order, hidden, rows_s, wide, count, scale):
    rows, half = hidden.shape
    deep = half // count
    step = 512 if wide % 512 == 0 else wide

    def body(order_ref, h_ref, s_ref, *refs):
        outs, scratch = refs[:count], refs[count]
        scratch[...] = mm(h_ref[...], s_ref[...], TN) * scale
        for j in range(count):
            place = pl.multiple_of(order_ref[j] * deep, deep)
            outs[j][...] = scratch[pl.ds(place, deep), :].astype(BF)

    shapes = [struct(deep, wide)] * count
    return pl.pallas_call(
        body,
        grid=(wide // step,),
        in_specs=[SMEM, whole(hidden), pl.BlockSpec((rows, step), lambda i: (0, i))],
        out_specs=[pl.BlockSpec((deep, step), lambda i: (0, i))] * count,
        out_shape=shapes,
        scratch_shapes=[pltpu.VMEM((half, step), F32)],
        compiler_params=params(),
        cost_estimate=LIGHT,
        name="down_grads",
    )(order, hidden, rows_s)


def popular_partials(select, packed, weights, hid):
    parts, count = select.shape[:2]
    narrow = packed.shape[1] // (2 * parts)
    columns = sum(w.shape[0] for w in weights)

    def body(sel_ref, in_ref, *refs):
        w_refs, (x_ref, s_ref, p_ref) = refs[: len(weights)], refs[len(weights) :]
        x = None
        s = None
        for q in range(parts):
            rows = mm(sel_ref[q], in_ref[...])
            one = rows[:, q * narrow : (q + 1) * narrow]
            two = rows[:, (parts + q) * narrow : (parts + q + 1) * narrow]
            x = one if x is None else x + one
            s = two if s is None else s + two
        x = x.astype(BF)
        s = s.astype(BF)
        x_ref[...] = x
        s_ref[...] = s
        at = 0
        for w_ref in w_refs:
            for top in range(0, w_ref.shape[0], 3 * hid):
                p_ref[:, at : at + 2 * hid] = mm(x, w_ref[top : top + 2 * hid, :], NT).astype(BF)
                p_ref[:, at + 2 * hid : at + 3 * hid] = mm(
                    s, w_ref[top + 2 * hid : top + 3 * hid, :], NT
                ).astype(BF)
                at += 3 * hid

    return pl.pallas_call(
        body,
        in_specs=[INSIDE] * (2 + len(weights)),
        out_specs=[INSIDE] * 3,
        out_shape=[
            struct(count, narrow),
            struct(count, narrow),
            struct(count, columns),
        ],
        compiler_params=params(),
        cost_estimate=LIGHT,
        name="popular_partials",
    )(select, packed, *weights)


def popular_middle(own, others, hid):
    rows, columns = own.shape

    def body(own_ref, *refs):
        parts, out_ref = refs[:-1], refs[-1]
        act = own_ref[...].astype(F32)
        for part in parts:
            act = act + part[...].astype(F32)
        for at in range(0, columns, 3 * hid):
            g = act[:, at : at + hid]
            u = act[:, at + hid : at + 2 * hid]
            dh = act[:, at + 2 * hid : at + 3 * hid]
            s = jax.nn.sigmoid(g)
            out_ref[:, at : at + hid] = (dh * u * s * (1.0 + g * (1.0 - s))).astype(BF)
            out_ref[:, at + hid : at + 2 * hid] = (dh * g * s).astype(BF)
            out_ref[:, at + 2 * hid : at + 3 * hid] = (g * s * u).astype(BF)

    return pl.pallas_call(
        body,
        in_specs=[INSIDE] * (1 + len(others)),
        out_specs=INSIDE,
        out_shape=struct(rows, columns),
        compiler_params=params(),
        cost_estimate=LIGHT,
        name="popular_middle",
    )(own, *others)


def popular_back(select, lines, x, s, weights, hid, scale):
    parts, count, spots = select.shape
    narrow = x.shape[1]
    m = len(weights)
    n = len(lines)
    columns = lines[0].shape[1]

    def body(sel_ref, x_ref, s_ref, *refs):
        ins, w_refs, back_ref = refs[:n], refs[n : n + m], refs[n + m]
        grads, mid_ref = refs[n + m + 1 : -1], refs[-1]
        stack_rows(ins, mid_ref)
        grad = None
        out = None
        at = 0
        for w_ref, g_ref in zip(w_refs, grads):
            for top in range(0, w_ref.shape[0], 3 * hid):
                d_gate = mid_ref[:, at : at + hid]
                d_up = mid_ref[:, at + hid : at + 2 * hid]
                hidden = mid_ref[:, at + 2 * hid : at + 3 * hid]
                sides = ((d_gate, x_ref), (d_up, x_ref), (hidden, s_ref))
                for i, (left, right) in enumerate(sides):
                    here = slice(top + i * hid, top + (i + 1) * hid)
                    product = mm(left, w_ref[here, :])
                    if i == 2:
                        out = product if out is None else out + product
                    else:
                        grad = product if grad is None else grad + product
                    g_ref[here, :] = (mm(left, right[...], TN) * scale).astype(BF)
                at += 3 * hid
        grad = grad.astype(BF)
        out = out.astype(BF)
        for q in range(parts):
            back_ref[:, q * narrow : (q + 1) * narrow] = mm(sel_ref[q], grad, TN).astype(BF)
            back_ref[:, (parts + q) * narrow : (parts + q + 1) * narrow] = mm(
                sel_ref[q], out, TN
            ).astype(BF)

    return pl.pallas_call(
        body,
        in_specs=[INSIDE] * (3 + n + m),
        out_specs=[INSIDE] * (1 + m),
        out_shape=[struct(spots, 2 * parts * narrow)]
        + [struct(w.shape[0], narrow) for w in weights],
        scratch_shapes=[pltpu.VMEM((count, columns), BF)],
        compiler_params=params(),
        cost_estimate=LIGHT,
        name="popular_back",
    )(select, x, s, *lines, *weights)


def slot_positions(route_block, count):
    flat = route_block.reshape(-1)
    onehot = (flat[:, None] == jnp.arange(count, dtype=jnp.int32)[None, :]).astype(jnp.int32)
    before = jnp.cumsum(onehot, axis=0) - onehot
    return (flat, jnp.sum(before * onehot, axis=1))


def exchange(blocks):
    return lax.all_to_all(blocks, "expert", split_axis=0, concat_axis=0, tiled=True)


def local(
    tokens, cotangent, routes, gates, hot_index, hot_gate, w_gate_up, w_down, w_hot_gu, w_hot_dn
):
    owners = lax.axis_size("expert")
    groups = lax.axis_size("dp")
    cores = 2 if groups % 2 == 0 else 1
    chips = groups // cores
    tok_dev, width_d = tokens.shape
    topk = routes.shape[1]
    slots = max(2, 3 * tok_dev * topk // (2 * owners))
    entries = tok_dev * topk
    rows = owners * slots
    inverse = 1.0 / (4 * groups)
    me = lax.axis_index("dp")
    chip, core = me // cores, me % cores

    def shift(value, r):
        pairs = [
            (i, ((i // cores + r) % chips) * cores + i % cores) for i in range(groups)
        ]
        return lax.ppermute(value, "dp", pairs)

    def swap(value):
        pairs = [(i, (i // cores) * cores + (i + 1) % cores) for i in range(groups)]
        return lax.ppermute(value, "dp", pairs)

    order = jnp.stack(
        [
            ((chip - r) % chips) * cores + (core + k) % cores
            for k in range(cores)
            for r in range(chips)
        ]
    ).astype(jnp.int32)

    across = 1
    while 2 * (2 * across) ** 2 <= owners:
        across *= 2
    depths = owners // across
    spot = lax.axis_index("expert")

    def hop(value, j):
        return lax.ppermute(value, "expert", [(i, i ^ j) for i in range(owners)])

    wide = width_d // groups
    hid = w_hot_dn.shape[0]
    narrow = width_d // owners
    hot_w = jnp.concatenate([w_hot_gu, w_hot_dn[None]], axis=0).reshape(3 * hid, narrow)
    hot_near = [hot_w] + [shift(hot_w, r) for r in range(1, chips)]
    down_own = after(w_down[0], hot_near[-1])
    gu_own = after(w_gate_up[0], hot_near[-1])
    gu_near = [w_gate_up[0]] + [shift(gu_own, r) for r in range(1, chips)]
    down_near = [w_down[0]] + [shift(down_own, r) for r in range(1, chips)]
    gu_far = [swap(w_gate_up[0])] if cores == 2 else []
    down_far = [swap(w_down[0])] if cores == 2 else []

    flat, pos = slot_positions(routes, owners)
    dest = flat * slots + pos
    slot_ids = jnp.arange(rows, dtype=jnp.int32)[:, None]
    pick = (slot_ids == dest[None, :]).astype(BF)

    def as_rows(value, width):
        value = value.reshape(owners, -1)
        spare = -value.shape[1] % width
        return jnp.pad(value, ((0, 0), (0, spare))).reshape(owners, -1, width)

    hot_dev = hot_index.shape[0]
    few = 2 * hot_dev // PIECES
    hot_pick = (
        hot_index[:, None] == jnp.arange(tok_dev, dtype=jnp.int32)[None, :]
    ).astype(BF)
    hot_x = mm(hot_pick, tokens).astype(BF)
    hot_s = (hot_gate[:, None] * mm(hot_pick, cotangent)).astype(BF)
    hot_send = jnp.concatenate([hot_x, hot_s], axis=0).reshape(PIECES, few, owners, narrow)
    hot_send = hot_send.transpose(2, 1, 0, 3).reshape(owners * few, PIECES * narrow)
    packed_id = jnp.arange(owners * few, dtype=jnp.int32)
    turn = ((packed_id ^ (spot * few))[:, None] == packed_id[None, :]).astype(BF)
    row = jnp.arange(owners * hot_dev, dtype=jnp.int32)
    step = row // hot_dev
    piece = (row % hot_dev) // few

    def selection(index):
        hit = (index * few + row % few)[:, None] == packed_id[None, :]
        return jnp.stack([hit & (piece == q)[:, None] for q in range(PIECES // 2)]).astype(BF)

    hot_send = mm(turn, hot_send).astype(BF).reshape(depths, across, few, PIECES * narrow)
    near = [hot_send[0]] + [hop(hot_send[j], j * across) for j in range(1, depths)]
    near = jnp.stack(near, axis=1)
    hot_recv = jnp.concatenate([near[0]] + [hop(near[j], j) for j in range(1, across)])
    hot_recv = hot_recv.reshape(owners * few, PIECES * narrow)

    scaled = (gates[:, :, None] * cotangent[:, None, :].astype(F32)).astype(BF)
    send_s = mm(pick, scaled.reshape(entries, width_d)).astype(BF)
    rows_s = exchange(send_s.reshape(owners, slots, width_d)).reshape(rows, width_d)

    tok_rel = jnp.concatenate(
        [
            lax.dynamic_slice_in_dim(tokens, order[j] * wide, wide, 1)
            for j in range(groups)
        ],
        axis=1,
    )
    tok_rel = jnp.repeat(tok_rel, topk, axis=0) if topk > 1 else tok_rel
    send_x = mm(pick, tok_rel).astype(BF).reshape(owners, slots, width_d)
    rows_x = exchange(send_x).reshape(rows, width_d)

    hot_near = jnp.concatenate(list(after(tuple(hot_near), send_x, *gu_far, *down_far)), axis=0)
    hot_ws = [hot_near] + ([swap(hot_near)] if cores == 2 else [])
    hot_x, hot_s, partial = popular_partials(selection(step), hot_recv, hot_ws, hid)
    share = depths * hot_dev
    level_in = [hop(partial[j * share : (j + 1) * share], j) for j in range(1, across)]
    if cores == 2:
        gu_far = gu_far + [swap(block) for block in gu_near[1:]]
    level_in = list(after(tuple(level_in), rows_s))
    level = partial[:share].astype(F32)
    for value in level_in:
        level = level + value.astype(F32)
    level = level.astype(BF)
    level = [level[j * hot_dev : (j + 1) * hot_dev] for j in range(depths)]
    depth_in = [hop(level[j], j * across) for j in range(1, depths)]
    rows_x = after(rows_x, *depth_in)
    hot_own = popular_middle(level[0], depth_in, hid)
    line = [hot_own] + [hop(hot_own, j * across) for j in range(1, depths)]
    down_near = list(after(tuple(down_near), hot_own))
    if cores == 2:
        down_far = down_far + [swap(block) for block in down_near[1:]]
    back, hidden, d_act = expert(order, rows_s, after(rows_x, hot_own), gu_near + gu_far, down_near + down_far)

    def columns_of(r):
        return jnp.concatenate(
            [
                rows_x[:, (k * chips + r) * wide : (k * chips + r + 1) * wide]
                for k in range(cores)
            ],
            axis=1,
        )

    xs = [columns_of(0)] + [shift(columns_of(r), -r) for r in range(1, chips)]
    ds = [d_act] + [shift(d_act, -r) for r in range(1, chips)]
    back = after(back, *line[1:])
    back = exchange(back.reshape(owners, slots, 2 * width_d)).reshape(rows, 2 * width_d)

    line = jnp.concatenate(list(after(tuple(line), d_act)))
    lines = [line] + [hop(line, j) for j in range(1, across)]
    hot_back, *hot_grads = popular_back(
        selection(step), lines, hot_x, hot_s, hot_ws, hid, inverse
    )

    dn_parts = down_grads(order, hidden, rows_s, width_d, groups, inverse)
    dn_sum = list(dn_parts[:chips])
    if cores == 2:
        dn_in = [swap(part) for part in dn_parts[chips:]]
        dn_sum = [
            (one.astype(F32) + two.astype(F32)).astype(BF) for one, two in zip(dn_sum, dn_in)
        ]
    dn_total = dn_sum[0].astype(F32)
    dn_recv = [shift(dn_sum[r], -r) for r in range(1, chips)]
    for value in dn_recv:
        dn_total = dn_total + value.astype(F32)
    grad_dn = dn_total.astype(BF)

    hot_back = hot_back.reshape(across, depths, few, PIECES * narrow)
    hot_back = [hot_back[0]] + [hop(hot_back[j], j) for j in range(1, across)]
    hot_back = jnp.stack(hot_back, axis=1)
    xs_late = list(after(tuple(xs), d_act))
    gu_in = None
    if cores == 2:
        gu_in = swap(gate_up_grads(xs_late, ds, 1, wide, inverse, None))

    hot_sum = hot_grads[0]
    if cores == 2:
        hot_sum = (hot_sum.astype(F32) + swap(hot_grads[1]).astype(F32)).astype(BF)
    hot_sum = hot_sum.reshape(chips, 3 * hid, narrow)
    hot_total = hot_sum[0].astype(F32)
    hot_far = [shift(hot_sum[r], -r) for r in range(1, chips)]
    for value in hot_far:
        hot_total = hot_total + value.astype(F32)
    grad_hot = hot_total.astype(BF).reshape(3, hid, narrow)
    xs_last = list(after(tuple(xs_late), *hot_far, *dn_recv))
    grad_gu = gate_up_grads(xs_last, ds, 0, wide, inverse, gu_in)

    hot_back = [hot_back[0]] + [hop(hot_back[j], j * across) for j in range(1, depths)]
    hot_back = list(after(tuple(hot_back), grad_gu))
    hot_back = jnp.concatenate(hot_back).reshape(owners * few, PIECES * narrow)
    hot_back = mm(turn, hot_back).astype(BF)

    hot_back = hot_back.reshape(owners, few, PIECES, narrow)
    hot_back = hot_back.transpose(2, 1, 0, 3).reshape(2, hot_dev, width_d)
    landed = mm(pick, back, TN)
    picked = landed[:, :width_d]
    layer_out = (
        (gates.reshape(entries)[:, None] * picked).reshape(tok_dev, topk, width_d).sum(axis=1)
    )
    token_gate = jnp.sum(jnp.where(hot_pick > 0, hot_gate[:, None], 0.0), axis=0)
    layer_out = layer_out + token_gate[:, None] * mm(hot_pick, hot_back[1], TN)
    returned = landed[:, width_d:]
    returned = returned.reshape(tok_dev, topk, width_d).sum(axis=1)
    blocks = jnp.stack([returned[:, j * wide : (j + 1) * wide] for j in range(groups)])
    input_grad = jnp.concatenate(
        [
            lax.dynamic_index_in_dim(
                blocks,
                ((q - core) % cores) * chips + (chip - p) % chips,
                0,
                keepdims=False,
            )
            for p in range(chips)
            for q in range(cores)
        ],
        axis=1,
    )
    input_grad = input_grad + mm(hot_pick, hot_back[0], TN)
    return (
        layer_out.astype(BF),
        input_grad.astype(BF),
        grad_gu[None],
        grad_dn[None],
        grad_hot[:2],
        grad_hot[2],
    )


def solution(mesh):
    tok = P(("dp", "expert"), None)
    flat = P(("dp", "expert"))
    rows = P("expert", "dp", None)
    hot = (P(None, "dp", "expert"), P("dp", "expert"))
    return jax.shard_map(
        local,
        mesh=mesh,
        in_specs=(tok, tok, tok, tok, flat, flat, rows, rows) + hot,
        out_specs=(tok, tok, rows, rows) + hot,
        check_vma=False,
    )
```

```python
import jax
import jax.numpy as jnp
from jax import lax
from jax.experimental import pallas as pl
from jax.experimental.pallas import tpu as pltpu
from jax.sharding import PartitionSpec as P

BF = jnp.bfloat16
F32 = jnp.float32
NN = (((1,), (0,)), ((), ()))
NT = (((1,), (1,)), ((), ()))
TN = (((0,), (0,)), ((), ()))
ROOM = 56 * 1024 * 1024
LIGHT = pl.CostEstimate(flops=1, bytes_accessed=1, transcendentals=0)
SMEM = pl.BlockSpec(memory_space=pltpu.SMEM)
ANYWHERE = pl.BlockSpec(memory_space=pl.ANY)
INSIDE = pl.BlockSpec(memory_space=pltpu.VMEM)
PIECES = 8


def mm(a, b, dims=NN):
    return lax.dot_general(a, b, dims, preferred_element_type=F32)


def after(value, *earlier):
    return lax.optimization_barrier((value,) + earlier)[0]


def params():
    return pltpu.CompilerParams(vmem_limit_bytes=ROOM)


LIGHT = pl.CostEstimate(flops=1, bytes_accessed=1, transcendentals=0)


def struct(*shape, dtype=BF):
    return jax.ShapeDtypeStruct(shape, dtype)


def whole(array):
    return pl.BlockSpec(array.shape, lambda *_: (0,) * len(array.shape))


def stack_rows(refs, scratch):
    rows = refs[0].shape[0]
    for i, ref in enumerate(refs):
        scratch[i * rows : (i + 1) * rows, :] = ref[...]


def fetch(order_ref, blocks, w_ref, sems):
    deep = blocks[0].shape[0]
    copies = []
    for j, block in enumerate(blocks):
        place = pl.multiple_of(order_ref[j] * deep, deep)
        copies.append(pltpu.make_async_copy(block, w_ref.at[pl.ds(place, deep)], sems.at[j]))
        copies[-1].start()
    return copies


def down_scratch(blocks):
    deep, width = blocks[0].shape
    return [pltpu.VMEM((len(blocks) * deep, width), BF), pltpu.SemaphoreType.DMA((len(blocks),))]


def fetch_each(blocks, w_ref, sems):
    copies = []
    for j, block in enumerate(blocks):
        copies.append(pltpu.make_async_copy(block, w_ref.at[j], sems.at[j]))
        copies[-1].start()
    return copies


def each_scratch(blocks):
    return [
        pltpu.VMEM((len(blocks),) + blocks[0].shape, BF),
        pltpu.SemaphoreType.DMA((len(blocks),)),
    ]


def expert(order, rows_s, rows_x, w_gu, w_down):
    rows = rows_s.shape[0]
    depth, width = w_gu[0].shape
    deep, wide = w_down[0].shape
    half = width // 2
    m = len(w_gu)
    step = 512 if wide % 512 == 0 else wide

    def body(order_ref, s_ref, x_ref, *refs):
        gu_in, dn_in, rest = refs[:m], refs[m : 2 * m], refs[2 * m :]
        back_ref, hid_ref, d_ref, acc, gu_ref, gu_sems, dn_ref, dn_sems = rest
        gu_copies = fetch_each(gu_in, gu_ref, gu_sems)
        dn_copies = fetch(order_ref, dn_in, dn_ref, dn_sems)
        for j, copy in enumerate(gu_copies):
            copy.wait()
            found = mm(x_ref[:, j * depth : (j + 1) * depth], gu_ref[j])
            if j == 0:
                acc[...] = found
            else:
                acc[...] += found
        g = acc[:, :half]
        u = acc[:, half:]
        s = jax.nn.sigmoid(g)
        hid_ref[...] = (g * s * u).astype(BF)
        for copy in dn_copies:
            copy.wait()
        d_hidden = mm(s_ref[...], dn_ref[...], NT)
        d_ref[:, :half] = (d_hidden * u * s * (1.0 + g * (1.0 - s))).astype(BF)
        d_ref[:, half:] = (d_hidden * g * s).astype(BF)
        for j in range(m):
            at = wide + j * depth
            back_ref[:, at : at + depth] = mm(d_ref[...], gu_ref[j], NT).astype(BF)
        for c in range(0, wide, step):
            back_ref[:, c : c + step] = mm(hid_ref[...], dn_ref[:, c : c + step]).astype(BF)

    return pl.pallas_call(
        body,
        in_specs=[SMEM, INSIDE, INSIDE] + [ANYWHERE] * (2 * m),
        out_specs=[INSIDE] * 3,
        out_shape=[struct(rows, 2 * wide), struct(rows, half), struct(rows, width)],
        scratch_shapes=[pltpu.VMEM((rows, width), F32)]
        + each_scratch(w_gu)
        + down_scratch(w_down),
        compiler_params=params(),
        cost_estimate=LIGHT,
        name="expert",
    )(order, rows_s, rows_x, *w_gu, *w_down)


def gate_up_grads(xs, ds, k, wide, scale, received):
    n, rows, width = len(xs), xs[0].shape[0], ds[0].shape[1]
    step = 512 if width % 512 == 0 else width
    extra = [] if received is None else [received]
    if wide % 128 != 0:
        xs, k = [x[:, k * wide : (k + 1) * wide] for x in xs], 0

    def body(*refs):
        x_refs, d_refs, rest = refs[:n], refs[n : 2 * n], refs[2 * n :]
        out_ref, x_scr, d_scr = rest[-3:]

        @pl.when(pl.program_id(0) == 0)
        def _():
            stack_rows(x_refs, x_scr)

        stack_rows(d_refs, d_scr)
        found = mm(x_scr[...], d_scr[...], TN) * scale
        if extra:
            found = found + rest[0][...].astype(F32)
        out_ref[...] = found.astype(BF)

    shape = struct(wide, width)
    column = lambda i: (0, i)
    return pl.pallas_call(
        body,
        grid=(width // step,),
        in_specs=[pl.BlockSpec((rows, wide), lambda i: (0, k))] * n
        + [pl.BlockSpec((rows, step), column)] * n
        + [pl.BlockSpec((wide, step), column)] * len(extra),
        out_specs=pl.BlockSpec((wide, step), column),
        out_shape=shape,
        scratch_shapes=[pltpu.VMEM((n * rows, wide), BF), pltpu.VMEM((n * rows, step), BF)],
        compiler_params=params(),
        cost_estimate=LIGHT,
        name="gate_up_grads",
    )(*xs, *ds, *extra)


def down_grads(order, hidden, rows_s, wide, count, scale):
    rows, half = hidden.shape
    deep = half // count
    step = 512 if wide % 512 == 0 else wide

    def body(order_ref, h_ref, s_ref, *refs):
        outs, scratch = refs[:count], refs[count]
        scratch[...] = mm(h_ref[...], s_ref[...], TN) * scale
        for j in range(count):
            place = pl.multiple_of(order_ref[j] * deep, deep)
            outs[j][...] = scratch[pl.ds(place, deep), :].astype(BF)

    shapes = [struct(deep, wide)] * count
    return pl.pallas_call(
        body,
        grid=(wide // step,),
        in_specs=[SMEM, whole(hidden), pl.BlockSpec((rows, step), lambda i: (0, i))],
        out_specs=[pl.BlockSpec((deep, step), lambda i: (0, i))] * count,
        out_shape=shapes,
        scratch_shapes=[pltpu.VMEM((half, step), F32)],
        compiler_params=params(),
        cost_estimate=LIGHT,
        name="down_grads",
    )(order, hidden, rows_s)


def popular_partials(select, packed, weights, hid):
    parts, count = select.shape[:2]
    narrow = packed.shape[1] // (2 * parts)
    columns = sum(w.shape[0] for w in weights)

    def body(sel_ref, in_ref, *refs):
        w_refs, (x_ref, s_ref, p_ref) = refs[: len(weights)], refs[len(weights) :]
        x = None
        s = None
        for q in range(parts):
            rows = mm(sel_ref[q], in_ref[...])
            one = rows[:, q * narrow : (q + 1) * narrow]
            two = rows[:, (parts + q) * narrow : (parts + q + 1) * narrow]
            x = one if x is None else x + one
            s = two if s is None else s + two
        x = x.astype(BF)
        s = s.astype(BF)
        x_ref[...] = x
        s_ref[...] = s
        at = 0
        for w_ref in w_refs:
            for top in range(0, w_ref.shape[0], 3 * hid):
                p_ref[:, at : at + 2 * hid] = mm(x, w_ref[top : top + 2 * hid, :], NT).astype(BF)
                p_ref[:, at + 2 * hid : at + 3 * hid] = mm(
                    s, w_ref[top + 2 * hid : top + 3 * hid, :], NT
                ).astype(BF)
                at += 3 * hid

    return pl.pallas_call(
        body,
        in_specs=[INSIDE] * (2 + len(weights)),
        out_specs=[INSIDE] * 3,
        out_shape=[
            struct(count, narrow),
            struct(count, narrow),
            struct(count, columns),
        ],
        compiler_params=params(),
        cost_estimate=LIGHT,
        name="popular_partials",
    )(select, packed, *weights)


def popular_middle(own, others, hid):
    rows, columns = own.shape

    def body(own_ref, *refs):
        parts, out_ref = refs[:-1], refs[-1]
        act = own_ref[...].astype(F32)
        for part in parts:
            act = act + part[...].astype(F32)
        for at in range(0, columns, 3 * hid):
            g = act[:, at : at + hid]
            u = act[:, at + hid : at + 2 * hid]
            dh = act[:, at + 2 * hid : at + 3 * hid]
            s = jax.nn.sigmoid(g)
            out_ref[:, at : at + hid] = (dh * u * s * (1.0 + g * (1.0 - s))).astype(BF)
            out_ref[:, at + hid : at + 2 * hid] = (dh * g * s).astype(BF)
            out_ref[:, at + 2 * hid : at + 3 * hid] = (g * s * u).astype(BF)

    return pl.pallas_call(
        body,
        in_specs=[INSIDE] * (1 + len(others)),
        out_specs=INSIDE,
        out_shape=struct(rows, columns),
        compiler_params=params(),
        cost_estimate=LIGHT,
        name="popular_middle",
    )(own, *others)


def popular_back(select, lines, x, s, weights, hid, scale):
    parts, count, spots = select.shape
    narrow = x.shape[1]
    m = len(weights)
    n = len(lines)
    columns = lines[0].shape[1]

    def body(sel_ref, x_ref, s_ref, *refs):
        ins, w_refs, back_ref = refs[:n], refs[n : n + m], refs[n + m]
        grads, mid_ref = refs[n + m + 1 : -1], refs[-1]
        stack_rows(ins, mid_ref)
        grad = None
        out = None
        at = 0
        for w_ref, g_ref in zip(w_refs, grads):
            for top in range(0, w_ref.shape[0], 3 * hid):
                d_gate = mid_ref[:, at : at + hid]
                d_up = mid_ref[:, at + hid : at + 2 * hid]
                hidden = mid_ref[:, at + 2 * hid : at + 3 * hid]
                sides = ((d_gate, x_ref), (d_up, x_ref), (hidden, s_ref))
                for i, (left, right) in enumerate(sides):
                    here = slice(top + i * hid, top + (i + 1) * hid)
                    product = mm(left, w_ref[here, :])
                    if i == 2:
                        out = product if out is None else out + product
                    else:
                        grad = product if grad is None else grad + product
                    g_ref[here, :] = (mm(left, right[...], TN) * scale).astype(BF)
                at += 3 * hid
        grad = grad.astype(BF)
        out = out.astype(BF)
        for q in range(parts):
            back_ref[:, q * narrow : (q + 1) * narrow] = mm(sel_ref[q], grad, TN).astype(BF)
            back_ref[:, (parts + q) * narrow : (parts + q + 1) * narrow] = mm(
                sel_ref[q], out, TN
            ).astype(BF)

    return pl.pallas_call(
        body,
        in_specs=[INSIDE] * (3 + n + m),
        out_specs=[INSIDE] * (1 + m),
        out_shape=[struct(spots, 2 * parts * narrow)]
        + [struct(w.shape[0], narrow) for w in weights],
        scratch_shapes=[pltpu.VMEM((count, columns), BF)],
        compiler_params=params(),
        cost_estimate=LIGHT,
        name="popular_back",
    )(select, x, s, *lines, *weights)


def slot_positions(route_block, count):
    flat = route_block.reshape(-1)
    onehot = (flat[:, None] == jnp.arange(count, dtype=jnp.int32)[None, :]).astype(jnp.int32)
    before = jnp.cumsum(onehot, axis=0) - onehot
    return (flat, jnp.sum(before * onehot, axis=1))


def exchange(blocks):
    return lax.all_to_all(blocks, "expert", split_axis=0, concat_axis=0, tiled=True)


def local(
    tokens, cotangent, routes, gates, hot_index, hot_gate, w_gate_up, w_down, w_hot_gu, w_hot_dn
):
    owners = lax.axis_size("expert")
    groups = lax.axis_size("dp")
    cores = 2 if groups % 2 == 0 else 1
    chips = groups // cores
    tok_dev, width_d = tokens.shape
    topk = routes.shape[1]
    slots = max(2, 3 * tok_dev * topk // (2 * owners))
    entries = tok_dev * topk
    rows = owners * slots
    inverse = 1.0 / (4 * groups)
    me = lax.axis_index("dp")
    chip, core = me // cores, me % cores

    def shift(value, r):
        pairs = [
            (i, ((i // cores + r) % chips) * cores + i % cores) for i in range(groups)
        ]
        return lax.ppermute(value, "dp", pairs)

    def swap(value):
        pairs = [(i, (i // cores) * cores + (i + 1) % cores) for i in range(groups)]
        return lax.ppermute(value, "dp", pairs)

    order = jnp.stack(
        [
            ((chip - r) % chips) * cores + (core + k) % cores
            for k in range(cores)
            for r in range(chips)
        ]
    ).astype(jnp.int32)

    across = 1
    while 2 * (2 * across) ** 2 <= owners:
        across *= 2
    depths = owners // across
    spot = lax.axis_index("expert")

    def hop(value, j):
        return lax.ppermute(value, "expert", [(i, i ^ j) for i in range(owners)])

    wide = width_d // groups
    hid = w_hot_dn.shape[0]
    narrow = width_d // owners
    hot_w = jnp.concatenate([w_hot_gu, w_hot_dn[None]], axis=0).reshape(3 * hid, narrow)
    hot_near = [hot_w] + [shift(hot_w, r) for r in range(1, chips)]
    down_own = after(w_down[0], hot_near[-1])
    gu_own = after(w_gate_up[0], hot_near[-1])
    gu_near = [w_gate_up[0]] + [shift(gu_own, r) for r in range(1, chips)]
    down_near = [w_down[0]] + [shift(down_own, r) for r in range(1, chips)]
    gu_far = [swap(w_gate_up[0])] if cores == 2 else []
    down_far = [swap(w_down[0])] if cores == 2 else []

    flat, pos = slot_positions(routes, owners)
    dest = flat * slots + pos
    slot_ids = jnp.arange(rows, dtype=jnp.int32)[:, None]
    pick = (slot_ids == dest[None, :]).astype(BF)

    def as_rows(value, width):
        value = value.reshape(owners, -1)
        spare = -value.shape[1] % width
        return jnp.pad(value, ((0, 0), (0, spare))).reshape(owners, -1, width)

    hot_dev = hot_index.shape[0]
    few = 2 * hot_dev // PIECES
    hot_pick = (
        hot_index[:, None] == jnp.arange(tok_dev, dtype=jnp.int32)[None, :]
    ).astype(BF)
    hot_x = mm(hot_pick, tokens).astype(BF)
    hot_s = (hot_gate[:, None] * mm(hot_pick, cotangent)).astype(BF)
    hot_send = jnp.concatenate([hot_x, hot_s], axis=0).reshape(PIECES, few, owners, narrow)
    hot_send = hot_send.transpose(2, 1, 0, 3).reshape(owners * few, PIECES * narrow)
    packed_id = jnp.arange(owners * few, dtype=jnp.int32)
    turn = ((packed_id ^ (spot * few))[:, None] == packed_id[None, :]).astype(BF)
    row = jnp.arange(owners * hot_dev, dtype=jnp.int32)
    step = row // hot_dev
    piece = (row % hot_dev) // few

    def selection(index):
        hit = (index * few + row % few)[:, None] == packed_id[None, :]
        return jnp.stack([hit & (piece == q)[:, None] for q in range(PIECES // 2)]).astype(BF)

    hot_send = mm(turn, hot_send).astype(BF).reshape(depths, across, few, PIECES * narrow)
    near = [hot_send[0]] + [hop(hot_send[j], j * across) for j in range(1, depths)]
    near = jnp.stack(near, axis=1)
    hot_recv = jnp.concatenate([near[0]] + [hop(near[j], j) for j in range(1, across)])
    hot_recv = hot_recv.reshape(owners * few, PIECES * narrow)

    scaled = (gates[:, :, None] * cotangent[:, None, :].astype(F32)).astype(BF)
    send_s = mm(pick, scaled.reshape(entries, width_d)).astype(BF)
    rows_s = exchange(send_s.reshape(owners, slots, width_d)).reshape(rows, width_d)

    tok_rel = jnp.concatenate(
        [
            lax.dynamic_slice_in_dim(tokens, order[j] * wide, wide, 1)
            for j in range(groups)
        ],
        axis=1,
    )
    tok_rel = jnp.repeat(tok_rel, topk, axis=0) if topk > 1 else tok_rel
    send_x = mm(pick, tok_rel).astype(BF).reshape(owners, slots, width_d)
    rows_x = exchange(send_x).reshape(rows, width_d)

    hot_near = jnp.concatenate(list(after(tuple(hot_near), send_x)), axis=0)
    hot_ws = [hot_near] + ([swap(hot_near)] if cores == 2 else [])
    hot_x, hot_s, partial = popular_partials(selection(step), hot_recv, hot_ws, hid)
    share = depths * hot_dev
    level_in = [hop(partial[j * share : (j + 1) * share], j) for j in range(1, across)]
    if cores == 2:
        gu_near = list(after(tuple(gu_near), rows_x))
        gu_far = gu_far + [swap(block) for block in gu_near[1:]]
    level_in = list(after(tuple(level_in), rows_s))
    level = partial[:share].astype(F32)
    for value in level_in:
        level = level + value.astype(F32)
    level = level.astype(BF)
    level = [level[j * hot_dev : (j + 1) * hot_dev] for j in range(depths)]
    depth_in = [hop(level[j], j * across) for j in range(1, depths)]
    rows_x = after(rows_x, *depth_in)
    hot_own = popular_middle(level[0], depth_in, hid)
    line = [hot_own] + [hop(hot_own, j * across) for j in range(1, depths)]
    down_near = list(after(tuple(down_near), hot_own))
    if cores == 2:
        down_far = down_far + [swap(block) for block in down_near[1:]]
    back, hidden, d_act = expert(order, rows_s, after(rows_x, hot_own), gu_near + gu_far, down_near + down_far)

    def columns_of(r):
        return jnp.concatenate(
            [
                rows_x[:, (k * chips + r) * wide : (k * chips + r + 1) * wide]
                for k in range(cores)
            ],
            axis=1,
        )

    xs = [columns_of(0)] + [shift(columns_of(r), -r) for r in range(1, chips)]
    ds = [d_act] + [shift(d_act, -r) for r in range(1, chips)]
    back = after(back, *line[1:])
    back = exchange(back.reshape(owners, slots, 2 * width_d)).reshape(rows, 2 * width_d)

    line = jnp.concatenate(list(after(tuple(line), d_act)))
    lines = [line] + [hop(line, j) for j in range(1, across)]
    hot_back, *hot_grads = popular_back(
        selection(step), lines, hot_x, hot_s, hot_ws, hid, inverse
    )

    dn_parts = down_grads(order, hidden, rows_s, width_d, groups, inverse)
    dn_sum = list(dn_parts[:chips])
    if cores == 2:
        dn_in = [swap(part) for part in dn_parts[chips:]]
        dn_sum = [
            (one.astype(F32) + two.astype(F32)).astype(BF) for one, two in zip(dn_sum, dn_in)
        ]
    dn_total = dn_sum[0].astype(F32)
    dn_recv = [shift(dn_sum[r], -r) for r in range(1, chips)]
    for value in dn_recv:
        dn_total = dn_total + value.astype(F32)
    grad_dn = dn_total.astype(BF)

    hot_back = hot_back.reshape(across, depths, few, PIECES * narrow)
    hot_back = [hot_back[0]] + [hop(hot_back[j], j) for j in range(1, across)]
    hot_back = jnp.stack(hot_back, axis=1)
    xs_late = list(after(tuple(xs), d_act))
    gu_in = None
    if cores == 2:
        gu_in = swap(gate_up_grads(xs_late, ds, 1, wide, inverse, None))

    hot_sum = hot_grads[0]
    if cores == 2:
        hot_sum = after(hot_sum, dn_in[0])
    if cores == 2:
        hot_sum = (hot_sum.astype(F32) + swap(hot_grads[1]).astype(F32)).astype(BF)
    hot_sum = hot_sum.reshape(chips, 3 * hid, narrow)
    hot_total = hot_sum[0].astype(F32)
    hot_far = [shift(hot_sum[r], -r) for r in range(1, chips)]
    for value in hot_far:
        hot_total = hot_total + value.astype(F32)
    grad_hot = hot_total.astype(BF).reshape(3, hid, narrow)
    xs_last = list(after(tuple(xs_late), *hot_far, *dn_recv))
    grad_gu = gate_up_grads(xs_last, ds, 0, wide, inverse, gu_in)

    if cores == 2:
        hot_back = after(hot_back, gu_in)
    hot_back = [hot_back[0]] + [hop(hot_back[j], j * across) for j in range(1, depths)]
    hot_back = list(after(tuple(hot_back), grad_gu))
    hot_back = jnp.concatenate(hot_back).reshape(owners * few, PIECES * narrow)
    hot_back = mm(turn, hot_back).astype(BF)

    hot_back = hot_back.reshape(owners, few, PIECES, narrow)
    hot_back = hot_back.transpose(2, 1, 0, 3).reshape(2, hot_dev, width_d)
    landed = mm(pick, back, TN)
    picked = landed[:, :width_d]
    layer_out = (
        (gates.reshape(entries)[:, None] * picked).reshape(tok_dev, topk, width_d).sum(axis=1)
    )
    token_gate = jnp.sum(jnp.where(hot_pick > 0, hot_gate[:, None], 0.0), axis=0)
    layer_out = layer_out + token_gate[:, None] * mm(hot_pick, hot_back[1], TN)
    returned = landed[:, width_d:]
    returned = returned.reshape(tok_dev, topk, width_d).sum(axis=1)
    blocks = jnp.stack([returned[:, j * wide : (j + 1) * wide] for j in range(groups)])
    input_grad = jnp.concatenate(
        [
            lax.dynamic_index_in_dim(
                blocks,
                ((q - core) % cores) * chips + (chip - p) % chips,
                0,
                keepdims=False,
            )
            for p in range(chips)
            for q in range(cores)
        ],
        axis=1,
    )
    input_grad = input_grad + mm(hot_pick, hot_back[0], TN)
    return (
        layer_out.astype(BF),
        input_grad.astype(BF),
        grad_gu[None],
        grad_dn[None],
        grad_hot[:2],
        grad_hot[2],
    )


def solution(mesh):
    tok = P(("dp", "expert"), None)
    flat = P(("dp", "expert"))
    rows = P("expert", "dp", None)
    hot = (P(None, "dp", "expert"), P("dp", "expert"))
    return jax.shard_map(
        local,
        mesh=mesh,
        in_specs=(tok, tok, tok, tok, flat, flat, rows, rows) + hot,
        out_specs=(tok, tok, rows, rows) + hot,
        check_vma=False,
    )
```

```python
import jax
import jax.numpy as jnp
from jax import lax
from jax.experimental import pallas as pl
from jax.experimental.pallas import tpu as pltpu
from jax.sharding import PartitionSpec as P

BF = jnp.bfloat16
F32 = jnp.float32
NN = (((1,), (0,)), ((), ()))
NT = (((1,), (1,)), ((), ()))
TN = (((0,), (0,)), ((), ()))
ROOM = 56 * 1024 * 1024
LIGHT = pl.CostEstimate(flops=1, bytes_accessed=1, transcendentals=0)
SMEM = pl.BlockSpec(memory_space=pltpu.SMEM)
ANYWHERE = pl.BlockSpec(memory_space=pl.ANY)
HEAVY = pl.CostEstimate(flops=10**11, bytes_accessed=1, transcendentals=0)
INSIDE = pl.BlockSpec(memory_space=pltpu.VMEM)
PIECES = 8


def mm(a, b, dims=NN):
    return lax.dot_general(a, b, dims, preferred_element_type=F32)


def after(value, *earlier):
    return lax.optimization_barrier((value,) + earlier)[0]


def params():
    return pltpu.CompilerParams(vmem_limit_bytes=ROOM)


LIGHT = pl.CostEstimate(flops=1, bytes_accessed=1, transcendentals=0)


def struct(*shape, dtype=BF):
    return jax.ShapeDtypeStruct(shape, dtype)


def whole(array):
    return pl.BlockSpec(array.shape, lambda *_: (0,) * len(array.shape))


def stack_rows(refs, scratch):
    rows = refs[0].shape[0]
    for i, ref in enumerate(refs):
        scratch[i * rows : (i + 1) * rows, :] = ref[...]


def fetch(order_ref, blocks, w_ref, sems):
    deep = blocks[0].shape[0]
    copies = []
    for j, block in enumerate(blocks):
        place = pl.multiple_of(order_ref[j] * deep, deep)
        copies.append(pltpu.make_async_copy(block, w_ref.at[pl.ds(place, deep)], sems.at[j]))
        copies[-1].start()
    return copies


def down_scratch(blocks):
    deep, width = blocks[0].shape
    return [pltpu.VMEM((len(blocks) * deep, width), BF), pltpu.SemaphoreType.DMA((len(blocks),))]


def fetch_each(blocks, w_ref, sems):
    copies = []
    for j, block in enumerate(blocks):
        copies.append(pltpu.make_async_copy(block, w_ref.at[j], sems.at[j]))
        copies[-1].start()
    return copies


def each_scratch(blocks):
    return [
        pltpu.VMEM((len(blocks),) + blocks[0].shape, BF),
        pltpu.SemaphoreType.DMA((len(blocks),)),
    ]


def expert(order, rows_s, rows_x, w_gu, w_down):
    rows = rows_s.shape[0]
    depth, width = w_gu[0].shape
    deep, wide = w_down[0].shape
    half = width // 2
    m = len(w_gu)
    step = 512 if wide % 512 == 0 else wide

    def body(order_ref, s_ref, x_ref, *refs):
        gu_in, dn_in, rest = refs[:m], refs[m : 2 * m], refs[2 * m :]
        back_ref, hid_ref, d_ref, acc, gu_ref, gu_sems, dn_ref, dn_sems = rest
        gu_copies = fetch_each(gu_in, gu_ref, gu_sems)
        dn_copies = fetch(order_ref, dn_in, dn_ref, dn_sems)
        for j, copy in enumerate(gu_copies):
            copy.wait()
            found = mm(x_ref[:, j * depth : (j + 1) * depth], gu_ref[j])
            if j == 0:
                acc[...] = found
            else:
                acc[...] += found
        g = acc[:, :half]
        u = acc[:, half:]
        s = jax.nn.sigmoid(g)
        hid_ref[...] = (g * s * u).astype(BF)
        for copy in dn_copies:
            copy.wait()
        d_hidden = mm(s_ref[...], dn_ref[...], NT)
        d_ref[:, :half] = (d_hidden * u * s * (1.0 + g * (1.0 - s))).astype(BF)
        d_ref[:, half:] = (d_hidden * g * s).astype(BF)
        for j in range(m):
            at = wide + j * depth
            back_ref[:, at : at + depth] = mm(d_ref[...], gu_ref[j], NT).astype(BF)
        for c in range(0, wide, step):
            back_ref[:, c : c + step] = mm(hid_ref[...], dn_ref[:, c : c + step]).astype(BF)

    return pl.pallas_call(
        body,
        in_specs=[SMEM, INSIDE, INSIDE] + [ANYWHERE] * (2 * m),
        out_specs=[INSIDE] * 3,
        out_shape=[struct(rows, 2 * wide), struct(rows, half), struct(rows, width)],
        scratch_shapes=[pltpu.VMEM((rows, width), F32)]
        + each_scratch(w_gu)
        + down_scratch(w_down),
        compiler_params=params(),
        cost_estimate=LIGHT,
        name="expert",
    )(order, rows_s, rows_x, *w_gu, *w_down)


def gate_up_grads(xs, ds, k, wide, scale, received):
    n, rows, width = len(xs), xs[0].shape[0], ds[0].shape[1]
    step = 512 if width % 512 == 0 else width
    extra = [] if received is None else [received]
    if wide % 128 != 0:
        xs, k = [x[:, k * wide : (k + 1) * wide] for x in xs], 0

    def body(*refs):
        x_refs, d_refs, rest = refs[:n], refs[n : 2 * n], refs[2 * n :]
        out_ref, x_scr, d_scr = rest[-3:]

        @pl.when(pl.program_id(0) == 0)
        def _():
            stack_rows(x_refs, x_scr)

        stack_rows(d_refs, d_scr)
        found = mm(x_scr[...], d_scr[...], TN) * scale
        if extra:
            found = found + rest[0][...].astype(F32)
        out_ref[...] = found.astype(BF)

    shape = struct(wide, width)
    column = lambda i: (0, i)
    return pl.pallas_call(
        body,
        grid=(width // step,),
        in_specs=[pl.BlockSpec((rows, wide), lambda i: (0, k))] * n
        + [pl.BlockSpec((rows, step), column)] * n
        + [pl.BlockSpec((wide, step), column)] * len(extra),
        out_specs=pl.BlockSpec((wide, step), column),
        out_shape=shape,
        scratch_shapes=[pltpu.VMEM((n * rows, wide), BF), pltpu.VMEM((n * rows, step), BF)],
        compiler_params=params(),
        cost_estimate=LIGHT,
        name="gate_up_grads",
    )(*xs, *ds, *extra)


def down_grads(order, hidden, rows_s, wide, count, scale):
    rows, half = hidden.shape
    deep = half // count
    step = 512 if wide % 512 == 0 else wide

    def body(order_ref, h_ref, s_ref, *refs):
        outs, scratch = refs[:count], refs[count]
        scratch[...] = mm(h_ref[...], s_ref[...], TN) * scale
        for j in range(count):
            place = pl.multiple_of(order_ref[j] * deep, deep)
            outs[j][...] = scratch[pl.ds(place, deep), :].astype(BF)

    shapes = [struct(deep, wide)] * count
    return pl.pallas_call(
        body,
        grid=(wide // step,),
        in_specs=[SMEM, whole(hidden), pl.BlockSpec((rows, step), lambda i: (0, i))],
        out_specs=[pl.BlockSpec((deep, step), lambda i: (0, i))] * count,
        out_shape=shapes,
        scratch_shapes=[pltpu.VMEM((half, step), F32)],
        compiler_params=params(),
        cost_estimate=LIGHT,
        name="down_grads",
    )(order, hidden, rows_s)


def land(pick, rows):
    count, wide = pick.shape[1], rows.shape[1]
    step = 512 if wide % 512 == 0 else wide

    def body(pick_ref, in_ref, out_ref):
        out_ref[...] = mm(pick_ref[...], in_ref[...], TN).astype(BF)

    return pl.pallas_call(
        body,
        grid=(wide // step,),
        in_specs=[whole(pick), pl.BlockSpec((rows.shape[0], step), lambda i: (0, i))],
        out_specs=pl.BlockSpec((count, step), lambda i: (0, i)),
        out_shape=struct(count, wide),
        compiler_params=params(),
        cost_estimate=HEAVY,
        name="land",
    )(pick, rows)


def popular_partials(select, packed, weights, hid):
    parts, count = select.shape[:2]
    narrow = packed.shape[1] // (2 * parts)
    columns = sum(w.shape[0] for w in weights)

    def body(sel_ref, in_ref, *refs):
        w_refs, (x_ref, s_ref, p_ref) = refs[: len(weights)], refs[len(weights) :]
        x = None
        s = None
        for q in range(parts):
            rows = mm(sel_ref[q], in_ref[...])
            one = rows[:, q * narrow : (q + 1) * narrow]
            two = rows[:, (parts + q) * narrow : (parts + q + 1) * narrow]
            x = one if x is None else x + one
            s = two if s is None else s + two
        x = x.astype(BF)
        s = s.astype(BF)
        x_ref[...] = x
        s_ref[...] = s
        at = 0
        for w_ref in w_refs:
            for top in range(0, w_ref.shape[0], 3 * hid):
                p_ref[:, at : at + 2 * hid] = mm(x, w_ref[top : top + 2 * hid, :], NT).astype(BF)
                p_ref[:, at + 2 * hid : at + 3 * hid] = mm(
                    s, w_ref[top + 2 * hid : top + 3 * hid, :], NT
                ).astype(BF)
                at += 3 * hid

    return pl.pallas_call(
        body,
        in_specs=[INSIDE] * (2 + len(weights)),
        out_specs=[INSIDE] * 3,
        out_shape=[
            struct(count, narrow),
            struct(count, narrow),
            struct(count, columns),
        ],
        compiler_params=params(),
        cost_estimate=LIGHT,
        name="popular_partials",
    )(select, packed, *weights)


def popular_middle(own, others, hid):
    rows, columns = own.shape

    def body(own_ref, *refs):
        parts, out_ref = refs[:-1], refs[-1]
        act = own_ref[...].astype(F32)
        for part in parts:
            act = act + part[...].astype(F32)
        for at in range(0, columns, 3 * hid):
            g = act[:, at : at + hid]
            u = act[:, at + hid : at + 2 * hid]
            dh = act[:, at + 2 * hid : at + 3 * hid]
            s = jax.nn.sigmoid(g)
            out_ref[:, at : at + hid] = (dh * u * s * (1.0 + g * (1.0 - s))).astype(BF)
            out_ref[:, at + hid : at + 2 * hid] = (dh * g * s).astype(BF)
            out_ref[:, at + 2 * hid : at + 3 * hid] = (g * s * u).astype(BF)

    return pl.pallas_call(
        body,
        in_specs=[INSIDE] * (1 + len(others)),
        out_specs=INSIDE,
        out_shape=struct(rows, columns),
        compiler_params=params(),
        cost_estimate=LIGHT,
        name="popular_middle",
    )(own, *others)


def popular_back(select, lines, x, s, weights, hid, scale):
    parts, count, spots = select.shape
    narrow = x.shape[1]
    m = len(weights)
    n = len(lines)
    columns = lines[0].shape[1]

    def body(sel_ref, x_ref, s_ref, *refs):
        ins, w_refs, back_ref = refs[:n], refs[n : n + m], refs[n + m]
        grads, mid_ref = refs[n + m + 1 : -1], refs[-1]
        stack_rows(ins, mid_ref)
        grad = None
        out = None
        at = 0
        for w_ref, g_ref in zip(w_refs, grads):
            for top in range(0, w_ref.shape[0], 3 * hid):
                d_gate = mid_ref[:, at : at + hid]
                d_up = mid_ref[:, at + hid : at + 2 * hid]
                hidden = mid_ref[:, at + 2 * hid : at + 3 * hid]
                sides = ((d_gate, x_ref), (d_up, x_ref), (hidden, s_ref))
                for i, (left, right) in enumerate(sides):
                    here = slice(top + i * hid, top + (i + 1) * hid)
                    product = mm(left, w_ref[here, :])
                    if i == 2:
                        out = product if out is None else out + product
                    else:
                        grad = product if grad is None else grad + product
                    g_ref[here, :] = (mm(left, right[...], TN) * scale).astype(BF)
                at += 3 * hid
        grad = grad.astype(BF)
        out = out.astype(BF)
        for q in range(parts):
            back_ref[:, q * narrow : (q + 1) * narrow] = mm(sel_ref[q], grad, TN).astype(BF)
            back_ref[:, (parts + q) * narrow : (parts + q + 1) * narrow] = mm(
                sel_ref[q], out, TN
            ).astype(BF)

    return pl.pallas_call(
        body,
        in_specs=[INSIDE] * (3 + n + m),
        out_specs=[INSIDE] * (1 + m),
        out_shape=[struct(spots, 2 * parts * narrow)]
        + [struct(w.shape[0], narrow) for w in weights],
        scratch_shapes=[pltpu.VMEM((count, columns), BF)],
        compiler_params=params(),
        cost_estimate=LIGHT,
        name="popular_back",
    )(select, x, s, *lines, *weights)


def slot_positions(route_block, count):
    flat = route_block.reshape(-1)
    onehot = (flat[:, None] == jnp.arange(count, dtype=jnp.int32)[None, :]).astype(jnp.int32)
    before = jnp.cumsum(onehot, axis=0) - onehot
    return (flat, jnp.sum(before * onehot, axis=1))


def exchange(blocks):
    return lax.all_to_all(blocks, "expert", split_axis=0, concat_axis=0, tiled=True)


def local(
    tokens, cotangent, routes, gates, hot_index, hot_gate, w_gate_up, w_down, w_hot_gu, w_hot_dn
):
    owners = lax.axis_size("expert")
    groups = lax.axis_size("dp")
    cores = 2 if groups % 2 == 0 else 1
    chips = groups // cores
    tok_dev, width_d = tokens.shape
    topk = routes.shape[1]
    slots = max(2, 3 * tok_dev * topk // (2 * owners))
    entries = tok_dev * topk
    rows = owners * slots
    inverse = 1.0 / (4 * groups)
    me = lax.axis_index("dp")
    chip, core = me // cores, me % cores

    def shift(value, r):
        pairs = [
            (i, ((i // cores + r) % chips) * cores + i % cores) for i in range(groups)
        ]
        return lax.ppermute(value, "dp", pairs)

    def swap(value):
        pairs = [(i, (i // cores) * cores + (i + 1) % cores) for i in range(groups)]
        return lax.ppermute(value, "dp", pairs)

    order = jnp.stack(
        [
            ((chip - r) % chips) * cores + (core + k) % cores
            for k in range(cores)
            for r in range(chips)
        ]
    ).astype(jnp.int32)

    across = 1
    while 2 * (2 * across) ** 2 <= owners:
        across *= 2
    depths = owners // across
    spot = lax.axis_index("expert")

    def hop(value, j):
        return lax.ppermute(value, "expert", [(i, i ^ j) for i in range(owners)])

    wide = width_d // groups
    hid = w_hot_dn.shape[0]
    narrow = width_d // owners
    hot_w = jnp.concatenate([w_hot_gu, w_hot_dn[None]], axis=0).reshape(3 * hid, narrow)
    hot_near = [hot_w] + [shift(hot_w, r) for r in range(1, chips)]
    down_own = after(w_down[0], hot_near[-1])
    gu_own = after(w_gate_up[0], hot_near[-1])
    gu_near = [w_gate_up[0]] + [shift(gu_own, r) for r in range(1, chips)]
    down_near = [w_down[0]] + [shift(down_own, r) for r in range(1, chips)]
    gu_far = [swap(w_gate_up[0])] if cores == 2 else []
    down_far = [swap(w_down[0])] if cores == 2 else []

    flat, pos = slot_positions(routes, owners)
    dest = flat * slots + pos
    slot_ids = jnp.arange(rows, dtype=jnp.int32)[:, None]
    pick = (slot_ids == dest[None, :]).astype(BF)

    def as_rows(value, width):
        value = value.reshape(owners, -1)
        spare = -value.shape[1] % width
        return jnp.pad(value, ((0, 0), (0, spare))).reshape(owners, -1, width)

    hot_dev = hot_index.shape[0]
    few = 2 * hot_dev // PIECES
    hot_pick = (
        hot_index[:, None] == jnp.arange(tok_dev, dtype=jnp.int32)[None, :]
    ).astype(BF)
    hot_x = mm(hot_pick, tokens).astype(BF)
    hot_s = (hot_gate[:, None] * mm(hot_pick, cotangent)).astype(BF)
    hot_send = jnp.concatenate([hot_x, hot_s], axis=0).reshape(PIECES, few, owners, narrow)
    hot_send = hot_send.transpose(2, 1, 0, 3).reshape(owners * few, PIECES * narrow)
    packed_id = jnp.arange(owners * few, dtype=jnp.int32)
    turn = ((packed_id ^ (spot * few))[:, None] == packed_id[None, :]).astype(BF)
    row = jnp.arange(owners * hot_dev, dtype=jnp.int32)
    step = row // hot_dev
    piece = (row % hot_dev) // few

    def selection(index):
        hit = (index * few + row % few)[:, None] == packed_id[None, :]
        return jnp.stack([hit & (piece == q)[:, None] for q in range(PIECES // 2)]).astype(BF)

    hot_send = mm(turn, hot_send).astype(BF).reshape(depths, across, few, PIECES * narrow)
    near = [hot_send[0]] + [hop(hot_send[j], j * across) for j in range(1, depths)]
    near = jnp.stack(near, axis=1)
    hot_recv = jnp.concatenate([near[0]] + [hop(near[j], j) for j in range(1, across)])
    hot_recv = hot_recv.reshape(owners * few, PIECES * narrow)

    scaled = (gates[:, :, None] * cotangent[:, None, :].astype(F32)).astype(BF)
    send_s = mm(pick, scaled.reshape(entries, width_d)).astype(BF)
    rows_s = exchange(send_s.reshape(owners, slots, width_d)).reshape(rows, width_d)

    tok_rel = jnp.concatenate(
        [
            lax.dynamic_slice_in_dim(tokens, order[j] * wide, wide, 1)
            for j in range(groups)
        ],
        axis=1,
    )
    tok_rel = jnp.repeat(tok_rel, topk, axis=0) if topk > 1 else tok_rel
    send_x = mm(pick, tok_rel).astype(BF).reshape(owners, slots, width_d)
    rows_x = exchange(send_x).reshape(rows, width_d)

    hot_near = jnp.concatenate(list(after(tuple(hot_near), send_x)), axis=0)
    hot_ws = [hot_near] + ([swap(hot_near)] if cores == 2 else [])
    hot_x, hot_s, partial = popular_partials(selection(step), hot_recv, hot_ws, hid)
    share = depths * hot_dev
    level_in = [hop(partial[j * share : (j + 1) * share], j) for j in range(1, across)]
    if cores == 2:
        gu_near = list(after(tuple(gu_near), rows_x))
        gu_far = gu_far + [swap(block) for block in gu_near[1:]]
    level_in = list(after(tuple(level_in), rows_s, *gu_far[:1], *down_far[:1]))
    level = partial[:share].astype(F32)
    for value in level_in:
        level = level + value.astype(F32)
    level = level.astype(BF)
    level = [level[j * hot_dev : (j + 1) * hot_dev] for j in range(depths)]
    depth_in = [hop(level[j], j * across) for j in range(1, depths)]
    rows_x = after(rows_x, *depth_in)
    hot_own = popular_middle(level[0], depth_in, hid)
    line = [hot_own] + [hop(hot_own, j * across) for j in range(1, depths)]
    down_near = list(after(tuple(down_near), hot_own))
    if cores == 2:
        down_far = down_far + [swap(block) for block in down_near[1:]]
    back, hidden, d_act = expert(order, rows_s, after(rows_x, hot_own), gu_near + gu_far, down_near + down_far)

    def columns_of(r):
        return jnp.concatenate(
            [
                rows_x[:, (k * chips + r) * wide : (k * chips + r + 1) * wide]
                for k in range(cores)
            ],
            axis=1,
        )

    xs = [columns_of(0)] + [shift(columns_of(r), -r) for r in range(1, chips)]
    ds = [d_act] + [shift(d_act, -r) for r in range(1, chips)]
    back = after(back, *line[1:])
    back = exchange(back.reshape(owners, slots, 2 * width_d)).reshape(rows, 2 * width_d)

    line = jnp.concatenate(list(after(tuple(line), d_act)))
    lines = [line] + [hop(line, j) for j in range(1, across)]
    hot_back, *hot_grads = popular_back(
        selection(step), lines, hot_x, hot_s, hot_ws, hid, inverse
    )

    dn_parts = down_grads(order, hidden, rows_s, width_d, groups, inverse)
    dn_sum = list(dn_parts[:chips])
    if cores == 2:
        dn_in = [swap(part) for part in dn_parts[chips:]]
        dn_sum = [
            (one.astype(F32) + two.astype(F32)).astype(BF) for one, two in zip(dn_sum, dn_in)
        ]
    dn_total = dn_sum[0].astype(F32)
    dn_recv = [shift(dn_sum[r], -r) for r in range(1, chips)]
    for value in dn_recv:
        dn_total = dn_total + value.astype(F32)
    grad_dn = dn_total.astype(BF)

    hot_back = hot_back.reshape(across, depths, few, PIECES * narrow)
    hot_back = [hot_back[0]] + [hop(hot_back[j], j) for j in range(1, across)]
    hot_back = jnp.stack(hot_back, axis=1)
    xs_late = list(after(tuple(xs), d_act))
    gu_in = None
    if cores == 2:
        gu_in = swap(gate_up_grads(xs_late, ds, 1, wide, inverse, None))

    hot_sum = hot_grads[0]
    if cores == 2:
        hot_sum = after(hot_sum, dn_in[0])
    if cores == 2:
        hot_sum = (hot_sum.astype(F32) + swap(hot_grads[1]).astype(F32)).astype(BF)
    hot_sum = hot_sum.reshape(chips, 3 * hid, narrow)
    hot_total = hot_sum[0].astype(F32)
    hot_far = [shift(hot_sum[r], -r) for r in range(1, chips)]
    for value in hot_far:
        hot_total = hot_total + value.astype(F32)
    grad_hot = hot_total.astype(BF).reshape(3, hid, narrow)
    xs_last = list(after(tuple(xs_late), *hot_far, *dn_recv))
    grad_gu = gate_up_grads(xs_last, ds, 0, wide, inverse, gu_in)

    if cores == 2:
        hot_back = after(hot_back, gu_in)
    hot_back = [hot_back[0]] + [hop(hot_back[j], j * across) for j in range(1, depths)]
    hot_back = list(after(tuple(hot_back), grad_gu))
    hot_back = jnp.concatenate(hot_back).reshape(owners * few, PIECES * narrow)
    hot_back = mm(turn, hot_back).astype(BF)

    hot_back = hot_back.reshape(owners, few, PIECES, narrow)
    hot_back = hot_back.transpose(2, 1, 0, 3).reshape(2, hot_dev, width_d)
    landed = land(pick, back).astype(F32)
    picked = landed[:, :width_d]
    layer_out = (
        (gates.reshape(entries)[:, None] * picked).reshape(tok_dev, topk, width_d).sum(axis=1)
    )
    token_gate = jnp.sum(jnp.where(hot_pick > 0, hot_gate[:, None], 0.0), axis=0)
    layer_out = layer_out + token_gate[:, None] * mm(hot_pick, hot_back[1], TN)
    returned = landed[:, width_d:]
    returned = returned.reshape(tok_dev, topk, width_d).sum(axis=1)
    blocks = jnp.stack([returned[:, j * wide : (j + 1) * wide] for j in range(groups)])
    input_grad = jnp.concatenate(
        [
            lax.dynamic_index_in_dim(
                blocks,
                ((q - core) % cores) * chips + (chip - p) % chips,
                0,
                keepdims=False,
            )
            for p in range(chips)
            for q in range(cores)
        ],
        axis=1,
    )
    input_grad = input_grad + mm(hot_pick, hot_back[0], TN)
    return (
        layer_out.astype(BF),
        input_grad.astype(BF),
        grad_gu[None],
        grad_dn[None],
        grad_hot[:2],
        grad_hot[2],
    )


def solution(mesh):
    tok = P(("dp", "expert"), None)
    flat = P(("dp", "expert"))
    rows = P("expert", "dp", None)
    hot = (P(None, "dp", "expert"), P("dp", "expert"))
    return jax.shard_map(
        local,
        mesh=mesh,
        in_specs=(tok, tok, tok, tok, flat, flat, rows, rows) + hot,
        out_specs=(tok, tok, rows, rows) + hot,
        check_vma=False,
    )
```

```python
import jax
import jax.numpy as jnp
from jax import lax
from jax.experimental import pallas as pl
from jax.experimental.pallas import tpu as pltpu
from jax.sharding import PartitionSpec as P

BF = jnp.bfloat16
F32 = jnp.float32
NN = (((1,), (0,)), ((), ()))
NT = (((1,), (1,)), ((), ()))
TN = (((0,), (0,)), ((), ()))
ROOM = 56 * 1024 * 1024
LIGHT = pl.CostEstimate(flops=1, bytes_accessed=1, transcendentals=0)
SMEM = pl.BlockSpec(memory_space=pltpu.SMEM)
ANYWHERE = pl.BlockSpec(memory_space=pl.ANY)
INSIDE = pl.BlockSpec(memory_space=pltpu.VMEM)
PIECES = 8


def mm(a, b, dims=NN):
    return lax.dot_general(a, b, dims, preferred_element_type=F32)


def after(value, *earlier):
    return lax.optimization_barrier((value,) + earlier)[0]


def params():
    return pltpu.CompilerParams(vmem_limit_bytes=ROOM)


LIGHT = pl.CostEstimate(flops=1, bytes_accessed=1, transcendentals=0)


def struct(*shape, dtype=BF):
    return jax.ShapeDtypeStruct(shape, dtype)


def whole(array):
    return pl.BlockSpec(array.shape, lambda *_: (0,) * len(array.shape))


def stack_rows(refs, scratch):
    rows = refs[0].shape[0]
    for i, ref in enumerate(refs):
        scratch[i * rows : (i + 1) * rows, :] = ref[...]


def fetch(order_ref, blocks, w_ref, sems):
    deep = blocks[0].shape[0]
    copies = []
    for j, block in enumerate(blocks):
        place = pl.multiple_of(order_ref[j] * deep, deep)
        copies.append(pltpu.make_async_copy(block, w_ref.at[pl.ds(place, deep)], sems.at[j]))
        copies[-1].start()
    return copies


def down_scratch(blocks):
    deep, width = blocks[0].shape
    return [pltpu.VMEM((len(blocks) * deep, width), BF), pltpu.SemaphoreType.DMA((len(blocks),))]


def fetch_each(blocks, w_ref, sems):
    copies = []
    for j, block in enumerate(blocks):
        copies.append(pltpu.make_async_copy(block, w_ref.at[j], sems.at[j]))
        copies[-1].start()
    return copies


def each_scratch(blocks):
    return [
        pltpu.VMEM((len(blocks),) + blocks[0].shape, BF),
        pltpu.SemaphoreType.DMA((len(blocks),)),
    ]


def expert(order, rows_s, rows_x, w_gu, w_down):
    rows = rows_s.shape[0]
    depth, width = w_gu[0].shape
    deep, wide = w_down[0].shape
    half = width // 2
    m = len(w_gu)
    step = 512 if wide % 512 == 0 else wide

    def body(order_ref, s_ref, x_ref, *refs):
        gu_in, dn_in, rest = refs[:m], refs[m : 2 * m], refs[2 * m :]
        back_ref, hid_ref, d_ref, acc, gu_ref, gu_sems, dn_ref, dn_sems = rest
        gu_copies = fetch_each(gu_in, gu_ref, gu_sems)
        dn_copies = fetch(order_ref, dn_in, dn_ref, dn_sems)
        for j, copy in enumerate(gu_copies):
            copy.wait()
            found = mm(x_ref[:, j * depth : (j + 1) * depth], gu_ref[j])
            if j == 0:
                acc[...] = found
            else:
                acc[...] += found
        g = acc[:, :half]
        u = acc[:, half:]
        s = jax.nn.sigmoid(g)
        hid_ref[...] = (g * s * u).astype(BF)
        for copy in dn_copies:
            copy.wait()
        d_hidden = mm(s_ref[...], dn_ref[...], NT)
        d_ref[:, :half] = (d_hidden * u * s * (1.0 + g * (1.0 - s))).astype(BF)
        d_ref[:, half:] = (d_hidden * g * s).astype(BF)
        for j in range(m):
            at = wide + j * depth
            back_ref[:, at : at + depth] = mm(d_ref[...], gu_ref[j], NT).astype(BF)
        for c in range(0, wide, step):
            back_ref[:, c : c + step] = mm(hid_ref[...], dn_ref[:, c : c + step]).astype(BF)

    return pl.pallas_call(
        body,
        in_specs=[SMEM, INSIDE, INSIDE] + [ANYWHERE] * (2 * m),
        out_specs=[INSIDE] * 3,
        out_shape=[struct(rows, 2 * wide), struct(rows, half), struct(rows, width)],
        scratch_shapes=[pltpu.VMEM((rows, width), F32)]
        + each_scratch(w_gu)
        + down_scratch(w_down),
        compiler_params=params(),
        cost_estimate=LIGHT,
        name="expert",
    )(order, rows_s, rows_x, *w_gu, *w_down)


def gate_up_grads(xs, ds, k, wide, scale, received):
    n, rows, width = len(xs), xs[0].shape[0], ds[0].shape[1]
    step = 512 if width % 512 == 0 else width
    extra = [] if received is None else [received]
    if wide % 128 != 0:
        xs, k = [x[:, k * wide : (k + 1) * wide] for x in xs], 0

    def body(*refs):
        x_refs, d_refs, rest = refs[:n], refs[n : 2 * n], refs[2 * n :]
        out_ref, x_scr, d_scr = rest[-3:]

        @pl.when(pl.program_id(0) == 0)
        def _():
            stack_rows(x_refs, x_scr)

        stack_rows(d_refs, d_scr)
        found = mm(x_scr[...], d_scr[...], TN) * scale
        if extra:
            found = found + rest[0][...].astype(F32)
        out_ref[...] = found.astype(BF)

    shape = struct(wide, width)
    column = lambda i: (0, i)
    return pl.pallas_call(
        body,
        grid=(width // step,),
        in_specs=[pl.BlockSpec((rows, wide), lambda i: (0, k))] * n
        + [pl.BlockSpec((rows, step), column)] * n
        + [pl.BlockSpec((wide, step), column)] * len(extra),
        out_specs=pl.BlockSpec((wide, step), column),
        out_shape=shape,
        scratch_shapes=[pltpu.VMEM((n * rows, wide), BF), pltpu.VMEM((n * rows, step), BF)],
        compiler_params=params(),
        cost_estimate=LIGHT,
        name="gate_up_grads",
    )(*xs, *ds, *extra)


def down_grads(order, hidden, rows_s, wide, count, share, scale):
    rows, half = hidden.shape
    deep = half // count
    step = 512 if wide % 512 == 0 else wide

    def body(order_ref, h_ref, s_ref, *refs):
        outs, scratch = refs[:-1], refs[-1]
        scratch[...] = mm(h_ref[...], s_ref[...], TN) * scale
        for j in range(count):
            place = pl.multiple_of(order_ref[j] * deep, deep)
            at = j % share * deep
            block = scratch[pl.ds(place, deep), :].astype(BF)
            outs[j // share][at : at + deep, :] = block

    shapes = [struct(share * deep, wide)] * (count // share)
    return pl.pallas_call(
        body,
        grid=(wide // step,),
        in_specs=[SMEM, whole(hidden), pl.BlockSpec((rows, step), lambda i: (0, i))],
        out_specs=[pl.BlockSpec((share * deep, step), lambda i: (0, i))] * (count // share),
        out_shape=shapes,
        scratch_shapes=[pltpu.VMEM((half, step), F32)],
        compiler_params=params(),
        cost_estimate=LIGHT,
        name="down_grads",
    )(order, hidden, rows_s)


def popular_partials(select, packed, weights, hid):
    parts, count = select.shape[:2]
    narrow = packed.shape[1] // (2 * parts)
    columns = sum(w.shape[0] for w in weights)

    def body(sel_ref, in_ref, *refs):
        w_refs, (x_ref, s_ref, p_ref) = refs[: len(weights)], refs[len(weights) :]
        x = None
        s = None
        for q in range(parts):
            rows = mm(sel_ref[q], in_ref[...])
            one = rows[:, q * narrow : (q + 1) * narrow]
            two = rows[:, (parts + q) * narrow : (parts + q + 1) * narrow]
            x = one if x is None else x + one
            s = two if s is None else s + two
        x = x.astype(BF)
        s = s.astype(BF)
        x_ref[...] = x
        s_ref[...] = s
        at = 0
        for w_ref in w_refs:
            for top in range(0, w_ref.shape[0], 3 * hid):
                p_ref[:, at : at + 2 * hid] = mm(x, w_ref[top : top + 2 * hid, :], NT).astype(BF)
                p_ref[:, at + 2 * hid : at + 3 * hid] = mm(
                    s, w_ref[top + 2 * hid : top + 3 * hid, :], NT
                ).astype(BF)
                at += 3 * hid

    return pl.pallas_call(
        body,
        in_specs=[INSIDE] * (2 + len(weights)),
        out_specs=[INSIDE] * 3,
        out_shape=[
            struct(count, narrow),
            struct(count, narrow),
            struct(count, columns),
        ],
        compiler_params=params(),
        cost_estimate=LIGHT,
        name="popular_partials",
    )(select, packed, *weights)


def popular_middle(own, others, hid):
    rows, columns = own.shape

    def body(own_ref, *refs):
        parts, out_ref = refs[:-1], refs[-1]
        act = own_ref[...].astype(F32)
        for part in parts:
            act = act + part[...].astype(F32)
        for at in range(0, columns, 3 * hid):
            g = act[:, at : at + hid]
            u = act[:, at + hid : at + 2 * hid]
            dh = act[:, at + 2 * hid : at + 3 * hid]
            s = jax.nn.sigmoid(g)
            out_ref[:, at : at + hid] = (dh * u * s * (1.0 + g * (1.0 - s))).astype(BF)
            out_ref[:, at + hid : at + 2 * hid] = (dh * g * s).astype(BF)
            out_ref[:, at + 2 * hid : at + 3 * hid] = (g * s * u).astype(BF)

    return pl.pallas_call(
        body,
        in_specs=[INSIDE] * (1 + len(others)),
        out_specs=INSIDE,
        out_shape=struct(rows, columns),
        compiler_params=params(),
        cost_estimate=LIGHT,
        name="popular_middle",
    )(own, *others)


def popular_back(select, lines, x, s, weights, hid, scale):
    parts, count, spots = select.shape
    narrow = x.shape[1]
    m = len(weights)
    n = len(lines)
    columns = lines[0].shape[1]

    def body(sel_ref, x_ref, s_ref, *refs):
        ins, w_refs, back_ref = refs[:n], refs[n : n + m], refs[n + m]
        grads, mid_ref = refs[n + m + 1 : -1], refs[-1]
        stack_rows(ins, mid_ref)
        grad = None
        out = None
        at = 0
        for w_ref, g_ref in zip(w_refs, grads):
            for top in range(0, w_ref.shape[0], 3 * hid):
                d_gate = mid_ref[:, at : at + hid]
                d_up = mid_ref[:, at + hid : at + 2 * hid]
                hidden = mid_ref[:, at + 2 * hid : at + 3 * hid]
                sides = ((d_gate, x_ref), (d_up, x_ref), (hidden, s_ref))
                for i, (left, right) in enumerate(sides):
                    here = slice(top + i * hid, top + (i + 1) * hid)
                    product = mm(left, w_ref[here, :])
                    if i == 2:
                        out = product if out is None else out + product
                    else:
                        grad = product if grad is None else grad + product
                    g_ref[here, :] = (mm(left, right[...], TN) * scale).astype(BF)
                at += 3 * hid
        grad = grad.astype(BF)
        out = out.astype(BF)
        for q in range(parts):
            back_ref[:, q * narrow : (q + 1) * narrow] = mm(sel_ref[q], grad, TN).astype(BF)
            back_ref[:, (parts + q) * narrow : (parts + q + 1) * narrow] = mm(
                sel_ref[q], out, TN
            ).astype(BF)

    return pl.pallas_call(
        body,
        in_specs=[INSIDE] * (3 + n + m),
        out_specs=[INSIDE] * (1 + m),
        out_shape=[struct(spots, 2 * parts * narrow)]
        + [struct(w.shape[0], narrow) for w in weights],
        scratch_shapes=[pltpu.VMEM((count, columns), BF)],
        compiler_params=params(),
        cost_estimate=LIGHT,
        name="popular_back",
    )(select, x, s, *lines, *weights)


def slot_positions(route_block, count):
    flat = route_block.reshape(-1)
    onehot = (flat[:, None] == jnp.arange(count, dtype=jnp.int32)[None, :]).astype(jnp.int32)
    before = jnp.cumsum(onehot, axis=0) - onehot
    return (flat, jnp.sum(before * onehot, axis=1))


def exchange(blocks):
    return lax.all_to_all(blocks, "expert", split_axis=0, concat_axis=0, tiled=True)


def local(
    tokens, cotangent, routes, gates, hot_index, hot_gate, w_gate_up, w_down, w_hot_gu, w_hot_dn
):
    owners = lax.axis_size("expert")
    groups = lax.axis_size("dp")
    cores = 2 if groups % 2 == 0 else 1
    chips = groups // cores
    tok_dev, width_d = tokens.shape
    topk = routes.shape[1]
    slots = max(2, 3 * tok_dev * topk // (2 * owners))
    entries = tok_dev * topk
    rows = owners * slots
    inverse = 1.0 / (4 * groups)
    me = lax.axis_index("dp")
    chip, core = me // cores, me % cores

    def shift(value, r):
        pairs = [
            (i, ((i // cores + r) % chips) * cores + i % cores) for i in range(groups)
        ]
        return lax.ppermute(value, "dp", pairs)

    def swap(value):
        pairs = [(i, (i // cores) * cores + (i + 1) % cores) for i in range(groups)]
        return lax.ppermute(value, "dp", pairs)

    order = jnp.stack(
        [
            ((chip - r) % chips) * cores + (core + k) % cores
            for k in range(cores)
            for r in range(chips)
        ]
    ).astype(jnp.int32)

    across = 1
    while 2 * (2 * across) ** 2 <= owners:
        across *= 2
    depths = owners // across
    spot = lax.axis_index("expert")

    def hop(value, j):
        return lax.ppermute(value, "expert", [(i, i ^ j) for i in range(owners)])

    wide = width_d // groups
    hid = w_hot_dn.shape[0]
    narrow = width_d // owners
    hot_w = jnp.concatenate([w_hot_gu, w_hot_dn[None]], axis=0).reshape(3 * hid, narrow)
    hot_near = [hot_w] + [shift(hot_w, r) for r in range(1, chips)]
    down_own = after(w_down[0], hot_near[-1])
    gu_own = after(w_gate_up[0], hot_near[-1])
    gu_near = [w_gate_up[0]] + [shift(gu_own, r) for r in range(1, chips)]
    down_near = [w_down[0]] + [shift(down_own, r) for r in range(1, chips)]

    flat, pos = slot_positions(routes, owners)
    dest = flat * slots + pos
    slot_ids = jnp.arange(rows, dtype=jnp.int32)[:, None]
    pick = (slot_ids == dest[None, :]).astype(BF)

    def as_rows(value, width):
        value = value.reshape(owners, -1)
        spare = -value.shape[1] % width
        return jnp.pad(value, ((0, 0), (0, spare))).reshape(owners, -1, width)

    hot_dev = hot_index.shape[0]
    few = 2 * hot_dev // PIECES
    hot_pick = (
        hot_index[:, None] == jnp.arange(tok_dev, dtype=jnp.int32)[None, :]
    ).astype(BF)
    hot_x = mm(hot_pick, tokens).astype(BF)
    hot_s = (hot_gate[:, None] * mm(hot_pick, cotangent)).astype(BF)
    hot_send = jnp.concatenate([hot_x, hot_s], axis=0).reshape(PIECES, few, owners, narrow)
    hot_send = hot_send.transpose(2, 1, 0, 3).reshape(owners * few, PIECES * narrow)
    packed_id = jnp.arange(owners * few, dtype=jnp.int32)
    turn = ((packed_id ^ (spot * few))[:, None] == packed_id[None, :]).astype(BF)
    row = jnp.arange(owners * hot_dev, dtype=jnp.int32)
    step = row // hot_dev
    piece = (row % hot_dev) // few

    def selection(index):
        hit = (index * few + row % few)[:, None] == packed_id[None, :]
        return jnp.stack([hit & (piece == q)[:, None] for q in range(PIECES // 2)]).astype(BF)

    hot_send = mm(turn, hot_send).astype(BF).reshape(depths, across, few, PIECES * narrow)
    near = [hot_send[0]] + [hop(hot_send[j], j * across) for j in range(1, depths)]
    near = jnp.stack(near, axis=1)
    hot_recv = jnp.concatenate([near[0]] + [hop(near[j], j) for j in range(1, across)])
    hot_recv = hot_recv.reshape(owners * few, PIECES * narrow)

    scaled = (gates[:, :, None] * cotangent[:, None, :].astype(F32)).astype(BF)
    send_s = mm(pick, scaled.reshape(entries, width_d)).astype(BF)
    rows_s = exchange(send_s.reshape(owners, slots, width_d)).reshape(rows, width_d)

    tok_rel = jnp.concatenate(
        [
            lax.dynamic_slice_in_dim(tokens, order[j] * wide, wide, 1)
            for j in range(groups)
        ],
        axis=1,
    )
    tok_rel = jnp.repeat(tok_rel, topk, axis=0) if topk > 1 else tok_rel
    send_x = mm(pick, tok_rel).astype(BF).reshape(owners, slots, width_d)
    rows_x = exchange(send_x).reshape(rows, width_d)

    hot_near = jnp.concatenate(list(after(tuple(hot_near), send_x)), axis=0)
    hot_ws = [hot_near] + ([swap(hot_near)] if cores == 2 else [])
    hot_x, hot_s, partial = popular_partials(selection(step), hot_recv, hot_ws, hid)
    share = depths * hot_dev
    level_in = [hop(partial[j * share : (j + 1) * share], j) for j in range(1, across)]
    gu_far = down_far = []
    if cores == 2:
        gu_near = list(after(tuple(gu_near), rows_x))
        gu_far = [swap(block) for block in gu_near[1:]]
    level_in = list(after(tuple(level_in), rows_s, *gu_near[1:]))
    level = partial[:share].astype(F32)
    for value in level_in:
        level = level + value.astype(F32)
    level = level.astype(BF)
    level = [level[j * hot_dev : (j + 1) * hot_dev] for j in range(depths)]
    depth_in = [hop(level[j], j * across) for j in range(1, depths)]
    rows_x = after(rows_x, *depth_in)
    hot_own = popular_middle(level[0], depth_in, hid)
    line = [hot_own] + [hop(hot_own, j * across) for j in range(1, depths)]
    down_near = list(after(tuple(down_near), hot_own))
    if cores == 2:
        gu_far = [swap(after(w_gate_up[0], hot_own))] + gu_far
        down_far = [swap(block) for block in down_near]
    back, hidden, d_act = expert(order, rows_s, after(rows_x, hot_own), gu_near + gu_far, down_near + down_far)

    def columns_of(r):
        return jnp.concatenate(
            [
                rows_x[:, (k * chips + r) * wide : (k * chips + r + 1) * wide]
                for k in range(cores)
            ],
            axis=1,
        )

    xs = [columns_of(0)] + [shift(columns_of(r), -r) for r in range(1, chips)]
    ds = [d_act] + [shift(d_act, -r) for r in range(1, chips)]
    back = after(back, *line[1:])
    back = exchange(back.reshape(owners, slots, 2 * width_d)).reshape(rows, 2 * width_d)

    line = jnp.concatenate(list(after(tuple(line), d_act)))
    lines = [line] + [hop(line, j) for j in range(1, across)]
    hot_back, *hot_grads = popular_back(
        selection(step), lines, hot_x, hot_s, hot_ws, hid, inverse
    )

    deep = w_down.shape[1]
    dn_parts = down_grads(order, hidden, rows_s, width_d, groups, chips, inverse)
    dn_sum = dn_parts[0]
    if cores == 2:
        dn_sum = (dn_sum.astype(F32) + swap(dn_parts[1]).astype(F32)).astype(BF)
    dn_sum = [dn_sum[r * deep : (r + 1) * deep] for r in range(chips)]
    dn_total = dn_sum[0].astype(F32)
    dn_recv = [shift(dn_sum[r], -r) for r in range(1, chips)]
    for value in dn_recv:
        dn_total = dn_total + value.astype(F32)
    grad_dn = dn_total.astype(BF)

    hot_back = hot_back.reshape(across, depths, few, PIECES * narrow)
    hot_back = [hot_back[0]] + [hop(hot_back[j], j) for j in range(1, across)]
    hot_back = jnp.stack(hot_back, axis=1)
    xs_late = list(after(tuple(xs), d_act))
    gu_in = None
    if cores == 2:
        gu_in = swap(gate_up_grads(xs_late, ds, 1, wide, inverse, None))

    hot_sum = hot_grads[0]
    if cores == 2:
        hot_sum = (hot_sum.astype(F32) + swap(hot_grads[1]).astype(F32)).astype(BF)
    hot_sum = hot_sum.reshape(chips, 3 * hid, narrow)
    hot_total = hot_sum[0].astype(F32)
    hot_far = [shift(hot_sum[r], -r) for r in range(1, chips)]
    for value in hot_far:
        hot_total = hot_total + value.astype(F32)
    grad_hot = hot_total.astype(BF).reshape(3, hid, narrow)
    xs_last = list(after(tuple(xs_late), *hot_far, *dn_recv))
    grad_gu = gate_up_grads(xs_last, ds, 0, wide, inverse, gu_in)

    hot_back = [hot_back[0]] + [hop(hot_back[j], j * across) for j in range(1, depths)]
    hot_back = list(after(tuple(hot_back), grad_gu))
    hot_back = jnp.concatenate(hot_back).reshape(owners * few, PIECES * narrow)
    hot_back = mm(turn, hot_back).astype(BF)

    hot_back = hot_back.reshape(owners, few, PIECES, narrow)
    hot_back = hot_back.transpose(2, 1, 0, 3).reshape(2, hot_dev, width_d)
    landed = mm(pick, back, TN)
    picked = landed[:, :width_d]
    layer_out = (
        (gates.reshape(entries)[:, None] * picked).reshape(tok_dev, topk, width_d).sum(axis=1)
    )
    token_gate = jnp.sum(jnp.where(hot_pick > 0, hot_gate[:, None], 0.0), axis=0)
    layer_out = layer_out + token_gate[:, None] * mm(hot_pick, hot_back[1], TN)
    returned = landed[:, width_d:]
    returned = returned.reshape(tok_dev, topk, width_d).sum(axis=1)
    blocks = jnp.stack([returned[:, j * wide : (j + 1) * wide] for j in range(groups)])
    input_grad = jnp.concatenate(
        [
            lax.dynamic_index_in_dim(
                blocks,
                ((q - core) % cores) * chips + (chip - p) % chips,
                0,
                keepdims=False,
            )
            for p in range(chips)
            for q in range(cores)
        ],
        axis=1,
    )
    input_grad = input_grad + mm(hot_pick, hot_back[0], TN)
    return (
        layer_out.astype(BF),
        input_grad.astype(BF),
        grad_gu[None],
        grad_dn[None],
        grad_hot[:2],
        grad_hot[2],
    )


def solution(mesh):
    tok = P(("dp", "expert"), None)
    flat = P(("dp", "expert"))
    rows = P("expert", "dp", None)
    hot = (P(None, "dp", "expert"), P("dp", "expert"))
    return jax.shard_map(
        local,
        mesh=mesh,
        in_specs=(tok, tok, tok, tok, flat, flat, rows, rows) + hot,
        out_specs=(tok, tok, rows, rows) + hot,
        check_vma=False,
    )
```

```python
import jax
import jax.numpy as jnp
from jax import lax
from jax.experimental import pallas as pl
from jax.experimental.pallas import tpu as pltpu
from jax.sharding import PartitionSpec as P

BF = jnp.bfloat16
F32 = jnp.float32
NN = (((1,), (0,)), ((), ()))
NT = (((1,), (1,)), ((), ()))
TN = (((0,), (0,)), ((), ()))
ROOM = 56 * 1024 * 1024
LIGHT = pl.CostEstimate(flops=1, bytes_accessed=1, transcendentals=0)
SMEM = pl.BlockSpec(memory_space=pltpu.SMEM)
ANYWHERE = pl.BlockSpec(memory_space=pl.ANY)
INSIDE = pl.BlockSpec(memory_space=pltpu.VMEM)
PIECES = 8


def mm(a, b, dims=NN):
    return lax.dot_general(a, b, dims, preferred_element_type=F32)


def after(value, *earlier):
    return lax.optimization_barrier((value,) + earlier)[0]


def params():
    return pltpu.CompilerParams(vmem_limit_bytes=ROOM)


LIGHT = pl.CostEstimate(flops=1, bytes_accessed=1, transcendentals=0)


def struct(*shape, dtype=BF):
    return jax.ShapeDtypeStruct(shape, dtype)


def whole(array):
    return pl.BlockSpec(array.shape, lambda *_: (0,) * len(array.shape))


def stack_rows(refs, scratch):
    rows = refs[0].shape[0]
    for i, ref in enumerate(refs):
        scratch[i * rows : (i + 1) * rows, :] = ref[...]


def fetch(order_ref, blocks, w_ref, sems):
    deep = blocks[0].shape[0]
    copies = []
    for j, block in enumerate(blocks):
        place = pl.multiple_of(order_ref[j] * deep, deep)
        copies.append(pltpu.make_async_copy(block, w_ref.at[pl.ds(place, deep)], sems.at[j]))
        copies[-1].start()
    return copies


def down_scratch(blocks):
    deep, width = blocks[0].shape
    return [pltpu.VMEM((len(blocks) * deep, width), BF), pltpu.SemaphoreType.DMA((len(blocks),))]


def fetch_each(blocks, w_ref, sems):
    copies = []
    for j, block in enumerate(blocks):
        copies.append(pltpu.make_async_copy(block, w_ref.at[j], sems.at[j]))
        copies[-1].start()
    return copies


def each_scratch(blocks):
    return [
        pltpu.VMEM((len(blocks),) + blocks[0].shape, BF),
        pltpu.SemaphoreType.DMA((len(blocks),)),
    ]


def expert(order, rows_s, rows_x, w_gu, w_down):
    rows = rows_s.shape[0]
    depth, width = w_gu[0].shape
    deep, wide = w_down[0].shape
    half = width // 2
    m = len(w_gu)
    step = 512 if wide % 512 == 0 else wide

    def body(order_ref, s_ref, x_ref, *refs):
        gu_in, dn_in, rest = refs[:m], refs[m : 2 * m], refs[2 * m :]
        back_ref, hid_ref, d_ref, acc, gu_ref, gu_sems, dn_ref, dn_sems = rest
        gu_copies = fetch_each(gu_in, gu_ref, gu_sems)
        dn_copies = fetch(order_ref, dn_in, dn_ref, dn_sems)
        for j, copy in enumerate(gu_copies):
            copy.wait()
            found = mm(x_ref[:, j * depth : (j + 1) * depth], gu_ref[j])
            if j == 0:
                acc[...] = found
            else:
                acc[...] += found
        g = acc[:, :half]
        u = acc[:, half:]
        s = jax.nn.sigmoid(g)
        hid_ref[...] = (g * s * u).astype(BF)
        for copy in dn_copies:
            copy.wait()
        d_hidden = mm(s_ref[...], dn_ref[...], NT)
        d_ref[:, :half] = (d_hidden * u * s * (1.0 + g * (1.0 - s))).astype(BF)
        d_ref[:, half:] = (d_hidden * g * s).astype(BF)
        for j in range(m):
            at = wide + j * depth
            back_ref[:, at : at + depth] = mm(d_ref[...], gu_ref[j], NT).astype(BF)
        for c in range(0, wide, step):
            back_ref[:, c : c + step] = mm(hid_ref[...], dn_ref[:, c : c + step]).astype(BF)

    return pl.pallas_call(
        body,
        in_specs=[SMEM, INSIDE, INSIDE] + [ANYWHERE] * (2 * m),
        out_specs=[INSIDE] * 3,
        out_shape=[struct(rows, 2 * wide), struct(rows, half), struct(rows, width)],
        scratch_shapes=[pltpu.VMEM((rows, width), F32)]
        + each_scratch(w_gu)
        + down_scratch(w_down),
        compiler_params=params(),
        cost_estimate=LIGHT,
        name="expert",
    )(order, rows_s, rows_x, *w_gu, *w_down)


def gate_up_grads(xs, ds, k, wide, scale, received):
    n, rows, width = len(xs), xs[0].shape[0], ds[0].shape[1]
    step = 512 if width % 512 == 0 else width
    extra = [] if received is None else [received]
    if wide % 128 != 0:
        xs, k = [x[:, k * wide : (k + 1) * wide] for x in xs], 0

    def body(*refs):
        x_refs, d_refs, rest = refs[:n], refs[n : 2 * n], refs[2 * n :]
        out_ref, x_scr, d_scr = rest[-3:]

        @pl.when(pl.program_id(0) == 0)
        def _():
            stack_rows(x_refs, x_scr)

        stack_rows(d_refs, d_scr)
        found = mm(x_scr[...], d_scr[...], TN) * scale
        if extra:
            found = found + rest[0][...].astype(F32)
        out_ref[...] = found.astype(BF)

    shape = struct(wide, width)
    column = lambda i: (0, i)
    return pl.pallas_call(
        body,
        grid=(width // step,),
        in_specs=[pl.BlockSpec((rows, wide), lambda i: (0, k))] * n
        + [pl.BlockSpec((rows, step), column)] * n
        + [pl.BlockSpec((wide, step), column)] * len(extra),
        out_specs=pl.BlockSpec((wide, step), column),
        out_shape=shape,
        scratch_shapes=[pltpu.VMEM((n * rows, wide), BF), pltpu.VMEM((n * rows, step), BF)],
        compiler_params=params(),
        cost_estimate=LIGHT,
        name="gate_up_grads",
    )(*xs, *ds, *extra)


def down_grads(order, hidden, rows_s, wide, count, scale):
    rows, half = hidden.shape
    deep = half // count
    step = 512 if wide % 512 == 0 else wide

    def body(order_ref, h_ref, s_ref, *refs):
        outs, scratch = refs[:count], refs[count]
        scratch[...] = mm(h_ref[...], s_ref[...], TN) * scale
        for j in range(count):
            place = pl.multiple_of(order_ref[j] * deep, deep)
            outs[j][...] = scratch[pl.ds(place, deep), :].astype(BF)

    shapes = [struct(deep, wide)] * count
    return pl.pallas_call(
        body,
        grid=(wide // step,),
        in_specs=[SMEM, whole(hidden), pl.BlockSpec((rows, step), lambda i: (0, i))],
        out_specs=[pl.BlockSpec((deep, step), lambda i: (0, i))] * count,
        out_shape=shapes,
        scratch_shapes=[pltpu.VMEM((half, step), F32)],
        compiler_params=params(),
        cost_estimate=LIGHT,
        name="down_grads",
    )(order, hidden, rows_s)


def popular_partials(select, packed, weights, hid):
    parts, count = select.shape[:2]
    narrow = packed.shape[1] // (2 * parts)
    columns = sum(w.shape[0] for w in weights)

    def body(sel_ref, in_ref, *refs):
        w_refs, (x_ref, s_ref, p_ref) = refs[: len(weights)], refs[len(weights) :]
        x = None
        s = None
        for q in range(parts):
            rows = mm(sel_ref[q], in_ref[...])
            one = rows[:, q * narrow : (q + 1) * narrow]
            two = rows[:, (parts + q) * narrow : (parts + q + 1) * narrow]
            x = one if x is None else x + one
            s = two if s is None else s + two
        x = x.astype(BF)
        s = s.astype(BF)
        x_ref[...] = x
        s_ref[...] = s
        at = 0
        for w_ref in w_refs:
            for top in range(0, w_ref.shape[0], 3 * hid):
                p_ref[:, at : at + 2 * hid] = mm(x, w_ref[top : top + 2 * hid, :], NT).astype(BF)
                p_ref[:, at + 2 * hid : at + 3 * hid] = mm(
                    s, w_ref[top + 2 * hid : top + 3 * hid, :], NT
                ).astype(BF)
                at += 3 * hid

    return pl.pallas_call(
        body,
        in_specs=[INSIDE] * (2 + len(weights)),
        out_specs=[INSIDE] * 3,
        out_shape=[
            struct(count, narrow),
            struct(count, narrow),
            struct(count, columns),
        ],
        compiler_params=params(),
        cost_estimate=LIGHT,
        name="popular_partials",
    )(select, packed, *weights)


def popular_middle(own, others, hid):
    rows, columns = own.shape

    def body(own_ref, *refs):
        parts, out_ref = refs[:-1], refs[-1]
        act = own_ref[...].astype(F32)
        for part in parts:
            act = act + part[...].astype(F32)
        for at in range(0, columns, 3 * hid):
            g = act[:, at : at + hid]
            u = act[:, at + hid : at + 2 * hid]
            dh = act[:, at + 2 * hid : at + 3 * hid]
            s = jax.nn.sigmoid(g)
            out_ref[:, at : at + hid] = (dh * u * s * (1.0 + g * (1.0 - s))).astype(BF)
            out_ref[:, at + hid : at + 2 * hid] = (dh * g * s).astype(BF)
            out_ref[:, at + 2 * hid : at + 3 * hid] = (g * s * u).astype(BF)

    return pl.pallas_call(
        body,
        in_specs=[INSIDE] * (1 + len(others)),
        out_specs=INSIDE,
        out_shape=struct(rows, columns),
        compiler_params=params(),
        cost_estimate=LIGHT,
        name="popular_middle",
    )(own, *others)


def popular_back(select, lines, x, s, weights, hid, scale):
    parts, count, spots = select.shape
    narrow = x.shape[1]
    m = len(weights)
    n = len(lines)
    columns = lines[0].shape[1]

    def body(sel_ref, x_ref, s_ref, *refs):
        ins, w_refs, back_ref = refs[:n], refs[n : n + m], refs[n + m]
        grads, mid_ref = refs[n + m + 1 : -1], refs[-1]
        stack_rows(ins, mid_ref)
        grad = None
        out = None
        at = 0
        for w_ref, g_ref in zip(w_refs, grads):
            for top in range(0, w_ref.shape[0], 3 * hid):
                d_gate = mid_ref[:, at : at + hid]
                d_up = mid_ref[:, at + hid : at + 2 * hid]
                hidden = mid_ref[:, at + 2 * hid : at + 3 * hid]
                sides = ((d_gate, x_ref), (d_up, x_ref), (hidden, s_ref))
                for i, (left, right) in enumerate(sides):
                    here = slice(top + i * hid, top + (i + 1) * hid)
                    product = mm(left, w_ref[here, :])
                    if i == 2:
                        out = product if out is None else out + product
                    else:
                        grad = product if grad is None else grad + product
                    g_ref[here, :] = (mm(left, right[...], TN) * scale).astype(BF)
                at += 3 * hid
        grad = grad.astype(BF)
        out = out.astype(BF)
        for q in range(parts):
            back_ref[:, q * narrow : (q + 1) * narrow] = mm(sel_ref[q], grad, TN).astype(BF)
            back_ref[:, (parts + q) * narrow : (parts + q + 1) * narrow] = mm(
                sel_ref[q], out, TN
            ).astype(BF)

    return pl.pallas_call(
        body,
        in_specs=[INSIDE] * (3 + n + m),
        out_specs=[INSIDE] * (1 + m),
        out_shape=[struct(spots, 2 * parts * narrow)]
        + [struct(w.shape[0], narrow) for w in weights],
        scratch_shapes=[pltpu.VMEM((count, columns), BF)],
        compiler_params=params(),
        cost_estimate=LIGHT,
        name="popular_back",
    )(select, x, s, *lines, *weights)


def slot_positions(route_block, count):
    flat = route_block.reshape(-1)
    onehot = (flat[:, None] == jnp.arange(count, dtype=jnp.int32)[None, :]).astype(jnp.int32)
    before = jnp.cumsum(onehot, axis=0) - onehot
    return (flat, jnp.sum(before * onehot, axis=1))


def exchange(blocks):
    return lax.all_to_all(blocks, "expert", split_axis=0, concat_axis=0, tiled=True)


def local(
    tokens, cotangent, routes, gates, hot_index, hot_gate, w_gate_up, w_down, w_hot_gu, w_hot_dn
):
    owners = lax.axis_size("expert")
    groups = lax.axis_size("dp")
    cores = 2 if groups % 2 == 0 else 1
    chips = groups // cores
    tok_dev, width_d = tokens.shape
    topk = routes.shape[1]
    slots = max(2, 3 * tok_dev * topk // (2 * owners))
    entries = tok_dev * topk
    rows = owners * slots
    inverse = 1.0 / (4 * groups)
    me = lax.axis_index("dp")
    chip, core = me // cores, me % cores

    def shift(value, r):
        pairs = [
            (i, ((i // cores + r) % chips) * cores + i % cores) for i in range(groups)
        ]
        return lax.ppermute(value, "dp", pairs)

    def swap(value):
        pairs = [(i, (i // cores) * cores + (i + 1) % cores) for i in range(groups)]
        return lax.ppermute(value, "dp", pairs)

    order = jnp.stack(
        [
            ((chip - r) % chips) * cores + (core + k) % cores
            for k in range(cores)
            for r in range(chips)
        ]
    ).astype(jnp.int32)

    across = 1
    while 2 * (2 * across) ** 2 <= owners:
        across *= 2
    depths = owners // across
    spot = lax.axis_index("expert")

    def hop(value, j):
        return lax.ppermute(value, "expert", [(i, i ^ j) for i in range(owners)])

    wide = width_d // groups
    hid = w_hot_dn.shape[0]
    narrow = width_d // owners
    hot_w = jnp.concatenate([w_hot_gu, w_hot_dn[None]], axis=0).reshape(3 * hid, narrow)
    hot_near = [hot_w] + [shift(hot_w, r) for r in range(1, chips)]
    down_own = after(w_down[0], hot_near[-1])
    gu_own = after(w_gate_up[0], hot_near[-1])
    gu_near = [w_gate_up[0]] + [shift(gu_own, r) for r in range(1, chips)]
    down_near = [w_down[0]] + [shift(down_own, r) for r in range(1, chips)]

    flat, pos = slot_positions(routes, owners)
    dest = flat * slots + pos
    slot_ids = jnp.arange(rows, dtype=jnp.int32)[:, None]
    pick = (slot_ids == dest[None, :]).astype(BF)

    def as_rows(value, width):
        value = value.reshape(owners, -1)
        spare = -value.shape[1] % width
        return jnp.pad(value, ((0, 0), (0, spare))).reshape(owners, -1, width)

    hot_dev = hot_index.shape[0]
    few = 2 * hot_dev // PIECES
    hot_pick = (
        hot_index[:, None] == jnp.arange(tok_dev, dtype=jnp.int32)[None, :]
    ).astype(BF)
    hot_x = mm(hot_pick, tokens).astype(BF)
    hot_s = (hot_gate[:, None] * mm(hot_pick, cotangent)).astype(BF)
    hot_send = jnp.concatenate([hot_x, hot_s], axis=0).reshape(PIECES, few, owners, narrow)
    hot_send = hot_send.transpose(2, 1, 0, 3).reshape(owners * few, PIECES * narrow)
    packed_id = jnp.arange(owners * few, dtype=jnp.int32)
    turn = ((packed_id ^ (spot * few))[:, None] == packed_id[None, :]).astype(BF)
    row = jnp.arange(owners * hot_dev, dtype=jnp.int32)
    step = row // hot_dev
    piece = (row % hot_dev) // few

    def selection(index):
        hit = (index * few + row % few)[:, None] == packed_id[None, :]
        return jnp.stack([hit & (piece == q)[:, None] for q in range(PIECES // 2)]).astype(BF)

    hot_send = mm(turn, hot_send).astype(BF).reshape(depths, across, few, PIECES * narrow)
    near = [hot_send[0]] + [hop(hot_send[j], j * across) for j in range(1, depths)]
    near = jnp.stack(near, axis=1)
    hot_recv = jnp.concatenate([near[0]] + [hop(near[j], j) for j in range(1, across)])
    hot_recv = hot_recv.reshape(owners * few, PIECES * narrow)

    scaled = (gates[:, :, None] * cotangent[:, None, :].astype(F32)).astype(BF)
    send_s = mm(pick, scaled.reshape(entries, width_d)).astype(BF)
    rows_s = exchange(send_s.reshape(owners, slots, width_d)).reshape(rows, width_d)

    tok_rel = jnp.concatenate(
        [
            lax.dynamic_slice_in_dim(tokens, order[j] * wide, wide, 1)
            for j in range(groups)
        ],
        axis=1,
    )
    tok_rel = jnp.repeat(tok_rel, topk, axis=0) if topk > 1 else tok_rel
    send_x = mm(pick, tok_rel).astype(BF).reshape(owners, slots, width_d)
    rows_x = exchange(send_x).reshape(rows, width_d)

    hot_near = jnp.concatenate(list(after(tuple(hot_near), send_x)), axis=0)
    hot_ws = [hot_near] + ([swap(hot_near)] if cores == 2 else [])
    hot_x, hot_s, partial = popular_partials(selection(step), hot_recv, hot_ws, hid)
    share = depths * hot_dev
    level_in = [hop(partial[j * share : (j + 1) * share], j) for j in range(1, across)]
    gu_far = down_far = []
    if cores == 2:
        gu_near = list(after(tuple(gu_near), rows_x))
        gu_far = [swap(block) for block in gu_near[1:]]
    level_in = list(after(tuple(level_in), rows_s, *gu_near[1:]))
    level = partial[:share].astype(F32)
    for value in level_in:
        level = level + value.astype(F32)
    level = level.astype(BF)
    level = [level[j * hot_dev : (j + 1) * hot_dev] for j in range(depths)]
    depth_in = [hop(level[j], j * across) for j in range(1, depths)]
    rows_x = after(rows_x, *depth_in)
    hot_own = popular_middle(level[0], depth_in, hid)
    line = [hot_own] + [hop(hot_own, j * across) for j in range(1, depths)]
    down_near = list(after(tuple(down_near), hot_own))
    if cores == 2:
        gu_far = [swap(after(w_gate_up[0], hot_own))] + gu_far
        down_far = [swap(block) for block in down_near]
    back, hidden, d_act = expert(order, rows_s, after(rows_x, hot_own), gu_near + gu_far, down_near + down_far)

    def columns_of(r):
        return jnp.concatenate(
            [
                rows_x[:, (k * chips + r) * wide : (k * chips + r + 1) * wide]
                for k in range(cores)
            ],
            axis=1,
        )

    xs = [columns_of(0)] + [shift(columns_of(r), -r) for r in range(1, chips)]
    ds = [d_act] + [shift(d_act, -r) for r in range(1, chips)]
    back = after(back, *line[1:])
    back = exchange(back.reshape(owners, slots, 2 * width_d)).reshape(rows, 2 * width_d)

    line = jnp.concatenate(list(after(tuple(line), d_act)))
    lines = [line] + [hop(line, j) for j in range(1, across)]
    hot_back, *hot_grads = popular_back(
        selection(step), lines, hot_x, hot_s, hot_ws, hid, inverse
    )

    dn_parts = down_grads(order, hidden, rows_s, width_d, groups, inverse)
    dn_sum = list(dn_parts[:chips])
    if cores == 2:
        dn_in = [swap(part) for part in dn_parts[chips:]]
        dn_sum = [
            (one.astype(F32) + two.astype(F32)).astype(BF) for one, two in zip(dn_sum, dn_in)
        ]
    dn_total = dn_sum[0].astype(F32)
    dn_recv = [shift(dn_sum[r], -r) for r in range(1, chips)]
    for value in dn_recv:
        dn_total = dn_total + value.astype(F32)
    grad_dn = dn_total.astype(BF)

    hot_back = hot_back.reshape(across, depths, few, PIECES * narrow)
    hot_back = [hot_back[0]] + [hop(hot_back[j], j) for j in range(1, across)]
    hot_back = jnp.stack(hot_back, axis=1)
    xs_late = list(after(tuple(xs), d_act))
    gu_in = None
    if cores == 2:
        gu_in = swap(gate_up_grads(xs_late, ds, 1, wide, inverse, None))

    hot_sum = hot_grads[0]
    if cores == 2:
        hot_sum = after(hot_sum, dn_in[0])
    if cores == 2:
        hot_sum = (hot_sum.astype(F32) + swap(hot_grads[1]).astype(F32)).astype(BF)
    hot_sum = hot_sum.reshape(chips, 3 * hid, narrow)
    hot_total = hot_sum[0].astype(F32)
    hot_far = [shift(hot_sum[r], -r) for r in range(1, chips)]
    for value in hot_far:
        hot_total = hot_total + value.astype(F32)
    grad_hot = hot_total.astype(BF).reshape(3, hid, narrow)
    xs_last = list(after(tuple(xs_late), *hot_far, *dn_recv))
    grad_gu = gate_up_grads(xs_last, ds, 0, wide, inverse, gu_in)

    if cores == 2:
        hot_back = after(hot_back, gu_in)
    hot_back = [hot_back[0]] + [hop(hot_back[j], j * across) for j in range(1, depths)]
    hot_back = list(after(tuple(hot_back), grad_gu))
    hot_back = jnp.concatenate(hot_back).reshape(owners * few, PIECES * narrow)
    hot_back = mm(turn, hot_back).astype(BF)

    hot_back = hot_back.reshape(owners, few, PIECES, narrow)
    hot_back = hot_back.transpose(2, 1, 0, 3).reshape(2, hot_dev, width_d)
    landed = mm(pick, back, TN)
    picked = landed[:, :width_d]
    layer_out = (
        (gates.reshape(entries)[:, None] * picked).reshape(tok_dev, topk, width_d).sum(axis=1)
    )
    token_gate = jnp.sum(jnp.where(hot_pick > 0, hot_gate[:, None], 0.0), axis=0)
    layer_out = layer_out + token_gate[:, None] * mm(hot_pick, hot_back[1], TN)
    returned = landed[:, width_d:]
    returned = returned.reshape(tok_dev, topk, width_d).sum(axis=1)
    blocks = jnp.stack([returned[:, j * wide : (j + 1) * wide] for j in range(groups)])
    input_grad = jnp.concatenate(
        [
            lax.dynamic_index_in_dim(
                blocks,
                ((q - core) % cores) * chips + (chip - p) % chips,
                0,
                keepdims=False,
            )
            for p in range(chips)
            for q in range(cores)
        ],
        axis=1,
    )
    input_grad = input_grad + mm(hot_pick, hot_back[0], TN)
    return (
        layer_out.astype(BF),
        input_grad.astype(BF),
        grad_gu[None],
        grad_dn[None],
        grad_hot[:2],
        grad_hot[2],
    )


def solution(mesh):
    tok = P(("dp", "expert"), None)
    flat = P(("dp", "expert"))
    rows = P("expert", "dp", None)
    hot = (P(None, "dp", "expert"), P("dp", "expert"))
    return jax.shard_map(
        local,
        mesh=mesh,
        in_specs=(tok, tok, tok, tok, flat, flat, rows, rows) + hot,
        out_specs=(tok, tok, rows, rows) + hot,
        check_vma=False,
    )
```

```python
import jax
import jax.numpy as jnp
from jax import lax
from jax.experimental import pallas as pl
from jax.experimental.pallas import tpu as pltpu
from jax.sharding import PartitionSpec as P

BF = jnp.bfloat16
F32 = jnp.float32
NN = (((1,), (0,)), ((), ()))
NT = (((1,), (1,)), ((), ()))
TN = (((0,), (0,)), ((), ()))
ROOM = 56 * 1024 * 1024
LIGHT = pl.CostEstimate(flops=1, bytes_accessed=1, transcendentals=0)
SMEM = pl.BlockSpec(memory_space=pltpu.SMEM)
ANYWHERE = pl.BlockSpec(memory_space=pl.ANY)
INSIDE = pl.BlockSpec(memory_space=pltpu.VMEM)
PIECES = 8


def mm(a, b, dims=NN):
    return lax.dot_general(a, b, dims, preferred_element_type=F32)


def after(value, *earlier):
    return lax.optimization_barrier((value,) + earlier)[0]


def params():
    return pltpu.CompilerParams(vmem_limit_bytes=ROOM)


LIGHT = pl.CostEstimate(flops=1, bytes_accessed=1, transcendentals=0)


def struct(*shape, dtype=BF):
    return jax.ShapeDtypeStruct(shape, dtype)


def whole(array):
    return pl.BlockSpec(array.shape, lambda *_: (0,) * len(array.shape))


def stack_rows(refs, scratch):
    rows = refs[0].shape[0]
    for i, ref in enumerate(refs):
        scratch[i * rows : (i + 1) * rows, :] = ref[...]


def fetch(order_ref, blocks, w_ref, sems):
    deep = blocks[0].shape[0]
    copies = []
    for j, block in enumerate(blocks):
        place = pl.multiple_of(order_ref[j] * deep, deep)
        copies.append(pltpu.make_async_copy(block, w_ref.at[pl.ds(place, deep)], sems.at[j]))
        copies[-1].start()
    return copies


def down_scratch(blocks):
    deep, width = blocks[0].shape
    return [pltpu.VMEM((len(blocks) * deep, width), BF), pltpu.SemaphoreType.DMA((len(blocks),))]


def fetch_each(blocks, w_ref, sems):
    copies = []
    for j, block in enumerate(blocks):
        copies.append(pltpu.make_async_copy(block, w_ref.at[j], sems.at[j]))
        copies[-1].start()
    return copies


def each_scratch(blocks):
    return [
        pltpu.VMEM((len(blocks),) + blocks[0].shape, BF),
        pltpu.SemaphoreType.DMA((len(blocks),)),
    ]


def expert(order, rows_s, rows_x, w_gu, w_down):
    rows = rows_s.shape[0]
    depth, width = w_gu[0].shape
    deep, wide = w_down[0].shape
    half = width // 2
    m = len(w_gu)
    step = 512 if wide % 512 == 0 else wide

    def body(order_ref, s_ref, x_ref, *refs):
        gu_in, dn_in, rest = refs[:m], refs[m : 2 * m], refs[2 * m :]
        back_ref, hid_ref, d_ref, acc, gu_ref, gu_sems, dn_ref, dn_sems = rest
        gu_copies = fetch_each(gu_in, gu_ref, gu_sems)
        dn_copies = fetch(order_ref, dn_in, dn_ref, dn_sems)
        for j, copy in enumerate(gu_copies):
            copy.wait()
            found = mm(x_ref[:, j * depth : (j + 1) * depth], gu_ref[j])
            if j == 0:
                acc[...] = found
            else:
                acc[...] += found
        g = acc[:, :half]
        u = acc[:, half:]
        s = jax.nn.sigmoid(g)
        hid_ref[...] = (g * s * u).astype(BF)
        for copy in dn_copies:
            copy.wait()
        d_hidden = mm(s_ref[...], dn_ref[...], NT)
        d_ref[:, :half] = (d_hidden * u * s * (1.0 + g * (1.0 - s))).astype(BF)
        d_ref[:, half:] = (d_hidden * g * s).astype(BF)
        for j in range(m):
            at = wide + j * depth
            back_ref[:, at : at + depth] = mm(d_ref[...], gu_ref[j], NT).astype(BF)
        for c in range(0, wide, step):
            back_ref[:, c : c + step] = mm(hid_ref[...], dn_ref[:, c : c + step]).astype(BF)

    return pl.pallas_call(
        body,
        in_specs=[SMEM, INSIDE, INSIDE] + [ANYWHERE] * (2 * m),
        out_specs=[INSIDE] * 3,
        out_shape=[struct(rows, 2 * wide), struct(rows, half), struct(rows, width)],
        scratch_shapes=[pltpu.VMEM((rows, width), F32)]
        + each_scratch(w_gu)
        + down_scratch(w_down),
        compiler_params=params(),
        cost_estimate=LIGHT,
        name="expert",
    )(order, rows_s, rows_x, *w_gu, *w_down)


def gate_up_grads(xs, ds, k, wide, scale, received):
    n, rows, width = len(xs), xs[0].shape[0], ds[0].shape[1]
    step = 512 if width % 512 == 0 else width
    extra = [] if received is None else [received]
    if wide % 128 != 0:
        xs, k = [x[:, k * wide : (k + 1) * wide] for x in xs], 0

    def body(*refs):
        x_refs, d_refs, rest = refs[:n], refs[n : 2 * n], refs[2 * n :]
        out_ref, x_scr, d_scr = rest[-3:]

        @pl.when(pl.program_id(0) == 0)
        def _():
            stack_rows(x_refs, x_scr)

        stack_rows(d_refs, d_scr)
        found = mm(x_scr[...], d_scr[...], TN) * scale
        if extra:
            found = found + rest[0][...].astype(F32)
        out_ref[...] = found.astype(BF)

    shape = struct(wide, width)
    column = lambda i: (0, i)
    return pl.pallas_call(
        body,
        grid=(width // step,),
        in_specs=[pl.BlockSpec((rows, wide), lambda i: (0, k))] * n
        + [pl.BlockSpec((rows, step), column)] * n
        + [pl.BlockSpec((wide, step), column)] * len(extra),
        out_specs=pl.BlockSpec((wide, step), column),
        out_shape=shape,
        scratch_shapes=[pltpu.VMEM((n * rows, wide), BF), pltpu.VMEM((n * rows, step), BF)],
        compiler_params=params(),
        cost_estimate=LIGHT,
        name="gate_up_grads",
    )(*xs, *ds, *extra)


def down_grads(order, hidden, rows_s, wide, count, scale):
    rows, half = hidden.shape
    deep = half // count
    step = 512 if wide % 512 == 0 else wide

    def body(order_ref, h_ref, s_ref, *refs):
        outs, scratch = refs[:count], refs[count]
        scratch[...] = mm(h_ref[...], s_ref[...], TN) * scale
        for j in range(count):
            place = pl.multiple_of(order_ref[j] * deep, deep)
            outs[j][...] = scratch[pl.ds(place, deep), :].astype(BF)

    shapes = [struct(deep, wide)] * count
    return pl.pallas_call(
        body,
        grid=(wide // step,),
        in_specs=[SMEM, whole(hidden), pl.BlockSpec((rows, step), lambda i: (0, i))],
        out_specs=[pl.BlockSpec((deep, step), lambda i: (0, i))] * count,
        out_shape=shapes,
        scratch_shapes=[pltpu.VMEM((half, step), F32)],
        compiler_params=params(),
        cost_estimate=LIGHT,
        name="down_grads",
    )(order, hidden, rows_s)


def popular_partials(select, packed, weights, hid):
    parts, count = select.shape[:2]
    narrow = packed.shape[1] // (2 * parts)
    columns = sum(w.shape[0] for w in weights)

    def body(sel_ref, in_ref, *refs):
        w_refs, (x_ref, s_ref, p_ref) = refs[: len(weights)], refs[len(weights) :]
        x = None
        s = None
        for q in range(parts):
            rows = mm(sel_ref[q], in_ref[...])
            one = rows[:, q * narrow : (q + 1) * narrow]
            two = rows[:, (parts + q) * narrow : (parts + q + 1) * narrow]
            x = one if x is None else x + one
            s = two if s is None else s + two
        x = x.astype(BF)
        s = s.astype(BF)
        x_ref[...] = x
        s_ref[...] = s
        at = 0
        for w_ref in w_refs:
            for top in range(0, w_ref.shape[0], 3 * hid):
                p_ref[:, at : at + 2 * hid] = mm(x, w_ref[top : top + 2 * hid, :], NT).astype(BF)
                p_ref[:, at + 2 * hid : at + 3 * hid] = mm(
                    s, w_ref[top + 2 * hid : top + 3 * hid, :], NT
                ).astype(BF)
                at += 3 * hid

    return pl.pallas_call(
        body,
        in_specs=[INSIDE] * (2 + len(weights)),
        out_specs=[INSIDE] * 3,
        out_shape=[
            struct(count, narrow),
            struct(count, narrow),
            struct(count, columns),
        ],
        compiler_params=params(),
        cost_estimate=LIGHT,
        name="popular_partials",
    )(select, packed, *weights)


def popular_middle(own, others, hid):
    rows, columns = own.shape

    def body(own_ref, *refs):
        parts, out_ref = refs[:-1], refs[-1]
        act = own_ref[...].astype(F32)
        for part in parts:
            act = act + part[...].astype(F32)
        for at in range(0, columns, 3 * hid):
            g = act[:, at : at + hid]
            u = act[:, at + hid : at + 2 * hid]
            dh = act[:, at + 2 * hid : at + 3 * hid]
            s = jax.nn.sigmoid(g)
            out_ref[:, at : at + hid] = (dh * u * s * (1.0 + g * (1.0 - s))).astype(BF)
            out_ref[:, at + hid : at + 2 * hid] = (dh * g * s).astype(BF)
            out_ref[:, at + 2 * hid : at + 3 * hid] = (g * s * u).astype(BF)

    return pl.pallas_call(
        body,
        in_specs=[INSIDE] * (1 + len(others)),
        out_specs=INSIDE,
        out_shape=struct(rows, columns),
        compiler_params=params(),
        cost_estimate=LIGHT,
        name="popular_middle",
    )(own, *others)


def popular_back(select, lines, x, s, weights, hid, scale):
    parts, count, spots = select.shape
    narrow = x.shape[1]
    m = len(weights)
    n = len(lines)
    columns = lines[0].shape[1]

    def body(sel_ref, x_ref, s_ref, *refs):
        ins, w_refs, back_ref = refs[:n], refs[n : n + m], refs[n + m]
        grads, mid_ref = refs[n + m + 1 : -1], refs[-1]
        stack_rows(ins, mid_ref)
        grad = None
        out = None
        at = 0
        for w_ref, g_ref in zip(w_refs, grads):
            for top in range(0, w_ref.shape[0], 3 * hid):
                d_gate = mid_ref[:, at : at + hid]
                d_up = mid_ref[:, at + hid : at + 2 * hid]
                hidden = mid_ref[:, at + 2 * hid : at + 3 * hid]
                sides = ((d_gate, x_ref), (d_up, x_ref), (hidden, s_ref))
                for i, (left, right) in enumerate(sides):
                    here = slice(top + i * hid, top + (i + 1) * hid)
                    product = mm(left, w_ref[here, :])
                    if i == 2:
                        out = product if out is None else out + product
                    else:
                        grad = product if grad is None else grad + product
                    g_ref[here, :] = (mm(left, right[...], TN) * scale).astype(BF)
                at += 3 * hid
        grad = grad.astype(BF)
        out = out.astype(BF)
        for q in range(parts):
            back_ref[:, q * narrow : (q + 1) * narrow] = mm(sel_ref[q], grad, TN).astype(BF)
            back_ref[:, (parts + q) * narrow : (parts + q + 1) * narrow] = mm(
                sel_ref[q], out, TN
            ).astype(BF)

    return pl.pallas_call(
        body,
        in_specs=[INSIDE] * (3 + n + m),
        out_specs=[INSIDE] * (1 + m),
        out_shape=[struct(spots, 2 * parts * narrow)]
        + [struct(w.shape[0], narrow) for w in weights],
        scratch_shapes=[pltpu.VMEM((count, columns), BF)],
        compiler_params=params(),
        cost_estimate=LIGHT,
        name="popular_back",
    )(select, x, s, *lines, *weights)


def slot_positions(route_block, count):
    flat = route_block.reshape(-1)
    onehot = (flat[:, None] == jnp.arange(count, dtype=jnp.int32)[None, :]).astype(jnp.int32)
    before = jnp.cumsum(onehot, axis=0) - onehot
    return (flat, jnp.sum(before * onehot, axis=1))


def exchange(blocks):
    return lax.all_to_all(blocks, "expert", split_axis=0, concat_axis=0, tiled=True)


def local(
    tokens, cotangent, routes, gates, hot_index, hot_gate, w_gate_up, w_down, w_hot_gu, w_hot_dn
):
    owners = lax.axis_size("expert")
    groups = lax.axis_size("dp")
    cores = 2 if groups % 2 == 0 else 1
    chips = groups // cores
    tok_dev, width_d = tokens.shape
    topk = routes.shape[1]
    slots = max(2, 3 * tok_dev * topk // (2 * owners))
    entries = tok_dev * topk
    rows = owners * slots
    inverse = 1.0 / (4 * groups)
    me = lax.axis_index("dp")
    chip, core = me // cores, me % cores

    def shift(value, r):
        pairs = [
            (i, ((i // cores + r) % chips) * cores + i % cores) for i in range(groups)
        ]
        return lax.ppermute(value, "dp", pairs)

    def swap(value):
        pairs = [(i, (i // cores) * cores + (i + 1) % cores) for i in range(groups)]
        return lax.ppermute(value, "dp", pairs)

    order = jnp.stack(
        [
            ((chip - r) % chips) * cores + (core + k) % cores
            for k in range(cores)
            for r in range(chips)
        ]
    ).astype(jnp.int32)

    across = 1
    while 2 * (2 * across) ** 2 <= owners:
        across *= 2
    depths = owners // across
    spot = lax.axis_index("expert")

    def hop(value, j):
        return lax.ppermute(value, "expert", [(i, i ^ j) for i in range(owners)])

    wide = width_d // groups
    hid = w_hot_dn.shape[0]
    narrow = width_d // owners
    hot_w = jnp.concatenate([w_hot_gu, w_hot_dn[None]], axis=0).reshape(3 * hid, narrow)
    hot_near = [hot_w] + [shift(hot_w, r) for r in range(1, chips)]
    down_own = after(w_down[0], hot_near[-1])
    gu_own = after(w_gate_up[0], hot_near[-1])
    gu_near = [w_gate_up[0]] + [shift(gu_own, r) for r in range(1, chips)]
    down_near = [w_down[0]] + [shift(down_own, r) for r in range(1, chips)]

    flat, pos = slot_positions(routes, owners)
    dest = flat * slots + pos
    slot_ids = jnp.arange(rows, dtype=jnp.int32)[:, None]
    pick = (slot_ids == dest[None, :]).astype(BF)

    def as_rows(value, width):
        value = value.reshape(owners, -1)
        spare = -value.shape[1] % width
        return jnp.pad(value, ((0, 0), (0, spare))).reshape(owners, -1, width)

    hot_dev = hot_index.shape[0]
    few = 2 * hot_dev // PIECES
    hot_pick = (
        hot_index[:, None] == jnp.arange(tok_dev, dtype=jnp.int32)[None, :]
    ).astype(BF)
    hot_x = mm(hot_pick, tokens).astype(BF)
    hot_s = (hot_gate[:, None] * mm(hot_pick, cotangent)).astype(BF)
    hot_send = jnp.concatenate([hot_x, hot_s], axis=0).reshape(PIECES, few, owners, narrow)
    hot_send = hot_send.transpose(2, 1, 0, 3).reshape(owners * few, PIECES * narrow)
    packed_id = jnp.arange(owners * few, dtype=jnp.int32)
    turn = ((packed_id ^ (spot * few))[:, None] == packed_id[None, :]).astype(BF)
    row = jnp.arange(owners * hot_dev, dtype=jnp.int32)
    step = row // hot_dev
    piece = (row % hot_dev) // few

    def selection(index):
        hit = (index * few + row % few)[:, None] == packed_id[None, :]
        return jnp.stack([hit & (piece == q)[:, None] for q in range(PIECES // 2)]).astype(BF)

    hot_send = mm(turn, hot_send).astype(BF).reshape(depths, across, few, PIECES * narrow)
    near = [hot_send[0]] + [hop(hot_send[j], j * across) for j in range(1, depths)]
    near = jnp.stack(near, axis=1)
    hot_recv = jnp.concatenate([near[0]] + [hop(near[j], j) for j in range(1, across)])
    hot_recv = hot_recv.reshape(owners * few, PIECES * narrow)

    scaled = (gates[:, :, None] * cotangent[:, None, :].astype(F32)).astype(BF)
    send_s = mm(pick, scaled.reshape(entries, width_d)).astype(BF)
    rows_s = exchange(send_s.reshape(owners, slots, width_d)).reshape(rows, width_d)

    tok_rel = jnp.concatenate(
        [
            lax.dynamic_slice_in_dim(tokens, order[j] * wide, wide, 1)
            for j in range(groups)
        ],
        axis=1,
    )
    tok_rel = jnp.repeat(tok_rel, topk, axis=0) if topk > 1 else tok_rel
    send_x = mm(pick, tok_rel).astype(BF).reshape(owners, slots, width_d)
    rows_x = exchange(send_x).reshape(rows, width_d)

    hot_near = jnp.concatenate(list(after(tuple(hot_near), send_x)), axis=0)
    hot_ws = [hot_near] + ([swap(hot_near)] if cores == 2 else [])
    hot_x, hot_s, partial = popular_partials(selection(step), hot_recv, hot_ws, hid)
    share = depths * hot_dev
    level_in = [hop(partial[j * share : (j + 1) * share], j) for j in range(1, across)]
    gu_far = down_far = []
    if cores == 2:
        gu_near = list(after(tuple(gu_near), rows_x))
        gu_far = [swap(block) for block in gu_near[1:]]
    level_in = list(after(tuple(level_in), rows_s, *gu_near[1:]))
    level = partial[:share].astype(F32)
    for value in level_in:
        level = level + value.astype(F32)
    level = level.astype(BF)
    level = [level[j * hot_dev : (j + 1) * hot_dev] for j in range(depths)]
    depth_in = [hop(level[j], j * across) for j in range(1, depths)]
    rows_x = after(rows_x, *depth_in)
    hot_own = popular_middle(level[0], depth_in, hid)
    line = [hot_own] + [hop(hot_own, j * across) for j in range(1, depths)]
    down_near = list(after(tuple(down_near), hot_own))
    if cores == 2:
        gu_far = [swap(after(w_gate_up[0], hot_own))] + gu_far
        down_far = [swap(block) for block in down_near]
    back, hidden, d_act = expert(order, rows_s, after(rows_x, hot_own), gu_near + gu_far, down_near + down_far)

    def columns_of(r):
        return jnp.concatenate(
            [
                rows_x[:, (k * chips + r) * wide : (k * chips + r + 1) * wide]
                for k in range(cores)
            ],
            axis=1,
        )

    xs = [columns_of(0)] + [shift(columns_of(r), -r) for r in range(1, chips)]
    ds = [d_act] + [shift(d_act, -r) for r in range(1, chips)]
    back = after(back, *line[1:])
    back = exchange(back.reshape(owners, slots, 2 * width_d)).reshape(rows, 2 * width_d)

    line = jnp.concatenate(list(after(tuple(line), d_act)))
    lines = [line] + [hop(line, j) for j in range(1, across)]
    hot_back, *hot_grads = popular_back(
        selection(step), lines, hot_x, hot_s, hot_ws, hid, inverse
    )

    dn_parts = down_grads(order, hidden, rows_s, width_d, groups, inverse)
    dn_sum = list(dn_parts[:chips])
    if cores == 2:
        dn_in = [swap(part) for part in dn_parts[chips:]]
        dn_sum = [
            (one.astype(F32) + two.astype(F32)).astype(BF) for one, two in zip(dn_sum, dn_in)
        ]
    dn_total = dn_sum[0].astype(F32)
    dn_recv = [shift(dn_sum[r], -r) for r in range(1, chips)]
    for value in dn_recv:
        dn_total = dn_total + value.astype(F32)
    grad_dn = dn_total.astype(BF)

    hot_back = hot_back.reshape(across, depths, few, PIECES * narrow)
    hot_back = [hot_back[0]] + [hop(hot_back[j], j) for j in range(1, across)]
    hot_back = jnp.stack(hot_back, axis=1)
    xs_late = list(after(tuple(xs), d_act))
    gu_in = None
    if cores == 2:
        gu_in = swap(gate_up_grads(xs_late, ds, 1, wide, inverse, None))

    hot_sum = hot_grads[0]
    if cores == 2:
        hot_sum = after(hot_sum, dn_in[0])
    if cores == 2:
        hot_sum = (hot_sum.astype(F32) + swap(hot_grads[1]).astype(F32)).astype(BF)
    hot_sum = hot_sum.reshape(chips, 3 * hid, narrow)
    hot_total = hot_sum[0].astype(F32)
    hot_far = [shift(hot_sum[r], -r) for r in range(1, chips)]
    for value in hot_far:
        hot_total = hot_total + value.astype(F32)
    grad_hot = hot_total.astype(BF).reshape(3, hid, narrow)
    xs_last = list(after(tuple(xs_late), *hot_far, *dn_recv))
    grad_gu = gate_up_grads(xs_last, ds, 0, wide, inverse, gu_in)

    hot_back = [hot_back[0]] + [hop(hot_back[j], j * across) for j in range(1, depths)]
    hot_back = list(after(tuple(hot_back), grad_gu))
    hot_back = jnp.concatenate(hot_back).reshape(owners * few, PIECES * narrow)
    hot_back = mm(turn, hot_back).astype(BF)

    hot_back = hot_back.reshape(owners, few, PIECES, narrow)
    hot_back = hot_back.transpose(2, 1, 0, 3).reshape(2, hot_dev, width_d)
    landed = mm(pick, back, TN)
    picked = landed[:, :width_d]
    layer_out = (
        (gates.reshape(entries)[:, None] * picked).reshape(tok_dev, topk, width_d).sum(axis=1)
    )
    token_gate = jnp.sum(jnp.where(hot_pick > 0, hot_gate[:, None], 0.0), axis=0)
    layer_out = layer_out + token_gate[:, None] * mm(hot_pick, hot_back[1], TN)
    returned = landed[:, width_d:]
    returned = returned.reshape(tok_dev, topk, width_d).sum(axis=1)
    blocks = jnp.stack([returned[:, j * wide : (j + 1) * wide] for j in range(groups)])
    input_grad = jnp.concatenate(
        [
            lax.dynamic_index_in_dim(
                blocks,
                ((q - core) % cores) * chips + (chip - p) % chips,
                0,
                keepdims=False,
            )
            for p in range(chips)
            for q in range(cores)
        ],
        axis=1,
    )
    input_grad = input_grad + mm(hot_pick, hot_back[0], TN)
    return (
        layer_out.astype(BF),
        input_grad.astype(BF),
        grad_gu[None],
        grad_dn[None],
        grad_hot[:2],
        grad_hot[2],
    )


def solution(mesh):
    tok = P(("dp", "expert"), None)
    flat = P(("dp", "expert"))
    rows = P("expert", "dp", None)
    hot = (P(None, "dp", "expert"), P("dp", "expert"))
    return jax.shard_map(
        local,
        mesh=mesh,
        in_specs=(tok, tok, tok, tok, flat, flat, rows, rows) + hot,
        out_specs=(tok, tok, rows, rows) + hot,
        check_vma=False,
    )
```
